32 devices in a mesh: rep: 8 (over z, core), shard: 4 (over y, x).
Axes of the slice: x: 2, y: 2, z: 4, core: 2. Of those that a mesh axis runs over, the one named last changes fastest.
Arguments:
- tokens: bfloat16 [6144, 2304], P(('rep', 'shard')), may hold values from -7 to 7
- seg_ids: int32 [6144], P(('rep', 'shard')), may hold values from 0 to 13, as said below
- parents: int32 [8, 13], P('rep'), may hold values from 0 to 12, as said below
- attn_gain: bfloat16 [2304], replicated, may hold values from 0.25 to 1.75
- w_query: bfloat16 [2304, 2048], P('shard'), may hold values from -1 to 1
- w_key: bfloat16 [2304, 1024], P('shard'), may hold values from -1 to 1
- w_value: bfloat16 [2304, 1024], P('shard'), may hold values from -0.125 to 0.125
- w_out: bfloat16 [2048, 2304], P('shard'), may hold values from -0.125 to 0.125
- post_attn_gain: bfloat16 [2304], replicated, may hold values from 0.25 to 1.75
- ffn_gain: bfloat16 [2304], replicated, may hold values from 0.25 to 1.75
- w_gate: bfloat16 [2304, 9216], P(None, 'shard'), may hold values from -0.125 to 0.125
- w_up: bfloat16 [2304, 9216], P(None, 'shard'), may hold values from -0.125 to 0.125
- w_down: bfloat16 [9216, 2304], P('shard'), may hold values from -0.0625 to 0.0625
- post_ffn_gain: bfloat16 [2304], replicated, may hold values from 0.25 to 1.75
- cotangent: bfloat16 [6144, 2304], P(('rep', 'shard')), may hold values from -6 to 6
Outputs:
- output: bfloat16 [6144, 2304], P(('rep', 'shard'))
- grad_tokens: bfloat16 [6144, 2304], P(('rep', 'shard'))
- attn_gain_grad: float32 [2304], replicated
- query_grad: float32 [2304, 2048], P('shard')
- key_grad: float32 [2304, 1024], P('shard')
- value_grad: float32 [2304, 1024], P('shard')
- out_grad: float32 [2048, 2304], P('shard')
- post_attn_gain_grad: float32 [2304], replicated
- ffn_gain_grad: float32 [2304], replicated
- gate_grad: float32 [2304, 9216], P(None, 'shard')
- up_grad: float32 [2304, 9216], P(None, 'shard')
- down_grad: float32 [9216, 2304], P('shard')
- post_ffn_gain_grad: float32 [2304], replicated
The draws below stay inside these ranges and needn't reach their ends.
Inputs may be any that keep to these rules, and one draw needn't show every extreme that they name: `seg_ids`: within each block of 768 tokens (one index of rep) the segments form one tree of 13: a root, four children of the root and two children of each of these. A segment's tokens are contiguous, a multiple of 12 in number, and come after its parent's; the root begins the block. Exactly the last 48 tokens of each block are padding and carry 13. `parents`: row r gives, for each segment of block r, its parent segment; the root's parent is the root itself.
All inputs are finite; a program needn't handle non-finite values.
Results may differ from the reference program's by a relative error of at most 0.024.
Values may be sent and summed in bfloat16 or wider, within the bound.
A program may use at most 640 MiB of HBM per device.

```python
import math
import jax
import jax.numpy as jnp
import numpy as np
from jax import lax

D = 2304
QUERY_HEADS = 8
KV = 4
HEAD_SIZE = 256
FF = 9216
SEGS = 13
GROUP = 768
UNIT = 12
TOKENS = 6144
N_REP = 8


def tree_layout(base):
    pieces = jax.random.split(base, 3)
    branch = jax.random.randint(pieces[0], (N_REP, 4), 2, 6)
    leaves = jax.random.randint(pieces[1], (N_REP, 8), 1, 5)
    trunk = 60 - jnp.sum(branch, axis=1) - jnp.sum(leaves, axis=1)
    columns = [trunk[:, None]]
    for index in range(4):
        columns.append(branch[:, index:index + 1])
        columns.append(leaves[:, 2 * index:2 * index + 1])
        columns.append(leaves[:, 2 * index + 1:2 * index + 2])
    lengths = jnp.concatenate(columns, axis=1).astype(jnp.int32)
    labels = jax.vmap(lambda sub_key: jax.random.permutation(sub_key, SEGS))(jax.random.split(pieces[2], N_REP)).astype(jnp.int32)
    return (lengths, labels)


def token_slots(lengths):
    ends = jnp.cumsum(lengths, axis=1)
    units = jnp.arange(GROUP) // UNIT
    return jnp.sum((units[None, :, None] >= ends[:, None, :]).astype(jnp.int32), axis=2)


def common_direction(base):
    pieces = jax.random.split(jax.random.fold_in(base, 101), 3)
    feature_signs = (2 * jax.random.randint(pieces[0], (D,), 0, 2) - 1).astype(jnp.float32)
    head_signs = (2 * jax.random.randint(pieces[1], (KV, HEAD_SIZE), 0, 2) - 1).astype(jnp.float32)
    levels = jax.random.uniform(pieces[2], (KV,), jnp.float32, 0.4, 1.0)
    return (feature_signs, head_signs, levels)


def head_columns(head_signs, levels):
    reach = 0.5 * math.sqrt(D) / math.sqrt(1.25)
    lengths = jnp.sqrt(levels * (math.sqrt(D) * math.sqrt(HEAD_SIZE))) / reach
    return lengths[:, None] * head_signs * (1.0 / math.sqrt(HEAD_SIZE))


def draw_tokens(key, part):
    feature_signs, head_signs, levels = common_direction(key)
    key = jax.random.fold_in(key, 21)
    noise = jnp.clip(jax.random.normal(key, (TOKENS, D), jnp.float32), -6.0, 6.0)
    return (noise + 0.5 * feature_signs[None, :]).astype(jnp.bfloat16)


def draw_w_query(key, part):
    feature_signs, head_signs, levels = common_direction(key)
    key = jax.random.fold_in(key, 22)
    spread = jnp.clip(jax.random.normal(key, (D, QUERY_HEADS * HEAD_SIZE), jnp.float32), -6.0, 6.0) * (1.0 / math.sqrt(D))
    columns = jnp.repeat(head_columns(head_signs, levels), QUERY_HEADS // KV, axis=0).reshape(QUERY_HEADS * HEAD_SIZE)
    lifted = (feature_signs * (1.0 / math.sqrt(D)))[:, None] * columns[None, :]
    return (spread + lifted).astype(jnp.bfloat16)


def draw_w_key(key, part):
    feature_signs, head_signs, levels = common_direction(key)
    key = jax.random.fold_in(key, 23)
    spread = jnp.clip(jax.random.normal(key, (D, KV * HEAD_SIZE), jnp.float32), -6.0, 6.0) * (1.0 / math.sqrt(D))
    columns = head_columns(head_signs, levels).reshape(KV * HEAD_SIZE)
    lifted = (feature_signs * (1.0 / math.sqrt(D)))[:, None] * columns[None, :]
    return (spread + lifted).astype(jnp.bfloat16)


def draw_seg_ids(key, part):
    lengths, labels = tree_layout(key)
    slots = token_slots(lengths)
    segs = jnp.take_along_axis(labels, jnp.minimum(slots, SEGS - 1), axis=1)
    segs = jnp.where(slots < SEGS, segs, SEGS)
    return segs.reshape(TOKENS).astype(jnp.int32)


def draw_parents(key, part):
    lengths, labels = tree_layout(key)
    parent_slot = jnp.asarray(np.array([0, 0, 1, 1, 0, 4, 4, 0, 7, 7, 0, 10, 10], dtype=np.int32))
    inverse = jnp.argsort(labels, axis=1, stable=True).astype(jnp.int32)
    slot_parent = parent_slot[inverse]
    return jnp.take_along_axis(labels, slot_parent, axis=1).astype(jnp.int32)


def shard_levels(rng, shape, cuts, low, high):
    factor_of = 1.0
    for axis_at, parts in cuts:
        draws = jax.random.uniform(jax.random.fold_in(jax.random.fold_in(rng, 6), axis_at), (parts,), jnp.float32, low / len(cuts), high / len(cuts))
        factor_of = factor_of * jnp.repeat(jnp.exp(draws), shape[axis_at] // parts).reshape((-1,) + (1,) * (len(shape) - 1 - axis_at))
    return factor_of


def scatter_about(key, extent, scale, bound, cuts=(), kind=jnp.bfloat16):
    entries = jax.random.normal(key, extent, jnp.float32) * scale
    if len(cuts) > 0:
        entries = shard_levels(key, extent, cuts, -0.22, 0.18) * entries
    return jnp.clip(entries, min=-bound, max=bound).astype(kind)


def setup_inputs(seed: int = 0) -> dict:
    streams_of = jax.random.split(jax.random.key(seed), 16)
    tokens = draw_tokens(jax.random.fold_in(streams_of[15], 71), 0)
    seg_ids = draw_seg_ids(jax.random.fold_in(streams_of[15], 71), 0)
    parents = draw_parents(jax.random.fold_in(streams_of[15], 71), 0)
    attn_gain = jnp.clip(1.0 + 0.15 * jax.random.normal(streams_of[3], (D,), jnp.float32), 0.25, 1.75).astype(jnp.bfloat16)
    w_query = draw_w_query(jax.random.fold_in(streams_of[15], 71), 0)
    w_key = draw_w_key(jax.random.fold_in(streams_of[15], 71), 0)
    w_value = scatter_about(streams_of[6], (D, KV * HEAD_SIZE), D ** -0.5, 0.125, ((0, 4),))
    w_out = scatter_about(streams_of[7], (QUERY_HEADS * HEAD_SIZE, D), (QUERY_HEADS * HEAD_SIZE) ** -0.5, 0.125, ((0, 4),))
    post_attn_gain = jnp.clip(1.0 + 0.15 * jax.random.normal(streams_of[8], (D,), jnp.float32), 0.25, 1.75).astype(jnp.bfloat16)
    ffn_gain = jnp.clip(1.0 + 0.15 * jax.random.normal(streams_of[9], (D,), jnp.float32), 0.25, 1.75).astype(jnp.bfloat16)
    w_gate = scatter_about(streams_of[10], (D, FF), D ** -0.5, 0.125, ((1, 4),))
    w_up = scatter_about(streams_of[11], (D, FF), D ** -0.5, 0.125, ((1, 4),))
    w_down = scatter_about(streams_of[12], (FF, D), FF ** -0.5, 0.0625, ((0, 4),))
    post_ffn_gain = jnp.clip(1.0 + 0.15 * jax.random.normal(streams_of[13], (D,), jnp.float32), 0.25, 1.75).astype(jnp.bfloat16)
    cotangent = scatter_about(streams_of[14], (TOKENS, D), 1.0, 6.0, ((0, 32),))
    return {"tokens": tokens, "seg_ids": seg_ids, "parents": parents, "attn_gain": attn_gain, "w_query": w_query, "w_key": w_key, "w_value": w_value, "w_out": w_out, "post_attn_gain": post_attn_gain, "ffn_gain": ffn_gain, "w_gate": w_gate, "w_up": w_up, "w_down": w_down, "post_ffn_gain": post_ffn_gain, "cotangent": cotangent}


@jax.custom_vjp
def low(v):
    return lax.optimization_barrier(v.astype(jnp.bfloat16)).astype(jnp.float32)

@jax.custom_vjp
def low_back(v):
    return v

def low_keep(v):
    return (low(v), None)

def low_pass(kept, grad):
    return (grad,)

def back_keep(v):
    return (v, None)

def back_low(kept, grad):
    return (low(grad),)
low.defvjp(low_keep, low_pass)
low_back.defvjp(back_keep, back_low)
softcap = 50.0
norm_eps = 1e-06
exact_precision = lax.Precision.HIGHEST

def rms_norm(values, gain_vec):
    return values * lax.rsqrt(lax.optimization_barrier(jnp.mean(values * values, axis=-1, keepdims=True)) + norm_eps) * gain_vec

def product(left, right):
    return jnp.dot(left, right, precision=exact_precision, preferred_element_type=jnp.float32)

def group_layer(group_tokens, group_segs, parent_row, weights):
    attn_gain, w_query, w_key, w_value, w_out, post_attn_gain, ffn_gain, w_gate, w_up, w_down, post_ffn_gain = weights
    token_count = group_tokens.shape[0]
    repeat = QUERY_HEADS // KV
    normed = low(rms_norm(group_tokens, attn_gain))
    queries = low(low_back(product(normed, w_query)))
    keys_all = low(low_back(product(normed, w_key)))
    values_all = low(low_back(product(normed, w_value)))
    grouped_queries = queries.reshape(token_count, KV, repeat, HEAD_SIZE)
    key_head_rows = keys_all.reshape(token_count, KV, HEAD_SIZE)
    value_head_rows = values_all.reshape(token_count, KV, HEAD_SIZE)
    score_matrix = low_back(jnp.einsum('ziwh,fih->iwzf', grouped_queries, key_head_rows, precision=exact_precision))
    capped = softcap * jnp.tanh(score_matrix * (HEAD_SIZE ** (-0.5) / softcap))
    positions = jnp.arange(token_count)
    extended = jnp.concatenate((parent_row, jnp.full((1,), SEGS, jnp.int32)), axis=0).astype(jnp.int32)
    parent_one = extended[group_segs]
    parent_two = extended[parent_one]
    real = group_segs < SEGS
    related = (group_segs[None, :] == group_segs[:, None]) | (group_segs[None, :] == parent_one[:, None]) | (group_segs[None, :] == parent_two[:, None])
    visible = (positions[None, :] <= positions[:, None]) & real[:, None] & real[None, :] & related | (positions[None, :] == positions[:, None])
    masked = jnp.where(visible[None, None], capped, -1e+30)
    attention_probabilities = jax.nn.softmax(masked, axis=-1)
    mixed_heads = jnp.einsum('xbcv,vxu->cxbu', low(attention_probabilities), value_head_rows, precision=exact_precision).reshape(token_count, QUERY_HEADS * HEAD_SIZE)
    mixed_heads = low(low_back(mixed_heads))
    attn_out = low_back(product(mixed_heads, w_out))
    middle = group_tokens + rms_norm(attn_out, post_attn_gain)
    normed_two = low(rms_norm(middle, ffn_gain))
    gate_pre = low_back(product(normed_two, w_gate))
    up_pre = low_back(product(normed_two, w_up))
    hidden = low(jax.nn.gelu(gate_pre, approximate=True) * up_pre)
    ffn_out = low_back(product(hidden, w_down))
    return middle + rms_norm(ffn_out, post_ffn_gain)

def reference(tokens, seg_ids, parents, attn_gain, w_query, w_key, w_value, w_out, post_attn_gain, ffn_gain, w_gate, w_up, w_down, post_ffn_gain, cotangent):
    weights = tuple((array.astype(jnp.float32) for array in (attn_gain, w_query, w_key, w_value, w_out, post_attn_gain, ffn_gain, w_gate, w_up, w_down, post_ffn_gain)))
    inputs = tokens.astype(jnp.float32).reshape(N_REP, GROUP, D)
    group_segs = seg_ids.reshape(N_REP, GROUP)

    def forward(inputs, weights):

        def one_group(packed):
            return group_layer(packed[0], packed[1], packed[2], weights)
        return lax.map(jax.checkpoint(one_group), (inputs, group_segs, parents))
    output, pullback = jax.vjp(forward, inputs, weights)
    grad_inputs, grads = pullback(cotangent.astype(jnp.float32).reshape(N_REP, GROUP, D))
    return (output.reshape(TOKENS, D).astype(jnp.bfloat16), grad_inputs.reshape(TOKENS, D).astype(jnp.bfloat16), grads[0], grads[1], grads[2], grads[3], grads[4], grads[5], grads[6], grads[7], grads[8], grads[9], grads[10])
```

```python
import jax
import jax.numpy as jnp
from jax import lax
from jax.sharding import PartitionSpec as P

QUERY_HEADS = 8
KV = 4
HEAD_SIZE = 256
SEGS = 13


softcap = 50.0
norm_eps = 1e-06


def normalize(values, gain_vec):
    inv_rms = lax.rsqrt(jnp.mean(values * values, axis=-1, keepdims=True) + norm_eps)
    return (values * inv_rms * gain_vec, inv_rms)


def norm_back(values, inv_rms, gain_vec, grad_in):
    weighted = grad_in * gain_vec
    row_mean = jnp.mean(weighted * values, axis=-1, keepdims=True)
    grad_back = inv_rms * weighted - values * (inv_rms * inv_rms * inv_rms) * row_mean
    return (grad_back, jnp.sum(grad_in * values * inv_rms, axis=0))


def geglu(gate_pre, up_pre):
    return jax.nn.gelu(gate_pre, approximate=True) * up_pre


def gather_rows(block):
    return lax.all_gather(block, "shard", axis=0, tiled=True)


def scatter_rows(partial):
    return lax.psum_scatter(partial, "shard", scatter_dimension=0, tiled=True)


def rep_sum(grads):
    return [lax.psum(grad, "rep").astype(jnp.float32) for grad in grads]


def body(
    tokens,
    seg_ids,
    parents,
    attn_gain,
    w_query,
    w_key,
    w_value,
    w_out,
    post_attn_gain,
    ffn_gain,
    w_gate,
    w_up,
    w_down,
    post_ffn_gain,
    cotangent,
):
    f32, bf16 = jnp.float32, jnp.bfloat16
    tok_rows, width = tokens.shape
    n = lax.axis_size("shard")
    me = lax.axis_index("shard")
    group_rows = tok_rows * n
    part_rows = w_query.shape[0]
    head_scale = HEAD_SIZE ** (-0.5)
    q_heads = QUERY_HEADS // n
    kv_heads = max(1, KV // n)
    share = n * kv_heads // KV
    repeat = q_heads // kv_heads
    q_cols = q_heads * HEAD_SIZE
    k_cols = kv_heads * HEAD_SIZE
    gain_one = attn_gain.astype(f32)
    gain_two = post_attn_gain.astype(f32)
    gain_three = ffn_gain.astype(f32)
    gain_four = post_ffn_gain.astype(f32)

    def by_device(weight):
        heads = weight.reshape(part_rows, KV, -1)
        if share > 1:
            heads = jnp.repeat(heads, share, axis=1)
        return heads.reshape(part_rows, n, -1)

    qkv_parts = jnp.concatenate(
        (w_query.reshape(part_rows, n, q_cols), by_device(w_key), by_device(w_value)), axis=2
    ).transpose(1, 0, 2)
    qkv_heads = lax.all_to_all(qkv_parts, "shard", 0, 0, tiled=True).reshape(width, -1)

    residual = tokens.astype(f32)
    normed, rms_one = normalize(residual, gain_one)
    normed_all = gather_rows(normed.astype(bf16))
    codes = gather_rows(seg_ids.astype(bf16)).astype(jnp.int32)
    qkv = jnp.dot(normed_all, qkv_heads, preferred_element_type=f32).astype(bf16)
    queries = qkv[:, :q_cols].reshape(group_rows, kv_heads, repeat, HEAD_SIZE)
    keys = qkv[:, q_cols : q_cols + k_cols].reshape(group_rows, kv_heads, HEAD_SIZE)
    values = qkv[:, q_cols + k_cols :].reshape(group_rows, kv_heads, HEAD_SIZE)

    parent_row = parents[0]
    labels = jnp.arange(SEGS)

    def lookup(ident):
        return jnp.sum(jnp.where(ident[:, None] == labels[None, :], parent_row[None, :], 0), axis=1)

    parent_one = lookup(codes)
    parent_two = lookup(parent_one)
    positions = jnp.arange(group_rows)
    real = codes < SEGS
    related = (
        (codes[None, :] == codes[:, None])
        | (codes[None, :] == parent_one[:, None])
        | (codes[None, :] == parent_two[:, None])
    )
    visible = (positions[None, :] <= positions[:, None]) & real[:, None] & real[
        None, :
    ] & related | (positions[None, :] == positions[:, None])

    score_matrix = jnp.einsum("tkrh,skh->krts", queries, keys, preferred_element_type=f32)
    tanh_part = jnp.tanh(score_matrix * (head_scale / softcap))
    masked = jnp.where(visible[None, None], softcap * tanh_part, -1e30)
    row_max = jnp.max(masked, axis=-1, keepdims=True)
    expo_terms = jnp.exp(masked - row_max)
    row_total = jnp.sum(expo_terms, axis=-1, keepdims=True)
    probs = expo_terms / row_total
    probs_b = probs.astype(bf16)
    mixed = jnp.einsum("krts,skh->tkrh", probs_b, values, preferred_element_type=f32)
    mixed = mixed.reshape(group_rows, q_cols).astype(bf16)
    attn_out = scatter_rows(
        jnp.dot(mixed, w_out, preferred_element_type=f32).astype(bf16)
    ).astype(f32)
    post_one, rms_two = normalize(attn_out, gain_two)
    middle = residual + post_one
    normed_two, rms_three = normalize(middle, gain_three)
    normed_two_all = gather_rows(normed_two.astype(bf16))
    gate_pre = jnp.dot(normed_two_all, w_gate, preferred_element_type=f32)
    up_pre = jnp.dot(normed_two_all, w_up, preferred_element_type=f32)
    hidden, geglu_back = jax.vjp(geglu, gate_pre, up_pre)
    hidden_b = hidden.astype(bf16)
    ffn_out = scatter_rows(
        jnp.dot(hidden_b, w_down, preferred_element_type=f32).astype(bf16)
    ).astype(f32)
    post_two, rms_four = normalize(ffn_out, gain_four)
    output = (middle + post_two).astype(bf16)

    grad_out = cotangent.astype(f32)
    grad_ffn, grad_gain_four = norm_back(ffn_out, rms_four, gain_four, grad_out)
    grad_ffn_all = gather_rows(grad_ffn.astype(bf16))
    down_part = jnp.einsum("tf,td->fd", hidden_b, grad_ffn_all, preferred_element_type=f32)
    grad_hidden = jnp.einsum("td,fd->tf", grad_ffn_all, w_down, preferred_element_type=f32)
    grad_gate, grad_up = geglu_back(grad_hidden)
    grad_gate_b = grad_gate.astype(bf16)
    grad_up_b = grad_up.astype(bf16)
    grad_normed_two = jnp.einsum("tf,df->td", grad_gate_b, w_gate, preferred_element_type=f32)
    grad_normed_two += jnp.einsum("tf,df->td", grad_up_b, w_up, preferred_element_type=f32)
    grad_normed_two = scatter_rows(grad_normed_two.astype(bf16)).astype(f32)
    gate_part = jnp.einsum("td,tf->df", normed_two_all, grad_gate_b, preferred_element_type=f32)
    up_part = jnp.einsum("td,tf->df", normed_two_all, grad_up_b, preferred_element_type=f32)
    grad_middle_part, grad_gain_three = norm_back(middle, rms_three, gain_three, grad_normed_two)
    grad_middle = grad_out + grad_middle_part
    grad_attn, grad_gain_two = norm_back(attn_out, rms_two, gain_two, grad_middle)
    grad_attn_all = gather_rows(grad_attn.astype(bf16))
    out_part = jnp.einsum("tj,td->jd", mixed, grad_attn_all, preferred_element_type=f32)
    grad_mixed = jnp.einsum("td,jd->tj", grad_attn_all, w_out, preferred_element_type=f32)
    grad_mixed = grad_mixed.astype(bf16).reshape(group_rows, kv_heads, repeat, HEAD_SIZE)
    grad_probs = jnp.einsum("tkrh,skh->krts", grad_mixed, values, preferred_element_type=f32)
    row_inner = jnp.sum(probs * grad_probs, axis=-1, keepdims=True)
    grad_dots = (
        probs * (grad_probs - row_inner) * (1.0 - tanh_part * tanh_part) * head_scale
    ).astype(bf16)
    grad_queries = jnp.einsum("krts,skh->tkrh", grad_dots, keys, preferred_element_type=f32)
    grad_keys = jnp.einsum("krts,tkrh->skh", grad_dots, queries, preferred_element_type=f32)
    grad_values = jnp.einsum("krts,tkrh->skh", probs_b, grad_mixed, preferred_element_type=f32)
    grad_parts = jnp.concatenate(
        (
            grad_queries.reshape(group_rows, q_cols),
            grad_keys.reshape(group_rows, k_cols),
            grad_values.reshape(group_rows, k_cols),
        ),
        axis=1,
    ).astype(bf16)
    grad_parts = lax.all_gather(grad_parts, "shard", axis=0)

    def whole_heads(parts):
        if share > 1:
            parts = parts.reshape(KV, share, group_rows, HEAD_SIZE).astype(f32).sum(axis=1).astype(bf16)
        return parts.transpose(1, 0, 2).reshape(group_rows, -1)

    grad_qkv = jnp.concatenate(
        (
            grad_parts[:, :, :q_cols].transpose(1, 0, 2).reshape(group_rows, -1),
            whole_heads(grad_parts[:, :, q_cols : q_cols + k_cols]),
            whole_heads(grad_parts[:, :, q_cols + k_cols :]),
        ),
        axis=1,
    )
    qkv_local = jnp.concatenate((w_query, w_key, w_value), axis=1)
    grad_normed = jnp.einsum("tj,dj->td", grad_qkv, qkv_local, preferred_element_type=f32)
    grad_normed = lax.all_to_all(
        grad_normed.astype(bf16).reshape(n, tok_rows, part_rows), "shard", 0, 0, tiled=True
    )
    grad_normed = grad_normed.transpose(1, 0, 2).reshape(tok_rows, width).astype(f32)
    normed_cols = lax.dynamic_slice_in_dim(normed_all, me * part_rows, part_rows, axis=1)
    qkv_part = jnp.einsum("td,tj->dj", normed_cols, grad_qkv, preferred_element_type=f32)
    grad_resid_part, grad_gain_one = norm_back(residual, rms_one, gain_one, grad_normed)
    grad_tokens = (grad_middle + grad_resid_part).astype(bf16)
    qkv_sum, out_sum, gate_sum, up_sum, down_sum = rep_sum(
        [part.astype(bf16) for part in (qkv_part, out_part, gate_part, up_part, down_part)]
    )
    gain_sum_one, gain_sum_two, gain_sum_three, gain_sum_four = lax.psum(
        (grad_gain_one, grad_gain_two, grad_gain_three, grad_gain_four), ("rep", "shard")
    )
    q_width = w_query.shape[1]
    k_width = w_key.shape[1]
    return (
        output,
        grad_tokens,
        gain_sum_one,
        qkv_sum[:, :q_width],
        qkv_sum[:, q_width : q_width + k_width],
        qkv_sum[:, q_width + k_width :],
        out_sum,
        gain_sum_two,
        gain_sum_three,
        gate_sum,
        up_sum,
        down_sum,
        gain_sum_four,
    )


def solution(mesh):
    return jax.shard_map(
        body,
        mesh=mesh,
        in_specs=(
            P(("rep", "shard"), None),
            P(("rep", "shard")),
            P("rep", None),
            P(),
            P("shard", None),
            P("shard", None),
            P("shard", None),
            P("shard", None),
            P(),
            P(),
            P(None, "shard"),
            P(None, "shard"),
            P("shard", None),
            P(),
            P(("rep", "shard"), None),
        ),
        out_specs=(
            P(("rep", "shard"), None),
            P(("rep", "shard"), None),
            P(),
            P("shard", None),
            P("shard", None),
            P("shard", None),
            P("shard", None),
            P(),
            P(),
            P(None, "shard"),
            P(None, "shard"),
            P("shard", None),
            P(),
        ),
        check_vma=False,
    )
```

```python
import functools

import jax
import jax.numpy as jnp
from jax import lax
from jax.experimental import pallas as pl
from jax.experimental.pallas import tpu as pltpu
from jax.sharding import PartitionSpec as P

SLOTS = 8
CHUNK = 64


def remote(src, dst, send_sem, recv_sem, where):
    return pltpu.make_async_remote_copy(
        src_ref=src,
        dst_ref=dst,
        send_sem=send_sem,
        recv_sem=recv_sem,
        device_id=where,
        device_id_type=pl.DeviceIdType.MESH,
    )


def add_low(left, right):
    return (left.astype(jnp.float32) + right.astype(jnp.float32)).astype(jnp.bfloat16)


def chain_kernel(counts, chunk, *refs):
    jobs = len(counts)
    ins, outs = refs[:jobs], refs[jobs : 2 * jobs]
    (
        mine, sib, acc, outer_in, inner_in, total,
        load_sem, sib_send, sib_recv, up_send, outer_recv, inner_recv,
        down_send, pair_send, pair_recv, store_sem,
        sib_credit, up_credit, down_credit,
    ) = refs[2 * jobs :]
    slots = mine.shape[0]
    steps = sum(counts)
    place = lax.axis_index("rep")
    chips = lax.axis_size("rep") // 2
    chip, core = place // 2, place % 2
    left = chip < chips // 2
    is_end = (chip == 0) | (chip == chips - 1)
    is_mid = (chip == chips // 2 - 1) | (chip == chips // 2)
    twin = {"rep": place + 1 - 2 * core}
    inner = {"rep": jnp.where(left, place + 2, place - 2)}
    outer = {"rep": jnp.where(is_end, place, jnp.where(left, place - 2, place + 2))}

    def tell(sem, where):
        pl.semaphore_signal(sem, inc=1, device_id=where, device_id_type=pl.DeviceIdType.MESH)

    barrier = pltpu.get_barrier_semaphore()
    tell(barrier, twin)
    tell(barrier, inner)

    @pl.when(is_end)
    def _():
        pl.semaphore_wait(barrier, 2)

    @pl.when(jnp.logical_not(is_end))
    def _():
        tell(barrier, outer)
        pl.semaphore_wait(barrier, 3)

    def with_rows(step, which, use):
        low = 0
        for job, count in enumerate(counts):
            first = low

            @pl.when((step >= low) & (step < low + count))
            def _():
                row = pl.multiple_of(((step - first) * 2 + which) * chunk, chunk)
                use(job, pl.ds(row, chunk))

            low += count

    def pair_copy(job, rows, slot, step):
        return remote(total.at[slot], outs[job].at[rows], pair_send.at[slot], pair_recv.at[step], twin)

    def up_copy(slot, dst, sem):
        return remote(acc.at[slot], dst.at[slot], up_send.at[slot], sem.at[slot], inner)

    def down_copy(slot):
        return remote(total.at[slot], inner_in.at[slot], down_send.at[slot], inner_recv.at[slot], outer)

    def sib_copy(job, rows, slot):
        return remote(ins[job].at[rows], sib.at[slot], sib_send.at[slot], sib_recv.at[slot], twin)

    def load_copy(job, rows, slot):
        return pltpu.make_async_copy(ins[job].at[rows], mine.at[slot], load_sem.at[slot])

    def store_copy(job, rows, slot):
        return pltpu.make_async_copy(total.at[slot], outs[job].at[rows], store_sem.at[slot])

    some = pl.ds(0, chunk)

    def take(step):
        slot = step % slots

        @pl.when(step >= slots)
        def _():
            pl.semaphore_wait(sib_credit, 1)

        with_rows(step, 1 - core, lambda job, rows: sib_copy(job, rows, slot).start())
        with_rows(step, core, lambda job, rows: load_copy(job, rows, slot).start())

    def send_up(step):
        slot = step % slots

        @pl.when(step >= slots)
        def _():
            pl.semaphore_wait(up_credit, 1)

        @pl.when(is_mid)
        def _():
            up_copy(slot, inner_in, inner_recv).start()

        @pl.when(jnp.logical_not(is_mid))
        def _():
            up_copy(slot, outer_in, outer_recv).start()

    def pair_up(step):
        slot = step % slots
        load_copy(0, some, slot).wait()
        sib_copy(0, some, slot).wait()

        @pl.when(step >= slots)
        def _():
            up_copy(slot, outer_in, outer_recv).wait_send()

        acc[slot] = add_low(mine[slot], sib[slot])

        @pl.when(step + slots < steps)
        def _():
            tell(sib_credit, twin)

        @pl.when(is_end)
        def _():
            send_up(step)

    def from_outer(step):
        slot = step % slots
        up_copy(slot, outer_in, outer_recv).wait_recv()
        acc[slot] = add_low(acc[slot], outer_in[slot])

        @pl.when(step + slots < steps)
        def _():
            tell(up_credit, outer)

        send_up(step)

    def sends_done(slot):
        pair_copy(0, some, slot, 0).wait_send()
        store_copy(0, some, slot).wait()

        @pl.when(jnp.logical_not(is_end))
        def _():
            down_copy(slot).wait_send()

    def from_inner(step):
        slot = step % slots
        down_copy(slot).wait_recv()

        @pl.when(step >= slots)
        def _():
            sends_done(slot)

        @pl.when(is_mid)
        def _():
            total[slot] = add_low(acc[slot], inner_in[slot])

            @pl.when(step + slots < steps)
            def _():
                tell(up_credit, inner)

        @pl.when(jnp.logical_not(is_mid))
        def _():
            total[slot] = inner_in[slot]

            @pl.when(step + slots < steps)
            def _():
                tell(down_credit, inner)

        @pl.when(jnp.logical_not(is_end))
        def _():
            @pl.when(step >= slots)
            def _():
                pl.semaphore_wait(down_credit, 1)

            down_copy(slot).start()

        with_rows(step, core, lambda job, rows: pair_copy(job, rows, slot, step).start())
        with_rows(step, core, lambda job, rows: store_copy(job, rows, slot).start())

    lag_outer = 3
    lag_inner = jnp.where(is_end, 8, 6)

    def tick(step, carry):
        @pl.when(step < steps)
        def _():
            take(step)

        @pl.when((step >= 1) & (step - 1 < steps))
        def _():
            pair_up(step - 1)

        @pl.when(jnp.logical_not(is_end) & (step >= lag_outer) & (step - lag_outer < steps))
        def _():
            from_outer(step - lag_outer)

        @pl.when((step >= lag_inner) & (step - lag_inner < steps))
        def _():
            from_inner(step - lag_inner)

        return carry

    lax.fori_loop(0, steps + 8, tick, 0)

    def finish(step, carry):
        slot = step % slots
        sends_done(slot)
        up_copy(slot, outer_in, outer_recv).wait_send()
        return carry

    lax.fori_loop(steps - slots, steps, finish, 0)

    def arrived(step, carry):
        pair_copy(0, some, 0, step).wait_recv()
        return carry

    lax.fori_loop(0, steps, arrived, 0)


def chain_sum(parts, chunk=CHUNK, collective_id=1):
    width = parts[0].shape[1]
    counts = tuple(part.shape[0] // (2 * chunk) for part in parts)
    steps = sum(counts)
    slots = min(SLOTS, steps)
    any_space = pl.BlockSpec(memory_space=pl.ANY)
    block = pltpu.VMEM((slots, chunk, width), jnp.bfloat16)
    sems = pltpu.SemaphoreType.DMA((slots,))
    credit = pltpu.SemaphoreType.REGULAR
    return pl.pallas_call(
        functools.partial(chain_kernel, counts, chunk),
        out_shape=[jax.ShapeDtypeStruct(part.shape, part.dtype) for part in parts],
        in_specs=[any_space] * len(parts),
        out_specs=[any_space] * len(parts),
        scratch_shapes=[block] * 6
        + [sems] * 8
        + [pltpu.SemaphoreType.DMA((steps,)), sems, credit, credit, credit],
        compiler_params=pltpu.CompilerParams(
            collective_id=collective_id, has_side_effects=True, vmem_limit_bytes=48 * 1024 * 1024
        ),
        cost_estimate=pl.CostEstimate(
            flops=0, bytes_accessed=8 * sum(part.size for part in parts), transcendentals=0
        ),
    )(*parts)


QUERY_HEADS = 8
KV = 4
HEAD_SIZE = 256
SEGS = 13


softcap = 50.0
norm_eps = 1e-06


def normalize(values, gain_vec):
    inv_rms = lax.rsqrt(jnp.mean(values * values, axis=-1, keepdims=True) + norm_eps)
    return (values * inv_rms * gain_vec, inv_rms)


def norm_back(values, inv_rms, gain_vec, grad_in):
    weighted = grad_in * gain_vec
    row_mean = jnp.mean(weighted * values, axis=-1, keepdims=True)
    grad_back = inv_rms * weighted - values * (inv_rms * inv_rms * inv_rms) * row_mean
    return (grad_back, jnp.sum(grad_in * values * inv_rms, axis=0))


def geglu(gate_pre, up_pre):
    return jax.nn.gelu(gate_pre, approximate=True) * up_pre


def gather_rows(block):
    return lax.all_gather(block, "shard", axis=0, tiled=True)


def scatter_rows(partial):
    return lax.psum_scatter(partial, "shard", scatter_dimension=0, tiled=True)


def rep_sum(grads, width):
    summed = chain_sum([grad.astype(jnp.bfloat16).reshape(-1, width) for grad in grads])
    return [
        total.reshape(grad.shape).astype(jnp.float32) for total, grad in zip(summed, grads)
    ]


def body(
    tokens,
    seg_ids,
    parents,
    attn_gain,
    w_query,
    w_key,
    w_value,
    w_out,
    post_attn_gain,
    ffn_gain,
    w_gate,
    w_up,
    w_down,
    post_ffn_gain,
    cotangent,
):
    f32, bf16 = jnp.float32, jnp.bfloat16
    tok_rows, width = tokens.shape
    n = lax.axis_size("shard")
    me = lax.axis_index("shard")
    group_rows = tok_rows * n
    part_rows = w_query.shape[0]
    head_scale = HEAD_SIZE ** (-0.5)
    q_heads = QUERY_HEADS // n
    kv_heads = max(1, KV // n)
    share = n * kv_heads // KV
    repeat = q_heads // kv_heads
    q_cols = q_heads * HEAD_SIZE
    k_cols = kv_heads * HEAD_SIZE
    gain_one = attn_gain.astype(f32)
    gain_two = post_attn_gain.astype(f32)
    gain_three = ffn_gain.astype(f32)
    gain_four = post_ffn_gain.astype(f32)

    def by_device(weight):
        heads = weight.reshape(part_rows, KV, -1)
        if share > 1:
            heads = jnp.repeat(heads, share, axis=1)
        return heads.reshape(part_rows, n, -1)

    qkv_parts = jnp.concatenate(
        (w_query.reshape(part_rows, n, q_cols), by_device(w_key), by_device(w_value)), axis=2
    ).transpose(1, 0, 2)
    qkv_heads = lax.all_to_all(qkv_parts, "shard", 0, 0, tiled=True).reshape(width, -1)

    residual = tokens.astype(f32)
    normed, rms_one = normalize(residual, gain_one)
    normed_all = gather_rows(normed.astype(bf16))
    codes = gather_rows(seg_ids.astype(bf16)).astype(jnp.int32)
    qkv = jnp.dot(normed_all, qkv_heads, preferred_element_type=f32).astype(bf16)
    queries = qkv[:, :q_cols].reshape(group_rows, kv_heads, repeat, HEAD_SIZE)
    keys = qkv[:, q_cols : q_cols + k_cols].reshape(group_rows, kv_heads, HEAD_SIZE)
    values = qkv[:, q_cols + k_cols :].reshape(group_rows, kv_heads, HEAD_SIZE)

    parent_row = parents[0]
    labels = jnp.arange(SEGS)

    def lookup(ident):
        return jnp.sum(jnp.where(ident[:, None] == labels[None, :], parent_row[None, :], 0), axis=1)

    parent_one = lookup(codes)
    parent_two = lookup(parent_one)
    positions = jnp.arange(group_rows)
    real = codes < SEGS
    related = (
        (codes[None, :] == codes[:, None])
        | (codes[None, :] == parent_one[:, None])
        | (codes[None, :] == parent_two[:, None])
    )
    visible = (positions[None, :] <= positions[:, None]) & real[:, None] & real[
        None, :
    ] & related | (positions[None, :] == positions[:, None])

    score_matrix = jnp.einsum("tkrh,skh->krts", queries, keys, preferred_element_type=f32)
    tanh_part = jnp.tanh(score_matrix * (head_scale / softcap))
    masked = jnp.where(visible[None, None], softcap * tanh_part, -1e30)
    row_max = jnp.max(masked, axis=-1, keepdims=True)
    expo_terms = jnp.exp(masked - row_max)
    row_total = jnp.sum(expo_terms, axis=-1, keepdims=True)
    probs = expo_terms / row_total
    probs_b = probs.astype(bf16)
    mixed = jnp.einsum("krts,skh->tkrh", probs_b, values, preferred_element_type=f32)
    mixed = mixed.reshape(group_rows, q_cols).astype(bf16)
    attn_out = scatter_rows(
        jnp.dot(mixed, w_out, preferred_element_type=f32).astype(bf16)
    ).astype(f32)
    post_one, rms_two = normalize(attn_out, gain_two)
    middle = residual + post_one
    normed_two, rms_three = normalize(middle, gain_three)
    normed_two_all = gather_rows(normed_two.astype(bf16))
    gate_pre = jnp.dot(normed_two_all, w_gate, preferred_element_type=f32)
    up_pre = jnp.dot(normed_two_all, w_up, preferred_element_type=f32)
    hidden, geglu_back = jax.vjp(geglu, gate_pre, up_pre)
    hidden_b = hidden.astype(bf16)
    ffn_out = scatter_rows(
        jnp.dot(hidden_b, w_down, preferred_element_type=f32).astype(bf16)
    ).astype(f32)
    post_two, rms_four = normalize(ffn_out, gain_four)
    output = (middle + post_two).astype(bf16)

    grad_out = cotangent.astype(f32)
    grad_ffn, grad_gain_four = norm_back(ffn_out, rms_four, gain_four, grad_out)
    grad_ffn_all = gather_rows(grad_ffn.astype(bf16))
    down_part = jnp.einsum("tf,td->fd", hidden_b, grad_ffn_all, preferred_element_type=f32)
    grad_hidden = jnp.einsum("td,fd->tf", grad_ffn_all, w_down, preferred_element_type=f32)
    grad_gate, grad_up = geglu_back(grad_hidden)
    grad_gate_b = grad_gate.astype(bf16)
    grad_up_b = grad_up.astype(bf16)
    grad_normed_two = jnp.einsum("tf,df->td", grad_gate_b, w_gate, preferred_element_type=f32)
    grad_normed_two += jnp.einsum("tf,df->td", grad_up_b, w_up, preferred_element_type=f32)
    grad_normed_two = scatter_rows(grad_normed_two.astype(bf16)).astype(f32)
    gate_part = jnp.einsum("td,tf->df", normed_two_all, grad_gate_b, preferred_element_type=f32)
    up_part = jnp.einsum("td,tf->df", normed_two_all, grad_up_b, preferred_element_type=f32)
    grad_middle_part, grad_gain_three = norm_back(middle, rms_three, gain_three, grad_normed_two)
    grad_middle = grad_out + grad_middle_part
    grad_attn, grad_gain_two = norm_back(attn_out, rms_two, gain_two, grad_middle)
    grad_attn_all = gather_rows(grad_attn.astype(bf16))
    out_part = jnp.einsum("tj,td->jd", mixed, grad_attn_all, preferred_element_type=f32)
    grad_mixed = jnp.einsum("td,jd->tj", grad_attn_all, w_out, preferred_element_type=f32)
    grad_mixed = grad_mixed.astype(bf16).reshape(group_rows, kv_heads, repeat, HEAD_SIZE)
    grad_probs = jnp.einsum("tkrh,skh->krts", grad_mixed, values, preferred_element_type=f32)
    row_inner = jnp.sum(probs * grad_probs, axis=-1, keepdims=True)
    grad_dots = (
        probs * (grad_probs - row_inner) * (1.0 - tanh_part * tanh_part) * head_scale
    ).astype(bf16)
    grad_queries = jnp.einsum("krts,skh->tkrh", grad_dots, keys, preferred_element_type=f32)
    grad_keys = jnp.einsum("krts,tkrh->skh", grad_dots, queries, preferred_element_type=f32)
    grad_values = jnp.einsum("krts,tkrh->skh", probs_b, grad_mixed, preferred_element_type=f32)
    grad_parts = jnp.concatenate(
        (
            grad_queries.reshape(group_rows, q_cols),
            grad_keys.reshape(group_rows, k_cols),
            grad_values.reshape(group_rows, k_cols),
        ),
        axis=1,
    ).astype(bf16)
    grad_parts = lax.all_gather(grad_parts, "shard", axis=0)

    def whole_heads(parts):
        if share > 1:
            parts = parts.reshape(KV, share, group_rows, HEAD_SIZE).astype(f32).sum(axis=1).astype(bf16)
        return parts.transpose(1, 0, 2).reshape(group_rows, -1)

    grad_qkv = jnp.concatenate(
        (
            grad_parts[:, :, :q_cols].transpose(1, 0, 2).reshape(group_rows, -1),
            whole_heads(grad_parts[:, :, q_cols : q_cols + k_cols]),
            whole_heads(grad_parts[:, :, q_cols + k_cols :]),
        ),
        axis=1,
    )
    qkv_local = jnp.concatenate((w_query, w_key, w_value), axis=1)
    grad_normed = jnp.einsum("tj,dj->td", grad_qkv, qkv_local, preferred_element_type=f32)
    grad_normed = lax.all_to_all(
        grad_normed.astype(bf16).reshape(n, tok_rows, part_rows), "shard", 0, 0, tiled=True
    )
    grad_normed = grad_normed.transpose(1, 0, 2).reshape(tok_rows, width).astype(f32)
    normed_cols = lax.dynamic_slice_in_dim(normed_all, me * part_rows, part_rows, axis=1)
    qkv_part = jnp.einsum("td,tj->dj", normed_cols, grad_qkv, preferred_element_type=f32)
    grad_resid_part, grad_gain_one = norm_back(residual, rms_one, gain_one, grad_normed)
    grad_tokens = (grad_middle + grad_resid_part).astype(bf16)
    gain_parts = jnp.stack((grad_gain_one, grad_gain_two, grad_gain_three, grad_gain_four))
    gain_sums = lax.all_gather(gain_parts, ("rep", "shard"), axis=0).sum(axis=0)
    down_sum, gate_sum, up_sum, out_sum, qkv_sum = rep_sum(
        (down_part, gate_part, up_part, out_part, qkv_part), width
    )
    q_width = w_query.shape[1]
    k_width = w_key.shape[1]
    return (
        output,
        grad_tokens,
        gain_sums[0],
        qkv_sum[:, :q_width],
        qkv_sum[:, q_width : q_width + k_width],
        qkv_sum[:, q_width + k_width :],
        out_sum,
        gain_sums[1],
        gain_sums[2],
        gate_sum,
        up_sum,
        down_sum,
        gain_sums[3],
    )


def solution(mesh):
    return jax.shard_map(
        body,
        mesh=mesh,
        in_specs=(
            P(("rep", "shard"), None),
            P(("rep", "shard")),
            P("rep", None),
            P(),
            P("shard", None),
            P("shard", None),
            P("shard", None),
            P("shard", None),
            P(),
            P(),
            P(None, "shard"),
            P(None, "shard"),
            P("shard", None),
            P(),
            P(("rep", "shard"), None),
        ),
        out_specs=(
            P(("rep", "shard"), None),
            P(("rep", "shard"), None),
            P(),
            P("shard", None),
            P("shard", None),
            P("shard", None),
            P("shard", None),
            P(),
            P(),
            P(None, "shard"),
            P(None, "shard"),
            P("shard", None),
            P(),
        ),
        check_vma=False,
    )
```

```python
import functools

import jax
import jax.numpy as jnp
from jax import lax
from jax.experimental import pallas as pl
from jax.experimental.pallas import tpu as pltpu
from jax.sharding import PartitionSpec as P

SLOTS = 8
CHUNK = 64


def remote(src, dst, send_sem, recv_sem, where):
    return pltpu.make_async_remote_copy(
        src_ref=src,
        dst_ref=dst,
        send_sem=send_sem,
        recv_sem=recv_sem,
        device_id=where,
        device_id_type=pl.DeviceIdType.MESH,
    )


def add_low(left, right):
    return (left.astype(jnp.float32) + right.astype(jnp.float32)).astype(jnp.bfloat16)


def chain_kernel(counts, chunk, *refs):
    jobs = len(counts)
    ins, outs = refs[:jobs], refs[jobs : 2 * jobs]
    (
        mine, sib, acc, outer_in, inner_in, total,
        load_sem, sib_send, sib_recv, up_send, outer_recv, inner_recv,
        down_send, pair_send, pair_recv, store_sem,
        sib_credit, up_credit, down_credit,
    ) = refs[2 * jobs :]
    slots = mine.shape[0]
    steps = sum(counts)
    place = lax.axis_index("rep")
    chips = lax.axis_size("rep") // 2
    chip, core = place // 2, place % 2
    left = chip < chips // 2
    is_end = (chip == 0) | (chip == chips - 1)
    is_mid = (chip == chips // 2 - 1) | (chip == chips // 2)
    twin = {"rep": place + 1 - 2 * core}
    inner = {"rep": jnp.where(left, place + 2, place - 2)}
    outer = {"rep": jnp.where(is_end, place, jnp.where(left, place - 2, place + 2))}

    def tell(sem, where):
        pl.semaphore_signal(sem, inc=1, device_id=where, device_id_type=pl.DeviceIdType.MESH)

    barrier = pltpu.get_barrier_semaphore()
    tell(barrier, twin)
    tell(barrier, inner)

    @pl.when(is_end)
    def _():
        pl.semaphore_wait(barrier, 2)

    @pl.when(jnp.logical_not(is_end))
    def _():
        tell(barrier, outer)
        pl.semaphore_wait(barrier, 3)

    def with_rows(step, which, use):
        low = 0
        for job, count in enumerate(counts):
            first = low

            @pl.when((step >= low) & (step < low + count))
            def _():
                row = pl.multiple_of(((step - first) * 2 + which) * chunk, chunk)
                use(job, pl.ds(row, chunk))

            low += count

    def pair_copy(job, rows, slot, step):
        return remote(total.at[slot], outs[job].at[rows], pair_send.at[slot], pair_recv.at[step], twin)

    def up_copy(slot, dst, sem):
        return remote(acc.at[slot], dst.at[slot], up_send.at[slot], sem.at[slot], inner)

    def down_copy(slot):
        return remote(total.at[slot], inner_in.at[slot], down_send.at[slot], inner_recv.at[slot], outer)

    def sib_copy(job, rows, slot):
        return remote(ins[job].at[rows], sib.at[slot], sib_send.at[slot], sib_recv.at[slot], twin)

    def load_copy(job, rows, slot):
        return pltpu.make_async_copy(ins[job].at[rows], mine.at[slot], load_sem.at[slot])

    def store_copy(job, rows, slot):
        return pltpu.make_async_copy(total.at[slot], outs[job].at[rows], store_sem.at[slot])

    some = pl.ds(0, chunk)

    def take(step):
        slot = step % slots

        @pl.when(step >= slots)
        def _():
            pl.semaphore_wait(sib_credit, 1)

        with_rows(step, 1 - core, lambda job, rows: sib_copy(job, rows, slot).start())
        with_rows(step, core, lambda job, rows: load_copy(job, rows, slot).start())

    def send_up(step):
        slot = step % slots

        @pl.when(step >= slots)
        def _():
            pl.semaphore_wait(up_credit, 1)

        @pl.when(is_mid)
        def _():
            up_copy(slot, inner_in, inner_recv).start()

        @pl.when(jnp.logical_not(is_mid))
        def _():
            up_copy(slot, outer_in, outer_recv).start()

    def pair_up(step):
        slot = step % slots
        load_copy(0, some, slot).wait()
        sib_copy(0, some, slot).wait()

        @pl.when(step >= slots)
        def _():
            up_copy(slot, outer_in, outer_recv).wait_send()

        acc[slot] = add_low(mine[slot], sib[slot])

        @pl.when(step + slots < steps)
        def _():
            tell(sib_credit, twin)

        @pl.when(is_end)
        def _():
            send_up(step)

    def from_outer(step):
        slot = step % slots
        up_copy(slot, outer_in, outer_recv).wait_recv()
        acc[slot] = add_low(acc[slot], outer_in[slot])

        @pl.when(step + slots < steps)
        def _():
            tell(up_credit, outer)

        send_up(step)

    def sends_done(slot):
        pair_copy(0, some, slot, 0).wait_send()
        store_copy(0, some, slot).wait()

        @pl.when(jnp.logical_not(is_end))
        def _():
            down_copy(slot).wait_send()

    def from_inner(step):
        slot = step % slots
        down_copy(slot).wait_recv()

        @pl.when(step >= slots)
        def _():
            sends_done(slot)

        @pl.when(is_mid)
        def _():
            total[slot] = add_low(acc[slot], inner_in[slot])

            @pl.when(step + slots < steps)
            def _():
                tell(up_credit, inner)

        @pl.when(jnp.logical_not(is_mid))
        def _():
            total[slot] = inner_in[slot]

            @pl.when(step + slots < steps)
            def _():
                tell(down_credit, inner)

        @pl.when(jnp.logical_not(is_end))
        def _():
            @pl.when(step >= slots)
            def _():
                pl.semaphore_wait(down_credit, 1)

            down_copy(slot).start()

        with_rows(step, core, lambda job, rows: pair_copy(job, rows, slot, step).start())
        with_rows(step, core, lambda job, rows: store_copy(job, rows, slot).start())

    lag_outer = 3
    lag_inner = jnp.where(is_end, 8, 6)

    def tick(step, carry):
        @pl.when(step < steps)
        def _():
            take(step)

        @pl.when((step >= 1) & (step - 1 < steps))
        def _():
            pair_up(step - 1)

        @pl.when(jnp.logical_not(is_end) & (step >= lag_outer) & (step - lag_outer < steps))
        def _():
            from_outer(step - lag_outer)

        @pl.when((step >= lag_inner) & (step - lag_inner < steps))
        def _():
            from_inner(step - lag_inner)

        return carry

    lax.fori_loop(0, steps + 8, tick, 0)

    def finish(step, carry):
        slot = step % slots
        sends_done(slot)
        up_copy(slot, outer_in, outer_recv).wait_send()
        return carry

    lax.fori_loop(steps - slots, steps, finish, 0)

    def arrived(step, carry):
        pair_copy(0, some, 0, step).wait_recv()
        return carry

    lax.fori_loop(0, steps, arrived, 0)


def chain_sum(parts, chunk=CHUNK, collective_id=1):
    width = parts[0].shape[1]
    counts = tuple(part.shape[0] // (2 * chunk) for part in parts)
    steps = sum(counts)
    slots = min(SLOTS, steps)
    any_space = pl.BlockSpec(memory_space=pl.ANY)
    block = pltpu.VMEM((slots, chunk, width), jnp.bfloat16)
    sems = pltpu.SemaphoreType.DMA((slots,))
    credit = pltpu.SemaphoreType.REGULAR
    return pl.pallas_call(
        functools.partial(chain_kernel, counts, chunk),
        out_shape=[jax.ShapeDtypeStruct(part.shape, part.dtype) for part in parts],
        in_specs=[any_space] * len(parts),
        out_specs=[any_space] * len(parts),
        scratch_shapes=[block] * 6
        + [sems] * 8
        + [pltpu.SemaphoreType.DMA((steps,)), sems, credit, credit, credit],
        compiler_params=pltpu.CompilerParams(
            collective_id=collective_id, has_side_effects=True, vmem_limit_bytes=48 * 1024 * 1024
        ),
        cost_estimate=pl.CostEstimate(
            flops=0, bytes_accessed=8 * sum(part.size for part in parts), transcendentals=0
        ),
    )(*parts)


def plane_places():
    me = lax.axis_index("shard")
    x_other = me + 1 - 2 * (me % 2)
    y_other = (me + 2) % 4
    far = x_other + y_other - me
    return me, x_other, y_other, far


def greet(places):
    barrier = pltpu.get_barrier_semaphore()
    for place in places:
        pl.semaphore_signal(
            barrier, inc=1, device_id={"shard": place}, device_id_type=pl.DeviceIdType.MESH
        )
    pl.semaphore_wait(barrier, len(places))


def gather_kernel(x_ref, out_ref, send_sem, recv_sem, local_sem):
    me, x_other, y_other, far = plane_places()
    rows = x_ref.shape[0]
    half = rows // 2

    def part(block, which):
        return out_ref.at[pl.ds(pl.multiple_of(block * rows + which * half, 16), half)]

    def own(which):
        return x_ref.at[pl.ds(which * half, half)]

    def send(src, dst, index, where):
        return remote(src, dst, send_sem.at[index], recv_sem.at[index], {"shard": where})

    greet((x_other, y_other))
    local = pltpu.make_async_copy(
        x_ref, out_ref.at[pl.ds(pl.multiple_of(me * rows, 16), rows)], local_sem
    )
    first = (
        send(own(0), part(me, 0), 0, x_other),
        send(own(1), part(me, 1), 1, y_other),
        send(own(1), part(me, 1), 2, x_other),
        send(own(0), part(me, 0), 3, y_other),
    )
    for copy in first:
        copy.start()
    local.start()
    first[0].wait_recv()
    on_y = send(part(x_other, 0), part(x_other, 0), 4, y_other)
    on_y.start()
    first[1].wait_recv()
    on_x = send(part(y_other, 1), part(y_other, 1), 5, x_other)
    on_x.start()
    first[2].wait_recv()
    first[3].wait_recv()
    on_y.wait_recv()
    on_x.wait_recv()
    for copy in first + (on_y, on_x):
        copy.wait_send()
    local.wait()


def gather4(block, collective_id):
    rows, width = block.shape
    sems = pltpu.SemaphoreType.DMA((6,))
    any_space = pl.BlockSpec(memory_space=pl.ANY)
    return pl.pallas_call(
        gather_kernel,
        out_shape=jax.ShapeDtypeStruct((4 * rows, width), block.dtype),
        in_specs=[any_space],
        out_specs=any_space,
        scratch_shapes=[sems, sems, pltpu.SemaphoreType.DMA],
        compiler_params=pltpu.CompilerParams(collective_id=collective_id, has_side_effects=True),
        cost_estimate=pl.CostEstimate(
            flops=0, bytes_accessed=40 * rows * width * 2, transcendentals=0
        ),
    )(block)


def scatter_kernel(part_ref, out_ref, *scratch):
    landed, mine, passed = scratch[:3]
    send_sem, recv_sem, load_sem = scratch[3:]
    me, x_other, y_other, far = plane_places()
    rows = out_ref.shape[0]
    half = rows // 2

    def part(block, which):
        return part_ref.at[pl.ds(pl.multiple_of(block * rows + which * half, 16), half)]

    def send(src, index, where):
        return remote(
            src, landed.at[index], send_sem.at[index], recv_sem.at[index], {"shard": where}
        )

    def load(src, index):
        return pltpu.make_async_copy(src, mine.at[index], load_sem.at[index])

    loads = (
        load(part(y_other, 0), 0),
        load(part(x_other, 1), 1),
        load(part(me, 0), 2),
        load(part(me, 1), 3),
    )
    for copy in loads:
        copy.start()
    greet((x_other, y_other))
    first = (
        send(part(far, 0), 0, x_other),
        send(part(far, 1), 1, y_other),
        send(part(x_other, 0), 2, x_other),
        send(part(y_other, 1), 3, y_other),
    )
    for copy in first:
        copy.start()
    for copy in loads:
        copy.wait()
    first[0].wait_recv()
    passed[0] = add_low(landed[0], mine[0])
    on_y = send(passed.at[0], 4, y_other)
    on_y.start()
    first[1].wait_recv()
    passed[1] = add_low(landed[1], mine[1])
    on_x = send(passed.at[1], 5, x_other)
    on_x.start()
    first[2].wait_recv()
    mine[2] = add_low(landed[2], mine[2])
    first[3].wait_recv()
    mine[3] = add_low(landed[3], mine[3])
    on_y.wait_recv()
    out_ref[pl.ds(0, half)] = mine[2].astype(jnp.float32) + landed[4].astype(jnp.float32)
    on_x.wait_recv()
    out_ref[pl.ds(half, half)] = mine[3].astype(jnp.float32) + landed[5].astype(jnp.float32)
    for copy in first + (on_y, on_x):
        copy.wait_send()


def scatter4(partial, collective_id):
    rows, width = partial.shape[0] // 4, partial.shape[1]
    half = rows // 2
    return pl.pallas_call(
        scatter_kernel,
        out_shape=jax.ShapeDtypeStruct((rows, width), jnp.float32),
        in_specs=[pl.BlockSpec(memory_space=pl.ANY)],
        out_specs=pl.BlockSpec(memory_space=pltpu.VMEM),
        scratch_shapes=[
            pltpu.VMEM((6, half, width), partial.dtype),
            pltpu.VMEM((4, half, width), partial.dtype),
            pltpu.VMEM((2, half, width), partial.dtype),
            pltpu.SemaphoreType.DMA((6,)),
            pltpu.SemaphoreType.DMA((6,)),
            pltpu.SemaphoreType.DMA((4,)),
        ],
        compiler_params=pltpu.CompilerParams(
            collective_id=collective_id, has_side_effects=True, vmem_limit_bytes=32 * 1024 * 1024
        ),
        cost_estimate=pl.CostEstimate(
            flops=0, bytes_accessed=40 * rows * width * 2, transcendentals=0
        ),
    )(partial)


def exchange_kernel(x_ref, out_ref, send_sem, recv_sem, local_sem):
    me = lax.axis_index("shard")
    others = [(me + step) % 4 for step in (1, 2, 3)]
    greet(others)
    local = pltpu.make_async_copy(x_ref.at[me], out_ref.at[me], local_sem)
    local.start()
    copies = [
        remote(x_ref.at[place], out_ref.at[me], send_sem.at[i], recv_sem.at[i], {"shard": place})
        for i, place in enumerate(others)
    ]
    for copy in copies:
        copy.start()
    for copy in copies:
        copy.wait()
    local.wait()


def exchange4(blocks, collective_id):
    any_space = pl.BlockSpec(memory_space=pl.ANY)
    sems = pltpu.SemaphoreType.DMA((3,))
    return pl.pallas_call(
        exchange_kernel,
        out_shape=jax.ShapeDtypeStruct(blocks.shape, blocks.dtype),
        in_specs=[any_space],
        out_specs=any_space,
        scratch_shapes=[sems, sems, pltpu.SemaphoreType.DMA],
        compiler_params=pltpu.CompilerParams(collective_id=collective_id, has_side_effects=True),
        cost_estimate=pl.CostEstimate(
            flops=0, bytes_accessed=10 * blocks.size * 2, transcendentals=0
        ),
    )(blocks)


def prologue_kernel(counts, x_ref, code_ref, query_ref, key_ref, value_ref, out_ref, codes_ref,
                    heads_ref, send_sem, recv_sem, local_sem, code_send, code_recv,
                    head_send, head_recv, twin_send, twin_recv, head_local):
    me, x_other, y_other, far = plane_places()
    place = lax.axis_index("rep")
    core = place % 2
    twin = {"rep": place + 1 - 2 * core}
    others = (x_other, y_other, far)
    rows = x_ref.shape[0]
    half = rows // 2
    depth = query_ref.shape[0]
    part_depth = depth // 2
    weights = (query_ref, key_ref, value_ref)
    starts = (0, counts[0], counts[0] + counts[1])

    barrier = pltpu.get_barrier_semaphore()
    for other in others:
        pl.semaphore_signal(
            barrier, inc=1, device_id={"shard": other}, device_id_type=pl.DeviceIdType.MESH
        )
    pl.semaphore_signal(barrier, inc=1, device_id=twin, device_id_type=pl.DeviceIdType.MESH)
    pl.semaphore_wait(barrier, 4)

    def my_rows(owner):
        return pl.ds(pl.multiple_of(owner * depth + core * part_depth, 16), part_depth)

    def head_copy(index, kind, other):
        columns = pl.ds(pl.multiple_of(other * counts[kind], 128), counts[kind])
        return remote(
            weights[kind].at[pl.ds(pl.multiple_of(core * part_depth, 16), part_depth), columns],
            heads_ref.at[my_rows(me), pl.ds(starts[kind], counts[kind])],
            head_send.at[index, kind],
            head_recv.at[index, kind],
            {"shard": other},
        )

    def part(block, which):
        return out_ref.at[pl.ds(pl.multiple_of(block * rows + which * half, 16), half)]

    def own(which):
        return x_ref.at[pl.ds(which * half, half)]

    def send(src, dst, index, where):
        return remote(src, dst, send_sem.at[index], recv_sem.at[index], {"shard": where})

    head_copies = [
        [head_copy(index, kind, other) for kind in range(3)] for index, other in enumerate(others)
    ]
    for index in (2, 0, 1):
        for copy in head_copies[index]:
            copy.start()
    code_copies = [
        remote(
            code_ref, codes_ref.at[me], code_send.at[index], code_recv.at[index], {"shard": other}
        )
        for index, other in enumerate(others)
    ]
    for copy in code_copies:
        copy.start()
    first = (
        send(own(0), part(me, 0), 0, x_other),
        send(own(1), part(me, 1), 1, y_other),
        send(own(1), part(me, 1), 2, x_other),
        send(own(0), part(me, 0), 3, y_other),
    )
    for copy in first:
        copy.start()
    locals_ = [
        pltpu.make_async_copy(
            x_ref, out_ref.at[pl.ds(pl.multiple_of(me * rows, 16), rows)], local_sem.at[0]
        ),
        pltpu.make_async_copy(code_ref, codes_ref.at[me], local_sem.at[1]),
    ]
    for kind in range(3):
        columns = pl.ds(pl.multiple_of(me * counts[kind], 128), counts[kind])
        locals_.append(
            pltpu.make_async_copy(
                weights[kind].at[:, columns],
                heads_ref.at[
                    pl.ds(pl.multiple_of(me * depth, 16), depth), pl.ds(starts[kind], counts[kind])
                ],
                head_local.at[kind],
            )
        )
    for copy in locals_:
        copy.start()
    twins = []
    for index in (0, 1, 2):
        for copy in head_copies[index]:
            copy.wait_recv()
        block = heads_ref.at[my_rows(others[index])]
        twins.append(remote(block, block, twin_send.at[index], twin_recv.at[index], twin))
        twins[-1].start()
    first[0].wait_recv()
    on_y = send(part(x_other, 0), part(x_other, 0), 4, y_other)
    on_y.start()
    first[1].wait_recv()
    on_x = send(part(y_other, 1), part(y_other, 1), 5, x_other)
    on_x.start()
    first[2].wait_recv()
    first[3].wait_recv()
    for copy in code_copies + twins:
        copy.wait_recv()
    on_y.wait_recv()
    on_x.wait_recv()
    for copy in list(first) + [on_y, on_x] + code_copies + twins:
        copy.wait_send()
    for group in head_copies:
        for copy in group:
            copy.wait_send()
    for copy in locals_:
        copy.wait()


def prologue4(block, codes, w_query, w_key, w_value, collective_id):
    rows, width = block.shape
    counts = tuple(weight.shape[1] // 4 for weight in (w_query, w_key, w_value))
    depth = w_query.shape[0]
    any_space = pl.BlockSpec(memory_space=pl.ANY)
    dma = pltpu.SemaphoreType.DMA
    return pl.pallas_call(
        functools.partial(prologue_kernel, counts),
        out_shape=(
            jax.ShapeDtypeStruct((4 * rows, width), block.dtype),
            jax.ShapeDtypeStruct((4,) + codes.shape, codes.dtype),
            jax.ShapeDtypeStruct((4 * depth, sum(counts)), w_query.dtype),
        ),
        in_specs=[any_space] * 5,
        out_specs=[any_space] * 3,
        scratch_shapes=[
            dma((6,)), dma((6,)), dma((2,)), dma((3,)), dma((3,)),
            dma((3, 3)), dma((3, 3)), dma((3,)), dma((3,)), dma((3,)),
        ],
        compiler_params=pltpu.CompilerParams(collective_id=collective_id, has_side_effects=True),
        cost_estimate=pl.CostEstimate(
            flops=0, bytes_accessed=80 * rows * width * 2, transcendentals=0
        ),
    )(block, codes, w_query, w_key, w_value)


QUERY_HEADS = 8
KV = 4
HEAD_SIZE = 256
SEGS = 13


softcap = 50.0
norm_eps = 1e-06


def normalize(values, gain_vec):
    inv_rms = lax.rsqrt(jnp.mean(values * values, axis=-1, keepdims=True) + norm_eps)
    return (values * inv_rms * gain_vec, inv_rms)


def norm_back(values, inv_rms, gain_vec, grad_in):
    weighted = grad_in * gain_vec
    row_mean = jnp.mean(weighted * values, axis=-1, keepdims=True)
    grad_back = inv_rms * weighted - values * (inv_rms * inv_rms * inv_rms) * row_mean
    return (grad_back, jnp.sum(grad_in * values * inv_rms, axis=0))


def geglu(gate_pre, up_pre):
    return jax.nn.gelu(gate_pre, approximate=True) * up_pre


def gather_rows(block, collective_id):
    if lax.axis_size("shard") == 4:
        return gather4(block, collective_id)
    return lax.all_gather(block, "shard", axis=0, tiled=True)


def scatter_rows(partial, collective_id):
    if lax.axis_size("shard") == 4:
        return scatter4(partial, collective_id)
    summed = lax.psum_scatter(partial, "shard", scatter_dimension=0, tiled=True)
    return summed.astype(jnp.float32)


def exchange(blocks, collective_id):
    if lax.axis_size("shard") == 4:
        return exchange4(blocks, collective_id)
    return lax.all_to_all(blocks, "shard", 0, 0, tiled=True)


def first_gather(normed, seg_ids, w_query, w_key, w_value):
    n = lax.axis_size("shard")
    tok_rows, width = normed.shape
    codes = seg_ids.astype(jnp.bfloat16)
    if n == 4:
        codes = jnp.pad(codes, (0, 2048 - tok_rows)).reshape(16, 128)
        normed_all, codes, heads = prologue4(normed, codes, w_query, w_key, w_value, 2)
        codes = codes.reshape(n, -1)[:, :tok_rows].reshape(-1)
        return normed_all, codes.astype(jnp.int32), heads
    part_rows = w_query.shape[0]
    share = max(1, n // KV)

    def by_device(weight):
        heads = weight.reshape(part_rows, KV, -1)
        if share > 1:
            heads = jnp.repeat(heads, share, axis=1)
        return heads.reshape(part_rows, n, -1)

    parts = jnp.concatenate(
        (w_query.reshape(part_rows, n, -1), by_device(w_key), by_device(w_value)), axis=2
    ).transpose(1, 0, 2)
    heads = lax.all_to_all(parts, "shard", 0, 0, tiled=True).reshape(width, -1)
    normed_all = lax.all_gather(normed, "shard", axis=0, tiled=True)
    codes = lax.all_gather(codes, "shard", axis=0, tiled=True)
    return normed_all, codes.astype(jnp.int32), heads


def rep_sum(grads, width):
    summed = chain_sum([grad.astype(jnp.bfloat16).reshape(-1, width) for grad in grads])
    return [
        total.reshape(grad.shape).astype(jnp.float32) for total, grad in zip(summed, grads)
    ]


def body(
    tokens,
    seg_ids,
    parents,
    attn_gain,
    w_query,
    w_key,
    w_value,
    w_out,
    post_attn_gain,
    ffn_gain,
    w_gate,
    w_up,
    w_down,
    post_ffn_gain,
    cotangent,
):
    f32, bf16 = jnp.float32, jnp.bfloat16
    tok_rows, width = tokens.shape
    n = lax.axis_size("shard")
    me = lax.axis_index("shard")
    group_rows = tok_rows * n
    part_rows = w_query.shape[0]
    head_scale = HEAD_SIZE ** (-0.5)
    q_heads = QUERY_HEADS // n
    kv_heads = max(1, KV // n)
    share = n * kv_heads // KV
    repeat = q_heads // kv_heads
    q_cols = q_heads * HEAD_SIZE
    k_cols = kv_heads * HEAD_SIZE
    gain_one = attn_gain.astype(f32)
    gain_two = post_attn_gain.astype(f32)
    gain_three = ffn_gain.astype(f32)
    gain_four = post_ffn_gain.astype(f32)

    residual = tokens.astype(f32)
    normed, rms_one = normalize(residual, gain_one)
    normed_all, codes, qkv_heads = first_gather(
        normed.astype(bf16), seg_ids, w_query, w_key, w_value
    )
    qkv = jnp.dot(normed_all, qkv_heads, preferred_element_type=f32).astype(bf16)
    queries = qkv[:, :q_cols].reshape(group_rows, kv_heads, repeat, HEAD_SIZE)
    keys = qkv[:, q_cols : q_cols + k_cols].reshape(group_rows, kv_heads, HEAD_SIZE)
    values = qkv[:, q_cols + k_cols :].reshape(group_rows, kv_heads, HEAD_SIZE)

    parent_row = parents[0]
    labels = jnp.arange(SEGS)

    def lookup(ident):
        return jnp.sum(jnp.where(ident[:, None] == labels[None, :], parent_row[None, :], 0), axis=1)

    parent_one = lookup(codes)
    parent_two = lookup(parent_one)
    positions = jnp.arange(group_rows)
    real = codes < SEGS
    related = (
        (codes[None, :] == codes[:, None])
        | (codes[None, :] == parent_one[:, None])
        | (codes[None, :] == parent_two[:, None])
    )
    visible = (positions[None, :] <= positions[:, None]) & real[:, None] & real[
        None, :
    ] & related | (positions[None, :] == positions[:, None])

    score_matrix = jnp.einsum("tkrh,skh->krts", queries, keys, preferred_element_type=f32)
    tanh_part = jnp.tanh(score_matrix * (head_scale / softcap))
    masked = jnp.where(visible[None, None], softcap * tanh_part, -1e30)
    row_max = jnp.max(masked, axis=-1, keepdims=True)
    expo_terms = jnp.exp(masked - row_max)
    row_total = jnp.sum(expo_terms, axis=-1, keepdims=True)
    probs = expo_terms / row_total
    probs_b = probs.astype(bf16)
    mixed = jnp.einsum("krts,skh->tkrh", probs_b, values, preferred_element_type=f32)
    mixed = mixed.reshape(group_rows, q_cols).astype(bf16)
    attn_out = scatter_rows(jnp.dot(mixed, w_out, preferred_element_type=f32).astype(bf16), 3)
    post_one, rms_two = normalize(attn_out, gain_two)
    middle = residual + post_one
    normed_two, rms_three = normalize(middle, gain_three)
    normed_two_all = gather_rows(normed_two.astype(bf16), 4)
    gate_pre = jnp.dot(normed_two_all, w_gate, preferred_element_type=f32)
    up_pre = jnp.dot(normed_two_all, w_up, preferred_element_type=f32)
    hidden, geglu_back = jax.vjp(geglu, gate_pre, up_pre)
    hidden_b = hidden.astype(bf16)
    ffn_out = scatter_rows(jnp.dot(hidden_b, w_down, preferred_element_type=f32).astype(bf16), 5)
    post_two, rms_four = normalize(ffn_out, gain_four)
    output = (middle + post_two).astype(bf16)

    grad_out = cotangent.astype(f32)
    grad_ffn, grad_gain_four = norm_back(ffn_out, rms_four, gain_four, grad_out)
    grad_ffn_all = gather_rows(grad_ffn.astype(bf16), 6)
    down_part = jnp.einsum("tf,td->fd", hidden_b, grad_ffn_all, preferred_element_type=f32)
    grad_hidden = jnp.einsum("td,fd->tf", grad_ffn_all, w_down, preferred_element_type=f32)
    grad_gate, grad_up = geglu_back(grad_hidden)
    grad_gate_b = grad_gate.astype(bf16)
    grad_up_b = grad_up.astype(bf16)
    grad_normed_two = jnp.einsum("tf,df->td", grad_gate_b, w_gate, preferred_element_type=f32)
    grad_normed_two += jnp.einsum("tf,df->td", grad_up_b, w_up, preferred_element_type=f32)
    grad_normed_two = scatter_rows(grad_normed_two.astype(bf16), 7)
    gate_part = jnp.einsum("td,tf->df", normed_two_all, grad_gate_b, preferred_element_type=f32)
    up_part = jnp.einsum("td,tf->df", normed_two_all, grad_up_b, preferred_element_type=f32)
    grad_middle_part, grad_gain_three = norm_back(middle, rms_three, gain_three, grad_normed_two)
    grad_middle = grad_out + grad_middle_part
    grad_attn, grad_gain_two = norm_back(attn_out, rms_two, gain_two, grad_middle)
    grad_attn_all = gather_rows(grad_attn.astype(bf16), 8)
    out_part = jnp.einsum("tj,td->jd", mixed, grad_attn_all, preferred_element_type=f32)
    grad_mixed = jnp.einsum("td,jd->tj", grad_attn_all, w_out, preferred_element_type=f32)
    grad_mixed = grad_mixed.astype(bf16).reshape(group_rows, kv_heads, repeat, HEAD_SIZE)
    grad_probs = jnp.einsum("tkrh,skh->krts", grad_mixed, values, preferred_element_type=f32)
    row_inner = jnp.sum(probs * grad_probs, axis=-1, keepdims=True)
    grad_dots = (
        probs * (grad_probs - row_inner) * (1.0 - tanh_part * tanh_part) * head_scale
    ).astype(bf16)
    grad_queries = jnp.einsum("krts,skh->tkrh", grad_dots, keys, preferred_element_type=f32)
    grad_keys = jnp.einsum("krts,tkrh->skh", grad_dots, queries, preferred_element_type=f32)
    grad_values = jnp.einsum("krts,tkrh->skh", probs_b, grad_mixed, preferred_element_type=f32)
    grad_parts = jnp.concatenate(
        (
            grad_queries.reshape(group_rows, q_cols),
            grad_keys.reshape(group_rows, k_cols),
            grad_values.reshape(group_rows, k_cols),
        ),
        axis=1,
    ).astype(bf16)
    grad_parts = gather_rows(grad_parts, 9).reshape(n, group_rows, -1)

    def whole_heads(parts):
        if share > 1:
            parts = parts.reshape(KV, share, group_rows, HEAD_SIZE).astype(f32).sum(axis=1).astype(bf16)
        return parts.transpose(1, 0, 2).reshape(group_rows, -1)

    grad_qkv = jnp.concatenate(
        (
            grad_parts[:, :, :q_cols].transpose(1, 0, 2).reshape(group_rows, -1),
            whole_heads(grad_parts[:, :, q_cols : q_cols + k_cols]),
            whole_heads(grad_parts[:, :, q_cols + k_cols :]),
        ),
        axis=1,
    )
    qkv_local = jnp.concatenate((w_query, w_key, w_value), axis=1)
    grad_normed = jnp.einsum("tj,dj->td", grad_qkv, qkv_local, preferred_element_type=f32)
    grad_normed = exchange(grad_normed.astype(bf16).reshape(n, tok_rows, part_rows), 10)
    grad_normed = grad_normed.transpose(1, 0, 2).reshape(tok_rows, width).astype(f32)
    normed_cols = lax.dynamic_slice_in_dim(normed_all, me * part_rows, part_rows, axis=1)
    qkv_part = jnp.einsum("td,tj->dj", normed_cols, grad_qkv, preferred_element_type=f32)
    grad_resid_part, grad_gain_one = norm_back(residual, rms_one, gain_one, grad_normed)
    grad_tokens = (grad_middle + grad_resid_part).astype(bf16)
    gain_parts = jnp.stack((grad_gain_one, grad_gain_two, grad_gain_three, grad_gain_four))
    gain_sums = lax.all_gather(gain_parts, ("rep", "shard"), axis=0).sum(axis=0)
    down_sum, gate_sum, up_sum, out_sum, qkv_sum = rep_sum(
        (down_part, gate_part, up_part, out_part, qkv_part), width
    )
    q_width = w_query.shape[1]
    k_width = w_key.shape[1]
    return (
        output,
        grad_tokens,
        gain_sums[0],
        qkv_sum[:, :q_width],
        qkv_sum[:, q_width : q_width + k_width],
        qkv_sum[:, q_width + k_width :],
        out_sum,
        gain_sums[1],
        gain_sums[2],
        gate_sum,
        up_sum,
        down_sum,
        gain_sums[3],
    )


def solution(mesh):
    return jax.shard_map(
        body,
        mesh=mesh,
        in_specs=(
            P(("rep", "shard"), None),
            P(("rep", "shard")),
            P("rep", None),
            P(),
            P("shard", None),
            P("shard", None),
            P("shard", None),
            P("shard", None),
            P(),
            P(),
            P(None, "shard"),
            P(None, "shard"),
            P("shard", None),
            P(),
            P(("rep", "shard"), None),
        ),
        out_specs=(
            P(("rep", "shard"), None),
            P(("rep", "shard"), None),
            P(),
            P("shard", None),
            P("shard", None),
            P("shard", None),
            P("shard", None),
            P(),
            P(),
            P(None, "shard"),
            P(None, "shard"),
            P("shard", None),
            P(),
        ),
        check_vma=False,
    )
```

```python
import functools
import math
import types

import jax
import jax.numpy as jnp
from jax import lax
from jax.experimental import pallas as pl
from jax.experimental.pallas import tpu as pltpu
from jax.sharding import PartitionSpec as P

SLOTS = 8
CHUNK = 64


def remote(src, dst, send_sem, recv_sem, where):
    return pltpu.make_async_remote_copy(
        src_ref=src,
        dst_ref=dst,
        send_sem=send_sem,
        recv_sem=recv_sem,
        device_id=where,
        device_id_type=pl.DeviceIdType.MESH,
    )


def add_low(left, right):
    return (left.astype(jnp.float32) + right.astype(jnp.float32)).astype(jnp.bfloat16)


def chain_kernel(counts, chunk, *refs):
    jobs = len(counts)
    ins, outs = refs[:jobs], refs[jobs : 2 * jobs]
    (
        mine, sib, acc, outer_in, inner_in, total,
        load_sem, sib_send, sib_recv, up_send, outer_recv, inner_recv,
        down_send, pair_send, pair_recv, store_sem,
        sib_credit, up_credit, down_credit,
    ) = refs[2 * jobs :]
    slots = mine.shape[0]
    steps = sum(counts)
    place = lax.axis_index("rep")
    chips = lax.axis_size("rep") // 2
    chip, core = place // 2, place % 2
    left = chip < chips // 2
    is_end = (chip == 0) | (chip == chips - 1)
    is_mid = (chip == chips // 2 - 1) | (chip == chips // 2)
    twin = {"rep": place + 1 - 2 * core}
    inner = {"rep": jnp.where(left, place + 2, place - 2)}
    outer = {"rep": jnp.where(is_end, place, jnp.where(left, place - 2, place + 2))}

    def tell(sem, where):
        pl.semaphore_signal(sem, inc=1, device_id=where, device_id_type=pl.DeviceIdType.MESH)

    barrier = pltpu.get_barrier_semaphore()
    tell(barrier, twin)
    tell(barrier, inner)

    @pl.when(is_end)
    def _():
        pl.semaphore_wait(barrier, 2)

    @pl.when(jnp.logical_not(is_end))
    def _():
        tell(barrier, outer)
        pl.semaphore_wait(barrier, 3)

    def with_rows(step, which, use):
        low = 0
        for job, count in enumerate(counts):
            first = low

            @pl.when((step >= low) & (step < low + count))
            def _():
                row = pl.multiple_of(((step - first) * 2 + which) * chunk, chunk)
                use(job, pl.ds(row, chunk))

            low += count

    def pair_copy(job, rows, slot, step):
        return remote(total.at[slot], outs[job].at[rows], pair_send.at[slot], pair_recv.at[step], twin)

    def up_copy(slot, dst, sem):
        return remote(acc.at[slot], dst.at[slot], up_send.at[slot], sem.at[slot], inner)

    def down_copy(slot):
        return remote(total.at[slot], inner_in.at[slot], down_send.at[slot], inner_recv.at[slot], outer)

    def sib_copy(job, rows, slot):
        return remote(ins[job].at[rows], sib.at[slot], sib_send.at[slot], sib_recv.at[slot], twin)

    def load_copy(job, rows, slot):
        return pltpu.make_async_copy(ins[job].at[rows], mine.at[slot], load_sem.at[slot])

    def store_copy(job, rows, slot):
        return pltpu.make_async_copy(total.at[slot], outs[job].at[rows], store_sem.at[slot])

    some = pl.ds(0, chunk)

    def take(step):
        slot = step % slots

        @pl.when(step >= slots)
        def _():
            pl.semaphore_wait(sib_credit, 1)

        with_rows(step, 1 - core, lambda job, rows: sib_copy(job, rows, slot).start())
        with_rows(step, core, lambda job, rows: load_copy(job, rows, slot).start())

    def send_up(step):
        slot = step % slots

        @pl.when(step >= slots)
        def _():
            pl.semaphore_wait(up_credit, 1)

        @pl.when(is_mid)
        def _():
            up_copy(slot, inner_in, inner_recv).start()

        @pl.when(jnp.logical_not(is_mid))
        def _():
            up_copy(slot, outer_in, outer_recv).start()

    def pair_up(step):
        slot = step % slots
        load_copy(0, some, slot).wait()
        sib_copy(0, some, slot).wait()

        @pl.when(step >= slots)
        def _():
            up_copy(slot, outer_in, outer_recv).wait_send()

        acc[slot] = add_low(mine[slot], sib[slot])

        @pl.when(step + slots < steps)
        def _():
            tell(sib_credit, twin)

        @pl.when(is_end)
        def _():
            send_up(step)

    def from_outer(step):
        slot = step % slots
        up_copy(slot, outer_in, outer_recv).wait_recv()
        acc[slot] = add_low(acc[slot], outer_in[slot])

        @pl.when(step + slots < steps)
        def _():
            tell(up_credit, outer)

        send_up(step)

    def sends_done(slot):
        pair_copy(0, some, slot, 0).wait_send()
        store_copy(0, some, slot).wait()

        @pl.when(jnp.logical_not(is_end))
        def _():
            down_copy(slot).wait_send()

    def from_inner(step):
        slot = step % slots
        down_copy(slot).wait_recv()

        @pl.when(step >= slots)
        def _():
            sends_done(slot)

        @pl.when(is_mid)
        def _():
            total[slot] = add_low(acc[slot], inner_in[slot])

            @pl.when(step + slots < steps)
            def _():
                tell(up_credit, inner)

        @pl.when(jnp.logical_not(is_mid))
        def _():
            total[slot] = inner_in[slot]

            @pl.when(step + slots < steps)
            def _():
                tell(down_credit, inner)

        @pl.when(jnp.logical_not(is_end))
        def _():
            @pl.when(step >= slots)
            def _():
                pl.semaphore_wait(down_credit, 1)

            down_copy(slot).start()

        with_rows(step, core, lambda job, rows: pair_copy(job, rows, slot, step).start())
        with_rows(step, core, lambda job, rows: store_copy(job, rows, slot).start())

    lag_outer = 3
    lag_inner = jnp.where(is_end, 8, 6)

    def tick(step, carry):
        @pl.when(step < steps)
        def _():
            take(step)

        @pl.when((step >= 1) & (step - 1 < steps))
        def _():
            pair_up(step - 1)

        @pl.when(jnp.logical_not(is_end) & (step >= lag_outer) & (step - lag_outer < steps))
        def _():
            from_outer(step - lag_outer)

        @pl.when((step >= lag_inner) & (step - lag_inner < steps))
        def _():
            from_inner(step - lag_inner)

        return carry

    lax.fori_loop(0, steps + 8, tick, 0)

    def finish(step, carry):
        slot = step % slots
        sends_done(slot)
        up_copy(slot, outer_in, outer_recv).wait_send()
        return carry

    lax.fori_loop(steps - slots, steps, finish, 0)

    def arrived(step, carry):
        pair_copy(0, some, 0, step).wait_recv()
        return carry

    lax.fori_loop(0, steps, arrived, 0)


def chain_sum(parts, chunk=CHUNK, collective_id=1):
    width = parts[0].shape[1]
    counts = tuple(part.shape[0] // (2 * chunk) for part in parts)
    steps = sum(counts)
    slots = min(SLOTS, steps)
    any_space = pl.BlockSpec(memory_space=pl.ANY)
    block = pltpu.VMEM((slots, chunk, width), jnp.bfloat16)
    sems = pltpu.SemaphoreType.DMA((slots,))
    credit = pltpu.SemaphoreType.REGULAR
    return pl.pallas_call(
        functools.partial(chain_kernel, counts, chunk),
        out_shape=[jax.ShapeDtypeStruct(part.shape, part.dtype) for part in parts],
        in_specs=[any_space] * len(parts),
        out_specs=[any_space] * len(parts),
        scratch_shapes=[block] * 6
        + [sems] * 8
        + [pltpu.SemaphoreType.DMA((steps,)), sems, credit, credit, credit],
        compiler_params=pltpu.CompilerParams(
            collective_id=collective_id, has_side_effects=True, vmem_limit_bytes=48 * 1024 * 1024
        ),
        cost_estimate=pl.CostEstimate(
            flops=0, bytes_accessed=8 * sum(part.size for part in parts), transcendentals=0
        ),
    )(*parts)


def plane_places():
    me = lax.axis_index("shard")
    x_other = me + 1 - 2 * (me % 2)
    y_other = (me + 2) % 4
    far = x_other + y_other - me
    return me, x_other, y_other, far


def greet(places):
    barrier = pltpu.get_barrier_semaphore()
    for place in places:
        pl.semaphore_signal(
            barrier, inc=1, device_id={"shard": place}, device_id_type=pl.DeviceIdType.MESH
        )
    pl.semaphore_wait(barrier, len(places))


def gather_kernel(x_ref, out_ref, send_sem, recv_sem, local_sem):
    me, x_other, y_other, far = plane_places()
    rows = x_ref.shape[0]
    half = rows // 2

    def part(block, which):
        return out_ref.at[pl.ds(pl.multiple_of(block * rows + which * half, 16), half)]

    def own(which):
        return x_ref.at[pl.ds(which * half, half)]

    def send(src, dst, index, where):
        return remote(src, dst, send_sem.at[index], recv_sem.at[index], {"shard": where})

    greet((x_other, y_other))
    local = pltpu.make_async_copy(
        x_ref, out_ref.at[pl.ds(pl.multiple_of(me * rows, 16), rows)], local_sem
    )
    first = (
        send(own(0), part(me, 0), 0, x_other),
        send(own(1), part(me, 1), 1, y_other),
        send(own(1), part(me, 1), 2, x_other),
        send(own(0), part(me, 0), 3, y_other),
    )
    for copy in first:
        copy.start()
    local.start()
    first[0].wait_recv()
    on_y = send(part(x_other, 0), part(x_other, 0), 4, y_other)
    on_y.start()
    first[1].wait_recv()
    on_x = send(part(y_other, 1), part(y_other, 1), 5, x_other)
    on_x.start()
    first[2].wait_recv()
    first[3].wait_recv()
    on_y.wait_recv()
    on_x.wait_recv()
    for copy in first + (on_y, on_x):
        copy.wait_send()
    local.wait()


def gather4(block, collective_id):
    rows, width = block.shape
    sems = pltpu.SemaphoreType.DMA((6,))
    any_space = pl.BlockSpec(memory_space=pl.ANY)
    return pl.pallas_call(
        gather_kernel,
        out_shape=jax.ShapeDtypeStruct((4 * rows, width), block.dtype),
        in_specs=[any_space],
        out_specs=any_space,
        scratch_shapes=[sems, sems, pltpu.SemaphoreType.DMA],
        compiler_params=pltpu.CompilerParams(collective_id=collective_id, has_side_effects=True),
        cost_estimate=pl.CostEstimate(
            flops=0, bytes_accessed=40 * rows * width * 2, transcendentals=0
        ),
    )(block)


def scatter_kernel(part_ref, out_ref, *scratch):
    landed, mine, passed = scratch[:3]
    send_sem, recv_sem, load_sem = scratch[3:]
    me, x_other, y_other, far = plane_places()
    rows = out_ref.shape[0]
    half = rows // 2

    def part(block, which):
        return part_ref.at[pl.ds(pl.multiple_of(block * rows + which * half, 16), half)]

    def send(src, index, where):
        return remote(
            src, landed.at[index], send_sem.at[index], recv_sem.at[index], {"shard": where}
        )

    def load(src, index):
        return pltpu.make_async_copy(src, mine.at[index], load_sem.at[index])

    loads = (
        load(part(y_other, 0), 0),
        load(part(x_other, 1), 1),
        load(part(me, 0), 2),
        load(part(me, 1), 3),
    )
    for copy in loads:
        copy.start()
    greet((x_other, y_other))
    first = (
        send(part(far, 0), 0, x_other),
        send(part(far, 1), 1, y_other),
        send(part(x_other, 0), 2, x_other),
        send(part(y_other, 1), 3, y_other),
    )
    for copy in first:
        copy.start()
    for copy in loads:
        copy.wait()
    first[0].wait_recv()
    passed[0] = add_low(landed[0], mine[0])
    on_y = send(passed.at[0], 4, y_other)
    on_y.start()
    first[1].wait_recv()
    passed[1] = add_low(landed[1], mine[1])
    on_x = send(passed.at[1], 5, x_other)
    on_x.start()
    first[2].wait_recv()
    mine[2] = add_low(landed[2], mine[2])
    first[3].wait_recv()
    mine[3] = add_low(landed[3], mine[3])
    on_y.wait_recv()
    out_ref[pl.ds(0, half)] = mine[2].astype(jnp.float32) + landed[4].astype(jnp.float32)
    on_x.wait_recv()
    out_ref[pl.ds(half, half)] = mine[3].astype(jnp.float32) + landed[5].astype(jnp.float32)
    for copy in first + (on_y, on_x):
        copy.wait_send()


def scatter4(partial, collective_id):
    rows, width = partial.shape[0] // 4, partial.shape[1]
    half = rows // 2
    return pl.pallas_call(
        scatter_kernel,
        out_shape=jax.ShapeDtypeStruct((rows, width), jnp.float32),
        in_specs=[pl.BlockSpec(memory_space=pl.ANY)],
        out_specs=pl.BlockSpec(memory_space=pltpu.VMEM),
        scratch_shapes=[
            pltpu.VMEM((6, half, width), partial.dtype),
            pltpu.VMEM((4, half, width), partial.dtype),
            pltpu.VMEM((2, half, width), partial.dtype),
            pltpu.SemaphoreType.DMA((6,)),
            pltpu.SemaphoreType.DMA((6,)),
            pltpu.SemaphoreType.DMA((4,)),
        ],
        compiler_params=pltpu.CompilerParams(
            collective_id=collective_id, has_side_effects=True, vmem_limit_bytes=32 * 1024 * 1024
        ),
        cost_estimate=pl.CostEstimate(
            flops=0, bytes_accessed=40 * rows * width * 2, transcendentals=0
        ),
    )(partial)


def exchange_kernel(x_ref, out_ref, send_sem, recv_sem, local_sem):
    me = lax.axis_index("shard")
    others = [(me + step) % 4 for step in (1, 2, 3)]
    greet(others)
    local = pltpu.make_async_copy(x_ref.at[me], out_ref.at[me], local_sem)
    local.start()
    copies = [
        remote(x_ref.at[place], out_ref.at[me], send_sem.at[i], recv_sem.at[i], {"shard": place})
        for i, place in enumerate(others)
    ]
    for copy in copies:
        copy.start()
    for copy in copies:
        copy.wait()
    local.wait()


def exchange4(blocks, collective_id):
    any_space = pl.BlockSpec(memory_space=pl.ANY)
    sems = pltpu.SemaphoreType.DMA((3,))
    return pl.pallas_call(
        exchange_kernel,
        out_shape=jax.ShapeDtypeStruct(blocks.shape, blocks.dtype),
        in_specs=[any_space],
        out_specs=any_space,
        scratch_shapes=[sems, sems, pltpu.SemaphoreType.DMA],
        compiler_params=pltpu.CompilerParams(collective_id=collective_id, has_side_effects=True),
        cost_estimate=pl.CostEstimate(
            flops=0, bytes_accessed=10 * blocks.size * 2, transcendentals=0
        ),
    )(blocks)


def prologue_kernel(counts, x_ref, code_ref, query_ref, key_ref, value_ref, out_ref, codes_ref,
                    heads_ref, send_sem, recv_sem, local_sem, code_send, code_recv,
                    head_send, head_recv, twin_send, twin_recv, head_local):
    me, x_other, y_other, far = plane_places()
    place = lax.axis_index("rep")
    core = place % 2
    twin = {"rep": place + 1 - 2 * core}
    others = (x_other, y_other, far)
    rows = x_ref.shape[0]
    half = rows // 2
    depth = query_ref.shape[0]
    part_depth = depth // 2
    weights = (query_ref, key_ref, value_ref)
    starts = (0, counts[0], counts[0] + counts[1])

    barrier = pltpu.get_barrier_semaphore()
    for other in others:
        pl.semaphore_signal(
            barrier, inc=1, device_id={"shard": other}, device_id_type=pl.DeviceIdType.MESH
        )
    pl.semaphore_signal(barrier, inc=1, device_id=twin, device_id_type=pl.DeviceIdType.MESH)
    pl.semaphore_wait(barrier, 4)

    def my_rows(owner):
        return pl.ds(pl.multiple_of(owner * depth + core * part_depth, 16), part_depth)

    def head_copy(index, kind, other):
        columns = pl.ds(pl.multiple_of(other * counts[kind], 128), counts[kind])
        return remote(
            weights[kind].at[pl.ds(pl.multiple_of(core * part_depth, 16), part_depth), columns],
            heads_ref.at[my_rows(me), pl.ds(starts[kind], counts[kind])],
            head_send.at[index, kind],
            head_recv.at[index, kind],
            {"shard": other},
        )

    def part(block, which):
        return out_ref.at[pl.ds(pl.multiple_of(block * rows + which * half, 16), half)]

    def own(which):
        return x_ref.at[pl.ds(which * half, half)]

    def send(src, dst, index, where):
        return remote(src, dst, send_sem.at[index], recv_sem.at[index], {"shard": where})

    head_copies = [
        [head_copy(index, kind, other) for kind in range(3)] for index, other in enumerate(others)
    ]
    for index in (2, 0, 1):
        for copy in head_copies[index]:
            copy.start()
    code_copies = [
        remote(
            code_ref, codes_ref.at[me], code_send.at[index], code_recv.at[index], {"shard": other}
        )
        for index, other in enumerate(others)
    ]
    for copy in code_copies:
        copy.start()
    first = (
        send(own(0), part(me, 0), 0, x_other),
        send(own(1), part(me, 1), 1, y_other),
        send(own(1), part(me, 1), 2, x_other),
        send(own(0), part(me, 0), 3, y_other),
    )
    for copy in first:
        copy.start()
    locals_ = [
        pltpu.make_async_copy(
            x_ref, out_ref.at[pl.ds(pl.multiple_of(me * rows, 16), rows)], local_sem.at[0]
        ),
        pltpu.make_async_copy(code_ref, codes_ref.at[me], local_sem.at[1]),
    ]
    for kind in range(3):
        columns = pl.ds(pl.multiple_of(me * counts[kind], 128), counts[kind])
        locals_.append(
            pltpu.make_async_copy(
                weights[kind].at[:, columns],
                heads_ref.at[
                    pl.ds(pl.multiple_of(me * depth, 16), depth), pl.ds(starts[kind], counts[kind])
                ],
                head_local.at[kind],
            )
        )
    for copy in locals_:
        copy.start()
    twins = []
    for index in (0, 1, 2):
        for copy in head_copies[index]:
            copy.wait_recv()
        block = heads_ref.at[my_rows(others[index])]
        twins.append(remote(block, block, twin_send.at[index], twin_recv.at[index], twin))
        twins[-1].start()
    first[0].wait_recv()
    on_y = send(part(x_other, 0), part(x_other, 0), 4, y_other)
    on_y.start()
    first[1].wait_recv()
    on_x = send(part(y_other, 1), part(y_other, 1), 5, x_other)
    on_x.start()
    first[2].wait_recv()
    first[3].wait_recv()
    for copy in code_copies + twins:
        copy.wait_recv()
    on_y.wait_recv()
    on_x.wait_recv()
    for copy in list(first) + [on_y, on_x] + code_copies + twins:
        copy.wait_send()
    for group in head_copies:
        for copy in group:
            copy.wait_send()
    for copy in locals_:
        copy.wait()


def prologue4(block, codes, w_query, w_key, w_value, collective_id):
    rows, width = block.shape
    counts = tuple(weight.shape[1] // 4 for weight in (w_query, w_key, w_value))
    depth = w_query.shape[0]
    any_space = pl.BlockSpec(memory_space=pl.ANY)
    dma = pltpu.SemaphoreType.DMA
    return pl.pallas_call(
        functools.partial(prologue_kernel, counts),
        out_shape=(
            jax.ShapeDtypeStruct((4 * rows, width), block.dtype),
            jax.ShapeDtypeStruct((4,) + codes.shape, codes.dtype),
            jax.ShapeDtypeStruct((4 * depth, sum(counts)), w_query.dtype),
        ),
        in_specs=[any_space] * 5,
        out_specs=[any_space] * 3,
        scratch_shapes=[
            dma((6,)), dma((6,)), dma((2,)), dma((3,)), dma((3,)),
            dma((3, 3)), dma((3, 3)), dma((3,)), dma((3,)), dma((3,)),
        ],
        compiler_params=pltpu.CompilerParams(collective_id=collective_id, has_side_effects=True),
        cost_estimate=pl.CostEstimate(
            flops=0, bytes_accessed=80 * rows * width * 2, transcendentals=0
        ),
    )(block, codes, w_query, w_key, w_value)


TILE = 256
PAIR = 2 * CHUNK
DEEP = 8
ROOT_TWO_PI = math.sqrt(2.0 / math.pi)


def dot_rows(left, right):
    return lax.dot_general(left, right, (((1,), (1,)), ((), ())), preferred_element_type=jnp.float32)


def dot_plain(left, right):
    return lax.dot_general(left, right, (((1,), (0,)), ((), ())), preferred_element_type=jnp.float32)


def dot_columns(left, right):
    return lax.dot_general(left, right, (((0,), (0,)), ((), ())), preferred_element_type=jnp.float32)


def backward_kernel(dims, names, *refs):
    r = types.SimpleNamespace(**dict(zip(names, refs)))
    tokens, local, width, inner_width, head_cols = dims
    f32, bf16 = jnp.float32, jnp.bfloat16
    half = local // 2
    q_cols = head_cols // 2
    k_cols = head_cols // 4
    heads = q_cols // HEAD_SIZE
    part = width // 4
    part_wide = r.gain_one.shape[1]
    side = 2 * head_cols
    n_a = inner_width // TILE
    n_b = width // TILE
    block = min(TILE, tokens)
    n_blocks = tokens // block

    counts = (
        inner_width // PAIR, width // PAIR, width // PAIR, r.w_out.shape[0] // PAIR, part // CHUNK
    )
    first = [sum(counts[:job]) for job in range(6)]
    steps = first[5]
    b_at = (n_a + 1) // 2
    c_at = b_at + n_b
    d_at = c_at + 5
    f_at = d_at + 5
    g_at = f_at + 1
    h_at = g_at + heads * n_blocks
    i_at = h_at + 9
    k_at = i_at + 3
    assert b_at <= first[1] and f_at < first[3] and i_at < first[4] and first[1] <= i_at
    assert first[2] <= i_at and k_at + 5 <= steps + 8

    place = lax.axis_index("rep")
    chips = lax.axis_size("rep") // 2
    chip, core = place // 2, place % 2
    left = chip < chips // 2
    is_end = (chip == 0) | (chip == chips - 1)
    is_mid = (chip == chips // 2 - 1) | (chip == chips // 2)
    twin = {"rep": place + 1 - 2 * core}
    inner = {"rep": jnp.where(left, place + 2, place - 2)}
    outer = {"rep": jnp.where(is_end, place, jnp.where(left, place - 2, place + 2))}
    next_chip = {"rep": place + 2 - 4 * (chip % 2)}
    far_chip = {"rep": (place + 4) % 8}
    me, x_place, y_place, far_place = plane_places()
    x_other, y_other = {"shard": x_place}, {"shard": y_place}
    plane = [{"shard": (me + step) % 4} for step in (1, 2, 3)]

    def tell(sem, where):
        pl.semaphore_signal(sem, inc=1, device_id=where, device_id_type=pl.DeviceIdType.MESH)

    def load(src, dst, index):
        return pltpu.make_async_copy(src, dst, r.load_sem.at[index])

    load_ffn = load(r.grad_ffn, r.ffn_buf.at[:, pl.ds(0, width)], 0)
    load_hidden = load(r.hidden, r.hidden_buf.at[:, pl.ds(0, inner_width)], 1)
    load_two = load(r.normed_two, r.two_buf, 2)
    load_small = (
        load(r.middle, r.middle_buf, 3),
        load(r.attn_out, r.attn_buf, 4),
        load(r.cotangent, r.cot_buf, 5),
        load(r.qkv, r.qkv_buf, 6),
        load(r.mixed, r.mixed_buf, 7),
        load(r.normed_cols, r.cols_buf, 8),
        load(r.token_blocks, r.token_buf, 9),
    )

    def weight_tile(index):
        return r.weights.at[pl.ds(pl.multiple_of(index * TILE, TILE), TILE)]

    def a_loads(tile, buf):
        rows = pl.ds(pl.multiple_of(tile * TILE, TILE), TILE)
        return (
            load(r.w_down.at[rows], weight_tile(buf).at[:, pl.ds(0, width)], 10 + buf),
            load(r.gate.at[:, rows], r.gate_buf.at[buf], 12 + buf),
            load(r.up.at[:, rows], r.up_buf.at[buf], 14 + buf),
        )

    def b_loads(tile):
        rows = pl.ds(pl.multiple_of(tile * TILE, TILE), TILE)
        buf = 2 - 2 * (tile % 2)
        sem = 16 + 2 * (tile % 2)
        return (
            load(r.w_gate.at[rows], weight_tile(buf).at[:, pl.ds(0, inner_width)], sem),
            load(r.w_up.at[rows], weight_tile(buf + 1).at[:, pl.ds(0, inner_width)], sem + 1),
        )

    def b_store(tile):
        columns = pl.ds(pl.multiple_of(tile * TILE, TILE), TILE)
        return pltpu.make_async_copy(
            r.stage.at[tile % 2], r.partial.at[:, columns], r.stage_sem.at[tile % 2]
        )

    load_ffn.start()
    for buf in range(2):
        for copy in a_loads(buf, buf):
            copy.start()
    load_hidden.start()
    load_two.start()
    for copy in load_small:
        copy.start()
    for copy in b_loads(0):
        copy.start()

    barrier = pltpu.get_barrier_semaphore()
    for where in [twin, inner, far_chip] + plane:
        tell(barrier, where)

    @pl.when(is_end)
    def _():
        pl.semaphore_wait(barrier, 6)

    @pl.when(jnp.logical_not(is_end))
    def _():
        tell(barrier, outer)
        pl.semaphore_wait(barrier, 7)

    load_ffn.wait()

    def a_tile(tile, buf):
        for copy in a_loads(tile, buf):
            copy.wait()
        r.wide[...] = dot_rows(r.ffn_buf[:, pl.ds(0, width)], weight_tile(buf)[:, pl.ds(0, width)])
        columns = pl.ds(pl.multiple_of(tile * TILE, TILE), TILE)

        def rows_of(index, carry):
            rows = pl.ds(pl.multiple_of(index * 32, 32), 32)
            grad = r.wide[rows]
            gate = r.gate_buf[buf, rows].astype(f32)
            up = r.up_buf[buf, rows].astype(f32)
            curve = jnp.tanh(ROOT_TWO_PI * (gate + 0.044715 * gate * gate * gate))
            slope = (1.0 - curve * curve) * (ROOT_TWO_PI * (1.0 + 3.0 * 0.044715 * gate * gate))
            gelu_slope = 0.5 * (1.0 + curve) + 0.5 * gate * slope
            r.gate_grad[rows, columns] = (grad * up * gelu_slope).astype(bf16)
            r.up_grad[rows, columns] = (grad * (0.5 * gate * (1.0 + curve))).astype(bf16)
            return carry

        lax.fori_loop(0, tokens // 32, rows_of, 0)

        @pl.when(tile + 2 < n_a)
        def _():
            for copy in a_loads(tile + 2, buf):
                copy.start()

    def b_tile(tile):
        for copy in b_loads(tile):
            copy.wait()

        @pl.when(tile >= 2)
        def _():
            b_store(tile - 2).wait()

        buf = 2 - 2 * (tile % 2)
        some = dot_rows(r.gate_grad[:, pl.ds(0, inner_width)], weight_tile(buf)[:, pl.ds(0, inner_width)])
        some += dot_rows(r.up_grad[...], weight_tile(buf + 1)[:, pl.ds(0, inner_width)])
        r.stage[tile % 2] = some.astype(bf16)
        b_store(tile).start()

        @pl.when(tile + 2 < n_b)
        def _():
            for copy in b_loads(tile + 2):
                copy.start()

    def partial_rows(owner, which):
        return r.partial.at[pl.ds(pl.multiple_of(owner * local + which * half, 16), half)]

    c_own = (
        load(partial_rows(y_place, 0), r.c_mine.at[0], 20),
        load(partial_rows(x_place, 1), r.c_mine.at[1], 21),
        load(partial_rows(me, 0), r.c_mine.at[2], 22),
        load(partial_rows(me, 1), r.c_mine.at[3], 23),
    )

    def c_send(src, index, where):
        return remote(src, r.c_landed.at[index], r.c_send.at[index], r.c_recv.at[index], where)

    c_first = (
        c_send(partial_rows(far_place, 0), 0, x_other),
        c_send(partial_rows(far_place, 1), 1, y_other),
        c_send(partial_rows(x_place, 0), 2, x_other),
        c_send(partial_rows(y_place, 1), 3, y_other),
    )
    c_on = (c_send(r.c_mine.at[0], 4, y_other), c_send(r.c_mine.at[1], 5, x_other))

    def c_start():
        b_store(n_b - 2).wait()
        b_store(n_b - 1).wait()
        for copy in c_first + c_own:
            copy.start()

    def c_pass():
        for copy in c_own:
            copy.wait()
        for index in range(2):
            c_first[index].wait_recv()
            r.c_mine[index] = add_low(r.c_mine[index], r.c_landed[index])
            c_on[index].start()

    def d_norms():
        for copy in load_small:
            copy.wait()
        for copy in c_first:
            copy.wait_send()
        for copy in c_first[2:] + c_on:
            copy.wait_recv()
        r.gain_own[...] = r.gain_parts[...]

        def rows_of(which, index, carry):
            here = pl.ds(pl.multiple_of(index * 16, 16), 16)
            rows = pl.ds(pl.multiple_of(which * half + index * 16, 16), 16)
            grad = (
                r.c_mine[2 + which, here].astype(f32)
                + r.c_landed[2 + which, here].astype(f32)
                + r.c_landed[4 + which, here].astype(f32)
            )
            middle = r.middle_buf[rows]
            inv = lax.rsqrt(jnp.mean(middle * middle, axis=-1, keepdims=True) + norm_eps)
            weighted = grad * r.gains[1:2]
            mean = jnp.mean(weighted * middle, axis=-1, keepdims=True)
            r.gain_own[2:3, 0:width] += jnp.sum(grad * middle * inv, axis=0, keepdims=True)
            grad_mid = (
                r.cot_buf[rows].astype(f32) + inv * weighted - middle * (inv * inv * inv) * mean
            )
            r.middle_buf[rows] = grad_mid
            attn = r.attn_buf[rows]
            inv = lax.rsqrt(jnp.mean(attn * attn, axis=-1, keepdims=True) + norm_eps)
            weighted = grad_mid * r.gains[0:1]
            mean = jnp.mean(weighted * attn, axis=-1, keepdims=True)
            r.gain_own[1:2, 0:width] += jnp.sum(grad_mid * attn * inv, axis=0, keepdims=True)
            grad_attn = inv * weighted - attn * (inv * inv * inv) * mean
            r.all_grad[pl.ds(pl.multiple_of(me * local + which * half + index * 16, 16), 16)] = (
                grad_attn.astype(bf16)
            )
            return carry

        for which in range(2):
            lax.fori_loop(0, half // 16, functools.partial(rows_of, which), 0)
        for copy in c_on:
            copy.wait_send()
        keep_middle.start()

    keep_middle = pltpu.make_async_copy(r.middle_buf, r.grad_middle, r.keep_sem.at[0])

    def gather_copies(rows, source, target, send_sem, recv_sem):
        def send(owner, which, index, where, src):
            here = pl.ds(pl.multiple_of(owner * 2 * rows + which * rows, 16), rows)
            return remote(
                src.at[here] if src is target else src.at[pl.ds(which * rows, rows)],
                target.at[here], send_sem.at[index], recv_sem.at[index], where,
            )

        starts = (
            send(me, 0, 0, x_other, source),
            send(me, 1, 1, y_other, source),
            send(me, 1, 2, x_other, source),
            send(me, 0, 3, y_other, source),
        )
        passes = (
            send(x_place, 0, 4, y_other, target), send(y_place, 1, 5, x_other, target)
        )
        return starts, passes

    e_first, e_on = gather_copies(half, r.all_grad, r.all_grad, r.e_send, r.e_recv)
    h_first, h_on = gather_copies(tokens // 2, r.head_grad, r.grad_qkv, r.h_send, r.h_recv)
    h_own = pltpu.make_async_copy(
        r.head_grad, r.grad_qkv.at[pl.ds(pl.multiple_of(me * tokens, 16), tokens)], r.keep_sem.at[1]
    )

    def pass_on(starts, passes):
        for index in range(2):
            starts[index].wait_recv()
            passes[index].start()

    def gathered(starts, passes):
        for copy in starts[2:] + passes:
            copy.wait_recv()
        for copy in starts + passes:
            copy.wait_send()

    load_out = load(r.w_out, r.weights.at[pl.ds(0, r.w_out.shape[0]), pl.ds(0, width)], 24)

    def g_loads(item):
        head, rows = item // n_blocks, pl.ds(pl.multiple_of((item % n_blocks) * block, block), block)
        return (
            load(r.probs.at[head, rows], r.probs_buf, 25),
            load(r.tanh.at[head, rows], r.tanh_buf, 26),
        )

    def f_mixed():
        gathered(e_first, e_on)
        load_out.wait()
        r.mixed_grad[...] = dot_rows(
            r.all_grad[...], r.weights[pl.ds(0, r.w_out.shape[0]), pl.ds(0, width)]
        ).astype(bf16)
        r.kv_grad[...] = jnp.zeros_like(r.kv_grad)
        for copy in g_loads(0):
            copy.start()

    def g_attention(item):
        head = item // n_blocks
        rows = pl.ds(pl.multiple_of((item % n_blocks) * block, block), block)
        columns = pl.ds(pl.multiple_of(head * HEAD_SIZE, HEAD_SIZE), HEAD_SIZE)
        for copy in g_loads(item):
            copy.wait()
        grad_out = r.mixed_grad[rows, columns]
        values = r.qkv_buf[:, pl.ds(q_cols + k_cols, k_cols)]
        r.score_grad[...] = dot_rows(grad_out, values)

        def rows_of(index, carry):
            here = pl.ds(pl.multiple_of(index * 16, 16), 16)
            probs = r.probs_buf[here]
            grad = r.score_grad[here]
            curve = r.tanh_buf[here]
            total = jnp.sum(probs * grad, axis=-1, keepdims=True)
            grad = probs * (grad - total) * (1.0 - curve * curve) * (HEAD_SIZE ** (-0.5))
            r.dots_grad[here] = grad.astype(bf16)
            r.probs_low[here] = probs.astype(bf16)
            return carry

        lax.fori_loop(0, block // 16, rows_of, 0)

        @pl.when(item + 1 < heads * n_blocks)
        def _():
            for copy in g_loads(item + 1):
                copy.start()

        keys = r.qkv_buf[:, pl.ds(q_cols, k_cols)]
        r.head_grad[rows, columns] = dot_plain(r.dots_grad[...], keys).astype(bf16)
        r.kv_grad[0] += dot_columns(r.dots_grad[...], r.qkv_buf[rows, columns])
        r.kv_grad[1] += dot_columns(r.probs_low[...], grad_out)

    def h_start():
        r.head_grad[:, pl.ds(q_cols, k_cols)] = r.kv_grad[0].astype(bf16)
        r.head_grad[:, pl.ds(q_cols + k_cols, k_cols)] = r.kv_grad[1].astype(bf16)
        for copy in h_first:
            copy.start()
        h_own.start()

    def side_of(owner, kind):
        buf = r.hidden_buf if owner < 2 else r.ffn_buf
        size = (q_cols, k_cols, k_cols)[kind]
        start = (0, 2 * q_cols, 2 * q_cols + 2 * k_cols)[kind] + (owner % 2) * size
        return buf.at[:, pl.ds(start, size)]

    i_loads = [
        load(
            r.grad_qkv.at[
                pl.ds(owner * tokens, tokens),
                pl.ds((0, q_cols, q_cols + k_cols)[kind], (q_cols, k_cols, k_cols)[kind]),
            ],
            side_of(owner, kind),
            27 + 3 * owner + kind,
        )
        for owner in range(4)
        for kind in range(3)
    ] + [
        load(r.w_query, r.gate_grad.at[pl.ds(0, part), pl.ds(0, 4 * q_cols)], 39),
        load(r.w_key, r.weights.at[pl.ds(0, part), pl.ds(0, 4 * k_cols)], 40),
        load(r.w_value, r.weights.at[pl.ds(0, part), pl.ds(4 * k_cols, 4 * k_cols)], 41),
    ]
    i_copies = [
        remote(
            r.head_grad.at[pl.ds(pl.multiple_of(((me + step) % 4) * local, 16), local), pl.ds(0, part_wide)],
            r.norm_grad.at[me], r.i_send.at[step - 1], r.i_recv.at[step - 1], plane[step - 1],
        )
        for step in (1, 2, 3)
    ]

    def i_start():
        gathered(h_first, h_on)
        h_own.wait()
        for copy in i_loads:
            copy.start()
        for copy in i_loads:
            copy.wait()

    def i_norm():
        def rows_of(index, carry):
            rows = pl.ds(pl.multiple_of(index * block, block), block)
            some = jnp.zeros((block, part_wide), f32)
            for owner in range(4):
                for kind, size in enumerate((q_cols, k_cols, k_cols)):
                    held = r.gate_grad if kind == 0 else r.weights
                    start = (0, 0, 4 * k_cols)[kind] + owner * size
                    some += dot_rows(
                        side_of(owner, kind)[rows], held[pl.ds(0, part_wide), pl.ds(start, size)]
                    )
            r.head_grad[rows, pl.ds(0, part_wide)] = some.astype(bf16)
            return carry

        lax.fori_loop(0, n_blocks, rows_of, 0)
        for copy in i_copies:
            copy.start()
        r.norm_grad[me] = r.head_grad[
            pl.ds(pl.multiple_of(me * local, 16), local), pl.ds(0, part_wide)
        ]

    def k_norm():
        for copy in i_copies:
            copy.wait()

        def rows_of(index, carry):
            rows = pl.ds(pl.multiple_of(index * 16, 16), 16)
            squares = jnp.zeros((16, 1), f32)
            mean = jnp.zeros((16, 1), f32)
            for owner in range(4):
                tokens_in = r.token_buf[owner, rows].astype(f32)
                weighted = r.norm_grad[owner, rows].astype(f32) * r.gain_one[owner : owner + 1]
                squares += jnp.sum(tokens_in * tokens_in, axis=-1, keepdims=True)
                mean += jnp.sum(weighted * tokens_in, axis=-1, keepdims=True)
            inv = lax.rsqrt(squares * (1.0 / width) + norm_eps)
            mean = mean * (1.0 / width)
            for owner in range(4):
                tokens_in = r.token_buf[owner, rows].astype(f32)
                grad = r.norm_grad[owner, rows].astype(f32)
                r.gain_own[4 + owner : 5 + owner, 0:part_wide] += jnp.sum(
                    grad * tokens_in * inv, axis=0, keepdims=True
                )
                weighted = grad * r.gain_one[owner : owner + 1]
                r.norm_grad[owner, rows] = (
                    inv * weighted - tokens_in * (inv * inv * inv) * mean
                ).astype(bf16)
            return carry

        lax.fori_loop(0, local // 16, rows_of, 0)
        keep_part.start()
        for copy in gain_plane:
            copy.start()

    keep_part = pltpu.make_async_copy(r.norm_grad, r.resid_part, r.keep_sem.at[2])
    gain_plane = [
        remote(r.gain_own, r.gain_plane.at[me], r.gain_send.at[i], r.gain_recv.at[i], where)
        for i, where in enumerate(plane)
    ]
    gain_rep = [
        remote(r.gain_mine.at[i], r.gain_theirs.at[i], r.gain_send.at[3 + i], r.gain_recv.at[3 + i], where)
        for i, where in enumerate((twin, next_chip, far_chip))
    ]

    def k_plane():
        for copy in gain_plane:
            copy.wait()
        r.gain_plane[me] = r.gain_own[...]
        r.gain_mine[0] = (r.gain_plane[0] + r.gain_plane[1]) + (r.gain_plane[2] + r.gain_plane[3])
        gain_rep[0].start()

    def k_rep(index):
        gain_rep[index].wait()
        total = r.gain_mine[index] + r.gain_theirs[index]
        if index < 2:
            r.gain_mine[index + 1] = total
            gain_rep[index + 1].start()
        else:
            r.gain_total[...] = total
            keep_gains.start()

    keep_gains = pltpu.make_async_copy(r.gain_total, r.gain_sums, r.keep_sem.at[3])

    sums = (r.down_sum, r.gate_sum, r.up_sum, r.out_sum)

    def by_job(step, use):
        for job in range(5):

            @pl.when((step >= first[job]) & (step < first[job + 1]))
            def _():
                use(job, step - first[job])

    def results(job, index, slot):
        if job < 4:
            rows = pl.ds(pl.multiple_of((2 * index + core) * CHUNK, CHUNK), CHUNK)
            return [(r.total.at[slot, :, pl.ds(0, sums[job].shape[1])], sums[job].at[rows])]
        rows = pl.ds(pl.multiple_of(index * CHUNK, CHUNK), CHUNK)
        pairs, start = [], 0
        for ref in (r.query_sum, r.key_sum, r.value_sum):
            size = ref.shape[1] // 2
            columns = pl.ds(pl.multiple_of(core * size, 128), size)
            pairs.append((r.total.at[slot, :, pl.ds(start, size)], ref.at[rows, columns]))
            start += size
        return pairs

    def pair_copies(job, index, step):
        slot = step % 4
        return [
            remote(src, dst, r.pair_send.at[slot, i], r.pair_recv.at[step, i], twin)
            for i, (src, dst) in enumerate(results(job, index, slot))
        ]

    def store_copies(job, index, step):
        slot = step % 4
        return [
            pltpu.make_async_copy(src, dst, r.store_sem.at[slot, i])
            for i, (src, dst) in enumerate(results(job, index, slot))
        ]

    def sib_copy(step):
        give = pl.ds(pl.multiple_of((1 - core) * CHUNK, CHUNK), CHUNK)
        return remote(
            r.made.at[step % 2, give], r.sib.at[step % 4],
            r.sib_send.at[step % 4], r.sib_recv.at[step % 4], twin,
        )

    def up_copy(step, dst, sem):
        slot = step % DEEP
        return remote(r.acc.at[slot], dst.at[slot], r.up_send.at[slot], sem.at[slot], inner)

    def down_copy(step):
        return remote(
            r.total.at[step % 4], r.inner_in.at[step % DEEP],
            r.down_send.at[step % 4], r.inner_recv.at[step % DEEP], outer,
        )

    def make(step):
        slot = step % 2

        def product(job, index):
            if job < 4:
                left_buf = (r.hidden_buf, r.two_buf, r.two_buf, r.mixed_buf)[job]
                right_buf = (r.ffn_buf, r.gate_grad, r.up_grad, r.all_grad)[job]
                columns = pl.ds(pl.multiple_of(index * PAIR, PAIR), PAIR)
                across = pl.ds(0, sums[job].shape[1])
                r.made[slot, :, across] = dot_columns(
                    left_buf[:, columns], right_buf[:, across]
                ).astype(bf16)
                return
            columns = pl.ds(pl.multiple_of((index // 2) * PAIR, PAIR), PAIR)
            for which, buf in enumerate((r.hidden_buf, r.ffn_buf)):
                r.both[...] = dot_columns(r.cols_buf[:, columns], buf[:, pl.ds(0, side)]).astype(bf16)
                r.made[slot, pl.ds(which * CHUNK, CHUNK), pl.ds(0, side)] = r.both[
                    pl.ds(pl.multiple_of((index % 2) * CHUNK, CHUNK), CHUNK)
                ]

        by_job(step, product)

        @pl.when(step >= 4)
        def _():
            pl.semaphore_wait(r.sib_credit, 1)

        sib_copy(step).start()

    def send_up(step):
        @pl.when(step >= DEEP)
        def _():
            pl.semaphore_wait(r.up_credit, 1)

        @pl.when(is_mid)
        def _():
            up_copy(step, r.inner_in, r.inner_recv).start()

        @pl.when(jnp.logical_not(is_mid))
        def _():
            up_copy(step, r.outer_in, r.outer_recv).start()

    def pair_up(step):
        slot = step % DEEP
        sib_copy(step).wait()

        @pl.when(step >= DEEP)
        def _():
            up_copy(step, r.outer_in, r.outer_recv).wait_send()

        mine = pl.ds(pl.multiple_of(core * CHUNK, CHUNK), CHUNK)
        r.acc[slot] = add_low(r.made[step % 2, mine], r.sib[step % 4])

        @pl.when(step + 4 < steps)
        def _():
            tell(r.sib_credit, twin)

        @pl.when(is_end)
        def _():
            send_up(step)

    def from_outer(step):
        slot = step % DEEP
        up_copy(step, r.outer_in, r.outer_recv).wait_recv()
        r.acc[slot] = add_low(r.acc[slot], r.outer_in[slot])

        @pl.when(step + DEEP < steps)
        def _():
            tell(r.up_credit, outer)

        send_up(step)

    def sends_done(step):
        def use(job, index):
            for copy in pair_copies(job, index, step):
                copy.wait_send()
            for copy in store_copies(job, index, step):
                copy.wait()

        by_job(step, use)

        @pl.when(jnp.logical_not(is_end))
        def _():
            down_copy(step).wait_send()

    def from_inner(step):
        slot = step % DEEP
        down_copy(step).wait_recv()

        @pl.when(step >= 4)
        def _():
            sends_done(step - 4)

        @pl.when(is_mid)
        def _():
            r.total[step % 4] = add_low(r.acc[slot], r.inner_in[slot])

            @pl.when(step + DEEP < steps)
            def _():
                tell(r.up_credit, inner)

        @pl.when(jnp.logical_not(is_mid))
        def _():
            r.total[step % 4] = r.inner_in[slot]

            @pl.when(step + DEEP < steps)
            def _():
                tell(r.down_credit, inner)

        @pl.when(jnp.logical_not(is_end))
        def _():
            @pl.when(step >= DEEP)
            def _():
                pl.semaphore_wait(r.down_credit, 1)

            down_copy(step).start()

        def use(job, index):
            for copy in pair_copies(job, index, step) + store_copies(job, index, step):
                copy.start()

        by_job(step, use)

    lag_outer = 3
    lag_inner = jnp.where(is_end, 8, 6)
    load_hidden.wait()
    load_two.wait()

    def at(now, step, use):
        @pl.when(now == step)
        def _():
            use()

    def tick(now, carry):
        @pl.when(now < steps)
        def _():
            make(now)

        @pl.when((now >= 1) & (now - 1 < steps))
        def _():
            pair_up(now - 1)

        @pl.when(jnp.logical_not(is_end) & (now >= lag_outer) & (now - lag_outer < steps))
        def _():
            from_outer(now - lag_outer)

        @pl.when((now >= lag_inner) & (now - lag_inner < steps))
        def _():
            from_inner(now - lag_inner)

        for buf in range(2):

            @pl.when(2 * now + buf < n_a)
            def _():
                a_tile(2 * now + buf, buf)

        @pl.when(now == b_at - 1)
        def _():
            for copy in b_loads(1):
                copy.start()

        @pl.when((now >= b_at) & (now < c_at))
        def _():
            b_tile(now - b_at)

        at(now, c_at, c_start)
        at(now, c_at + 1, load_out.start)
        at(now, c_at + 2, c_pass)

        @pl.when(now == d_at)
        def _():
            d_norms()
            for copy in e_first:
                copy.start()

        at(now, d_at + 2, lambda: pass_on(e_first, e_on))
        at(now, f_at, f_mixed)

        @pl.when((now >= g_at) & (now < h_at))
        def _():
            g_attention(now - g_at)

        at(now, h_at, h_start)
        at(now, h_at + 4, lambda: pass_on(h_first, h_on))
        at(now, i_at, i_start)
        at(now, i_at + 1, i_norm)
        at(now, k_at, k_norm)
        at(now, k_at + 1, k_plane)
        for index in range(3):
            at(now, k_at + 2 + index, functools.partial(k_rep, index))
        return carry

    lax.fori_loop(0, steps + 8, tick, 0)

    def finish(step, carry):
        sends_done(step)
        return carry

    lax.fori_loop(steps - 4, steps, finish, 0)

    def finish_up(step, carry):
        up_copy(step, r.outer_in, r.outer_recv).wait_send()
        return carry

    lax.fori_loop(steps - DEEP, steps, finish_up, 0)

    def arrived(step, carry):
        def use(job, index):
            for copy in pair_copies(job, index, step):
                copy.wait_recv()

        by_job(step, use)
        return carry

    lax.fori_loop(0, steps, arrived, 0)
    for copy in (keep_middle, keep_part, keep_gains):
        copy.wait()


def backward(collective_id, **args):
    f32, bf16 = jnp.float32, jnp.bfloat16
    given = types.SimpleNamespace(**args)
    tokens, width = given.grad_ffn.shape
    inner_width = given.hidden.shape[1]
    local = tokens // 4
    half = local // 2
    head_cols = given.qkv.shape[1]
    part = width // 4
    part_wide = given.gain_one.shape[1]
    out_rows = given.w_out.shape[0]
    side = 2 * head_cols
    slot_width = max(width, inner_width, side)
    block = min(TILE, tokens)
    steps = (inner_width + 2 * width + out_rows) // PAIR + part // CHUNK
    vmem, dma, credit = pltpu.VMEM, pltpu.SemaphoreType.DMA, pltpu.SemaphoreType.REGULAR
    shape = jax.ShapeDtypeStruct
    outs = dict(
        down_sum=shape((inner_width, width), bf16),
        gate_sum=shape((width, inner_width), bf16),
        up_sum=shape((width, inner_width), bf16),
        out_sum=shape((out_rows, width), bf16),
        query_sum=shape((part, side), bf16),
        key_sum=shape((part, side // 2), bf16),
        value_sum=shape((part, side // 2), bf16),
        grad_middle=shape((local, width), f32),
        resid_part=shape((4, local, part_wide), bf16),
        gain_sums=shape((8, width), f32),
        partial=shape((tokens, width), bf16),
        grad_qkv=shape((4 * tokens, head_cols), bf16),
    )
    scratch = dict(
        ffn_buf=vmem((tokens, slot_width), bf16),
        hidden_buf=vmem((tokens, slot_width), bf16),
        two_buf=vmem((tokens, width), bf16),
        gate_grad=vmem((tokens, slot_width), bf16),
        up_grad=vmem((tokens, inner_width), bf16),
        weights=vmem((4 * TILE, slot_width), bf16),
        gate_buf=vmem((2, tokens, TILE), bf16),
        up_buf=vmem((2, tokens, TILE), bf16),
        wide=vmem((tokens, TILE), f32),
        stage=vmem((2, tokens, TILE), bf16),
        c_mine=vmem((4, half, width), bf16),
        c_landed=vmem((6, half, width), bf16),
        middle_buf=vmem((local, width), f32),
        attn_buf=vmem((local, width), f32),
        cot_buf=vmem((local, width), bf16),
        qkv_buf=vmem((tokens, head_cols), bf16),
        mixed_buf=vmem((tokens, out_rows), bf16),
        cols_buf=vmem((tokens, -(-part // PAIR) * PAIR), bf16),
        token_buf=vmem((4, local, part_wide), bf16),
        all_grad=vmem((tokens, width), bf16),
        mixed_grad=vmem((tokens, out_rows), bf16),
        probs_buf=vmem((block, tokens), f32),
        tanh_buf=vmem((block, tokens), f32),
        score_grad=vmem((block, tokens), f32),
        dots_grad=vmem((block, tokens), bf16),
        probs_low=vmem((block, tokens), bf16),
        kv_grad=vmem((2, tokens, head_cols // 4), f32),
        head_grad=vmem((tokens, head_cols), bf16),
        norm_grad=vmem((4, local, part_wide), bf16),
        gain_own=vmem((8, width), f32),
        gain_plane=vmem((4, 8, width), f32),
        gain_mine=vmem((3, 8, width), f32),
        gain_theirs=vmem((3, 8, width), f32),
        gain_total=vmem((8, width), f32),
        made=vmem((2, PAIR, slot_width), bf16),
        both=vmem((PAIR, side), bf16),
        sib=vmem((4, CHUNK, slot_width), bf16),
        acc=vmem((DEEP, CHUNK, slot_width), bf16),
        outer_in=vmem((DEEP, CHUNK, slot_width), bf16),
        inner_in=vmem((DEEP, CHUNK, slot_width), bf16),
        total=vmem((4, CHUNK, slot_width), bf16),
        load_sem=dma((42,)),
        stage_sem=dma((2,)),
        keep_sem=dma((4,)),
        c_send=dma((6,)),
        c_recv=dma((6,)),
        e_send=dma((6,)),
        e_recv=dma((6,)),
        h_send=dma((6,)),
        h_recv=dma((6,)),
        i_send=dma((3,)),
        i_recv=dma((3,)),
        gain_send=dma((6,)),
        gain_recv=dma((6,)),
        sib_send=dma((4,)),
        sib_recv=dma((4,)),
        up_send=dma((DEEP,)),
        outer_recv=dma((DEEP,)),
        inner_recv=dma((DEEP,)),
        down_send=dma((4,)),
        pair_send=dma((4, 3)),
        pair_recv=dma((steps, 3)),
        store_sem=dma((4, 3)),
        sib_credit=credit,
        up_credit=credit,
        down_credit=credit,
    )
    any_space = pl.BlockSpec(memory_space=pl.ANY)
    small = pl.BlockSpec(memory_space=pltpu.VMEM)
    in_specs = [
        small if value.ndim == 2 and value.shape[0] <= 8 else any_space for value in args.values()
    ]
    results = pl.pallas_call(
        functools.partial(
            backward_kernel,
            (tokens, local, width, inner_width, head_cols),
            tuple(args) + tuple(outs) + tuple(scratch),
        ),
        out_shape=list(outs.values()),
        in_specs=in_specs,
        out_specs=[any_space] * len(outs),
        scratch_shapes=list(scratch.values()),
        compiler_params=pltpu.CompilerParams(
            collective_id=collective_id,
            has_side_effects=True,
            vmem_limit_bytes=VMEM_LIMIT,
        ),
        cost_estimate=pl.CostEstimate(
            flops=80 * tokens * width * width, bytes_accessed=400 * 2**20, transcendentals=0
        ),
    )(*args.values())
    return types.SimpleNamespace(**dict(zip(outs, results)))


VMEM_LIMIT = 63 * 2**20


QUERY_HEADS = 8
KV = 4
HEAD_SIZE = 256
SEGS = 13


softcap = 50.0
norm_eps = 1e-06


def normalize(values, gain_vec):
    inv_rms = lax.rsqrt(jnp.mean(values * values, axis=-1, keepdims=True) + norm_eps)
    return (values * inv_rms * gain_vec, inv_rms)


def norm_back(values, inv_rms, gain_vec, grad_in):
    weighted = grad_in * gain_vec
    row_mean = jnp.mean(weighted * values, axis=-1, keepdims=True)
    grad_back = inv_rms * weighted - values * (inv_rms * inv_rms * inv_rms) * row_mean
    return (grad_back, jnp.sum(grad_in * values * inv_rms, axis=0))


def geglu(gate_pre, up_pre):
    return jax.nn.gelu(gate_pre, approximate=True) * up_pre


def gather_rows(block, collective_id):
    if lax.axis_size("shard") == 4:
        return gather4(block, collective_id)
    return lax.all_gather(block, "shard", axis=0, tiled=True)


def scatter_rows(partial, collective_id):
    if lax.axis_size("shard") == 4:
        return scatter4(partial, collective_id)
    summed = lax.psum_scatter(partial, "shard", scatter_dimension=0, tiled=True)
    return summed.astype(jnp.float32)


def exchange(blocks, collective_id):
    if lax.axis_size("shard") == 4:
        return exchange4(blocks, collective_id)
    return lax.all_to_all(blocks, "shard", 0, 0, tiled=True)


def first_gather(normed, seg_ids, w_query, w_key, w_value):
    n = lax.axis_size("shard")
    tok_rows, width = normed.shape
    codes = seg_ids.astype(jnp.bfloat16)
    if n == 4:
        codes = jnp.pad(codes, (0, 2048 - tok_rows)).reshape(16, 128)
        normed_all, codes, heads = prologue4(normed, codes, w_query, w_key, w_value, 2)
        codes = codes.reshape(n, -1)[:, :tok_rows].reshape(-1)
        return normed_all, codes.astype(jnp.int32), heads
    part_rows = w_query.shape[0]
    share = max(1, n // KV)

    def by_device(weight):
        heads = weight.reshape(part_rows, KV, -1)
        if share > 1:
            heads = jnp.repeat(heads, share, axis=1)
        return heads.reshape(part_rows, n, -1)

    parts = jnp.concatenate(
        (w_query.reshape(part_rows, n, -1), by_device(w_key), by_device(w_value)), axis=2
    ).transpose(1, 0, 2)
    heads = lax.all_to_all(parts, "shard", 0, 0, tiled=True).reshape(width, -1)
    normed_all = lax.all_gather(normed, "shard", axis=0, tiled=True)
    codes = lax.all_gather(codes, "shard", axis=0, tiled=True)
    return normed_all, codes.astype(jnp.int32), heads


def rep_sum(grads, width):
    summed = chain_sum([grad.astype(jnp.bfloat16).reshape(-1, width) for grad in grads])
    return [
        total.reshape(grad.shape).astype(jnp.float32) for total, grad in zip(summed, grads)
    ]


def body(
    tokens,
    seg_ids,
    parents,
    attn_gain,
    w_query,
    w_key,
    w_value,
    w_out,
    post_attn_gain,
    ffn_gain,
    w_gate,
    w_up,
    w_down,
    post_ffn_gain,
    cotangent,
):
    f32, bf16 = jnp.float32, jnp.bfloat16
    tok_rows, width = tokens.shape
    n = lax.axis_size("shard")
    me = lax.axis_index("shard")
    group_rows = tok_rows * n
    part_rows = w_query.shape[0]
    head_scale = HEAD_SIZE ** (-0.5)
    q_heads = QUERY_HEADS // n
    kv_heads = max(1, KV // n)
    share = n * kv_heads // KV
    repeat = q_heads // kv_heads
    q_cols = q_heads * HEAD_SIZE
    k_cols = kv_heads * HEAD_SIZE
    gain_one = attn_gain.astype(f32)
    gain_two = post_attn_gain.astype(f32)
    gain_three = ffn_gain.astype(f32)
    gain_four = post_ffn_gain.astype(f32)

    residual = tokens.astype(f32)
    normed, rms_one = normalize(residual, gain_one)
    normed_all, codes, qkv_heads = first_gather(
        normed.astype(bf16), seg_ids, w_query, w_key, w_value
    )
    qkv = jnp.dot(normed_all, qkv_heads, preferred_element_type=f32).astype(bf16)
    queries = qkv[:, :q_cols].reshape(group_rows, kv_heads, repeat, HEAD_SIZE)
    keys = qkv[:, q_cols : q_cols + k_cols].reshape(group_rows, kv_heads, HEAD_SIZE)
    values = qkv[:, q_cols + k_cols :].reshape(group_rows, kv_heads, HEAD_SIZE)

    parent_row = parents[0]
    labels = jnp.arange(SEGS)

    def lookup(ident):
        return jnp.sum(jnp.where(ident[:, None] == labels[None, :], parent_row[None, :], 0), axis=1)

    parent_one = lookup(codes)
    parent_two = lookup(parent_one)
    positions = jnp.arange(group_rows)
    real = codes < SEGS
    related = (
        (codes[None, :] == codes[:, None])
        | (codes[None, :] == parent_one[:, None])
        | (codes[None, :] == parent_two[:, None])
    )
    visible = (positions[None, :] <= positions[:, None]) & real[:, None] & real[
        None, :
    ] & related | (positions[None, :] == positions[:, None])

    score_matrix = jnp.einsum("tkrh,skh->krts", queries, keys, preferred_element_type=f32)
    tanh_part = jnp.tanh(score_matrix * (head_scale / softcap))
    masked = jnp.where(visible[None, None], softcap * tanh_part, -1e30)
    row_max = jnp.max(masked, axis=-1, keepdims=True)
    expo_terms = jnp.exp(masked - row_max)
    row_total = jnp.sum(expo_terms, axis=-1, keepdims=True)
    probs = expo_terms / row_total
    probs_b = probs.astype(bf16)
    mixed = jnp.einsum("krts,skh->tkrh", probs_b, values, preferred_element_type=f32)
    mixed = mixed.reshape(group_rows, q_cols).astype(bf16)
    attn_out = scatter_rows(jnp.dot(mixed, w_out, preferred_element_type=f32).astype(bf16), 3)
    post_one, rms_two = normalize(attn_out, gain_two)
    middle = residual + post_one
    normed_two, rms_three = normalize(middle, gain_three)
    normed_two_all = gather_rows(normed_two.astype(bf16), 4)
    gate_pre = jnp.dot(normed_two_all, w_gate, preferred_element_type=f32)
    up_pre = jnp.dot(normed_two_all, w_up, preferred_element_type=f32)
    hidden, geglu_back = jax.vjp(geglu, gate_pre, up_pre)
    hidden_b = hidden.astype(bf16)
    ffn_out = scatter_rows(jnp.dot(hidden_b, w_down, preferred_element_type=f32).astype(bf16), 5)
    post_two, rms_four = normalize(ffn_out, gain_four)
    output = (middle + post_two).astype(bf16)

    grad_out = cotangent.astype(f32)
    grad_ffn, grad_gain_four = norm_back(ffn_out, rms_four, gain_four, grad_out)
    grad_ffn_all = gather_rows(grad_ffn.astype(bf16), 6)
    if n == 4 and lax.axis_size("rep") == 8:
        part_wide = -(-part_rows // 128) * 128
        widen = lambda array: jnp.pad(array, [(0, 0)] * (array.ndim - 1) + [(0, part_wide - part_rows)])
        normed_cols = lax.dynamic_slice_in_dim(normed_all, me * part_rows, part_rows, axis=1)
        nothing = jnp.zeros((width,), f32)
        found = backward(
            7,
            grad_ffn=grad_ffn_all,
            hidden=hidden_b,
            gate=gate_pre.astype(bf16),
            up=up_pre.astype(bf16),
            normed_two=normed_two_all,
            w_down=w_down,
            w_gate=w_gate,
            w_up=w_up,
            w_out=w_out,
            middle=middle,
            attn_out=attn_out,
            cotangent=cotangent,
            gains=jnp.stack([gain_two, gain_three] + [nothing] * 6),
            gain_parts=jnp.stack([grad_gain_four] + [nothing] * 7),
            gain_one=widen(gain_one.reshape(4, part_rows)),
            qkv=qkv,
            mixed=mixed,
            probs=probs.reshape(q_heads, group_rows, group_rows),
            tanh=tanh_part.reshape(q_heads, group_rows, group_rows),
            normed_cols=widen(normed_cols),
            w_query=w_query,
            w_key=w_key,
            w_value=w_value,
            token_blocks=widen(tokens.reshape(tok_rows, 4, part_rows).transpose(1, 0, 2)),
        )
        resid = found.resid_part[:, :, :part_rows].transpose(1, 0, 2).reshape(tok_rows, width)
        grad_tokens = (found.grad_middle + resid.astype(f32)).astype(bf16)
        gains = found.gain_sums
        return (
            output,
            grad_tokens,
            gains[4:, :part_rows].reshape(width),
            found.query_sum.astype(f32),
            found.key_sum.astype(f32),
            found.value_sum.astype(f32),
            found.out_sum.astype(f32),
            gains[1],
            gains[2],
            found.gate_sum.astype(f32),
            found.up_sum.astype(f32),
            found.down_sum.astype(f32),
            gains[0],
        )
    down_part = jnp.einsum("tf,td->fd", hidden_b, grad_ffn_all, preferred_element_type=f32)
    grad_hidden = jnp.einsum("td,fd->tf", grad_ffn_all, w_down, preferred_element_type=f32)
    grad_gate, grad_up = geglu_back(grad_hidden)
    grad_gate_b = grad_gate.astype(bf16)
    grad_up_b = grad_up.astype(bf16)
    grad_normed_two = jnp.einsum("tf,df->td", grad_gate_b, w_gate, preferred_element_type=f32)
    grad_normed_two += jnp.einsum("tf,df->td", grad_up_b, w_up, preferred_element_type=f32)
    grad_normed_two = scatter_rows(grad_normed_two.astype(bf16), 7)
    gate_part = jnp.einsum("td,tf->df", normed_two_all, grad_gate_b, preferred_element_type=f32)
    up_part = jnp.einsum("td,tf->df", normed_two_all, grad_up_b, preferred_element_type=f32)
    grad_middle_part, grad_gain_three = norm_back(middle, rms_three, gain_three, grad_normed_two)
    grad_middle = grad_out + grad_middle_part
    grad_attn, grad_gain_two = norm_back(attn_out, rms_two, gain_two, grad_middle)
    grad_attn_all = gather_rows(grad_attn.astype(bf16), 8)
    out_part = jnp.einsum("tj,td->jd", mixed, grad_attn_all, preferred_element_type=f32)
    grad_mixed = jnp.einsum("td,jd->tj", grad_attn_all, w_out, preferred_element_type=f32)
    grad_mixed = grad_mixed.astype(bf16).reshape(group_rows, kv_heads, repeat, HEAD_SIZE)
    grad_probs = jnp.einsum("tkrh,skh->krts", grad_mixed, values, preferred_element_type=f32)
    row_inner = jnp.sum(probs * grad_probs, axis=-1, keepdims=True)
    grad_dots = (
        probs * (grad_probs - row_inner) * (1.0 - tanh_part * tanh_part) * head_scale
    ).astype(bf16)
    grad_queries = jnp.einsum("krts,skh->tkrh", grad_dots, keys, preferred_element_type=f32)
    grad_keys = jnp.einsum("krts,tkrh->skh", grad_dots, queries, preferred_element_type=f32)
    grad_values = jnp.einsum("krts,tkrh->skh", probs_b, grad_mixed, preferred_element_type=f32)
    grad_parts = jnp.concatenate(
        (
            grad_queries.reshape(group_rows, q_cols),
            grad_keys.reshape(group_rows, k_cols),
            grad_values.reshape(group_rows, k_cols),
        ),
        axis=1,
    ).astype(bf16)
    grad_parts = gather_rows(grad_parts, 9).reshape(n, group_rows, -1)

    def whole_heads(parts):
        if share > 1:
            parts = parts.reshape(KV, share, group_rows, HEAD_SIZE).astype(f32).sum(axis=1).astype(bf16)
        return parts.transpose(1, 0, 2).reshape(group_rows, -1)

    grad_qkv = jnp.concatenate(
        (
            grad_parts[:, :, :q_cols].transpose(1, 0, 2).reshape(group_rows, -1),
            whole_heads(grad_parts[:, :, q_cols : q_cols + k_cols]),
            whole_heads(grad_parts[:, :, q_cols + k_cols :]),
        ),
        axis=1,
    )
    qkv_local = jnp.concatenate((w_query, w_key, w_value), axis=1)
    grad_normed = jnp.einsum("tj,dj->td", grad_qkv, qkv_local, preferred_element_type=f32)
    grad_normed = exchange(grad_normed.astype(bf16).reshape(n, tok_rows, part_rows), 10)
    grad_normed = grad_normed.transpose(1, 0, 2).reshape(tok_rows, width).astype(f32)
    normed_cols = lax.dynamic_slice_in_dim(normed_all, me * part_rows, part_rows, axis=1)
    qkv_part = jnp.einsum("td,tj->dj", normed_cols, grad_qkv, preferred_element_type=f32)
    grad_resid_part, grad_gain_one = norm_back(residual, rms_one, gain_one, grad_normed)
    grad_tokens = (grad_middle + grad_resid_part).astype(bf16)
    gain_parts = jnp.stack((grad_gain_one, grad_gain_two, grad_gain_three, grad_gain_four))
    gain_sums = lax.all_gather(gain_parts, ("rep", "shard"), axis=0).sum(axis=0)
    down_sum, gate_sum, up_sum, out_sum, qkv_sum = rep_sum(
        (down_part, gate_part, up_part, out_part, qkv_part), width
    )
    q_width = w_query.shape[1]
    k_width = w_key.shape[1]
    return (
        output,
        grad_tokens,
        gain_sums[0],
        qkv_sum[:, :q_width],
        qkv_sum[:, q_width : q_width + k_width],
        qkv_sum[:, q_width + k_width :],
        out_sum,
        gain_sums[1],
        gain_sums[2],
        gate_sum,
        up_sum,
        down_sum,
        gain_sums[3],
    )


def solution(mesh):
    return jax.shard_map(
        body,
        mesh=mesh,
        in_specs=(
            P(("rep", "shard"), None),
            P(("rep", "shard")),
            P("rep", None),
            P(),
            P("shard", None),
            P("shard", None),
            P("shard", None),
            P("shard", None),
            P(),
            P(),
            P(None, "shard"),
            P(None, "shard"),
            P("shard", None),
            P(),
            P(("rep", "shard"), None),
        ),
        out_specs=(
            P(("rep", "shard"), None),
            P(("rep", "shard"), None),
            P(),
            P("shard", None),
            P("shard", None),
            P("shard", None),
            P("shard", None),
            P(),
            P(),
            P(None, "shard"),
            P(None, "shard"),
            P("shard", None),
            P(),
        ),
        check_vma=False,
    )
```

```python
import functools
import math
import types

import jax
import jax.numpy as jnp
from jax import lax
from jax.experimental import pallas as pl
from jax.experimental.pallas import tpu as pltpu
from jax.sharding import PartitionSpec as P

SLOTS = 8
CHUNK = 64


def remote(src, dst, send_sem, recv_sem, where):
    return pltpu.make_async_remote_copy(
        src_ref=src,
        dst_ref=dst,
        send_sem=send_sem,
        recv_sem=recv_sem,
        device_id=where,
        device_id_type=pl.DeviceIdType.MESH,
    )


def add_low(left, right):
    return (left.astype(jnp.float32) + right.astype(jnp.float32)).astype(jnp.bfloat16)


def chain_kernel(counts, chunk, *refs):
    jobs = len(counts)
    ins, outs = refs[:jobs], refs[jobs : 2 * jobs]
    (
        mine, sib, acc, outer_in, inner_in, total,
        load_sem, sib_send, sib_recv, up_send, outer_recv, inner_recv,
        down_send, pair_send, pair_recv, store_sem,
        sib_credit, up_credit, down_credit,
    ) = refs[2 * jobs :]
    slots = mine.shape[0]
    steps = sum(counts)
    place = lax.axis_index("rep")
    chips = lax.axis_size("rep") // 2
    chip, core = place // 2, place % 2
    left = chip < chips // 2
    is_end = (chip == 0) | (chip == chips - 1)
    is_mid = (chip == chips // 2 - 1) | (chip == chips // 2)
    twin = {"rep": place + 1 - 2 * core}
    inner = {"rep": jnp.where(left, place + 2, place - 2)}
    outer = {"rep": jnp.where(is_end, place, jnp.where(left, place - 2, place + 2))}

    def tell(sem, where):
        pl.semaphore_signal(sem, inc=1, device_id=where, device_id_type=pl.DeviceIdType.MESH)

    barrier = pltpu.get_barrier_semaphore()
    tell(barrier, twin)
    tell(barrier, inner)

    @pl.when(is_end)
    def _():
        pl.semaphore_wait(barrier, 2)

    @pl.when(jnp.logical_not(is_end))
    def _():
        tell(barrier, outer)
        pl.semaphore_wait(barrier, 3)

    def with_rows(step, which, use):
        low = 0
        for job, count in enumerate(counts):
            first = low

            @pl.when((step >= low) & (step < low + count))
            def _():
                row = pl.multiple_of(((step - first) * 2 + which) * chunk, chunk)
                use(job, pl.ds(row, chunk))

            low += count

    def pair_copy(job, rows, slot, step):
        return remote(total.at[slot], outs[job].at[rows], pair_send.at[slot], pair_recv.at[step], twin)

    def up_copy(slot, dst, sem):
        return remote(acc.at[slot], dst.at[slot], up_send.at[slot], sem.at[slot], inner)

    def down_copy(slot):
        return remote(total.at[slot], inner_in.at[slot], down_send.at[slot], inner_recv.at[slot], outer)

    def sib_copy(job, rows, slot):
        return remote(ins[job].at[rows], sib.at[slot], sib_send.at[slot], sib_recv.at[slot], twin)

    def load_copy(job, rows, slot):
        return pltpu.make_async_copy(ins[job].at[rows], mine.at[slot], load_sem.at[slot])

    def store_copy(job, rows, slot):
        return pltpu.make_async_copy(total.at[slot], outs[job].at[rows], store_sem.at[slot])

    some = pl.ds(0, chunk)

    def take(step):
        slot = step % slots

        @pl.when(step >= slots)
        def _():
            pl.semaphore_wait(sib_credit, 1)

        with_rows(step, 1 - core, lambda job, rows: sib_copy(job, rows, slot).start())
        with_rows(step, core, lambda job, rows: load_copy(job, rows, slot).start())

    def send_up(step):
        slot = step % slots

        @pl.when(step >= slots)
        def _():
            pl.semaphore_wait(up_credit, 1)

        @pl.when(is_mid)
        def _():
            up_copy(slot, inner_in, inner_recv).start()

        @pl.when(jnp.logical_not(is_mid))
        def _():
            up_copy(slot, outer_in, outer_recv).start()

    def pair_up(step):
        slot = step % slots
        load_copy(0, some, slot).wait()
        sib_copy(0, some, slot).wait()

        @pl.when(step >= slots)
        def _():
            up_copy(slot, outer_in, outer_recv).wait_send()

        acc[slot] = add_low(mine[slot], sib[slot])

        @pl.when(step + slots < steps)
        def _():
            tell(sib_credit, twin)

        @pl.when(is_end)
        def _():
            send_up(step)

    def from_outer(step):
        slot = step % slots
        up_copy(slot, outer_in, outer_recv).wait_recv()
        acc[slot] = add_low(acc[slot], outer_in[slot])

        @pl.when(step + slots < steps)
        def _():
            tell(up_credit, outer)

        send_up(step)

    def sends_done(slot):
        pair_copy(0, some, slot, 0).wait_send()
        store_copy(0, some, slot).wait()

        @pl.when(jnp.logical_not(is_end))
        def _():
            down_copy(slot).wait_send()

    def from_inner(step):
        slot = step % slots
        down_copy(slot).wait_recv()

        @pl.when(step >= slots)
        def _():
            sends_done(slot)

        @pl.when(is_mid)
        def _():
            total[slot] = add_low(acc[slot], inner_in[slot])

            @pl.when(step + slots < steps)
            def _():
                tell(up_credit, inner)

        @pl.when(jnp.logical_not(is_mid))
        def _():
            total[slot] = inner_in[slot]

            @pl.when(step + slots < steps)
            def _():
                tell(down_credit, inner)

        @pl.when(jnp.logical_not(is_end))
        def _():
            @pl.when(step >= slots)
            def _():
                pl.semaphore_wait(down_credit, 1)

            down_copy(slot).start()

        with_rows(step, core, lambda job, rows: pair_copy(job, rows, slot, step).start())
        with_rows(step, core, lambda job, rows: store_copy(job, rows, slot).start())

    lag_outer = 3
    lag_inner = jnp.where(is_end, 8, 6)

    def tick(step, carry):
        @pl.when(step < steps)
        def _():
            take(step)

        @pl.when((step >= 1) & (step - 1 < steps))
        def _():
            pair_up(step - 1)

        @pl.when(jnp.logical_not(is_end) & (step >= lag_outer) & (step - lag_outer < steps))
        def _():
            from_outer(step - lag_outer)

        @pl.when((step >= lag_inner) & (step - lag_inner < steps))
        def _():
            from_inner(step - lag_inner)

        return carry

    lax.fori_loop(0, steps + 8, tick, 0)

    def finish(step, carry):
        slot = step % slots
        sends_done(slot)
        up_copy(slot, outer_in, outer_recv).wait_send()
        return carry

    lax.fori_loop(steps - slots, steps, finish, 0)

    def arrived(step, carry):
        pair_copy(0, some, 0, step).wait_recv()
        return carry

    lax.fori_loop(0, steps, arrived, 0)


def chain_sum(parts, chunk=CHUNK, collective_id=1):
    width = parts[0].shape[1]
    counts = tuple(part.shape[0] // (2 * chunk) for part in parts)
    steps = sum(counts)
    slots = min(SLOTS, steps)
    any_space = pl.BlockSpec(memory_space=pl.ANY)
    block = pltpu.VMEM((slots, chunk, width), jnp.bfloat16)
    sems = pltpu.SemaphoreType.DMA((slots,))
    credit = pltpu.SemaphoreType.REGULAR
    return pl.pallas_call(
        functools.partial(chain_kernel, counts, chunk),
        out_shape=[jax.ShapeDtypeStruct(part.shape, part.dtype) for part in parts],
        in_specs=[any_space] * len(parts),
        out_specs=[any_space] * len(parts),
        scratch_shapes=[block] * 6
        + [sems] * 8
        + [pltpu.SemaphoreType.DMA((steps,)), sems, credit, credit, credit],
        compiler_params=pltpu.CompilerParams(
            collective_id=collective_id, has_side_effects=True, vmem_limit_bytes=48 * 1024 * 1024
        ),
        cost_estimate=pl.CostEstimate(
            flops=0, bytes_accessed=8 * sum(part.size for part in parts), transcendentals=0
        ),
    )(*parts)


def plane_places():
    me = lax.axis_index("shard")
    x_other = me + 1 - 2 * (me % 2)
    y_other = (me + 2) % 4
    far = x_other + y_other - me
    return me, x_other, y_other, far


def greet(places):
    barrier = pltpu.get_barrier_semaphore()
    for place in places:
        pl.semaphore_signal(
            barrier, inc=1, device_id={"shard": place}, device_id_type=pl.DeviceIdType.MESH
        )
    pl.semaphore_wait(barrier, len(places))


def gather_kernel(x_ref, out_ref, send_sem, recv_sem, local_sem):
    me, x_other, y_other, far = plane_places()
    rows = x_ref.shape[0]
    half = rows // 2

    def part(block, which):
        return out_ref.at[pl.ds(pl.multiple_of(block * rows + which * half, 16), half)]

    def own(which):
        return x_ref.at[pl.ds(which * half, half)]

    def send(src, dst, index, where):
        return remote(src, dst, send_sem.at[index], recv_sem.at[index], {"shard": where})

    greet((x_other, y_other))
    local = pltpu.make_async_copy(
        x_ref, out_ref.at[pl.ds(pl.multiple_of(me * rows, 16), rows)], local_sem
    )
    first = (
        send(own(0), part(me, 0), 0, x_other),
        send(own(1), part(me, 1), 1, y_other),
        send(own(1), part(me, 1), 2, x_other),
        send(own(0), part(me, 0), 3, y_other),
    )
    for copy in first:
        copy.start()
    local.start()
    first[0].wait_recv()
    on_y = send(part(x_other, 0), part(x_other, 0), 4, y_other)
    on_y.start()
    first[1].wait_recv()
    on_x = send(part(y_other, 1), part(y_other, 1), 5, x_other)
    on_x.start()
    first[2].wait_recv()
    first[3].wait_recv()
    on_y.wait_recv()
    on_x.wait_recv()
    for copy in first + (on_y, on_x):
        copy.wait_send()
    local.wait()


def gather4(block, collective_id):
    rows, width = block.shape
    sems = pltpu.SemaphoreType.DMA((6,))
    any_space = pl.BlockSpec(memory_space=pl.ANY)
    return pl.pallas_call(
        gather_kernel,
        out_shape=jax.ShapeDtypeStruct((4 * rows, width), block.dtype),
        in_specs=[any_space],
        out_specs=any_space,
        scratch_shapes=[sems, sems, pltpu.SemaphoreType.DMA],
        compiler_params=pltpu.CompilerParams(collective_id=collective_id, has_side_effects=True),
        cost_estimate=pl.CostEstimate(
            flops=0, bytes_accessed=40 * rows * width * 2, transcendentals=0
        ),
    )(block)


def scatter_kernel(part_ref, out_ref, *scratch):
    landed, mine, passed = scratch[:3]
    send_sem, recv_sem, load_sem = scratch[3:]
    me, x_other, y_other, far = plane_places()
    rows = out_ref.shape[0]
    half = rows // 2

    def part(block, which):
        return part_ref.at[pl.ds(pl.multiple_of(block * rows + which * half, 16), half)]

    def send(src, index, where):
        return remote(
            src, landed.at[index], send_sem.at[index], recv_sem.at[index], {"shard": where}
        )

    def load(src, index):
        return pltpu.make_async_copy(src, mine.at[index], load_sem.at[index])

    loads = (
        load(part(y_other, 0), 0),
        load(part(x_other, 1), 1),
        load(part(me, 0), 2),
        load(part(me, 1), 3),
    )
    for copy in loads:
        copy.start()
    greet((x_other, y_other))
    first = (
        send(part(far, 0), 0, x_other),
        send(part(far, 1), 1, y_other),
        send(part(x_other, 0), 2, x_other),
        send(part(y_other, 1), 3, y_other),
    )
    for copy in first:
        copy.start()
    for copy in loads:
        copy.wait()
    first[0].wait_recv()
    passed[0] = add_low(landed[0], mine[0])
    on_y = send(passed.at[0], 4, y_other)
    on_y.start()
    first[1].wait_recv()
    passed[1] = add_low(landed[1], mine[1])
    on_x = send(passed.at[1], 5, x_other)
    on_x.start()
    first[2].wait_recv()
    mine[2] = add_low(landed[2], mine[2])
    first[3].wait_recv()
    mine[3] = add_low(landed[3], mine[3])
    on_y.wait_recv()
    out_ref[pl.ds(0, half)] = mine[2].astype(jnp.float32) + landed[4].astype(jnp.float32)
    on_x.wait_recv()
    out_ref[pl.ds(half, half)] = mine[3].astype(jnp.float32) + landed[5].astype(jnp.float32)
    for copy in first + (on_y, on_x):
        copy.wait_send()


def scatter4(partial, collective_id):
    rows, width = partial.shape[0] // 4, partial.shape[1]
    half = rows // 2
    return pl.pallas_call(
        scatter_kernel,
        out_shape=jax.ShapeDtypeStruct((rows, width), jnp.float32),
        in_specs=[pl.BlockSpec(memory_space=pl.ANY)],
        out_specs=pl.BlockSpec(memory_space=pltpu.VMEM),
        scratch_shapes=[
            pltpu.VMEM((6, half, width), partial.dtype),
            pltpu.VMEM((4, half, width), partial.dtype),
            pltpu.VMEM((2, half, width), partial.dtype),
            pltpu.SemaphoreType.DMA((6,)),
            pltpu.SemaphoreType.DMA((6,)),
            pltpu.SemaphoreType.DMA((4,)),
        ],
        compiler_params=pltpu.CompilerParams(
            collective_id=collective_id, has_side_effects=True, vmem_limit_bytes=32 * 1024 * 1024
        ),
        cost_estimate=pl.CostEstimate(
            flops=0, bytes_accessed=40 * rows * width * 2, transcendentals=0
        ),
    )(partial)


def exchange_kernel(x_ref, out_ref, send_sem, recv_sem, local_sem):
    me = lax.axis_index("shard")
    others = [(me + step) % 4 for step in (1, 2, 3)]
    greet(others)
    local = pltpu.make_async_copy(x_ref.at[me], out_ref.at[me], local_sem)
    local.start()
    copies = [
        remote(x_ref.at[place], out_ref.at[me], send_sem.at[i], recv_sem.at[i], {"shard": place})
        for i, place in enumerate(others)
    ]
    for copy in copies:
        copy.start()
    for copy in copies:
        copy.wait()
    local.wait()


def exchange4(blocks, collective_id):
    any_space = pl.BlockSpec(memory_space=pl.ANY)
    sems = pltpu.SemaphoreType.DMA((3,))
    return pl.pallas_call(
        exchange_kernel,
        out_shape=jax.ShapeDtypeStruct(blocks.shape, blocks.dtype),
        in_specs=[any_space],
        out_specs=any_space,
        scratch_shapes=[sems, sems, pltpu.SemaphoreType.DMA],
        compiler_params=pltpu.CompilerParams(collective_id=collective_id, has_side_effects=True),
        cost_estimate=pl.CostEstimate(
            flops=0, bytes_accessed=10 * blocks.size * 2, transcendentals=0
        ),
    )(blocks)


def prologue_kernel(counts, x_ref, code_ref, query_ref, key_ref, value_ref, out_ref, codes_ref,
                    heads_ref, send_sem, recv_sem, local_sem, code_send, code_recv,
                    head_send, head_recv, twin_send, twin_recv, head_local):
    me, x_other, y_other, far = plane_places()
    place = lax.axis_index("rep")
    core = place % 2
    twin = {"rep": place + 1 - 2 * core}
    others = (x_other, y_other, far)
    rows = x_ref.shape[0]
    half = rows // 2
    depth = query_ref.shape[0]
    part_depth = depth // 2
    weights = (query_ref, key_ref, value_ref)
    starts = (0, counts[0], counts[0] + counts[1])

    barrier = pltpu.get_barrier_semaphore()
    for other in others:
        pl.semaphore_signal(
            barrier, inc=1, device_id={"shard": other}, device_id_type=pl.DeviceIdType.MESH
        )
    pl.semaphore_signal(barrier, inc=1, device_id=twin, device_id_type=pl.DeviceIdType.MESH)
    pl.semaphore_wait(barrier, 4)

    def my_rows(owner):
        return pl.ds(pl.multiple_of(owner * depth + core * part_depth, 16), part_depth)

    def head_copy(index, kind, other):
        columns = pl.ds(pl.multiple_of(other * counts[kind], 128), counts[kind])
        return remote(
            weights[kind].at[pl.ds(pl.multiple_of(core * part_depth, 16), part_depth), columns],
            heads_ref.at[my_rows(me), pl.ds(starts[kind], counts[kind])],
            head_send.at[index, kind],
            head_recv.at[index, kind],
            {"shard": other},
        )

    def part(block, which):
        return out_ref.at[pl.ds(pl.multiple_of(block * rows + which * half, 16), half)]

    def own(which):
        return x_ref.at[pl.ds(which * half, half)]

    def send(src, dst, index, where):
        return remote(src, dst, send_sem.at[index], recv_sem.at[index], {"shard": where})

    head_copies = [
        [head_copy(index, kind, other) for kind in range(3)] for index, other in enumerate(others)
    ]
    for index in (2, 0, 1):
        for copy in head_copies[index]:
            copy.start()
    code_copies = [
        remote(
            code_ref, codes_ref.at[me], code_send.at[index], code_recv.at[index], {"shard": other}
        )
        for index, other in enumerate(others)
    ]
    for copy in code_copies:
        copy.start()
    first = (
        send(own(0), part(me, 0), 0, x_other),
        send(own(1), part(me, 1), 1, y_other),
        send(own(1), part(me, 1), 2, x_other),
        send(own(0), part(me, 0), 3, y_other),
    )
    for copy in first:
        copy.start()
    locals_ = [
        pltpu.make_async_copy(
            x_ref, out_ref.at[pl.ds(pl.multiple_of(me * rows, 16), rows)], local_sem.at[0]
        ),
        pltpu.make_async_copy(code_ref, codes_ref.at[me], local_sem.at[1]),
    ]
    for kind in range(3):
        columns = pl.ds(pl.multiple_of(me * counts[kind], 128), counts[kind])
        locals_.append(
            pltpu.make_async_copy(
                weights[kind].at[:, columns],
                heads_ref.at[
                    pl.ds(pl.multiple_of(me * depth, 16), depth), pl.ds(starts[kind], counts[kind])
                ],
                head_local.at[kind],
            )
        )
    for copy in locals_:
        copy.start()
    twins = []
    for index in (0, 1, 2):
        for copy in head_copies[index]:
            copy.wait_recv()
        block = heads_ref.at[my_rows(others[index])]
        twins.append(remote(block, block, twin_send.at[index], twin_recv.at[index], twin))
        twins[-1].start()
    first[0].wait_recv()
    on_y = send(part(x_other, 0), part(x_other, 0), 4, y_other)
    on_y.start()
    first[1].wait_recv()
    on_x = send(part(y_other, 1), part(y_other, 1), 5, x_other)
    on_x.start()
    first[2].wait_recv()
    first[3].wait_recv()
    for copy in code_copies + twins:
        copy.wait_recv()
    on_y.wait_recv()
    on_x.wait_recv()
    for copy in list(first) + [on_y, on_x] + code_copies + twins:
        copy.wait_send()
    for group in head_copies:
        for copy in group:
            copy.wait_send()
    for copy in locals_:
        copy.wait()


def prologue4(block, codes, w_query, w_key, w_value, collective_id):
    rows, width = block.shape
    counts = tuple(weight.shape[1] // 4 for weight in (w_query, w_key, w_value))
    depth = w_query.shape[0]
    any_space = pl.BlockSpec(memory_space=pl.ANY)
    dma = pltpu.SemaphoreType.DMA
    return pl.pallas_call(
        functools.partial(prologue_kernel, counts),
        out_shape=(
            jax.ShapeDtypeStruct((4 * rows, width), block.dtype),
            jax.ShapeDtypeStruct((4,) + codes.shape, codes.dtype),
            jax.ShapeDtypeStruct((4 * depth, sum(counts)), w_query.dtype),
        ),
        in_specs=[any_space] * 5,
        out_specs=[any_space] * 3,
        scratch_shapes=[
            dma((6,)), dma((6,)), dma((2,)), dma((3,)), dma((3,)),
            dma((3, 3)), dma((3, 3)), dma((3,)), dma((3,)), dma((3,)),
        ],
        compiler_params=pltpu.CompilerParams(collective_id=collective_id, has_side_effects=True),
        cost_estimate=pl.CostEstimate(
            flops=0, bytes_accessed=80 * rows * width * 2, transcendentals=0
        ),
    )(block, codes, w_query, w_key, w_value)


TILE = 256
PAIR = 2 * CHUNK
DEEP = 8
ROOT_TWO_PI = math.sqrt(2.0 / math.pi)


def dot_rows(left, right):
    return lax.dot_general(left, right, (((1,), (1,)), ((), ())), preferred_element_type=jnp.float32)


def dot_plain(left, right):
    return lax.dot_general(left, right, (((1,), (0,)), ((), ())), preferred_element_type=jnp.float32)


def dot_columns(left, right):
    return lax.dot_general(left, right, (((0,), (0,)), ((), ())), preferred_element_type=jnp.float32)


def backward_kernel(dims, names, *refs):
    r = types.SimpleNamespace(**dict(zip(names, refs)))
    tokens, local, width, inner_width, head_cols = dims
    f32, bf16 = jnp.float32, jnp.bfloat16
    half = local // 2
    q_cols = head_cols // 2
    k_cols = head_cols // 4
    heads = q_cols // HEAD_SIZE
    part = width // 4
    part_wide = r.gain_one.shape[1]
    side = 2 * head_cols
    n_a = inner_width // TILE
    n_b = width // TILE
    block = min(TILE, tokens)
    n_blocks = tokens // block

    counts = (
        inner_width // PAIR, width // PAIR, width // PAIR, r.w_out.shape[0] // PAIR, part // CHUNK
    )
    first = [sum(counts[:job]) for job in range(6)]
    steps = first[5]
    b_at = (n_a + 1) // 2
    c_at = b_at + n_b
    d_at = c_at + 5
    f_at = d_at + 5
    g_at = f_at + 1
    h_at = g_at + heads * n_blocks
    i_at = h_at + 9
    k_at = i_at + 3
    assert b_at <= first[1] and f_at < first[3] and i_at < first[4] and first[1] <= i_at
    assert first[2] <= i_at and k_at + 5 <= steps + 8

    place = lax.axis_index("rep")
    chips = lax.axis_size("rep") // 2
    chip, core = place // 2, place % 2
    left = chip < chips // 2
    is_end = (chip == 0) | (chip == chips - 1)
    is_mid = (chip == chips // 2 - 1) | (chip == chips // 2)
    twin = {"rep": place + 1 - 2 * core}
    inner = {"rep": jnp.where(left, place + 2, place - 2)}
    outer = {"rep": jnp.where(is_end, place, jnp.where(left, place - 2, place + 2))}
    next_chip = {"rep": place + 2 - 4 * (chip % 2)}
    far_chip = {"rep": (place + 4) % 8}
    me, x_place, y_place, far_place = plane_places()
    x_other, y_other = {"shard": x_place}, {"shard": y_place}
    plane = [{"shard": (me + step) % 4} for step in (1, 2, 3)]

    def tell(sem, where):
        pl.semaphore_signal(sem, inc=1, device_id=where, device_id_type=pl.DeviceIdType.MESH)

    def load(src, dst, index):
        return pltpu.make_async_copy(src, dst, r.load_sem.at[index])

    load_ffn = load(r.grad_ffn, r.ffn_buf.at[:, pl.ds(0, width)], 0)
    load_hidden = load(r.hidden, r.hidden_buf.at[:, pl.ds(0, inner_width)], 1)
    load_two = load(r.normed_two, r.two_buf, 2)
    load_small = (
        load(r.middle, r.middle_buf, 3),
        load(r.attn_out, r.attn_buf, 4),
        load(r.cotangent, r.cot_buf, 5),
        load(r.qkv, r.qkv_buf, 6),
        load(r.mixed, r.mixed_buf, 7),
        load(r.normed_cols, r.cols_buf, 8),
        load(r.token_blocks, r.token_buf, 9),
    )

    def weight_tile(index):
        return r.weights.at[pl.ds(pl.multiple_of(index * TILE, TILE), TILE)]

    def a_loads(tile, buf):
        rows = pl.ds(pl.multiple_of(tile * TILE, TILE), TILE)
        return (
            load(r.w_down.at[rows], weight_tile(buf).at[:, pl.ds(0, width)], 10 + buf),
            load(r.gate.at[:, rows], r.gate_buf.at[buf], 12 + buf),
            load(r.up.at[:, rows], r.up_buf.at[buf], 14 + buf),
        )

    def b_loads(tile):
        rows = pl.ds(pl.multiple_of(tile * TILE, TILE), TILE)
        buf = 2 - 2 * (tile % 2)
        sem = 16 + 2 * (tile % 2)
        return (
            load(r.w_gate.at[rows], weight_tile(buf).at[:, pl.ds(0, inner_width)], sem),
            load(r.w_up.at[rows], weight_tile(buf + 1).at[:, pl.ds(0, inner_width)], sem + 1),
        )

    def b_store(tile):
        columns = pl.ds(pl.multiple_of(tile * TILE, TILE), TILE)
        return pltpu.make_async_copy(
            r.stage.at[tile % 2], r.partial.at[:, columns], r.stage_sem.at[tile % 2]
        )

    load_ffn.start()
    for buf in range(2):
        for copy in a_loads(buf, buf):
            copy.start()
    load_hidden.start()
    load_two.start()
    for copy in load_small:
        copy.start()
    for copy in b_loads(0):
        copy.start()

    barrier = pltpu.get_barrier_semaphore()
    for where in [twin, inner, far_chip] + plane:
        tell(barrier, where)

    @pl.when(is_end)
    def _():
        pl.semaphore_wait(barrier, 6)

    @pl.when(jnp.logical_not(is_end))
    def _():
        tell(barrier, outer)
        pl.semaphore_wait(barrier, 7)

    load_ffn.wait()

    def a_tile(tile, buf):
        for copy in a_loads(tile, buf):
            copy.wait()
        r.wide[...] = dot_rows(r.ffn_buf[:, pl.ds(0, width)], weight_tile(buf)[:, pl.ds(0, width)])
        columns = pl.ds(pl.multiple_of(tile * TILE, TILE), TILE)

        def rows_of(index, carry):
            rows = pl.ds(pl.multiple_of(index * 32, 32), 32)
            grad = r.wide[rows]
            gate = r.gate_buf[buf, rows].astype(f32)
            up = r.up_buf[buf, rows].astype(f32)
            curve = jnp.tanh(ROOT_TWO_PI * (gate + 0.044715 * gate * gate * gate))
            slope = (1.0 - curve * curve) * (ROOT_TWO_PI * (1.0 + 3.0 * 0.044715 * gate * gate))
            gelu_slope = 0.5 * (1.0 + curve) + 0.5 * gate * slope
            r.gate_grad[rows, columns] = (grad * up * gelu_slope).astype(bf16)
            r.up_grad[rows, columns] = (grad * (0.5 * gate * (1.0 + curve))).astype(bf16)
            return carry

        lax.fori_loop(0, tokens // 32, rows_of, 0)

        @pl.when(tile + 2 < n_a)
        def _():
            for copy in a_loads(tile + 2, buf):
                copy.start()

    def b_tile(tile):
        for copy in b_loads(tile):
            copy.wait()

        @pl.when(tile >= 2)
        def _():
            b_store(tile - 2).wait()

        buf = 2 - 2 * (tile % 2)
        some = dot_rows(r.gate_grad[:, pl.ds(0, inner_width)], weight_tile(buf)[:, pl.ds(0, inner_width)])
        some += dot_rows(r.up_grad[...], weight_tile(buf + 1)[:, pl.ds(0, inner_width)])
        r.stage[tile % 2] = some.astype(bf16)
        b_store(tile).start()

        @pl.when(tile + 2 < n_b)
        def _():
            for copy in b_loads(tile + 2):
                copy.start()

    def partial_rows(owner, which):
        return r.partial.at[pl.ds(pl.multiple_of(owner * local + which * half, 16), half)]

    c_own = (
        load(partial_rows(y_place, 0), r.c_mine.at[0], 20),
        load(partial_rows(x_place, 1), r.c_mine.at[1], 21),
        load(partial_rows(me, 0), r.c_mine.at[2], 22),
        load(partial_rows(me, 1), r.c_mine.at[3], 23),
    )

    def c_send(src, index, where):
        return remote(src, r.c_landed.at[index], r.c_send.at[index], r.c_recv.at[index], where)

    c_first = (
        c_send(partial_rows(far_place, 0), 0, x_other),
        c_send(partial_rows(far_place, 1), 1, y_other),
        c_send(partial_rows(x_place, 0), 2, x_other),
        c_send(partial_rows(y_place, 1), 3, y_other),
    )
    c_on = (c_send(r.c_mine.at[0], 4, y_other), c_send(r.c_mine.at[1], 5, x_other))

    def c_start():
        b_store(n_b - 2).wait()
        b_store(n_b - 1).wait()
        for copy in c_first + c_own:
            copy.start()

    def c_pass():
        for copy in c_own:
            copy.wait()
        for index in range(2):
            c_first[index].wait_recv()
            r.c_mine[index] = add_low(r.c_mine[index], r.c_landed[index])
            c_on[index].start()

    def d_norms():
        for copy in load_small:
            copy.wait()
        for copy in c_first:
            copy.wait_send()
        for copy in c_first[2:] + c_on:
            copy.wait_recv()
        r.gain_own[...] = r.gain_parts[...]

        def rows_of(which, index, carry):
            here = pl.ds(pl.multiple_of(index * 16, 16), 16)
            rows = pl.ds(pl.multiple_of(which * half + index * 16, 16), 16)
            grad = (
                r.c_mine[2 + which, here].astype(f32)
                + r.c_landed[2 + which, here].astype(f32)
                + r.c_landed[4 + which, here].astype(f32)
            )
            middle = r.middle_buf[rows]
            inv = lax.rsqrt(jnp.mean(middle * middle, axis=-1, keepdims=True) + norm_eps)
            weighted = grad * r.gains[1:2]
            mean = jnp.mean(weighted * middle, axis=-1, keepdims=True)
            r.gain_own[2:3, 0:width] += jnp.sum(grad * middle * inv, axis=0, keepdims=True)
            grad_mid = (
                r.cot_buf[rows].astype(f32) + inv * weighted - middle * (inv * inv * inv) * mean
            )
            r.middle_buf[rows] = grad_mid
            attn = r.attn_buf[rows]
            inv = lax.rsqrt(jnp.mean(attn * attn, axis=-1, keepdims=True) + norm_eps)
            weighted = grad_mid * r.gains[0:1]
            mean = jnp.mean(weighted * attn, axis=-1, keepdims=True)
            r.gain_own[1:2, 0:width] += jnp.sum(grad_mid * attn * inv, axis=0, keepdims=True)
            grad_attn = inv * weighted - attn * (inv * inv * inv) * mean
            r.all_grad[pl.ds(pl.multiple_of(me * local + which * half + index * 16, 16), 16)] = (
                grad_attn.astype(bf16)
            )
            return carry

        for which in range(2):
            lax.fori_loop(0, half // 16, functools.partial(rows_of, which), 0)
        for copy in c_on:
            copy.wait_send()
        keep_middle.start()

    keep_middle = pltpu.make_async_copy(r.middle_buf, r.grad_middle, r.keep_sem.at[0])

    def gather_copies(rows, source, target, send_sem, recv_sem):
        def send(owner, which, index, where, src):
            here = pl.ds(pl.multiple_of(owner * 2 * rows + which * rows, 16), rows)
            return remote(
                src.at[here] if src is target else src.at[pl.ds(which * rows, rows)],
                target.at[here], send_sem.at[index], recv_sem.at[index], where,
            )

        starts = (
            send(me, 0, 0, x_other, source),
            send(me, 1, 1, y_other, source),
            send(me, 1, 2, x_other, source),
            send(me, 0, 3, y_other, source),
        )
        passes = (
            send(x_place, 0, 4, y_other, target), send(y_place, 1, 5, x_other, target)
        )
        return starts, passes

    e_first, e_on = gather_copies(half, r.all_grad, r.all_grad, r.e_send, r.e_recv)
    h_first, h_on = gather_copies(tokens // 2, r.head_grad, r.grad_qkv, r.h_send, r.h_recv)
    h_own = pltpu.make_async_copy(
        r.head_grad, r.grad_qkv.at[pl.ds(pl.multiple_of(me * tokens, 16), tokens)], r.keep_sem.at[1]
    )

    def pass_on(starts, passes):
        for index in range(2):
            starts[index].wait_recv()
            passes[index].start()

    def gathered(starts, passes):
        for copy in starts[2:] + passes:
            copy.wait_recv()
        for copy in starts + passes:
            copy.wait_send()

    load_out = load(r.w_out, r.weights.at[pl.ds(0, r.w_out.shape[0]), pl.ds(0, width)], 24)

    def g_loads(item):
        head, rows = item // n_blocks, pl.ds(pl.multiple_of((item % n_blocks) * block, block), block)
        return (
            load(r.probs.at[head, rows], r.probs_buf, 25),
            load(r.tanh.at[head, rows], r.tanh_buf, 26),
        )

    def f_mixed():
        gathered(e_first, e_on)
        load_out.wait()
        r.mixed_grad[...] = dot_rows(
            r.all_grad[...], r.weights[pl.ds(0, r.w_out.shape[0]), pl.ds(0, width)]
        ).astype(bf16)
        r.kv_grad[...] = jnp.zeros_like(r.kv_grad)
        for copy in g_loads(0):
            copy.start()

    def g_attention(item):
        head = item // n_blocks
        rows = pl.ds(pl.multiple_of((item % n_blocks) * block, block), block)
        columns = pl.ds(pl.multiple_of(head * HEAD_SIZE, HEAD_SIZE), HEAD_SIZE)
        for copy in g_loads(item):
            copy.wait()
        grad_out = r.mixed_grad[rows, columns]
        values = r.qkv_buf[:, pl.ds(q_cols + k_cols, k_cols)]
        r.score_grad[...] = dot_rows(grad_out, values)

        def rows_of(index, carry):
            here = pl.ds(pl.multiple_of(index * 16, 16), 16)
            probs = r.probs_buf[here]
            grad = r.score_grad[here]
            curve = r.tanh_buf[here]
            total = jnp.sum(probs * grad, axis=-1, keepdims=True)
            grad = probs * (grad - total) * (1.0 - curve * curve) * (HEAD_SIZE ** (-0.5))
            r.dots_grad[here] = grad.astype(bf16)
            r.probs_low[here] = probs.astype(bf16)
            return carry

        lax.fori_loop(0, block // 16, rows_of, 0)

        @pl.when(item + 1 < heads * n_blocks)
        def _():
            for copy in g_loads(item + 1):
                copy.start()

        keys = r.qkv_buf[:, pl.ds(q_cols, k_cols)]
        r.head_grad[rows, columns] = dot_plain(r.dots_grad[...], keys).astype(bf16)
        r.kv_grad[0] += dot_columns(r.dots_grad[...], r.qkv_buf[rows, columns])
        r.kv_grad[1] += dot_columns(r.probs_low[...], grad_out)

    def h_start():
        r.head_grad[:, pl.ds(q_cols, k_cols)] = r.kv_grad[0].astype(bf16)
        r.head_grad[:, pl.ds(q_cols + k_cols, k_cols)] = r.kv_grad[1].astype(bf16)
        for copy in h_first:
            copy.start()
        h_own.start()

    def side_of(owner, kind):
        buf = r.hidden_buf if owner < 2 else r.ffn_buf
        size = (q_cols, k_cols, k_cols)[kind]
        start = (0, 2 * q_cols, 2 * q_cols + 2 * k_cols)[kind] + (owner % 2) * size
        return buf.at[:, pl.ds(start, size)]

    i_loads = [
        load(
            r.grad_qkv.at[
                pl.ds(owner * tokens, tokens),
                pl.ds((0, q_cols, q_cols + k_cols)[kind], (q_cols, k_cols, k_cols)[kind]),
            ],
            side_of(owner, kind),
            27 + 3 * owner + kind,
        )
        for owner in range(4)
        for kind in range(3)
    ] + [
        load(r.w_query, r.gate_grad.at[pl.ds(0, part), pl.ds(0, 4 * q_cols)], 39),
        load(r.w_key, r.weights.at[pl.ds(0, part), pl.ds(0, 4 * k_cols)], 40),
        load(r.w_value, r.weights.at[pl.ds(0, part), pl.ds(4 * k_cols, 4 * k_cols)], 41),
    ]
    i_copies = [
        remote(
            r.head_grad.at[pl.ds(pl.multiple_of(((me + step) % 4) * local, 16), local), pl.ds(0, part_wide)],
            r.norm_grad.at[me], r.i_send.at[step - 1], r.i_recv.at[step - 1], plane[step - 1],
        )
        for step in (1, 2, 3)
    ]

    def i_start():
        gathered(h_first, h_on)
        h_own.wait()
        for copy in i_loads:
            copy.start()
        for copy in i_loads:
            copy.wait()

    def i_norm():
        def rows_of(index, carry):
            rows = pl.ds(pl.multiple_of(index * block, block), block)
            some = jnp.zeros((block, part_wide), f32)
            for owner in range(4):
                for kind, size in enumerate((q_cols, k_cols, k_cols)):
                    held = r.gate_grad if kind == 0 else r.weights
                    start = (0, 0, 4 * k_cols)[kind] + owner * size
                    some += dot_rows(
                        side_of(owner, kind)[rows], held[pl.ds(0, part_wide), pl.ds(start, size)]
                    )
            r.head_grad[rows, pl.ds(0, part_wide)] = some.astype(bf16)
            return carry

        lax.fori_loop(0, n_blocks, rows_of, 0)
        for copy in i_copies:
            copy.start()
        r.norm_grad[me] = r.head_grad[
            pl.ds(pl.multiple_of(me * local, 16), local), pl.ds(0, part_wide)
        ]

    def k_norm():
        for copy in i_copies:
            copy.wait()

        def rows_of(index, carry):
            rows = pl.ds(pl.multiple_of(index * 16, 16), 16)
            squares = jnp.zeros((16, 1), f32)
            mean = jnp.zeros((16, 1), f32)
            for owner in range(4):
                tokens_in = r.token_buf[owner, rows].astype(f32)
                weighted = r.norm_grad[owner, rows].astype(f32) * r.gain_one[owner : owner + 1]
                squares += jnp.sum(tokens_in * tokens_in, axis=-1, keepdims=True)
                mean += jnp.sum(weighted * tokens_in, axis=-1, keepdims=True)
            inv = lax.rsqrt(squares * (1.0 / width) + norm_eps)
            mean = mean * (1.0 / width)
            for owner in range(4):
                tokens_in = r.token_buf[owner, rows].astype(f32)
                grad = r.norm_grad[owner, rows].astype(f32)
                r.gain_own[4 + owner : 5 + owner, 0:part_wide] += jnp.sum(
                    grad * tokens_in * inv, axis=0, keepdims=True
                )
                weighted = grad * r.gain_one[owner : owner + 1]
                r.norm_grad[owner, rows] = (
                    inv * weighted - tokens_in * (inv * inv * inv) * mean
                ).astype(bf16)
            return carry

        lax.fori_loop(0, local // 16, rows_of, 0)
        keep_part.start()
        for copy in gain_plane:
            copy.start()

    keep_part = pltpu.make_async_copy(r.norm_grad, r.resid_part, r.keep_sem.at[2])
    gain_plane = [
        remote(r.gain_own, r.gain_plane.at[me], r.gain_send.at[i], r.gain_recv.at[i], where)
        for i, where in enumerate(plane)
    ]
    gain_rep = [
        remote(r.gain_mine.at[i], r.gain_theirs.at[i], r.gain_send.at[3 + i], r.gain_recv.at[3 + i], where)
        for i, where in enumerate((twin, next_chip, far_chip))
    ]

    def k_plane():
        for copy in gain_plane:
            copy.wait()
        r.gain_plane[me] = r.gain_own[...]
        r.gain_mine[0] = (r.gain_plane[0] + r.gain_plane[1]) + (r.gain_plane[2] + r.gain_plane[3])
        gain_rep[0].start()

    def k_rep(index):
        gain_rep[index].wait()
        total = r.gain_mine[index] + r.gain_theirs[index]
        if index < 2:
            r.gain_mine[index + 1] = total
            gain_rep[index + 1].start()
        else:
            r.gain_total[...] = total
            keep_gains.start()

    keep_gains = pltpu.make_async_copy(r.gain_total, r.gain_sums, r.keep_sem.at[3])

    sums = (r.down_sum, r.gate_sum, r.up_sum, r.out_sum)

    def by_job(step, use):
        for job in range(5):

            @pl.when((step >= first[job]) & (step < first[job + 1]))
            def _():
                use(job, step - first[job])

    def results(job, index, slot):
        if job < 4:
            rows = pl.ds(pl.multiple_of((2 * index + core) * CHUNK, CHUNK), CHUNK)
            return [(r.total.at[slot, :, pl.ds(0, sums[job].shape[1])], sums[job].at[rows])]
        rows = pl.ds(pl.multiple_of(index * CHUNK, CHUNK), CHUNK)
        pairs, start = [], 0
        for ref in (r.query_sum, r.key_sum, r.value_sum):
            size = ref.shape[1] // 2
            columns = pl.ds(pl.multiple_of(core * size, 128), size)
            pairs.append((r.total.at[slot, :, pl.ds(start, size)], ref.at[rows, columns]))
            start += size
        return pairs

    def pair_copies(job, index, step):
        slot = step % 4
        return [
            remote(src, dst, r.pair_send.at[slot, i], r.pair_recv.at[step, i], twin)
            for i, (src, dst) in enumerate(results(job, index, slot))
        ]

    def store_copies(job, index, step):
        slot = step % 4
        return [
            pltpu.make_async_copy(src, dst, r.store_sem.at[slot, i])
            for i, (src, dst) in enumerate(results(job, index, slot))
        ]

    def sib_copy(step):
        give = pl.ds(pl.multiple_of((1 - core) * CHUNK, CHUNK), CHUNK)
        return remote(
            r.made.at[step % 2, give], r.sib.at[step % 4],
            r.sib_send.at[step % 4], r.sib_recv.at[step % 4], twin,
        )

    def up_copy(step, dst, sem):
        slot = step % DEEP
        return remote(r.acc.at[slot], dst.at[slot], r.up_send.at[slot], sem.at[slot], inner)

    def down_copy(step):
        return remote(
            r.total.at[step % 4], r.inner_in.at[step % DEEP],
            r.down_send.at[step % 4], r.inner_recv.at[step % DEEP], outer,
        )

    def make(step):
        slot = step % 2

        def product(job, index):
            if job < 4:
                left_buf = (r.hidden_buf, r.two_buf, r.two_buf, r.mixed_buf)[job]
                right_buf = (r.ffn_buf, r.gate_grad, r.up_grad, r.all_grad)[job]
                columns = pl.ds(pl.multiple_of(index * PAIR, PAIR), PAIR)
                across = pl.ds(0, sums[job].shape[1])
                r.made[slot, :, across] = dot_columns(
                    left_buf[:, columns], right_buf[:, across]
                ).astype(bf16)
                return
            columns = pl.ds(pl.multiple_of((index // 2) * PAIR, PAIR), PAIR)
            for which, buf in enumerate((r.hidden_buf, r.ffn_buf)):
                r.both[...] = dot_columns(r.cols_buf[:, columns], buf[:, pl.ds(0, side)]).astype(bf16)
                r.made[slot, pl.ds(which * CHUNK, CHUNK), pl.ds(0, side)] = r.both[
                    pl.ds(pl.multiple_of((index % 2) * CHUNK, CHUNK), CHUNK)
                ]

        by_job(step, product)

        @pl.when(step >= 4)
        def _():
            pl.semaphore_wait(r.sib_credit, 1)

        sib_copy(step).start()

    def send_up(step):
        @pl.when(step >= DEEP)
        def _():
            pl.semaphore_wait(r.up_credit, 1)

        @pl.when(is_mid)
        def _():
            up_copy(step, r.inner_in, r.inner_recv).start()

        @pl.when(jnp.logical_not(is_mid))
        def _():
            up_copy(step, r.outer_in, r.outer_recv).start()

    def pair_up(step):
        slot = step % DEEP
        sib_copy(step).wait()

        @pl.when(step >= DEEP)
        def _():
            up_copy(step, r.outer_in, r.outer_recv).wait_send()

        mine = pl.ds(pl.multiple_of(core * CHUNK, CHUNK), CHUNK)
        r.acc[slot] = add_low(r.made[step % 2, mine], r.sib[step % 4])

        @pl.when(step + 4 < steps)
        def _():
            tell(r.sib_credit, twin)

        @pl.when(is_end)
        def _():
            send_up(step)

    def from_outer(step):
        slot = step % DEEP
        up_copy(step, r.outer_in, r.outer_recv).wait_recv()
        r.acc[slot] = add_low(r.acc[slot], r.outer_in[slot])

        @pl.when(step + DEEP < steps)
        def _():
            tell(r.up_credit, outer)

        send_up(step)

    def sends_done(step):
        def use(job, index):
            for copy in pair_copies(job, index, step):
                copy.wait_send()
            for copy in store_copies(job, index, step):
                copy.wait()

        by_job(step, use)

        @pl.when(jnp.logical_not(is_end))
        def _():
            down_copy(step).wait_send()

    def from_inner(step):
        slot = step % DEEP
        down_copy(step).wait_recv()

        @pl.when(step >= 4)
        def _():
            sends_done(step - 4)

        @pl.when(is_mid)
        def _():
            r.total[step % 4] = add_low(r.acc[slot], r.inner_in[slot])

            @pl.when(step + DEEP < steps)
            def _():
                tell(r.up_credit, inner)

        @pl.when(jnp.logical_not(is_mid))
        def _():
            r.total[step % 4] = r.inner_in[slot]

            @pl.when(step + DEEP < steps)
            def _():
                tell(r.down_credit, inner)

        @pl.when(jnp.logical_not(is_end))
        def _():
            @pl.when(step >= DEEP)
            def _():
                pl.semaphore_wait(r.down_credit, 1)

            down_copy(step).start()

        def use(job, index):
            for copy in pair_copies(job, index, step) + store_copies(job, index, step):
                copy.start()

        by_job(step, use)

    lag_outer = 3
    lag_inner = jnp.where(is_end, 8, 6)
    load_hidden.wait()
    load_two.wait()

    def at(now, step, use):
        @pl.when(now == step)
        def _():
            use()

    def tick(now, carry):
        @pl.when(now < steps)
        def _():
            make(now)

        @pl.when((now >= 1) & (now - 1 < steps))
        def _():
            pair_up(now - 1)

        @pl.when(jnp.logical_not(is_end) & (now >= lag_outer) & (now - lag_outer < steps))
        def _():
            from_outer(now - lag_outer)

        @pl.when((now >= lag_inner) & (now - lag_inner < steps))
        def _():
            from_inner(now - lag_inner)

        for buf in range(2):

            @pl.when(2 * now + buf < n_a)
            def _():
                a_tile(2 * now + buf, buf)

        @pl.when(now == b_at - 1)
        def _():
            for copy in b_loads(1):
                copy.start()

        @pl.when((now >= b_at) & (now < c_at))
        def _():
            b_tile(now - b_at)

        at(now, c_at, c_start)
        at(now, c_at + 1, load_out.start)
        at(now, c_at + 2, c_pass)

        @pl.when(now == d_at)
        def _():
            d_norms()
            for copy in e_first:
                copy.start()

        at(now, d_at + 2, lambda: pass_on(e_first, e_on))
        at(now, f_at, f_mixed)

        @pl.when((now >= g_at) & (now < h_at))
        def _():
            g_attention(now - g_at)

        at(now, h_at, h_start)
        at(now, h_at + 4, lambda: pass_on(h_first, h_on))
        at(now, i_at, i_start)
        at(now, i_at + 1, i_norm)
        at(now, k_at, k_norm)
        at(now, k_at + 1, k_plane)
        for index in range(3):
            at(now, k_at + 2 + index, functools.partial(k_rep, index))
        return carry

    lax.fori_loop(0, steps + 8, tick, 0)

    def finish(step, carry):
        sends_done(step)
        return carry

    lax.fori_loop(steps - 4, steps, finish, 0)

    def finish_up(step, carry):
        up_copy(step, r.outer_in, r.outer_recv).wait_send()
        return carry

    lax.fori_loop(steps - DEEP, steps, finish_up, 0)

    def arrived(step, carry):
        def use(job, index):
            for copy in pair_copies(job, index, step):
                copy.wait_recv()

        by_job(step, use)
        return carry

    lax.fori_loop(0, steps, arrived, 0)
    for copy in (keep_middle, keep_part, keep_gains):
        copy.wait()


def backward(collective_id, **args):
    f32, bf16 = jnp.float32, jnp.bfloat16
    given = types.SimpleNamespace(**args)
    tokens, width = given.grad_ffn.shape
    inner_width = given.hidden.shape[1]
    local = tokens // 4
    half = local // 2
    head_cols = given.qkv.shape[1]
    part = width // 4
    part_wide = given.gain_one.shape[1]
    out_rows = given.w_out.shape[0]
    side = 2 * head_cols
    slot_width = max(width, inner_width, side)
    block = min(TILE, tokens)
    steps = (inner_width + 2 * width + out_rows) // PAIR + part // CHUNK
    vmem, dma, credit = pltpu.VMEM, pltpu.SemaphoreType.DMA, pltpu.SemaphoreType.REGULAR
    shape = jax.ShapeDtypeStruct
    outs = dict(
        down_sum=shape((inner_width, width), bf16),
        gate_sum=shape((width, inner_width), bf16),
        up_sum=shape((width, inner_width), bf16),
        out_sum=shape((out_rows, width), bf16),
        query_sum=shape((part, side), bf16),
        key_sum=shape((part, side // 2), bf16),
        value_sum=shape((part, side // 2), bf16),
        grad_middle=shape((local, width), f32),
        resid_part=shape((4, local, part_wide), bf16),
        gain_sums=shape((8, width), f32),
        partial=shape((tokens, width), bf16),
        grad_qkv=shape((4 * tokens, head_cols), bf16),
    )
    scratch = dict(
        ffn_buf=vmem((tokens, slot_width), bf16),
        hidden_buf=vmem((tokens, slot_width), bf16),
        two_buf=vmem((tokens, width), bf16),
        gate_grad=vmem((tokens, slot_width), bf16),
        up_grad=vmem((tokens, inner_width), bf16),
        weights=vmem((4 * TILE, slot_width), bf16),
        gate_buf=vmem((2, tokens, TILE), bf16),
        up_buf=vmem((2, tokens, TILE), bf16),
        wide=vmem((tokens, TILE), f32),
        stage=vmem((2, tokens, TILE), bf16),
        c_mine=vmem((4, half, width), bf16),
        c_landed=vmem((6, half, width), bf16),
        middle_buf=vmem((local, width), f32),
        attn_buf=vmem((local, width), f32),
        cot_buf=vmem((local, width), bf16),
        qkv_buf=vmem((tokens, head_cols), bf16),
        mixed_buf=vmem((tokens, out_rows), bf16),
        cols_buf=vmem((tokens, -(-part // PAIR) * PAIR), bf16),
        token_buf=vmem((4, local, part_wide), bf16),
        all_grad=vmem((tokens, width), bf16),
        mixed_grad=vmem((tokens, out_rows), bf16),
        probs_buf=vmem((block, tokens), f32),
        tanh_buf=vmem((block, tokens), f32),
        score_grad=vmem((block, tokens), f32),
        dots_grad=vmem((block, tokens), bf16),
        probs_low=vmem((block, tokens), bf16),
        kv_grad=vmem((2, tokens, head_cols // 4), f32),
        head_grad=vmem((tokens, head_cols), bf16),
        norm_grad=vmem((4, local, part_wide), bf16),
        gain_own=vmem((8, width), f32),
        gain_plane=vmem((4, 8, width), f32),
        gain_mine=vmem((3, 8, width), f32),
        gain_theirs=vmem((3, 8, width), f32),
        gain_total=vmem((8, width), f32),
        made=vmem((2, PAIR, slot_width), bf16),
        both=vmem((PAIR, side), bf16),
        sib=vmem((4, CHUNK, slot_width), bf16),
        acc=vmem((DEEP, CHUNK, slot_width), bf16),
        outer_in=vmem((DEEP, CHUNK, slot_width), bf16),
        inner_in=vmem((DEEP, CHUNK, slot_width), bf16),
        total=vmem((4, CHUNK, slot_width), bf16),
        load_sem=dma((42,)),
        stage_sem=dma((2,)),
        keep_sem=dma((4,)),
        c_send=dma((6,)),
        c_recv=dma((6,)),
        e_send=dma((6,)),
        e_recv=dma((6,)),
        h_send=dma((6,)),
        h_recv=dma((6,)),
        i_send=dma((3,)),
        i_recv=dma((3,)),
        gain_send=dma((6,)),
        gain_recv=dma((6,)),
        sib_send=dma((4,)),
        sib_recv=dma((4,)),
        up_send=dma((DEEP,)),
        outer_recv=dma((DEEP,)),
        inner_recv=dma((DEEP,)),
        down_send=dma((4,)),
        pair_send=dma((4, 3)),
        pair_recv=dma((steps, 3)),
        store_sem=dma((4, 3)),
        sib_credit=credit,
        up_credit=credit,
        down_credit=credit,
    )
    any_space = pl.BlockSpec(memory_space=pl.ANY)
    small = pl.BlockSpec(memory_space=pltpu.VMEM)
    in_specs = [
        small if value.ndim == 2 and value.shape[0] <= 8 else any_space for value in args.values()
    ]
    results = pl.pallas_call(
        functools.partial(
            backward_kernel,
            (tokens, local, width, inner_width, head_cols),
            tuple(args) + tuple(outs) + tuple(scratch),
        ),
        out_shape=list(outs.values()),
        in_specs=in_specs,
        out_specs=[any_space] * len(outs),
        scratch_shapes=list(scratch.values()),
        compiler_params=pltpu.CompilerParams(
            collective_id=collective_id,
            has_side_effects=True,
            vmem_limit_bytes=VMEM_LIMIT,
        ),
        cost_estimate=pl.CostEstimate(
            flops=80 * tokens * width * width, bytes_accessed=400 * 2**20, transcendentals=0
        ),
    )(*args.values())
    return types.SimpleNamespace(**dict(zip(outs, results)))


VMEM_LIMIT = 63 * 2**20


def forward_kernel(names, *refs):
    r = types.SimpleNamespace(**dict(zip(names, refs)))
    f32, bf16 = jnp.float32, jnp.bfloat16
    tokens, inner_width = r.hidden.shape
    local, width = r.tokens.shape
    half = local // 2
    me, x_place, y_place, far_place = plane_places()
    x_other, y_other = {"shard": x_place}, {"shard": y_place}

    def load(src, dst, index):
        return pltpu.make_async_copy(src, dst, r.load_sem.at[index])

    def block_rows(owner):
        return pl.ds(pl.multiple_of(owner * local, 16), local)

    def half_rows(owner, which):
        return pl.ds(pl.multiple_of(owner * local + which * half, 16), half)

    early = (load(r.mixed, r.mixed_buf, 0), load(r.w_out, r.out_buf, 1))
    small = (load(r.tokens, r.token_buf, 2), load(r.cotangent, r.cot_buf, 3))
    big = (
        load(r.w_gate, r.gate_weight, 4),
        load(r.w_up, r.up_weight, 5),
        load(r.w_down, r.down_weight, 6),
    )
    for copy in early + small + big:
        copy.start()
    greet((x_place, y_place))

    def summing(landed, send_sem, recv_sem):
        def send(src, index, where):
            return remote(src, landed.at[index], send_sem.at[index], recv_sem.at[index], where)

        far = (
            send(r.partial.at[half_rows(far_place, 0)], 0, x_other),
            send(r.partial.at[half_rows(far_place, 1)], 1, y_other),
        )
        near = (
            send(r.partial.at[half_rows(x_place, 0)], 2, x_other),
            send(r.partial.at[half_rows(y_place, 1)], 3, y_other),
        )
        on = (send(r.passed.at[0], 4, y_other), send(r.passed.at[1], 5, x_other))
        return far, near, on

    def pass_sums(landed, far, on):
        for index, owner in enumerate((y_place, x_place)):
            far[index].wait_recv()
            r.passed[index] = add_low(r.partial[half_rows(owner, index)], landed[index])
            on[index].start()

    def gathering(source, target, send_sem, recv_sem):
        def send(owner, which, index, where, src):
            return remote(
                src, target.at[half_rows(owner, which)],
                send_sem.at[index], recv_sem.at[index], where,
            )

        starts = [
            [send(me, which, 2 * which + i, where, source(which)) for i, where in enumerate((x_other, y_other))]
            for which in range(2)
        ]
        on = (
            send(x_place, 0, 4, y_other, target.at[half_rows(x_place, 0)]),
            send(y_place, 1, 5, x_other, target.at[half_rows(y_place, 1)]),
        )
        return starts, on

    a_far, a_near, a_on = summing(r.a_landed, r.a_send, r.a_recv)
    c_far, c_near, c_on = summing(r.c_landed, r.c_send, r.c_recv)
    b_starts, b_on = gathering(
        lambda which: r.two_buf.at[half_rows(me, which)], r.two_buf, r.b_send, r.b_recv
    )
    d_starts, d_on = gathering(
        lambda which: r.cot_buf.at[pl.ds(which * half, half)], r.grad_ffn, r.d_send, r.d_recv
    )

    for copy in early:
        copy.wait()

    def project(owner):
        rows = block_rows(owner)
        r.partial[rows] = dot_plain(r.mixed_buf[rows], r.out_buf[...]).astype(bf16)

    project(far_place)
    for copy in a_far:
        copy.start()
    project(x_place)
    a_near[0].start()
    project(y_place)
    a_near[1].start()
    project(me)
    pass_sums(r.a_landed, a_far, a_on)
    for copy in small:
        copy.wait()

    def sum_rows(landed, which, index):
        rows = pl.ds(pl.multiple_of(me * local + which * half + index * 16, 16), 16)
        here = pl.ds(pl.multiple_of(index * 16, 16), 16)
        return (
            r.partial[rows].astype(f32)
            + landed[2 + which, here].astype(f32)
            + landed[4 + which, here].astype(f32)
        )

    def middle_rows(which, index, carry):
        rows = pl.ds(pl.multiple_of(which * half + index * 16, 16), 16)
        attn = sum_rows(r.a_landed, which, index)
        r.attn_buf[rows] = attn
        inv = lax.rsqrt(jnp.mean(attn * attn, axis=-1, keepdims=True) + norm_eps)
        middle = r.token_buf[rows].astype(f32) + attn * inv * r.gains[0:1]
        r.middle_buf[rows] = middle
        inv = lax.rsqrt(jnp.mean(middle * middle, axis=-1, keepdims=True) + norm_eps)
        r.two_buf[pl.ds(pl.multiple_of(me * local + which * half + index * 16, 16), 16)] = (
            middle * inv * r.gains[1:2]
        ).astype(bf16)
        return carry

    for which in range(2):
        a_near[which].wait_recv()
        a_on[which].wait_recv()
        lax.fori_loop(0, half // 16, functools.partial(middle_rows, which), 0)
        for copy in b_starts[which]:
            copy.start()
    keep = [
        pltpu.make_async_copy(r.attn_buf, r.attn_out, r.keep_sem.at[0]),
        pltpu.make_async_copy(r.middle_buf, r.middle, r.keep_sem.at[1]),
    ]
    for copy in keep:
        copy.start()
    for copy in a_far + a_near + a_on:
        copy.wait_send()

    def keep_block(owner):
        rows = block_rows(owner)
        return [
            pltpu.make_async_copy(buf, dst.at[rows], r.keep_sem.at[2 + i])
            for i, (buf, dst) in enumerate(
                ((r.gate_stage, r.gate), (r.up_stage, r.up), (r.hidden_buf.at[rows], r.hidden))
            )
        ]

    def feed(owner, before):
        rows = block_rows(owner)
        if before is not None:
            for copy in keep_block(before):
                copy.wait()

        def tile(index, carry):
            columns = pl.ds(pl.multiple_of(index * TILE, TILE), TILE)
            block = r.two_buf[rows]
            r.gate_wide[...] = dot_plain(block, r.gate_weight[:, columns])
            r.up_wide[...] = dot_plain(block, r.up_weight[:, columns])

            def rows_of(index, carry):
                here = pl.ds(pl.multiple_of(index * 32, 32), 32)
                gate, up = r.gate_wide[here], r.up_wide[here]
                r.gate_stage[here, columns] = gate.astype(bf16)
                r.up_stage[here, columns] = up.astype(bf16)
                curve = jnp.tanh(ROOT_TWO_PI * (gate + 0.044715 * (gate * gate * gate)))
                r.hidden_buf[
                    pl.ds(pl.multiple_of(owner * local + index * 32, 32), 32), columns
                ] = (0.5 * gate * (1.0 + curve) * up).astype(bf16)
                return carry

            lax.fori_loop(0, local // 32, rows_of, 0)
            return carry

        lax.fori_loop(0, inner_width // TILE, tile, 0)
        for copy in keep_block(owner):
            copy.start()

    def shrink(owner):
        rows = block_rows(owner)

        def tile(index, carry):
            columns = pl.ds(pl.multiple_of(index * TILE, TILE), TILE)
            r.partial[rows, columns] = dot_plain(
                r.hidden_buf[rows], r.down_weight[:, columns]
            ).astype(bf16)
            return carry

        lax.fori_loop(0, width // TILE, tile, 0)

    big[0].wait()
    big[1].wait()
    feed(me, None)
    big[2].wait()
    b_starts[0][0].wait_recv()
    b_on[0].start()
    b_starts[1][1].wait_recv()
    b_on[1].start()
    shrink(me)
    b_starts[1][0].wait_recv()
    feed(x_place, me)
    shrink(x_place)
    c_near[0].start()
    b_starts[0][1].wait_recv()
    feed(y_place, x_place)
    shrink(y_place)
    c_near[1].start()
    for copy in b_on:
        copy.wait_recv()
    feed(far_place, y_place)
    shrink(far_place)
    for copy in c_far:
        copy.start()
    keep_two = pltpu.make_async_copy(r.two_buf, r.normed_two, r.keep_sem.at[5])
    keep_two.start()
    r.gain_part[...] = jnp.zeros_like(r.gain_part)
    pass_sums(r.c_landed, c_far, c_on)

    def last_rows(which, index, carry):
        rows = pl.ds(pl.multiple_of(which * half + index * 16, 16), 16)
        ffn = sum_rows(r.c_landed, which, index)
        inv = lax.rsqrt(jnp.mean(ffn * ffn, axis=-1, keepdims=True) + norm_eps)
        r.token_buf[rows] = (r.middle_buf[rows] + ffn * inv * r.gains[2:3]).astype(bf16)
        grad = r.cot_buf[rows].astype(f32)
        weighted = grad * r.gains[2:3]
        mean = jnp.mean(weighted * ffn, axis=-1, keepdims=True)
        r.gain_part[0:1] += jnp.sum(grad * ffn * inv, axis=0, keepdims=True)
        r.cot_buf[rows] = (inv * weighted - ffn * (inv * inv * inv) * mean).astype(bf16)
        return carry

    for which in range(2):
        c_near[which].wait_recv()
        c_on[which].wait_recv()
        lax.fori_loop(0, half // 16, functools.partial(last_rows, which), 0)
        for copy in d_starts[which]:
            copy.start()
    keep_own = pltpu.make_async_copy(r.cot_buf, r.grad_ffn.at[block_rows(me)], r.keep_sem.at[6])
    keep_out = pltpu.make_async_copy(r.token_buf, r.output, r.keep_sem.at[7])
    keep_own.start()
    keep_out.start()
    d_starts[0][0].wait_recv()
    d_on[0].start()
    d_starts[1][1].wait_recv()
    d_on[1].start()
    d_starts[1][0].wait_recv()
    d_starts[0][1].wait_recv()
    for copy in d_on:
        copy.wait_recv()
    for copy in b_starts[0] + b_starts[1] + list(b_on + c_far + c_near + c_on) + d_starts[0] + d_starts[1] + list(d_on):
        copy.wait_send()
    for copy in keep + keep_block(far_place) + [keep_two, keep_own, keep_out]:
        copy.wait()


def forward(collective_id, **args):
    f32, bf16 = jnp.float32, jnp.bfloat16
    given = types.SimpleNamespace(**args)
    local, width = given.tokens.shape
    tokens = 4 * local
    half = local // 2
    inner_width = given.w_down.shape[0]
    vmem, dma, shape = pltpu.VMEM, pltpu.SemaphoreType.DMA, jax.ShapeDtypeStruct
    outs = dict(
        grad_ffn=shape((tokens, width), bf16),
        hidden=shape((tokens, inner_width), bf16),
        gate=shape((tokens, inner_width), bf16),
        up=shape((tokens, inner_width), bf16),
        normed_two=shape((tokens, width), bf16),
        middle=shape((local, width), f32),
        attn_out=shape((local, width), f32),
        output=shape((local, width), bf16),
        gain_part=shape((8, width), f32),
    )
    scratch = dict(
        mixed_buf=vmem(given.mixed.shape, bf16),
        out_buf=vmem(given.w_out.shape, bf16),
        token_buf=vmem((local, width), bf16),
        cot_buf=vmem((local, width), bf16),
        gate_weight=vmem((width, inner_width), bf16),
        up_weight=vmem((width, inner_width), bf16),
        down_weight=vmem((inner_width, width), bf16),
        partial=vmem((tokens, width), bf16),
        passed=vmem((2, half, width), bf16),
        a_landed=vmem((6, half, width), bf16),
        c_landed=vmem((6, half, width), bf16),
        attn_buf=vmem((local, width), f32),
        middle_buf=vmem((local, width), f32),
        two_buf=vmem((tokens, width), bf16),
        hidden_buf=vmem((tokens, inner_width), bf16),
        gate_stage=vmem((local, inner_width), bf16),
        up_stage=vmem((local, inner_width), bf16),
        gate_wide=vmem((local, TILE), f32),
        up_wide=vmem((local, TILE), f32),
        load_sem=dma((7,)),
        keep_sem=dma((8,)),
        a_send=dma((6,)),
        a_recv=dma((6,)),
        b_send=dma((6,)),
        b_recv=dma((6,)),
        c_send=dma((6,)),
        c_recv=dma((6,)),
        d_send=dma((6,)),
        d_recv=dma((6,)),
    )
    any_space = pl.BlockSpec(memory_space=pl.ANY)
    small = pl.BlockSpec(memory_space=pltpu.VMEM)
    results = pl.pallas_call(
        functools.partial(forward_kernel, tuple(args) + tuple(outs) + tuple(scratch)),
        out_shape=list(outs.values()),
        in_specs=[
            small if value.ndim == 2 and value.shape[0] <= 8 else any_space
            for value in args.values()
        ],
        out_specs=[small if value.shape[0] <= 8 else any_space for value in outs.values()],
        scratch_shapes=list(scratch.values()),
        compiler_params=pltpu.CompilerParams(
            collective_id=collective_id, has_side_effects=True, vmem_limit_bytes=VMEM_LIMIT
        ),
        cost_estimate=pl.CostEstimate(
            flops=8 * tokens * width * inner_width, bytes_accessed=100 * 2**20, transcendentals=0
        ),
    )(*args.values())
    return types.SimpleNamespace(**dict(zip(outs, results)))


QUERY_HEADS = 8
KV = 4
HEAD_SIZE = 256
SEGS = 13


softcap = 50.0
norm_eps = 1e-06


def normalize(values, gain_vec):
    inv_rms = lax.rsqrt(jnp.mean(values * values, axis=-1, keepdims=True) + norm_eps)
    return (values * inv_rms * gain_vec, inv_rms)


def norm_back(values, inv_rms, gain_vec, grad_in):
    weighted = grad_in * gain_vec
    row_mean = jnp.mean(weighted * values, axis=-1, keepdims=True)
    grad_back = inv_rms * weighted - values * (inv_rms * inv_rms * inv_rms) * row_mean
    return (grad_back, jnp.sum(grad_in * values * inv_rms, axis=0))


def geglu(gate_pre, up_pre):
    return jax.nn.gelu(gate_pre, approximate=True) * up_pre


def gather_rows(block, collective_id):
    if lax.axis_size("shard") == 4:
        return gather4(block, collective_id)
    return lax.all_gather(block, "shard", axis=0, tiled=True)


def scatter_rows(partial, collective_id):
    if lax.axis_size("shard") == 4:
        return scatter4(partial, collective_id)
    summed = lax.psum_scatter(partial, "shard", scatter_dimension=0, tiled=True)
    return summed.astype(jnp.float32)


def exchange(blocks, collective_id):
    if lax.axis_size("shard") == 4:
        return exchange4(blocks, collective_id)
    return lax.all_to_all(blocks, "shard", 0, 0, tiled=True)


def first_gather(normed, seg_ids, w_query, w_key, w_value):
    n = lax.axis_size("shard")
    tok_rows, width = normed.shape
    codes = seg_ids.astype(jnp.bfloat16)
    if n == 4:
        codes = jnp.pad(codes, (0, 2048 - tok_rows)).reshape(16, 128)
        normed_all, codes, heads = prologue4(normed, codes, w_query, w_key, w_value, 2)
        codes = codes.reshape(n, -1)[:, :tok_rows].reshape(-1)
        return normed_all, codes.astype(jnp.int32), heads
    part_rows = w_query.shape[0]
    share = max(1, n // KV)

    def by_device(weight):
        heads = weight.reshape(part_rows, KV, -1)
        if share > 1:
            heads = jnp.repeat(heads, share, axis=1)
        return heads.reshape(part_rows, n, -1)

    parts = jnp.concatenate(
        (w_query.reshape(part_rows, n, -1), by_device(w_key), by_device(w_value)), axis=2
    ).transpose(1, 0, 2)
    heads = lax.all_to_all(parts, "shard", 0, 0, tiled=True).reshape(width, -1)
    normed_all = lax.all_gather(normed, "shard", axis=0, tiled=True)
    codes = lax.all_gather(codes, "shard", axis=0, tiled=True)
    return normed_all, codes.astype(jnp.int32), heads


def rep_sum(grads, width):
    summed = chain_sum([grad.astype(jnp.bfloat16).reshape(-1, width) for grad in grads])
    return [
        total.reshape(grad.shape).astype(jnp.float32) for total, grad in zip(summed, grads)
    ]


def body(
    tokens,
    seg_ids,
    parents,
    attn_gain,
    w_query,
    w_key,
    w_value,
    w_out,
    post_attn_gain,
    ffn_gain,
    w_gate,
    w_up,
    w_down,
    post_ffn_gain,
    cotangent,
):
    f32, bf16 = jnp.float32, jnp.bfloat16
    tok_rows, width = tokens.shape
    n = lax.axis_size("shard")
    me = lax.axis_index("shard")
    group_rows = tok_rows * n
    part_rows = w_query.shape[0]
    head_scale = HEAD_SIZE ** (-0.5)
    q_heads = QUERY_HEADS // n
    kv_heads = max(1, KV // n)
    share = n * kv_heads // KV
    repeat = q_heads // kv_heads
    q_cols = q_heads * HEAD_SIZE
    k_cols = kv_heads * HEAD_SIZE
    gain_one = attn_gain.astype(f32)
    gain_two = post_attn_gain.astype(f32)
    gain_three = ffn_gain.astype(f32)
    gain_four = post_ffn_gain.astype(f32)

    residual = tokens.astype(f32)
    normed, rms_one = normalize(residual, gain_one)
    normed_all, codes, qkv_heads = first_gather(
        normed.astype(bf16), seg_ids, w_query, w_key, w_value
    )
    qkv = jnp.dot(normed_all, qkv_heads, preferred_element_type=f32).astype(bf16)
    queries = qkv[:, :q_cols].reshape(group_rows, kv_heads, repeat, HEAD_SIZE)
    keys = qkv[:, q_cols : q_cols + k_cols].reshape(group_rows, kv_heads, HEAD_SIZE)
    values = qkv[:, q_cols + k_cols :].reshape(group_rows, kv_heads, HEAD_SIZE)

    parent_row = parents[0]
    labels = jnp.arange(SEGS)

    def lookup(ident):
        return jnp.sum(jnp.where(ident[:, None] == labels[None, :], parent_row[None, :], 0), axis=1)

    parent_one = lookup(codes)
    parent_two = lookup(parent_one)
    positions = jnp.arange(group_rows)
    real = codes < SEGS
    related = (
        (codes[None, :] == codes[:, None])
        | (codes[None, :] == parent_one[:, None])
        | (codes[None, :] == parent_two[:, None])
    )
    visible = (positions[None, :] <= positions[:, None]) & real[:, None] & real[
        None, :
    ] & related | (positions[None, :] == positions[:, None])

    score_matrix = jnp.einsum("tkrh,skh->krts", queries, keys, preferred_element_type=f32)
    tanh_part = jnp.tanh(score_matrix * (head_scale / softcap))
    masked = jnp.where(visible[None, None], softcap * tanh_part, -1e30)
    row_max = jnp.max(masked, axis=-1, keepdims=True)
    expo_terms = jnp.exp(masked - row_max)
    row_total = jnp.sum(expo_terms, axis=-1, keepdims=True)
    probs = expo_terms / row_total
    probs_b = probs.astype(bf16)
    mixed = jnp.einsum("krts,skh->tkrh", probs_b, values, preferred_element_type=f32)
    mixed = mixed.reshape(group_rows, q_cols).astype(bf16)
    if n == 4 and lax.axis_size("rep") == 8:
        part_wide = -(-part_rows // 128) * 128
        widen = lambda array: jnp.pad(array, [(0, 0)] * (array.ndim - 1) + [(0, part_wide - part_rows)])
        normed_cols = lax.dynamic_slice_in_dim(normed_all, me * part_rows, part_rows, axis=1)
        nothing = jnp.zeros((width,), f32)
        gains = jnp.stack([gain_two, gain_three, gain_four] + [nothing] * 5)
        ahead = forward(
            3,
            mixed=mixed,
            w_out=w_out,
            tokens=tokens,
            cotangent=cotangent,
            gains=gains,
            w_gate=w_gate,
            w_up=w_up,
            w_down=w_down,
        )
        found = backward(
            7,
            grad_ffn=ahead.grad_ffn,
            hidden=ahead.hidden,
            gate=ahead.gate,
            up=ahead.up,
            normed_two=ahead.normed_two,
            w_down=w_down,
            w_gate=w_gate,
            w_up=w_up,
            w_out=w_out,
            middle=ahead.middle,
            attn_out=ahead.attn_out,
            cotangent=cotangent,
            gains=gains,
            gain_parts=ahead.gain_part,
            gain_one=widen(gain_one.reshape(4, part_rows)),
            qkv=qkv,
            mixed=mixed,
            probs=probs.reshape(q_heads, group_rows, group_rows),
            tanh=tanh_part.reshape(q_heads, group_rows, group_rows),
            normed_cols=widen(normed_cols),
            w_query=w_query,
            w_key=w_key,
            w_value=w_value,
            token_blocks=widen(tokens.reshape(tok_rows, 4, part_rows).transpose(1, 0, 2)),
        )
        resid = found.resid_part[:, :, :part_rows].transpose(1, 0, 2).reshape(tok_rows, width)
        grad_tokens = (found.grad_middle + resid.astype(f32)).astype(bf16)
        gains = found.gain_sums
        return (
            ahead.output,
            grad_tokens,
            gains[4:, :part_rows].reshape(width),
            found.query_sum.astype(f32),
            found.key_sum.astype(f32),
            found.value_sum.astype(f32),
            found.out_sum.astype(f32),
            gains[1],
            gains[2],
            found.gate_sum.astype(f32),
            found.up_sum.astype(f32),
            found.down_sum.astype(f32),
            gains[0],
        )
    attn_out = scatter_rows(jnp.dot(mixed, w_out, preferred_element_type=f32).astype(bf16), 3)
    post_one, rms_two = normalize(attn_out, gain_two)
    middle = residual + post_one
    normed_two, rms_three = normalize(middle, gain_three)
    normed_two_all = gather_rows(normed_two.astype(bf16), 4)
    gate_pre = jnp.dot(normed_two_all, w_gate, preferred_element_type=f32)
    up_pre = jnp.dot(normed_two_all, w_up, preferred_element_type=f32)
    hidden, geglu_back = jax.vjp(geglu, gate_pre, up_pre)
    hidden_b = hidden.astype(bf16)
    ffn_out = scatter_rows(jnp.dot(hidden_b, w_down, preferred_element_type=f32).astype(bf16), 5)
    post_two, rms_four = normalize(ffn_out, gain_four)
    output = (middle + post_two).astype(bf16)

    grad_out = cotangent.astype(f32)
    grad_ffn, grad_gain_four = norm_back(ffn_out, rms_four, gain_four, grad_out)
    grad_ffn_all = gather_rows(grad_ffn.astype(bf16), 6)
    down_part = jnp.einsum("tf,td->fd", hidden_b, grad_ffn_all, preferred_element_type=f32)
    grad_hidden = jnp.einsum("td,fd->tf", grad_ffn_all, w_down, preferred_element_type=f32)
    grad_gate, grad_up = geglu_back(grad_hidden)
    grad_gate_b = grad_gate.astype(bf16)
    grad_up_b = grad_up.astype(bf16)
    grad_normed_two = jnp.einsum("tf,df->td", grad_gate_b, w_gate, preferred_element_type=f32)
    grad_normed_two += jnp.einsum("tf,df->td", grad_up_b, w_up, preferred_element_type=f32)
    grad_normed_two = scatter_rows(grad_normed_two.astype(bf16), 7)
    gate_part = jnp.einsum("td,tf->df", normed_two_all, grad_gate_b, preferred_element_type=f32)
    up_part = jnp.einsum("td,tf->df", normed_two_all, grad_up_b, preferred_element_type=f32)
    grad_middle_part, grad_gain_three = norm_back(middle, rms_three, gain_three, grad_normed_two)
    grad_middle = grad_out + grad_middle_part
    grad_attn, grad_gain_two = norm_back(attn_out, rms_two, gain_two, grad_middle)
    grad_attn_all = gather_rows(grad_attn.astype(bf16), 8)
    out_part = jnp.einsum("tj,td->jd", mixed, grad_attn_all, preferred_element_type=f32)
    grad_mixed = jnp.einsum("td,jd->tj", grad_attn_all, w_out, preferred_element_type=f32)
    grad_mixed = grad_mixed.astype(bf16).reshape(group_rows, kv_heads, repeat, HEAD_SIZE)
    grad_probs = jnp.einsum("tkrh,skh->krts", grad_mixed, values, preferred_element_type=f32)
    row_inner = jnp.sum(probs * grad_probs, axis=-1, keepdims=True)
    grad_dots = (
        probs * (grad_probs - row_inner) * (1.0 - tanh_part * tanh_part) * head_scale
    ).astype(bf16)
    grad_queries = jnp.einsum("krts,skh->tkrh", grad_dots, keys, preferred_element_type=f32)
    grad_keys = jnp.einsum("krts,tkrh->skh", grad_dots, queries, preferred_element_type=f32)
    grad_values = jnp.einsum("krts,tkrh->skh", probs_b, grad_mixed, preferred_element_type=f32)
    grad_parts = jnp.concatenate(
        (
            grad_queries.reshape(group_rows, q_cols),
            grad_keys.reshape(group_rows, k_cols),
            grad_values.reshape(group_rows, k_cols),
        ),
        axis=1,
    ).astype(bf16)
    grad_parts = gather_rows(grad_parts, 9).reshape(n, group_rows, -1)

    def whole_heads(parts):
        if share > 1:
            parts = parts.reshape(KV, share, group_rows, HEAD_SIZE).astype(f32).sum(axis=1).astype(bf16)
        return parts.transpose(1, 0, 2).reshape(group_rows, -1)

    grad_qkv = jnp.concatenate(
        (
            grad_parts[:, :, :q_cols].transpose(1, 0, 2).reshape(group_rows, -1),
            whole_heads(grad_parts[:, :, q_cols : q_cols + k_cols]),
            whole_heads(grad_parts[:, :, q_cols + k_cols :]),
        ),
        axis=1,
    )
    qkv_local = jnp.concatenate((w_query, w_key, w_value), axis=1)
    grad_normed = jnp.einsum("tj,dj->td", grad_qkv, qkv_local, preferred_element_type=f32)
    grad_normed = exchange(grad_normed.astype(bf16).reshape(n, tok_rows, part_rows), 10)
    grad_normed = grad_normed.transpose(1, 0, 2).reshape(tok_rows, width).astype(f32)
    normed_cols = lax.dynamic_slice_in_dim(normed_all, me * part_rows, part_rows, axis=1)
    qkv_part = jnp.einsum("td,tj->dj", normed_cols, grad_qkv, preferred_element_type=f32)
    grad_resid_part, grad_gain_one = norm_back(residual, rms_one, gain_one, grad_normed)
    grad_tokens = (grad_middle + grad_resid_part).astype(bf16)
    gain_parts = jnp.stack((grad_gain_one, grad_gain_two, grad_gain_three, grad_gain_four))
    gain_sums = lax.all_gather(gain_parts, ("rep", "shard"), axis=0).sum(axis=0)
    down_sum, gate_sum, up_sum, out_sum, qkv_sum = rep_sum(
        (down_part, gate_part, up_part, out_part, qkv_part), width
    )
    q_width = w_query.shape[1]
    k_width = w_key.shape[1]
    return (
        output,
        grad_tokens,
        gain_sums[0],
        qkv_sum[:, :q_width],
        qkv_sum[:, q_width : q_width + k_width],
        qkv_sum[:, q_width + k_width :],
        out_sum,
        gain_sums[1],
        gain_sums[2],
        gate_sum,
        up_sum,
        down_sum,
        gain_sums[3],
    )


def solution(mesh):
    return jax.shard_map(
        body,
        mesh=mesh,
        in_specs=(
            P(("rep", "shard"), None),
            P(("rep", "shard")),
            P("rep", None),
            P(),
            P("shard", None),
            P("shard", None),
            P("shard", None),
            P("shard", None),
            P(),
            P(),
            P(None, "shard"),
            P(None, "shard"),
            P("shard", None),
            P(),
            P(("rep", "shard"), None),
        ),
        out_specs=(
            P(("rep", "shard"), None),
            P(("rep", "shard"), None),
            P(),
            P("shard", None),
            P("shard", None),
            P("shard", None),
            P("shard", None),
            P(),
            P(),
            P(None, "shard"),
            P(None, "shard"),
            P("shard", None),
            P(),
        ),
        check_vma=False,
    )
```

```python
import functools
import math
import types

import jax
import jax.numpy as jnp
from jax import lax
from jax.experimental import pallas as pl
from jax.experimental.pallas import tpu as pltpu
from jax.sharding import PartitionSpec as P

SLOTS = 8
CHUNK = 64


def remote(src, dst, send_sem, recv_sem, where):
    return pltpu.make_async_remote_copy(
        src_ref=src,
        dst_ref=dst,
        send_sem=send_sem,
        recv_sem=recv_sem,
        device_id=where,
        device_id_type=pl.DeviceIdType.MESH,
    )


def add_low(left, right):
    return (left.astype(jnp.float32) + right.astype(jnp.float32)).astype(jnp.bfloat16)


def chain_kernel(counts, chunk, *refs):
    jobs = len(counts)
    ins, outs = refs[:jobs], refs[jobs : 2 * jobs]
    (
        mine, sib, acc, outer_in, inner_in, total,
        load_sem, sib_send, sib_recv, up_send, outer_recv, inner_recv,
        down_send, pair_send, pair_recv, store_sem,
        sib_credit, up_credit, down_credit,
    ) = refs[2 * jobs :]
    slots = mine.shape[0]
    steps = sum(counts)
    place = lax.axis_index("rep")
    chips = lax.axis_size("rep") // 2
    chip, core = place // 2, place % 2
    left = chip < chips // 2
    is_end = (chip == 0) | (chip == chips - 1)
    is_mid = (chip == chips // 2 - 1) | (chip == chips // 2)
    twin = {"rep": place + 1 - 2 * core}
    inner = {"rep": jnp.where(left, place + 2, place - 2)}
    outer = {"rep": jnp.where(is_end, place, jnp.where(left, place - 2, place + 2))}

    def tell(sem, where):
        pl.semaphore_signal(sem, inc=1, device_id=where, device_id_type=pl.DeviceIdType.MESH)

    barrier = pltpu.get_barrier_semaphore()
    tell(barrier, twin)
    tell(barrier, inner)

    @pl.when(is_end)
    def _():
        pl.semaphore_wait(barrier, 2)

    @pl.when(jnp.logical_not(is_end))
    def _():
        tell(barrier, outer)
        pl.semaphore_wait(barrier, 3)

    def with_rows(step, which, use):
        low = 0
        for job, count in enumerate(counts):
            first = low

            @pl.when((step >= low) & (step < low + count))
            def _():
                row = pl.multiple_of(((step - first) * 2 + which) * chunk, chunk)
                use(job, pl.ds(row, chunk))

            low += count

    def pair_copy(job, rows, slot, step):
        return remote(total.at[slot], outs[job].at[rows], pair_send.at[slot], pair_recv.at[step], twin)

    def up_copy(slot, dst, sem):
        return remote(acc.at[slot], dst.at[slot], up_send.at[slot], sem.at[slot], inner)

    def down_copy(slot):
        return remote(total.at[slot], inner_in.at[slot], down_send.at[slot], inner_recv.at[slot], outer)

    def sib_copy(job, rows, slot):
        return remote(ins[job].at[rows], sib.at[slot], sib_send.at[slot], sib_recv.at[slot], twin)

    def load_copy(job, rows, slot):
        return pltpu.make_async_copy(ins[job].at[rows], mine.at[slot], load_sem.at[slot])

    def store_copy(job, rows, slot):
        return pltpu.make_async_copy(total.at[slot], outs[job].at[rows], store_sem.at[slot])

    some = pl.ds(0, chunk)

    def take(step):
        slot = step % slots

        @pl.when(step >= slots)
        def _():
            pl.semaphore_wait(sib_credit, 1)

        with_rows(step, 1 - core, lambda job, rows: sib_copy(job, rows, slot).start())
        with_rows(step, core, lambda job, rows: load_copy(job, rows, slot).start())

    def send_up(step):
        slot = step % slots

        @pl.when(step >= slots)
        def _():
            pl.semaphore_wait(up_credit, 1)

        @pl.when(is_mid)
        def _():
            up_copy(slot, inner_in, inner_recv).start()

        @pl.when(jnp.logical_not(is_mid))
        def _():
            up_copy(slot, outer_in, outer_recv).start()

    def pair_up(step):
        slot = step % slots
        load_copy(0, some, slot).wait()
        sib_copy(0, some, slot).wait()

        @pl.when(step >= slots)
        def _():
            up_copy(slot, outer_in, outer_recv).wait_send()

        acc[slot] = add_low(mine[slot], sib[slot])

        @pl.when(step + slots < steps)
        def _():
            tell(sib_credit, twin)

        @pl.when(is_end)
        def _():
            send_up(step)

    def from_outer(step):
        slot = step % slots
        up_copy(slot, outer_in, outer_recv).wait_recv()
        acc[slot] = add_low(acc[slot], outer_in[slot])

        @pl.when(step + slots < steps)
        def _():
            tell(up_credit, outer)

        send_up(step)

    def sends_done(slot):
        pair_copy(0, some, slot, 0).wait_send()
        store_copy(0, some, slot).wait()

        @pl.when(jnp.logical_not(is_end))
        def _():
            down_copy(slot).wait_send()

    def from_inner(step):
        slot = step % slots
        down_copy(slot).wait_recv()

        @pl.when(step >= slots)
        def _():
            sends_done(slot)

        @pl.when(is_mid)
        def _():
            total[slot] = add_low(acc[slot], inner_in[slot])

            @pl.when(step + slots < steps)
            def _():
                tell(up_credit, inner)

        @pl.when(jnp.logical_not(is_mid))
        def _():
            total[slot] = inner_in[slot]

            @pl.when(step + slots < steps)
            def _():
                tell(down_credit, inner)

        @pl.when(jnp.logical_not(is_end))
        def _():
            @pl.when(step >= slots)
            def _():
                pl.semaphore_wait(down_credit, 1)

            down_copy(slot).start()

        with_rows(step, core, lambda job, rows: pair_copy(job, rows, slot, step).start())
        with_rows(step, core, lambda job, rows: store_copy(job, rows, slot).start())

    lag_outer = 3
    lag_inner = jnp.where(is_end, 8, 6)

    def tick(step, carry):
        @pl.when(step < steps)
        def _():
            take(step)

        @pl.when((step >= 1) & (step - 1 < steps))
        def _():
            pair_up(step - 1)

        @pl.when(jnp.logical_not(is_end) & (step >= lag_outer) & (step - lag_outer < steps))
        def _():
            from_outer(step - lag_outer)

        @pl.when((step >= lag_inner) & (step - lag_inner < steps))
        def _():
            from_inner(step - lag_inner)

        return carry

    lax.fori_loop(0, steps + 8, tick, 0)

    def finish(step, carry):
        slot = step % slots
        sends_done(slot)
        up_copy(slot, outer_in, outer_recv).wait_send()
        return carry

    lax.fori_loop(steps - slots, steps, finish, 0)

    def arrived(step, carry):
        pair_copy(0, some, 0, step).wait_recv()
        return carry

    lax.fori_loop(0, steps, arrived, 0)


def chain_sum(parts, chunk=CHUNK, collective_id=1):
    width = parts[0].shape[1]
    counts = tuple(part.shape[0] // (2 * chunk) for part in parts)
    steps = sum(counts)
    slots = min(SLOTS, steps)
    any_space = pl.BlockSpec(memory_space=pl.ANY)
    block = pltpu.VMEM((slots, chunk, width), jnp.bfloat16)
    sems = pltpu.SemaphoreType.DMA((slots,))
    credit = pltpu.SemaphoreType.REGULAR
    return pl.pallas_call(
        functools.partial(chain_kernel, counts, chunk),
        out_shape=[jax.ShapeDtypeStruct(part.shape, part.dtype) for part in parts],
        in_specs=[any_space] * len(parts),
        out_specs=[any_space] * len(parts),
        scratch_shapes=[block] * 6
        + [sems] * 8
        + [pltpu.SemaphoreType.DMA((steps,)), sems, credit, credit, credit],
        compiler_params=pltpu.CompilerParams(
            collective_id=collective_id, has_side_effects=True, vmem_limit_bytes=48 * 1024 * 1024
        ),
        cost_estimate=pl.CostEstimate(
            flops=0, bytes_accessed=8 * sum(part.size for part in parts), transcendentals=0
        ),
    )(*parts)


def plane_places():
    me = lax.axis_index("shard")
    x_other = me + 1 - 2 * (me % 2)
    y_other = (me + 2) % 4
    far = x_other + y_other - me
    return me, x_other, y_other, far


def greet(places):
    barrier = pltpu.get_barrier_semaphore()
    for place in places:
        pl.semaphore_signal(
            barrier, inc=1, device_id={"shard": place}, device_id_type=pl.DeviceIdType.MESH
        )
    pl.semaphore_wait(barrier, len(places))


TILE = 256
PAIR = 2 * CHUNK
DEEP = 8
ROOT_TWO_PI = math.sqrt(2.0 / math.pi)


def dot_rows(left, right):
    return lax.dot_general(left, right, (((1,), (1,)), ((), ())), preferred_element_type=jnp.float32)


def dot_plain(left, right):
    return lax.dot_general(left, right, (((1,), (0,)), ((), ())), preferred_element_type=jnp.float32)


def dot_columns(left, right):
    return lax.dot_general(left, right, (((0,), (0,)), ((), ())), preferred_element_type=jnp.float32)


def backward_kernel(dims, names, *refs):
    r = types.SimpleNamespace(**dict(zip(names, refs)))
    tokens, local, width, inner_width, head_cols = dims
    f32, bf16 = jnp.float32, jnp.bfloat16
    half = local // 2
    q_cols = head_cols // 2
    k_cols = head_cols // 4
    heads = q_cols // HEAD_SIZE
    part = width // 4
    part_wide = r.normed_cols.shape[1]
    side = 2 * head_cols
    n_a = inner_width // TILE
    n_b = width // TILE
    block = min(TILE, tokens)
    n_blocks = tokens // block

    counts = (
        inner_width // PAIR, width // PAIR, width // PAIR, r.w_out.shape[0] // PAIR, part // CHUNK
    )
    first = [sum(counts[:job]) for job in range(6)]
    steps = first[5]
    b_at = (n_a + 1) // 2
    c_at = b_at + n_b
    d_at = c_at + 5
    f_at = d_at + 5
    g_at = f_at + 1
    h_at = g_at + heads * n_blocks
    i_at = h_at + 9
    k_at = i_at + 3
    assert b_at <= first[1] and f_at < first[3] and i_at < first[4] and first[1] <= i_at
    assert first[2] <= i_at and k_at + 5 <= steps + 8

    place = lax.axis_index("rep")
    chips = lax.axis_size("rep") // 2
    chip, core = place // 2, place % 2
    left = chip < chips // 2
    is_end = (chip == 0) | (chip == chips - 1)
    is_mid = (chip == chips // 2 - 1) | (chip == chips // 2)
    twin = {"rep": place + 1 - 2 * core}
    inner = {"rep": jnp.where(left, place + 2, place - 2)}
    outer = {"rep": jnp.where(is_end, place, jnp.where(left, place - 2, place + 2))}
    next_chip = {"rep": place + 2 - 4 * (chip % 2)}
    far_chip = {"rep": (place + 4) % 8}
    me, x_place, y_place, far_place = plane_places()
    x_other, y_other = {"shard": x_place}, {"shard": y_place}
    plane = [{"shard": (me + step) % 4} for step in (1, 2, 3)]

    def tell(sem, where):
        pl.semaphore_signal(sem, inc=1, device_id=where, device_id_type=pl.DeviceIdType.MESH)

    def load(src, dst, index):
        return pltpu.make_async_copy(src, dst, r.load_sem.at[index])

    load_ffn = load(r.grad_ffn, r.ffn_buf.at[:, pl.ds(0, width)], 0)
    load_hidden = load(r.hidden, r.hidden_buf.at[:, pl.ds(0, inner_width)], 1)
    load_two = load(r.normed_two, r.two_buf, 2)
    load_small = (
        load(r.middle, r.middle_buf, 3),
        load(r.attn_out, r.attn_buf, 4),
        load(r.cotangent, r.cot_buf, 5),
        load(r.qkv, r.qkv_buf, 6),
        load(r.mixed, r.mixed_buf, 7),
        load(r.normed_cols, r.cols_buf, 8),
        load(r.tokens, r.token_buf, 9),
    )

    def weight_tile(index):
        return r.weights.at[pl.ds(pl.multiple_of(index * TILE, TILE), TILE)]

    def a_loads(tile, buf):
        rows = pl.ds(pl.multiple_of(tile * TILE, TILE), TILE)
        return (
            load(r.w_down.at[rows], weight_tile(buf).at[:, pl.ds(0, width)], 10 + buf),
            load(r.gate.at[:, rows], r.gate_buf.at[buf], 12 + buf),
            load(r.up.at[:, rows], r.up_buf.at[buf], 14 + buf),
        )

    def b_loads(tile):
        rows = pl.ds(pl.multiple_of(tile * TILE, TILE), TILE)
        buf = 2 - 2 * (tile % 2)
        sem = 16 + 2 * (tile % 2)
        return (
            load(r.w_gate.at[rows], weight_tile(buf).at[:, pl.ds(0, inner_width)], sem),
            load(r.w_up.at[rows], weight_tile(buf + 1).at[:, pl.ds(0, inner_width)], sem + 1),
        )

    def b_store(tile):
        columns = pl.ds(pl.multiple_of(tile * TILE, TILE), TILE)
        return pltpu.make_async_copy(
            r.stage.at[tile % 2], r.partial.at[:, columns], r.stage_sem.at[tile % 2]
        )

    load_ffn.start()
    for buf in range(2):
        for copy in a_loads(buf, buf):
            copy.start()
    load_hidden.start()
    load_two.start()
    for copy in load_small:
        copy.start()
    for copy in b_loads(0):
        copy.start()

    barrier = pltpu.get_barrier_semaphore()
    for where in [twin, inner, far_chip] + plane:
        tell(barrier, where)

    @pl.when(is_end)
    def _():
        pl.semaphore_wait(barrier, 6)

    @pl.when(jnp.logical_not(is_end))
    def _():
        tell(barrier, outer)
        pl.semaphore_wait(barrier, 7)

    load_ffn.wait()

    def a_tile(tile, buf):
        for copy in a_loads(tile, buf):
            copy.wait()
        r.wide[...] = dot_rows(r.ffn_buf[:, pl.ds(0, width)], weight_tile(buf)[:, pl.ds(0, width)])
        columns = pl.ds(pl.multiple_of(tile * TILE, TILE), TILE)

        def rows_of(index, carry):
            rows = pl.ds(pl.multiple_of(index * 128, 128), 128)
            grad = r.wide[rows]
            gate = r.gate_buf[buf, rows].astype(f32)
            up = r.up_buf[buf, rows].astype(f32)
            curve = jnp.tanh(ROOT_TWO_PI * (gate + 0.044715 * gate * gate * gate))
            slope = (1.0 - curve * curve) * (ROOT_TWO_PI * (1.0 + 3.0 * 0.044715 * gate * gate))
            gelu_slope = 0.5 * (1.0 + curve) + 0.5 * gate * slope
            r.gate_grad[rows, columns] = (grad * up * gelu_slope).astype(bf16)
            r.up_grad[rows, columns] = (grad * (0.5 * gate * (1.0 + curve))).astype(bf16)
            return carry

        lax.fori_loop(0, tokens // 128, rows_of, 0)

        @pl.when(tile + 2 < n_a)
        def _():
            for copy in a_loads(tile + 2, buf):
                copy.start()

    def b_tile(tile):
        for copy in b_loads(tile):
            copy.wait()

        @pl.when(tile >= 2)
        def _():
            b_store(tile - 2).wait()

        buf = 2 - 2 * (tile % 2)
        some = dot_rows(r.gate_grad[:, pl.ds(0, inner_width)], weight_tile(buf)[:, pl.ds(0, inner_width)])
        some += dot_rows(r.up_grad[...], weight_tile(buf + 1)[:, pl.ds(0, inner_width)])
        r.stage[tile % 2] = some.astype(bf16)
        b_store(tile).start()

        @pl.when(tile + 2 < n_b)
        def _():
            for copy in b_loads(tile + 2):
                copy.start()

    def partial_rows(owner, which):
        return r.partial.at[pl.ds(pl.multiple_of(owner * local + which * half, 16), half)]

    c_own = (
        load(partial_rows(y_place, 0), r.c_mine.at[0], 20),
        load(partial_rows(x_place, 1), r.c_mine.at[1], 21),
        load(partial_rows(me, 0), r.c_mine.at[2], 22),
        load(partial_rows(me, 1), r.c_mine.at[3], 23),
    )

    def c_send(src, index, where):
        return remote(src, r.c_landed.at[index], r.c_send.at[index], r.c_recv.at[index], where)

    c_first = (
        c_send(partial_rows(far_place, 0), 0, x_other),
        c_send(partial_rows(far_place, 1), 1, y_other),
        c_send(partial_rows(x_place, 0), 2, x_other),
        c_send(partial_rows(y_place, 1), 3, y_other),
    )
    c_on = (c_send(r.c_mine.at[0], 4, y_other), c_send(r.c_mine.at[1], 5, x_other))

    def c_start():
        b_store(n_b - 2).wait()
        b_store(n_b - 1).wait()
        for copy in c_first + c_own:
            copy.start()

    def c_pass():
        for copy in c_own:
            copy.wait()
        for index in range(2):
            c_first[index].wait_recv()
            r.c_mine[index] = add_low(r.c_mine[index], r.c_landed[index])
            c_on[index].start()

    def d_norms():
        for copy in load_small:
            copy.wait()
        for copy in c_first:
            copy.wait_send()
        for copy in c_first[2:] + c_on:
            copy.wait_recv()
        r.gain_own[...] = r.gain_parts[...]

        def rows_of(which, index, carry):
            here = pl.ds(pl.multiple_of(index * 16, 16), 16)
            rows = pl.ds(pl.multiple_of(which * half + index * 16, 16), 16)
            grad = (
                r.c_mine[2 + which, here].astype(f32)
                + r.c_landed[2 + which, here].astype(f32)
                + r.c_landed[4 + which, here].astype(f32)
            )
            middle = r.middle_buf[rows]
            inv = lax.rsqrt(jnp.mean(middle * middle, axis=-1, keepdims=True) + norm_eps)
            weighted = grad * r.gains[1:2]
            mean = jnp.mean(weighted * middle, axis=-1, keepdims=True)
            r.gain_own[2:3, 0:width] += jnp.sum(grad * middle * inv, axis=0, keepdims=True)
            grad_mid = (
                r.cot_buf[rows].astype(f32) + inv * weighted - middle * (inv * inv * inv) * mean
            )
            r.middle_buf[rows] = grad_mid
            attn = r.attn_buf[rows]
            inv = lax.rsqrt(jnp.mean(attn * attn, axis=-1, keepdims=True) + norm_eps)
            weighted = grad_mid * r.gains[0:1]
            mean = jnp.mean(weighted * attn, axis=-1, keepdims=True)
            r.gain_own[1:2, 0:width] += jnp.sum(grad_mid * attn * inv, axis=0, keepdims=True)
            grad_attn = inv * weighted - attn * (inv * inv * inv) * mean
            r.all_grad[pl.ds(pl.multiple_of(me * local + which * half + index * 16, 16), 16)] = (
                grad_attn.astype(bf16)
            )
            return carry

        for which in range(2):
            lax.fori_loop(0, half // 16, functools.partial(rows_of, which), 0)
        for copy in c_on:
            copy.wait_send()

    def gather_copies(rows, source, target, send_sem, recv_sem):
        def send(owner, which, index, where, src):
            here = pl.ds(pl.multiple_of(owner * 2 * rows + which * rows, 16), rows)
            return remote(
                src.at[here] if src is target else src.at[pl.ds(which * rows, rows)],
                target.at[here], send_sem.at[index], recv_sem.at[index], where,
            )

        starts = (
            send(me, 0, 0, x_other, source),
            send(me, 1, 1, y_other, source),
            send(me, 1, 2, x_other, source),
            send(me, 0, 3, y_other, source),
        )
        passes = (
            send(x_place, 0, 4, y_other, target), send(y_place, 1, 5, x_other, target)
        )
        return starts, passes

    e_first, e_on = gather_copies(half, r.all_grad, r.all_grad, r.e_send, r.e_recv)
    h_first, h_on = gather_copies(tokens // 2, r.head_grad, r.grad_qkv, r.h_send, r.h_recv)
    h_own = pltpu.make_async_copy(
        r.head_grad, r.grad_qkv.at[pl.ds(pl.multiple_of(me * tokens, 16), tokens)], r.keep_sem.at[1]
    )

    def pass_on(starts, passes):
        for index in range(2):
            starts[index].wait_recv()
            passes[index].start()

    def gathered(starts, passes):
        for copy in starts[2:] + passes:
            copy.wait_recv()
        for copy in starts + passes:
            copy.wait_send()

    load_out = load(r.w_out, r.weights.at[pl.ds(0, r.w_out.shape[0]), pl.ds(0, width)], 24)

    def g_loads(item):
        head, rows = item // n_blocks, pl.ds(pl.multiple_of((item % n_blocks) * block, block), block)
        return (
            load(r.probs.at[head, rows], r.probs_buf, 25),
            load(r.tanh.at[head, rows], r.tanh_buf, 26),
        )

    def f_mixed():
        gathered(e_first, e_on)
        load_out.wait()
        r.mixed_grad[...] = dot_rows(
            r.all_grad[...], r.weights[pl.ds(0, r.w_out.shape[0]), pl.ds(0, width)]
        ).astype(bf16)
        r.kv_grad[...] = jnp.zeros_like(r.kv_grad)
        for copy in g_loads(0):
            copy.start()

    def g_attention(item):
        head = item // n_blocks
        rows = pl.ds(pl.multiple_of((item % n_blocks) * block, block), block)
        columns = pl.ds(pl.multiple_of(head * HEAD_SIZE, HEAD_SIZE), HEAD_SIZE)
        for copy in g_loads(item):
            copy.wait()
        grad_out = r.mixed_grad[rows, columns]
        values = r.qkv_buf[:, pl.ds(q_cols + k_cols, k_cols)]
        r.score_grad[...] = dot_rows(grad_out, values)

        def rows_of(index, carry):
            here = pl.ds(pl.multiple_of(index * 64, 64), 64)
            probs = r.probs_buf[here]
            grad = r.score_grad[here]
            curve = r.tanh_buf[here]
            total = jnp.sum(probs * grad, axis=-1, keepdims=True)
            grad = probs * (grad - total) * (1.0 - curve * curve) * (HEAD_SIZE ** (-0.5))
            r.dots_grad[here] = grad.astype(bf16)
            r.probs_low[here] = probs.astype(bf16)
            return carry

        lax.fori_loop(0, block // 64, rows_of, 0)

        @pl.when(item + 1 < heads * n_blocks)
        def _():
            for copy in g_loads(item + 1):
                copy.start()

        keys = r.qkv_buf[:, pl.ds(q_cols, k_cols)]
        r.head_grad[rows, columns] = dot_plain(r.dots_grad[...], keys).astype(bf16)
        r.kv_grad[0] += dot_columns(r.dots_grad[...], r.qkv_buf[rows, columns])
        r.kv_grad[1] += dot_columns(r.probs_low[...], grad_out)

    def h_start():
        r.head_grad[:, pl.ds(q_cols, k_cols)] = r.kv_grad[0].astype(bf16)
        r.head_grad[:, pl.ds(q_cols + k_cols, k_cols)] = r.kv_grad[1].astype(bf16)
        for copy in h_first:
            copy.start()
        h_own.start()

    def side_of(owner, kind):
        buf = r.hidden_buf if owner < 2 else r.ffn_buf
        size = (q_cols, k_cols, k_cols)[kind]
        start = (0, 2 * q_cols, 2 * q_cols + 2 * k_cols)[kind] + (owner % 2) * size
        return buf.at[:, pl.ds(start, size)]

    i_loads = [
        load(
            r.grad_qkv.at[
                pl.ds(owner * tokens, tokens),
                pl.ds((0, q_cols, q_cols + k_cols)[kind], (q_cols, k_cols, k_cols)[kind]),
            ],
            side_of(owner, kind),
            27 + 3 * owner + kind,
        )
        for owner in range(4)
        for kind in range(3)
    ] + [
        load(r.w_query, r.gate_grad.at[pl.ds(0, part), pl.ds(0, 4 * q_cols)], 39),
        load(r.w_key, r.weights.at[pl.ds(0, part), pl.ds(0, 4 * k_cols)], 40),
        load(r.w_value, r.weights.at[pl.ds(0, part), pl.ds(4 * k_cols, 4 * k_cols)], 41),
    ]
    i_copies = [
        remote(
            r.head_grad.at[pl.ds(pl.multiple_of(((me + step) % 4) * local, 16), local), pl.ds(0, part_wide)],
            r.norm_grad.at[me], r.i_send.at[step - 1], r.i_recv.at[step - 1], plane[step - 1],
        )
        for step in (1, 2, 3)
    ]

    def i_start():
        gathered(h_first, h_on)
        h_own.wait()
        for copy in i_loads:
            copy.start()
        for copy in i_loads:
            copy.wait()

    def i_norm():
        def rows_of(index, carry):
            rows = pl.ds(pl.multiple_of(index * block, block), block)
            some = jnp.zeros((block, part_wide), f32)
            for owner in range(4):
                for kind, size in enumerate((q_cols, k_cols, k_cols)):
                    held = r.gate_grad if kind == 0 else r.weights
                    start = (0, 0, 4 * k_cols)[kind] + owner * size
                    some += dot_rows(
                        side_of(owner, kind)[rows], held[pl.ds(0, part_wide), pl.ds(start, size)]
                    )
            r.head_grad[rows, pl.ds(0, part_wide)] = some.astype(bf16)
            return carry

        lax.fori_loop(0, n_blocks, rows_of, 0)
        for copy in i_copies:
            copy.start()
        r.norm_grad[me] = r.head_grad[
            pl.ds(pl.multiple_of(me * local, 16), local), pl.ds(0, part_wide)
        ]

    def k_norm():
        for copy in i_copies:
            copy.wait()

        def rows_of(index, carry):
            rows = pl.ds(pl.multiple_of(index * 16, 16), 16)
            grad = jnp.concatenate(
                [r.norm_grad[owner, rows].astype(f32)[:, :part] for owner in range(4)], axis=1
            )
            values = r.token_buf[rows].astype(f32)
            inv = lax.rsqrt(jnp.mean(values * values, axis=-1, keepdims=True) + norm_eps)
            weighted = grad * r.gains[3:4]
            mean = jnp.mean(weighted * values, axis=-1, keepdims=True)
            r.gain_own[3:4] += jnp.sum(grad * values * inv, axis=0, keepdims=True)
            r.cot_buf[rows] = (
                r.middle_buf[rows] + inv * weighted - values * (inv * inv * inv) * mean
            ).astype(bf16)
            return carry

        lax.fori_loop(0, local // 16, rows_of, 0)
        keep_part.start()
        for copy in gain_plane:
            copy.start()

    keep_part = pltpu.make_async_copy(r.cot_buf, r.grad_tokens, r.keep_sem.at[0])
    gain_plane = [
        remote(r.gain_own, r.gain_plane.at[me], r.gain_send.at[i], r.gain_recv.at[i], where)
        for i, where in enumerate(plane)
    ]
    gain_rep = [
        remote(r.gain_mine.at[i], r.gain_theirs.at[i], r.gain_send.at[3 + i], r.gain_recv.at[3 + i], where)
        for i, where in enumerate((twin, next_chip, far_chip))
    ]

    def k_plane():
        for copy in gain_plane:
            copy.wait()
        r.gain_plane[me] = r.gain_own[...]
        r.gain_mine[0] = (r.gain_plane[0] + r.gain_plane[1]) + (r.gain_plane[2] + r.gain_plane[3])
        gain_rep[0].start()

    def k_rep(index):
        gain_rep[index].wait()
        total = r.gain_mine[index] + r.gain_theirs[index]
        if index < 2:
            r.gain_mine[index + 1] = total
            gain_rep[index + 1].start()
        else:
            r.gain_total[...] = total
            keep_gains.start()

    keep_gains = pltpu.make_async_copy(r.gain_total, r.gain_sums, r.keep_sem.at[3])

    sums = (r.down_sum, r.gate_sum, r.up_sum, r.out_sum)

    def by_job(step, use):
        for job in range(5):

            @pl.when((step >= first[job]) & (step < first[job + 1]))
            def _():
                use(job, step - first[job])

    def results(job, index, slot):
        if job < 4:
            rows = pl.ds(pl.multiple_of((2 * index + core) * CHUNK, CHUNK), CHUNK)
            return [(r.total.at[slot, :, pl.ds(0, sums[job].shape[1])], sums[job].at[rows])]
        rows = pl.ds(pl.multiple_of(index * CHUNK, CHUNK), CHUNK)
        pairs, start = [], 0
        for ref in (r.query_sum, r.key_sum, r.value_sum):
            size = ref.shape[1] // 2
            columns = pl.ds(pl.multiple_of(core * size, 128), size)
            pairs.append((r.total.at[slot, :, pl.ds(start, size)], ref.at[rows, columns]))
            start += size
        return pairs

    def pair_copies(job, index, step):
        slot = step % 4
        return [
            remote(src, dst, r.pair_send.at[slot, i], r.pair_recv.at[step, i], twin)
            for i, (src, dst) in enumerate(results(job, index, slot))
        ]

    def store_copies(job, index, step):
        slot = step % 4
        return [
            pltpu.make_async_copy(src, dst, r.store_sem.at[slot, i])
            for i, (src, dst) in enumerate(results(job, index, slot))
        ]

    def sib_copy(step):
        give = pl.ds(pl.multiple_of((1 - core) * CHUNK, CHUNK), CHUNK)
        return remote(
            r.made.at[step % 2, give], r.sib.at[step % 4],
            r.sib_send.at[step % 4], r.sib_recv.at[step % 4], twin,
        )

    def up_copy(step, dst, sem):
        slot = step % DEEP
        return remote(r.acc.at[slot], dst.at[slot], r.up_send.at[slot], sem.at[slot], inner)

    def down_copy(step):
        return remote(
            r.total.at[step % 4], r.inner_in.at[step % DEEP],
            r.down_send.at[step % 4], r.inner_recv.at[step % DEEP], outer,
        )

    def make(step):
        slot = step % 2

        def product(job, index):
            if job < 4:
                left_buf = (r.hidden_buf, r.two_buf, r.two_buf, r.mixed_buf)[job]
                right_buf = (r.ffn_buf, r.gate_grad, r.up_grad, r.all_grad)[job]
                columns = pl.ds(pl.multiple_of(index * PAIR, PAIR), PAIR)
                across = pl.ds(0, sums[job].shape[1])
                r.made[slot, :, across] = dot_columns(
                    left_buf[:, columns], right_buf[:, across]
                ).astype(bf16)
                return
            columns = pl.ds(pl.multiple_of((index // 2) * PAIR, PAIR), PAIR)
            for which, buf in enumerate((r.hidden_buf, r.ffn_buf)):
                r.both[...] = dot_columns(r.cols_buf[:, columns], buf[:, pl.ds(0, side)]).astype(bf16)
                r.made[slot, pl.ds(which * CHUNK, CHUNK), pl.ds(0, side)] = r.both[
                    pl.ds(pl.multiple_of((index % 2) * CHUNK, CHUNK), CHUNK)
                ]

        by_job(step, product)

        @pl.when(step >= 4)
        def _():
            pl.semaphore_wait(r.sib_credit, 1)

        sib_copy(step).start()

    def send_up(step):
        @pl.when(step >= DEEP)
        def _():
            pl.semaphore_wait(r.up_credit, 1)

        @pl.when(is_mid)
        def _():
            up_copy(step, r.inner_in, r.inner_recv).start()

        @pl.when(jnp.logical_not(is_mid))
        def _():
            up_copy(step, r.outer_in, r.outer_recv).start()

    def pair_up(step):
        slot = step % DEEP
        sib_copy(step).wait()

        @pl.when(step >= DEEP)
        def _():
            up_copy(step, r.outer_in, r.outer_recv).wait_send()

        mine = pl.ds(pl.multiple_of(core * CHUNK, CHUNK), CHUNK)
        r.acc[slot] = add_low(r.made[step % 2, mine], r.sib[step % 4])

        @pl.when(step + 4 < steps)
        def _():
            tell(r.sib_credit, twin)

        @pl.when(is_end)
        def _():
            send_up(step)

    def from_outer(step):
        slot = step % DEEP
        up_copy(step, r.outer_in, r.outer_recv).wait_recv()
        r.acc[slot] = add_low(r.acc[slot], r.outer_in[slot])

        @pl.when(step + DEEP < steps)
        def _():
            tell(r.up_credit, outer)

        send_up(step)

    def sends_done(step):
        def use(job, index):
            for copy in pair_copies(job, index, step):
                copy.wait_send()
            for copy in store_copies(job, index, step):
                copy.wait()

        by_job(step, use)

        @pl.when(jnp.logical_not(is_end))
        def _():
            down_copy(step).wait_send()

    def from_inner(step):
        slot = step % DEEP
        down_copy(step).wait_recv()

        @pl.when(step >= 4)
        def _():
            sends_done(step - 4)

        @pl.when(is_mid)
        def _():
            r.total[step % 4] = add_low(r.acc[slot], r.inner_in[slot])

            @pl.when(step + DEEP < steps)
            def _():
                tell(r.up_credit, inner)

        @pl.when(jnp.logical_not(is_mid))
        def _():
            r.total[step % 4] = r.inner_in[slot]

            @pl.when(step + DEEP < steps)
            def _():
                tell(r.down_credit, inner)

        @pl.when(jnp.logical_not(is_end))
        def _():
            @pl.when(step >= DEEP)
            def _():
                pl.semaphore_wait(r.down_credit, 1)

            down_copy(step).start()

        def use(job, index):
            for copy in pair_copies(job, index, step) + store_copies(job, index, step):
                copy.start()

        by_job(step, use)

    lag_outer = 3
    lag_inner = jnp.where(is_end, 8, 6)
    load_hidden.wait()
    load_two.wait()

    def at(now, step, use):
        @pl.when(now == step)
        def _():
            use()

    def tick(now, carry):
        @pl.when(now < steps)
        def _():
            make(now)

        @pl.when((now >= 1) & (now - 1 < steps))
        def _():
            pair_up(now - 1)

        @pl.when(jnp.logical_not(is_end) & (now >= lag_outer) & (now - lag_outer < steps))
        def _():
            from_outer(now - lag_outer)

        @pl.when((now >= lag_inner) & (now - lag_inner < steps))
        def _():
            from_inner(now - lag_inner)

        for buf in range(2):

            @pl.when(2 * now + buf < n_a)
            def _():
                a_tile(2 * now + buf, buf)

        @pl.when(now == b_at - 1)
        def _():
            for copy in b_loads(1):
                copy.start()

        @pl.when((now >= b_at) & (now < c_at))
        def _():
            b_tile(now - b_at)

        at(now, c_at, c_start)
        at(now, c_at + 1, load_out.start)
        at(now, c_at + 2, c_pass)

        @pl.when(now == d_at)
        def _():
            d_norms()
            for copy in e_first:
                copy.start()

        at(now, d_at + 2, lambda: pass_on(e_first, e_on))
        at(now, f_at, f_mixed)

        @pl.when((now >= g_at) & (now < h_at))
        def _():
            g_attention(now - g_at)

        at(now, h_at, h_start)
        at(now, h_at + 4, lambda: pass_on(h_first, h_on))
        at(now, i_at, i_start)
        at(now, i_at + 1, i_norm)
        at(now, k_at, k_norm)
        at(now, k_at + 1, k_plane)
        for index in range(3):
            at(now, k_at + 2 + index, functools.partial(k_rep, index))
        return carry

    lax.fori_loop(0, steps + 8, tick, 0)

    def finish(step, carry):
        sends_done(step)
        return carry

    lax.fori_loop(steps - 4, steps, finish, 0)

    def finish_up(step, carry):
        up_copy(step, r.outer_in, r.outer_recv).wait_send()
        return carry

    lax.fori_loop(steps - DEEP, steps, finish_up, 0)

    def arrived(step, carry):
        def use(job, index):
            for copy in pair_copies(job, index, step):
                copy.wait_recv()

        by_job(step, use)
        return carry

    lax.fori_loop(0, steps, arrived, 0)
    for copy in (keep_part, keep_gains):
        copy.wait()


def backward(collective_id, **args):
    f32, bf16 = jnp.float32, jnp.bfloat16
    given = types.SimpleNamespace(**args)
    tokens, width = given.grad_ffn.shape
    inner_width = given.hidden.shape[1]
    local = tokens // 4
    half = local // 2
    head_cols = given.qkv.shape[1]
    part = width // 4
    part_wide = given.normed_cols.shape[1]
    out_rows = given.w_out.shape[0]
    side = 2 * head_cols
    slot_width = max(width, inner_width, side)
    block = min(TILE, tokens)
    steps = (inner_width + 2 * width + out_rows) // PAIR + part // CHUNK
    vmem, dma, credit = pltpu.VMEM, pltpu.SemaphoreType.DMA, pltpu.SemaphoreType.REGULAR
    shape = jax.ShapeDtypeStruct
    outs = dict(
        down_sum=shape((inner_width, width), bf16),
        gate_sum=shape((width, inner_width), bf16),
        up_sum=shape((width, inner_width), bf16),
        out_sum=shape((out_rows, width), bf16),
        query_sum=shape((part, side), bf16),
        key_sum=shape((part, side // 2), bf16),
        value_sum=shape((part, side // 2), bf16),
        grad_tokens=shape((local, width), bf16),
        gain_sums=shape((8, width), f32),
        partial=shape((tokens, width), bf16),
        grad_qkv=shape((4 * tokens, head_cols), bf16),
    )
    scratch = dict(
        ffn_buf=vmem((tokens, slot_width), bf16),
        hidden_buf=vmem((tokens, slot_width), bf16),
        two_buf=vmem((tokens, width), bf16),
        gate_grad=vmem((tokens, slot_width), bf16),
        up_grad=vmem((tokens, inner_width), bf16),
        weights=vmem((4 * TILE, slot_width), bf16),
        gate_buf=vmem((2, tokens, TILE), bf16),
        up_buf=vmem((2, tokens, TILE), bf16),
        wide=vmem((tokens, TILE), f32),
        stage=vmem((2, tokens, TILE), bf16),
        c_mine=vmem((4, half, width), bf16),
        c_landed=vmem((6, half, width), bf16),
        middle_buf=vmem((local, width), f32),
        attn_buf=vmem((local, width), f32),
        cot_buf=vmem((local, width), bf16),
        qkv_buf=vmem((tokens, head_cols), bf16),
        mixed_buf=vmem((tokens, out_rows), bf16),
        cols_buf=vmem((tokens, -(-part // PAIR) * PAIR), bf16),
        token_buf=vmem((local, width), bf16),
        all_grad=vmem((tokens, width), bf16),
        mixed_grad=vmem((tokens, out_rows), bf16),
        probs_buf=vmem((block, tokens), f32),
        tanh_buf=vmem((block, tokens), f32),
        score_grad=vmem((block, tokens), f32),
        dots_grad=vmem((block, tokens), bf16),
        probs_low=vmem((block, tokens), bf16),
        kv_grad=vmem((2, tokens, head_cols // 4), f32),
        head_grad=vmem((tokens, head_cols), bf16),
        norm_grad=vmem((4, local, part_wide), bf16),
        gain_own=vmem((8, width), f32),
        gain_plane=vmem((4, 8, width), f32),
        gain_mine=vmem((3, 8, width), f32),
        gain_theirs=vmem((3, 8, width), f32),
        gain_total=vmem((8, width), f32),
        made=vmem((2, PAIR, slot_width), bf16),
        both=vmem((PAIR, side), bf16),
        sib=vmem((4, CHUNK, slot_width), bf16),
        acc=vmem((DEEP, CHUNK, slot_width), bf16),
        outer_in=vmem((DEEP, CHUNK, slot_width), bf16),
        inner_in=vmem((DEEP, CHUNK, slot_width), bf16),
        total=vmem((4, CHUNK, slot_width), bf16),
        load_sem=dma((42,)),
        stage_sem=dma((2,)),
        keep_sem=dma((4,)),
        c_send=dma((6,)),
        c_recv=dma((6,)),
        e_send=dma((6,)),
        e_recv=dma((6,)),
        h_send=dma((6,)),
        h_recv=dma((6,)),
        i_send=dma((3,)),
        i_recv=dma((3,)),
        gain_send=dma((6,)),
        gain_recv=dma((6,)),
        sib_send=dma((4,)),
        sib_recv=dma((4,)),
        up_send=dma((DEEP,)),
        outer_recv=dma((DEEP,)),
        inner_recv=dma((DEEP,)),
        down_send=dma((4,)),
        pair_send=dma((4, 3)),
        pair_recv=dma((steps, 3)),
        store_sem=dma((4, 3)),
        sib_credit=credit,
        up_credit=credit,
        down_credit=credit,
    )
    any_space = pl.BlockSpec(memory_space=pl.ANY)
    small = pl.BlockSpec(memory_space=pltpu.VMEM)
    in_specs = [
        small if value.ndim == 2 and value.shape[0] <= 8 else any_space for value in args.values()
    ]
    results = pl.pallas_call(
        functools.partial(
            backward_kernel,
            (tokens, local, width, inner_width, head_cols),
            tuple(args) + tuple(outs) + tuple(scratch),
        ),
        out_shape=list(outs.values()),
        in_specs=in_specs,
        out_specs=[any_space] * len(outs),
        scratch_shapes=list(scratch.values()),
        compiler_params=pltpu.CompilerParams(
            collective_id=collective_id,
            has_side_effects=True,
            vmem_limit_bytes=VMEM_LIMIT,
        ),
        cost_estimate=pl.CostEstimate(
            flops=80 * tokens * width * width, bytes_accessed=400 * 2**20, transcendentals=0
        ),
    )(*args.values())
    return types.SimpleNamespace(**dict(zip(outs, results)))


VMEM_LIMIT = 63 * 2**20


def forward_kernel(names, *refs):
    r = types.SimpleNamespace(**dict(zip(names, refs)))
    f32, bf16 = jnp.float32, jnp.bfloat16
    tokens, inner_width = r.hidden.shape
    local, width = r.tokens.shape
    half = local // 2
    me, x_place, y_place, far_place = plane_places()
    x_other, y_other = {"shard": x_place}, {"shard": y_place}

    def load(src, dst, index):
        return pltpu.make_async_copy(src, dst, r.load_sem.at[index])

    def block_rows(owner):
        return pl.ds(pl.multiple_of(owner * local, 16), local)

    def half_rows(owner, which):
        return pl.ds(pl.multiple_of(owner * local + which * half, 16), half)

    early = (load(r.mixed, r.mixed_buf, 0), load(r.w_out, r.out_buf, 1))
    small = (load(r.tokens, r.token_buf, 2), load(r.cotangent, r.cot_buf, 3))
    big = (
        load(r.w_gate, r.gate_weight, 4),
        load(r.w_up, r.up_weight, 5),
        load(r.w_down, r.down_weight, 6),
    )
    for copy in early + small + big:
        copy.start()
    greet((x_place, y_place))

    def summing(landed, send_sem, recv_sem):
        def send(src, index, where):
            return remote(src, landed.at[index], send_sem.at[index], recv_sem.at[index], where)

        far = (
            send(r.partial.at[half_rows(far_place, 0)], 0, x_other),
            send(r.partial.at[half_rows(far_place, 1)], 1, y_other),
        )
        near = (
            send(r.partial.at[half_rows(x_place, 0)], 2, x_other),
            send(r.partial.at[half_rows(y_place, 1)], 3, y_other),
        )
        on = (send(r.passed.at[0], 4, y_other), send(r.passed.at[1], 5, x_other))
        return far, near, on

    def pass_sums(landed, far, on):
        for index, owner in enumerate((y_place, x_place)):
            far[index].wait_recv()
            r.passed[index] = add_low(r.partial[half_rows(owner, index)], landed[index])
            on[index].start()

    def gathering(source, target, send_sem, recv_sem):
        def send(owner, which, index, where, src):
            return remote(
                src, target.at[half_rows(owner, which)],
                send_sem.at[index], recv_sem.at[index], where,
            )

        starts = [
            [send(me, which, 2 * which + i, where, source(which)) for i, where in enumerate((x_other, y_other))]
            for which in range(2)
        ]
        on = (
            send(x_place, 0, 4, y_other, target.at[half_rows(x_place, 0)]),
            send(y_place, 1, 5, x_other, target.at[half_rows(y_place, 1)]),
        )
        return starts, on

    a_far, a_near, a_on = summing(r.a_landed, r.a_send, r.a_recv)
    c_far, c_near, c_on = summing(r.c_landed, r.c_send, r.c_recv)
    b_starts, b_on = gathering(
        lambda which: r.two_buf.at[half_rows(me, which)], r.two_buf, r.b_send, r.b_recv
    )
    d_starts, d_on = gathering(
        lambda which: r.cot_buf.at[pl.ds(which * half, half)], r.grad_ffn, r.d_send, r.d_recv
    )

    for copy in early:
        copy.wait()

    def project(owner):
        rows = block_rows(owner)
        r.partial[rows] = dot_plain(r.mixed_buf[rows], r.out_buf[...]).astype(bf16)

    project(far_place)
    for copy in a_far:
        copy.start()
    project(x_place)
    a_near[0].start()
    project(y_place)
    a_near[1].start()
    project(me)
    pass_sums(r.a_landed, a_far, a_on)
    for copy in small:
        copy.wait()

    def sum_rows(landed, which, index):
        rows = pl.ds(pl.multiple_of(me * local + which * half + index * 32, 16), 32)
        here = pl.ds(pl.multiple_of(index * 32, 16), 32)
        return (
            r.partial[rows].astype(f32)
            + landed[2 + which, here].astype(f32)
            + landed[4 + which, here].astype(f32)
        )

    def middle_rows(which, index, carry):
        rows = pl.ds(pl.multiple_of(which * half + index * 32, 16), 32)
        attn = sum_rows(r.a_landed, which, index)
        r.attn_buf[rows] = attn
        inv = lax.rsqrt(jnp.mean(attn * attn, axis=-1, keepdims=True) + norm_eps)
        middle = r.token_buf[rows].astype(f32) + attn * inv * r.gains[0:1]
        r.middle_buf[rows] = middle
        inv = lax.rsqrt(jnp.mean(middle * middle, axis=-1, keepdims=True) + norm_eps)
        r.two_buf[pl.ds(pl.multiple_of(me * local + which * half + index * 32, 16), 32)] = (
            middle * inv * r.gains[1:2]
        ).astype(bf16)
        return carry

    for which in range(2):
        a_near[which].wait_recv()
        a_on[which].wait_recv()
        lax.fori_loop(0, half // 32, functools.partial(middle_rows, which), 0)
        for copy in b_starts[which]:
            copy.start()
    keep = [
        pltpu.make_async_copy(r.attn_buf, r.attn_out, r.keep_sem.at[0]),
        pltpu.make_async_copy(r.middle_buf, r.middle, r.keep_sem.at[1]),
    ]
    for copy in keep:
        copy.start()
    for copy in a_far + a_near + a_on:
        copy.wait_send()

    def keep_block(owner):
        rows = block_rows(owner)
        return [
            pltpu.make_async_copy(buf, dst.at[rows], r.keep_sem.at[2 + i])
            for i, (buf, dst) in enumerate(
                ((r.gate_stage, r.gate), (r.up_stage, r.up), (r.hidden_buf.at[rows], r.hidden))
            )
        ]

    def feed(owner, before):
        rows = block_rows(owner)
        if before is not None:
            for copy in keep_block(before):
                copy.wait()

        def tile(index, carry):
            columns = pl.ds(pl.multiple_of(index * TILE, TILE), TILE)
            block = r.two_buf[rows]
            r.gate_wide[...] = dot_plain(block, r.gate_weight[:, columns])
            r.up_wide[...] = dot_plain(block, r.up_weight[:, columns])

            def rows_of(index, carry):
                here = pl.ds(pl.multiple_of(index * half, 16), half)
                gate, up = r.gate_wide[here], r.up_wide[here]
                r.gate_stage[here, columns] = gate.astype(bf16)
                r.up_stage[here, columns] = up.astype(bf16)
                curve = jnp.tanh(ROOT_TWO_PI * (gate + 0.044715 * (gate * gate * gate)))
                r.hidden_buf[
                    pl.ds(pl.multiple_of(owner * local + index * half, 16), half), columns
                ] = (0.5 * gate * (1.0 + curve) * up).astype(bf16)
                return carry

            lax.fori_loop(0, 2, rows_of, 0)
            return carry

        lax.fori_loop(0, inner_width // TILE, tile, 0)
        for copy in keep_block(owner):
            copy.start()

    def shrink(owner):
        rows = block_rows(owner)

        def tile(index, carry):
            columns = pl.ds(pl.multiple_of(index * TILE, TILE), TILE)
            r.partial[rows, columns] = dot_plain(
                r.hidden_buf[rows], r.down_weight[:, columns]
            ).astype(bf16)
            return carry

        lax.fori_loop(0, width // TILE, tile, 0)

    big[0].wait()
    big[1].wait()
    feed(me, None)
    big[2].wait()
    b_starts[0][0].wait_recv()
    b_on[0].start()
    b_starts[1][1].wait_recv()
    b_on[1].start()
    shrink(me)
    b_starts[1][0].wait_recv()
    feed(x_place, me)
    shrink(x_place)
    c_near[0].start()
    b_starts[0][1].wait_recv()
    feed(y_place, x_place)
    shrink(y_place)
    c_near[1].start()
    for copy in b_on:
        copy.wait_recv()
    feed(far_place, y_place)
    shrink(far_place)
    for copy in c_far:
        copy.start()
    keep_two = pltpu.make_async_copy(r.two_buf, r.normed_two, r.keep_sem.at[5])
    keep_two.start()
    r.gain_part[...] = jnp.zeros_like(r.gain_part)
    pass_sums(r.c_landed, c_far, c_on)

    def last_rows(which, index, carry):
        rows = pl.ds(pl.multiple_of(which * half + index * 32, 16), 32)
        ffn = sum_rows(r.c_landed, which, index)
        inv = lax.rsqrt(jnp.mean(ffn * ffn, axis=-1, keepdims=True) + norm_eps)
        r.token_buf[rows] = (r.middle_buf[rows] + ffn * inv * r.gains[2:3]).astype(bf16)
        grad = r.cot_buf[rows].astype(f32)
        weighted = grad * r.gains[2:3]
        mean = jnp.mean(weighted * ffn, axis=-1, keepdims=True)
        r.gain_part[0:1] += jnp.sum(grad * ffn * inv, axis=0, keepdims=True)
        r.cot_buf[rows] = (inv * weighted - ffn * (inv * inv * inv) * mean).astype(bf16)
        return carry

    for which in range(2):
        c_near[which].wait_recv()
        c_on[which].wait_recv()
        lax.fori_loop(0, half // 32, functools.partial(last_rows, which), 0)
        for copy in d_starts[which]:
            copy.start()
    keep_own = pltpu.make_async_copy(r.cot_buf, r.grad_ffn.at[block_rows(me)], r.keep_sem.at[6])
    keep_out = pltpu.make_async_copy(r.token_buf, r.output, r.keep_sem.at[7])
    keep_own.start()
    keep_out.start()
    d_starts[0][0].wait_recv()
    d_on[0].start()
    d_starts[1][1].wait_recv()
    d_on[1].start()
    d_starts[1][0].wait_recv()
    d_starts[0][1].wait_recv()
    for copy in d_on:
        copy.wait_recv()
    for copy in b_starts[0] + b_starts[1] + list(b_on + c_far + c_near + c_on) + d_starts[0] + d_starts[1] + list(d_on):
        copy.wait_send()
    for copy in keep + keep_block(far_place) + [keep_two, keep_own, keep_out]:
        copy.wait()


def forward(collective_id, **args):
    f32, bf16 = jnp.float32, jnp.bfloat16
    given = types.SimpleNamespace(**args)
    local, width = given.tokens.shape
    tokens = 4 * local
    half = local // 2
    inner_width = given.w_down.shape[0]
    vmem, dma, shape = pltpu.VMEM, pltpu.SemaphoreType.DMA, jax.ShapeDtypeStruct
    outs = dict(
        grad_ffn=shape((tokens, width), bf16),
        hidden=shape((tokens, inner_width), bf16),
        gate=shape((tokens, inner_width), bf16),
        up=shape((tokens, inner_width), bf16),
        normed_two=shape((tokens, width), bf16),
        middle=shape((local, width), f32),
        attn_out=shape((local, width), f32),
        output=shape((local, width), bf16),
        gain_part=shape((8, width), f32),
    )
    scratch = dict(
        mixed_buf=vmem(given.mixed.shape, bf16),
        out_buf=vmem(given.w_out.shape, bf16),
        token_buf=vmem((local, width), bf16),
        cot_buf=vmem((local, width), bf16),
        gate_weight=vmem((width, inner_width), bf16),
        up_weight=vmem((width, inner_width), bf16),
        down_weight=vmem((inner_width, width), bf16),
        partial=vmem((tokens, width), bf16),
        passed=vmem((2, half, width), bf16),
        a_landed=vmem((6, half, width), bf16),
        c_landed=vmem((6, half, width), bf16),
        attn_buf=vmem((local, width), f32),
        middle_buf=vmem((local, width), f32),
        two_buf=vmem((tokens, width), bf16),
        hidden_buf=vmem((tokens, inner_width), bf16),
        gate_stage=vmem((local, inner_width), bf16),
        up_stage=vmem((local, inner_width), bf16),
        gate_wide=vmem((local, TILE), f32),
        up_wide=vmem((local, TILE), f32),
        load_sem=dma((7,)),
        keep_sem=dma((8,)),
        a_send=dma((6,)),
        a_recv=dma((6,)),
        b_send=dma((6,)),
        b_recv=dma((6,)),
        c_send=dma((6,)),
        c_recv=dma((6,)),
        d_send=dma((6,)),
        d_recv=dma((6,)),
    )
    any_space = pl.BlockSpec(memory_space=pl.ANY)
    small = pl.BlockSpec(memory_space=pltpu.VMEM)
    results = pl.pallas_call(
        functools.partial(forward_kernel, tuple(args) + tuple(outs) + tuple(scratch)),
        out_shape=list(outs.values()),
        in_specs=[
            small if value.ndim == 2 and value.shape[0] <= 8 else any_space
            for value in args.values()
        ],
        out_specs=[small if value.shape[0] <= 8 else any_space for value in outs.values()],
        scratch_shapes=list(scratch.values()),
        compiler_params=pltpu.CompilerParams(
            collective_id=collective_id, has_side_effects=True, vmem_limit_bytes=VMEM_LIMIT
        ),
        cost_estimate=pl.CostEstimate(
            flops=8 * tokens * width * inner_width, bytes_accessed=100 * 2**20, transcendentals=0
        ),
    )(*args.values())
    return types.SimpleNamespace(**dict(zip(outs, results)))


def attend_kernel(names, *refs):
    r = types.SimpleNamespace(**dict(zip(names, refs)))
    f32, bf16 = jnp.float32, jnp.bfloat16
    local, width = r.tokens.shape
    tokens, head_cols = r.qkv.shape
    part = r.w_query.shape[0]
    piece = part // 4
    half = local // 2
    weights = (r.w_query, r.w_key, r.w_value)
    sizes = [weight.shape[1] // 4 for weight in weights]
    starts = (0, sizes[0], sizes[0] + sizes[1])
    q_cols, k_cols = sizes[0], sizes[1]
    heads = q_cols // HEAD_SIZE
    block = min(TILE, tokens)
    n_blocks = tokens // block
    head_scale = HEAD_SIZE ** (-0.5)

    me, x_place, y_place, far_place = plane_places()
    others = (x_place, y_place, far_place)
    x_other, y_other = {"shard": x_place}, {"shard": y_place}
    place = lax.axis_index("rep")
    chip, core = place // 2, place % 2
    twin = {"rep": place + 1 - 2 * core}
    next_chip = {"rep": place + 2 - 4 * (chip % 2)}
    quarter = (chip % 2) * 2 + core
    next_quarter = (1 - chip % 2) * 2 + core

    load_tokens = pltpu.make_async_copy(r.tokens, r.token_buf, r.load_sem.at[0])
    load_info = pltpu.make_async_copy(
        r.info, r.info_buf.at[pl.ds(pl.multiple_of(me * local, 16), local)], r.load_sem.at[1]
    )
    load_heads = [
        pltpu.make_async_copy(
            weights[kind].at[:, pl.ds(pl.multiple_of(me * sizes[kind], 128), sizes[kind])],
            r.heads_buf.at[
                pl.ds(pl.multiple_of(me * part, 16), part), pl.ds(starts[kind], sizes[kind])
            ],
            r.load_sem.at[2 + kind],
        )
        for kind in range(3)
    ]
    load_tokens.start()
    load_info.start()
    for copy in load_heads:
        copy.start()

    barrier = pltpu.get_barrier_semaphore()
    for where in [{"shard": other} for other in others] + [twin, next_chip]:
        pl.semaphore_signal(barrier, inc=1, device_id=where, device_id_type=pl.DeviceIdType.MESH)
    pl.semaphore_wait(barrier, 5)

    def piece_rows(owner, which):
        return pl.ds(pl.multiple_of(owner * part + which * piece, 16), piece)

    fetch = [
        [
            remote(
                weights[kind].at[
                    pl.ds(pl.multiple_of(quarter * piece, 16), piece),
                    pl.ds(pl.multiple_of(other * sizes[kind], 128), sizes[kind]),
                ],
                r.heads_buf.at[piece_rows(me, quarter), pl.ds(starts[kind], sizes[kind])],
                r.fetch_send.at[i, kind], r.fetch_recv.at[i, kind], {"shard": other},
            )
            for kind in range(3)
        ]
        for i, other in enumerate(others)
    ]
    for i in (2, 0, 1):
        for copy in fetch[i]:
            copy.start()
    tell_info = [
        remote(
            r.info, r.info_buf.at[pl.ds(pl.multiple_of(me * local, 16), local)],
            r.info_send.at[i], r.info_recv.at[i], {"shard": other},
        )
        for i, other in enumerate(others)
    ]
    for copy in tell_info:
        copy.start()

    def pass_piece(i, which, where, index):
        ref = r.heads_buf.at[piece_rows(others[i], which)]
        return remote(ref, ref, r.pass_send.at[index, i], r.pass_recv.at[index, i], where)

    to_chip = [pass_piece(i, quarter, next_chip, 0) for i in range(3)]
    to_twin = [pass_piece(i, quarter, twin, 1) for i in range(3)]
    on_twin = [pass_piece(i, next_quarter, twin, 2) for i in range(3)]

    def half_rows(owner, which):
        return r.all_buf.at[pl.ds(pl.multiple_of(owner * local + which * half, 16), half)]

    def send(owner, which, index, where):
        ref = half_rows(owner, which)
        return remote(ref, ref, r.all_send.at[index], r.all_recv.at[index], where)

    own = [
        [send(me, which, 2 * which + i, where) for i, where in enumerate((x_other, y_other))]
        for which in range(2)
    ]
    on = (send(x_place, 0, 4, y_other), send(y_place, 1, 5, x_other))

    load_tokens.wait()

    def norm_rows(which, index, carry):
        rows = pl.ds(pl.multiple_of(which * half + index * 32, 16), 32)
        values = r.token_buf[rows].astype(f32)
        inv = lax.rsqrt(jnp.mean(values * values, axis=-1, keepdims=True) + norm_eps)
        r.all_buf[pl.ds(pl.multiple_of(me * local + which * half + index * 32, 16), 32)] = (
            values * inv * r.gains[3:4]
        ).astype(bf16)
        return carry

    for which in range(2):
        lax.fori_loop(0, half // 32, functools.partial(norm_rows, which), 0)
        for copy in own[which]:
            copy.start()

    for i in (2, 0, 1):
        for copy in fetch[i]:
            copy.wait_recv()
        to_chip[i].start()
        to_twin[i].start()
    own[0][0].wait_recv()
    on[0].start()
    own[1][1].wait_recv()
    on[1].start()
    for i in (2, 0, 1):
        to_chip[i].wait_recv()
        on_twin[i].start()

    load_info.wait()
    for copy in tell_info:
        copy.wait_recv()
    r.key_info[...] = jnp.transpose(r.info_buf[...].astype(f32))[0:8]
    for copy in load_heads:
        copy.wait()
    for copy in to_twin + on_twin:
        copy.wait_recv()

    def project(owner):
        rows = pl.ds(pl.multiple_of(owner * local, 16), local)
        r.qkv_buf[rows] = dot_plain(r.all_buf[rows], r.heads_buf[...]).astype(bf16)

    project(me)
    own[1][0].wait_recv()
    project(x_place)
    own[0][1].wait_recv()
    project(y_place)
    for copy in on:
        copy.wait_recv()
    project(far_place)
    keep = [pltpu.make_async_copy(r.qkv_buf, r.qkv, r.keep_sem.at[0])]
    keep[0].start()

    def keep_item(item):
        head, rows = item // n_blocks, pl.ds((item % n_blocks) * block, block)
        slot = item % 2
        return [
            pltpu.make_async_copy(r.probs_stage.at[slot], r.probs.at[head, rows], r.stage_sem.at[slot, 0]),
            pltpu.make_async_copy(r.tanh_stage.at[slot], r.tanh.at[head, rows], r.stage_sem.at[slot, 1]),
        ]

    for item in range(heads * n_blocks):
        head, first, slot = item // n_blocks, (item % n_blocks) * block, item % 2
        limit = first + block
        columns = pl.ds(head * HEAD_SIZE, HEAD_SIZE)
        r.score[:, pl.ds(0, limit)] = dot_rows(
            r.qkv_buf[pl.ds(first, block), columns], r.qkv_buf[pl.ds(0, limit), pl.ds(q_cols, k_cols)]
        )
        if item >= 2:
            for copy in keep_item(item - 2):
                copy.wait()
        if limit < tokens:
            nothing = jnp.zeros((block, tokens - limit), f32)
            r.probs_stage[slot, :, pl.ds(limit, tokens - limit)] = nothing
            r.tanh_stage[slot, :, pl.ds(limit, tokens - limit)] = nothing

        def rows_of(index, carry, first=first, limit=limit, slot=slot):
            here = pl.ds(pl.multiple_of(index * 64, 64), 64)
            info = r.info_buf[pl.ds(pl.multiple_of(first + index * 64, 64), 64)].astype(f32)
            keys = r.key_info[3:4, pl.ds(0, limit)]
            query_at = lax.broadcasted_iota(jnp.int32, (64, limit), 0) + (first + index * 64)
            key_at = lax.broadcasted_iota(jnp.int32, (64, limit), 1)
            related = (keys == info[:, 0:1]) | (keys == info[:, 1:2]) | (keys == info[:, 2:3])
            visible = ((key_at <= query_at) & related) | (key_at == query_at)
            curve = jnp.tanh(r.score[here, pl.ds(0, limit)] * (head_scale / softcap))
            masked = jnp.where(visible, softcap * curve, -1e30)
            terms = jnp.exp(masked - jnp.max(masked, axis=-1, keepdims=True))
            probs = terms / jnp.sum(terms, axis=-1, keepdims=True)
            r.tanh_stage[slot, here, pl.ds(0, limit)] = curve
            r.probs_stage[slot, here, pl.ds(0, limit)] = probs
            r.probs_low[here, pl.ds(0, limit)] = probs.astype(bf16)
            return carry

        lax.fori_loop(0, block // 64, rows_of, 0)
        for copy in keep_item(item):
            copy.start()
        r.mixed_buf[pl.ds(first, block), columns] = dot_plain(
            r.probs_low[:, pl.ds(0, limit)],
            r.qkv_buf[pl.ds(0, limit), pl.ds(q_cols + k_cols, k_cols)],
        ).astype(bf16)

    keep.append(pltpu.make_async_copy(r.mixed_buf, r.mixed, r.keep_sem.at[1]))
    keep[1].start()

    wide = r.cols_buf.shape[1]
    for owner in range(4):

        @pl.when(me == owner)
        def _():
            def rows_of(index, carry):
                rows = pl.ds(pl.multiple_of(index * 64, 64), 64)
                some = r.all_buf[rows, owner * part : (owner + 1) * part]
                if wide > part:
                    some = jnp.concatenate((some, jnp.zeros((64, wide - part), bf16)), axis=1)
                r.cols_buf[rows] = some
                return carry

            lax.fori_loop(0, tokens // 64, rows_of, 0)

    keep.append(pltpu.make_async_copy(r.cols_buf, r.normed_cols, r.keep_sem.at[2]))
    keep[2].start()
    for group in fetch + own:
        for copy in group:
            copy.wait_send()
    for copy in list(on) + tell_info + to_chip + to_twin + on_twin:
        copy.wait_send()
    last = heads * n_blocks
    for item in range(max(0, last - 2), last):
        for copy in keep_item(item):
            copy.wait()
    for copy in keep:
        copy.wait()


def attend(collective_id, **args):
    f32, bf16 = jnp.float32, jnp.bfloat16
    given = types.SimpleNamespace(**args)
    local, width = given.tokens.shape
    tokens = 4 * local
    part = given.w_query.shape[0]
    part_wide = -(-part // PAIR) * PAIR
    q_cols, k_cols = given.w_query.shape[1] // 4, given.w_key.shape[1] // 4
    head_cols = q_cols + 2 * k_cols
    heads = q_cols // HEAD_SIZE
    block = min(TILE, tokens)
    vmem, dma, shape = pltpu.VMEM, pltpu.SemaphoreType.DMA, jax.ShapeDtypeStruct
    outs = dict(
        qkv=shape((tokens, head_cols), bf16),
        mixed=shape((tokens, q_cols), bf16),
        probs=shape((heads, tokens, tokens), f32),
        tanh=shape((heads, tokens, tokens), f32),
        normed_cols=shape((tokens, part_wide), bf16),
    )
    scratch = dict(
        token_buf=vmem((local, width), bf16),
        all_buf=vmem((tokens, width), bf16),
        heads_buf=vmem((width, head_cols), bf16),
        info_buf=vmem((tokens, 128), bf16),
        key_info=vmem((8, tokens), f32),
        qkv_buf=vmem((tokens, head_cols), bf16),
        mixed_buf=vmem((tokens, q_cols), bf16),
        cols_buf=vmem((tokens, part_wide), bf16),
        score=vmem((block, tokens), f32),
        probs_stage=vmem((2, block, tokens), f32),
        tanh_stage=vmem((2, block, tokens), f32),
        probs_low=vmem((block, tokens), bf16),
        load_sem=dma((5,)),
        keep_sem=dma((3,)),
        stage_sem=dma((2, 2)),
        fetch_send=dma((3, 3)),
        fetch_recv=dma((3, 3)),
        info_send=dma((3,)),
        info_recv=dma((3,)),
        pass_send=dma((3, 3)),
        pass_recv=dma((3, 3)),
        all_send=dma((6,)),
        all_recv=dma((6,)),
    )
    any_space = pl.BlockSpec(memory_space=pl.ANY)
    small = pl.BlockSpec(memory_space=pltpu.VMEM)
    results = pl.pallas_call(
        functools.partial(attend_kernel, tuple(args) + tuple(outs) + tuple(scratch)),
        out_shape=list(outs.values()),
        in_specs=[
            small if value.ndim == 2 and value.shape[0] <= 8 else any_space
            for value in args.values()
        ],
        out_specs=[any_space] * len(outs),
        scratch_shapes=list(scratch.values()),
        compiler_params=pltpu.CompilerParams(
            collective_id=collective_id, has_side_effects=True, vmem_limit_bytes=VMEM_LIMIT
        ),
        cost_estimate=pl.CostEstimate(
            flops=4 * tokens * width * head_cols, bytes_accessed=100 * 2**20, transcendentals=0
        ),
    )(*args.values())
    return types.SimpleNamespace(**dict(zip(outs, results)))


QUERY_HEADS = 8
KV = 4
HEAD_SIZE = 256
SEGS = 13


softcap = 50.0
norm_eps = 1e-06


def normalize(values, gain_vec):
    inv_rms = lax.rsqrt(jnp.mean(values * values, axis=-1, keepdims=True) + norm_eps)
    return (values * inv_rms * gain_vec, inv_rms)


def norm_back(values, inv_rms, gain_vec, grad_in):
    weighted = grad_in * gain_vec
    row_mean = jnp.mean(weighted * values, axis=-1, keepdims=True)
    grad_back = inv_rms * weighted - values * (inv_rms * inv_rms * inv_rms) * row_mean
    return (grad_back, jnp.sum(grad_in * values * inv_rms, axis=0))


def geglu(gate_pre, up_pre):
    return jax.nn.gelu(gate_pre, approximate=True) * up_pre


def gather_rows(block):
    return lax.all_gather(block, "shard", axis=0, tiled=True)


def scatter_rows(partial):
    summed = lax.psum_scatter(partial, "shard", scatter_dimension=0, tiled=True)
    return summed.astype(jnp.float32)


def exchange(blocks):
    return lax.all_to_all(blocks, "shard", 0, 0, tiled=True)


def first_gather(normed, seg_ids, w_query, w_key, w_value):
    n = lax.axis_size("shard")
    width = normed.shape[1]
    part_rows = w_query.shape[0]
    share = max(1, n // KV)

    def by_device(weight):
        heads = weight.reshape(part_rows, KV, -1)
        if share > 1:
            heads = jnp.repeat(heads, share, axis=1)
        return heads.reshape(part_rows, n, -1)

    parts = jnp.concatenate(
        (w_query.reshape(part_rows, n, -1), by_device(w_key), by_device(w_value)), axis=2
    ).transpose(1, 0, 2)
    heads = exchange(parts).reshape(width, -1)
    codes = gather_rows(seg_ids.astype(jnp.bfloat16))
    return gather_rows(normed), codes.astype(jnp.int32), heads


def rep_sum(grads, width):
    summed = chain_sum([grad.astype(jnp.bfloat16).reshape(-1, width) for grad in grads])
    return [
        total.reshape(grad.shape).astype(jnp.float32) for total, grad in zip(summed, grads)
    ]


def plane_layer(
    tokens, seg_ids, parents, attn_gain, w_query, w_key, w_value, w_out, post_attn_gain,
    ffn_gain, w_gate, w_up, w_down, post_ffn_gain, cotangent,
):
    f32, bf16 = jnp.float32, jnp.bfloat16
    tok_rows, width = tokens.shape
    nothing = jnp.zeros((width,), f32)
    gains = jnp.stack(
        [gain.astype(f32) for gain in (post_attn_gain, ffn_gain, post_ffn_gain, attn_gain)]
        + [nothing] * 4
    )
    parent_row = parents[0]
    labels = jnp.arange(SEGS)

    def lookup(ident):
        return jnp.sum(jnp.where(ident[:, None] == labels[None, :], parent_row[None, :], 0), axis=1)

    real = seg_ids < SEGS
    parent_one = lookup(seg_ids)
    codes = [jnp.where(real, code, -1) for code in (seg_ids, parent_one, lookup(parent_one))]
    codes.append(jnp.where(real, seg_ids, -2))
    info = jnp.pad(jnp.stack(codes, axis=1).astype(bf16), ((0, 0), (0, 124)))
    heads = attend(
        2, tokens=tokens, gains=gains, info=info, w_query=w_query, w_key=w_key, w_value=w_value
    )
    ahead = forward(
        3,
        mixed=heads.mixed,
        w_out=w_out,
        tokens=tokens,
        cotangent=cotangent,
        gains=gains,
        w_gate=w_gate,
        w_up=w_up,
        w_down=w_down,
    )
    found = backward(
        4,
        grad_ffn=ahead.grad_ffn,
        hidden=ahead.hidden,
        gate=ahead.gate,
        up=ahead.up,
        normed_two=ahead.normed_two,
        w_down=w_down,
        w_gate=w_gate,
        w_up=w_up,
        w_out=w_out,
        middle=ahead.middle,
        attn_out=ahead.attn_out,
        cotangent=cotangent,
        gains=gains,
        gain_parts=ahead.gain_part,
        qkv=heads.qkv,
        mixed=heads.mixed,
        probs=heads.probs,
        tanh=heads.tanh,
        normed_cols=heads.normed_cols,
        w_query=w_query,
        w_key=w_key,
        w_value=w_value,
        tokens=tokens,
    )
    gain_sums = found.gain_sums
    return (
        ahead.output,
        found.grad_tokens,
        gain_sums[3],
        found.query_sum.astype(f32),
        found.key_sum.astype(f32),
        found.value_sum.astype(f32),
        found.out_sum.astype(f32),
        gain_sums[1],
        gain_sums[2],
        found.gate_sum.astype(f32),
        found.up_sum.astype(f32),
        found.down_sum.astype(f32),
        gain_sums[0],
    )


def body(
    tokens,
    seg_ids,
    parents,
    attn_gain,
    w_query,
    w_key,
    w_value,
    w_out,
    post_attn_gain,
    ffn_gain,
    w_gate,
    w_up,
    w_down,
    post_ffn_gain,
    cotangent,
):
    if lax.axis_size("shard") == 4 and lax.axis_size("rep") == 8:
        return plane_layer(
            tokens, seg_ids, parents, attn_gain, w_query, w_key, w_value, w_out, post_attn_gain,
            ffn_gain, w_gate, w_up, w_down, post_ffn_gain, cotangent,
        )
    f32, bf16 = jnp.float32, jnp.bfloat16
    tok_rows, width = tokens.shape
    n = lax.axis_size("shard")
    me = lax.axis_index("shard")
    group_rows = tok_rows * n
    part_rows = w_query.shape[0]
    head_scale = HEAD_SIZE ** (-0.5)
    q_heads = QUERY_HEADS // n
    kv_heads = max(1, KV // n)
    share = n * kv_heads // KV
    repeat = q_heads // kv_heads
    q_cols = q_heads * HEAD_SIZE
    k_cols = kv_heads * HEAD_SIZE
    gain_one = attn_gain.astype(f32)
    gain_two = post_attn_gain.astype(f32)
    gain_three = ffn_gain.astype(f32)
    gain_four = post_ffn_gain.astype(f32)

    residual = tokens.astype(f32)
    normed, rms_one = normalize(residual, gain_one)
    normed_all, codes, qkv_heads = first_gather(
        normed.astype(bf16), seg_ids, w_query, w_key, w_value
    )
    qkv = jnp.dot(normed_all, qkv_heads, preferred_element_type=f32).astype(bf16)
    queries = qkv[:, :q_cols].reshape(group_rows, kv_heads, repeat, HEAD_SIZE)
    keys = qkv[:, q_cols : q_cols + k_cols].reshape(group_rows, kv_heads, HEAD_SIZE)
    values = qkv[:, q_cols + k_cols :].reshape(group_rows, kv_heads, HEAD_SIZE)

    parent_row = parents[0]
    labels = jnp.arange(SEGS)

    def lookup(ident):
        return jnp.sum(jnp.where(ident[:, None] == labels[None, :], parent_row[None, :], 0), axis=1)

    parent_one = lookup(codes)
    parent_two = lookup(parent_one)
    positions = jnp.arange(group_rows)
    real = codes < SEGS
    related = (
        (codes[None, :] == codes[:, None])
        | (codes[None, :] == parent_one[:, None])
        | (codes[None, :] == parent_two[:, None])
    )
    visible = (positions[None, :] <= positions[:, None]) & real[:, None] & real[
        None, :
    ] & related | (positions[None, :] == positions[:, None])

    score_matrix = jnp.einsum("tkrh,skh->krts", queries, keys, preferred_element_type=f32)
    tanh_part = jnp.tanh(score_matrix * (head_scale / softcap))
    masked = jnp.where(visible[None, None], softcap * tanh_part, -1e30)
    row_max = jnp.max(masked, axis=-1, keepdims=True)
    expo_terms = jnp.exp(masked - row_max)
    row_total = jnp.sum(expo_terms, axis=-1, keepdims=True)
    probs = expo_terms / row_total
    probs_b = probs.astype(bf16)
    mixed = jnp.einsum("krts,skh->tkrh", probs_b, values, preferred_element_type=f32)
    mixed = mixed.reshape(group_rows, q_cols).astype(bf16)
    attn_out = scatter_rows(jnp.dot(mixed, w_out, preferred_element_type=f32).astype(bf16))
    post_one, rms_two = normalize(attn_out, gain_two)
    middle = residual + post_one
    normed_two, rms_three = normalize(middle, gain_three)
    normed_two_all = gather_rows(normed_two.astype(bf16))
    gate_pre = jnp.dot(normed_two_all, w_gate, preferred_element_type=f32)
    up_pre = jnp.dot(normed_two_all, w_up, preferred_element_type=f32)
    hidden, geglu_back = jax.vjp(geglu, gate_pre, up_pre)
    hidden_b = hidden.astype(bf16)
    ffn_out = scatter_rows(jnp.dot(hidden_b, w_down, preferred_element_type=f32).astype(bf16))
    post_two, rms_four = normalize(ffn_out, gain_four)
    output = (middle + post_two).astype(bf16)

    grad_out = cotangent.astype(f32)
    grad_ffn, grad_gain_four = norm_back(ffn_out, rms_four, gain_four, grad_out)
    grad_ffn_all = gather_rows(grad_ffn.astype(bf16))
    down_part = jnp.einsum("tf,td->fd", hidden_b, grad_ffn_all, preferred_element_type=f32)
    grad_hidden = jnp.einsum("td,fd->tf", grad_ffn_all, w_down, preferred_element_type=f32)
    grad_gate, grad_up = geglu_back(grad_hidden)
    grad_gate_b = grad_gate.astype(bf16)
    grad_up_b = grad_up.astype(bf16)
    grad_normed_two = jnp.einsum("tf,df->td", grad_gate_b, w_gate, preferred_element_type=f32)
    grad_normed_two += jnp.einsum("tf,df->td", grad_up_b, w_up, preferred_element_type=f32)
    grad_normed_two = scatter_rows(grad_normed_two.astype(bf16))
    gate_part = jnp.einsum("td,tf->df", normed_two_all, grad_gate_b, preferred_element_type=f32)
    up_part = jnp.einsum("td,tf->df", normed_two_all, grad_up_b, preferred_element_type=f32)
    grad_middle_part, grad_gain_three = norm_back(middle, rms_three, gain_three, grad_normed_two)
    grad_middle = grad_out + grad_middle_part
    grad_attn, grad_gain_two = norm_back(attn_out, rms_two, gain_two, grad_middle)
    grad_attn_all = gather_rows(grad_attn.astype(bf16))
    out_part = jnp.einsum("tj,td->jd", mixed, grad_attn_all, preferred_element_type=f32)
    grad_mixed = jnp.einsum("td,jd->tj", grad_attn_all, w_out, preferred_element_type=f32)
    grad_mixed = grad_mixed.astype(bf16).reshape(group_rows, kv_heads, repeat, HEAD_SIZE)
    grad_probs = jnp.einsum("tkrh,skh->krts", grad_mixed, values, preferred_element_type=f32)
    row_inner = jnp.sum(probs * grad_probs, axis=-1, keepdims=True)
    grad_dots = (
        probs * (grad_probs - row_inner) * (1.0 - tanh_part * tanh_part) * head_scale
    ).astype(bf16)
    grad_queries = jnp.einsum("krts,skh->tkrh", grad_dots, keys, preferred_element_type=f32)
    grad_keys = jnp.einsum("krts,tkrh->skh", grad_dots, queries, preferred_element_type=f32)
    grad_values = jnp.einsum("krts,tkrh->skh", probs_b, grad_mixed, preferred_element_type=f32)
    grad_parts = jnp.concatenate(
        (
            grad_queries.reshape(group_rows, q_cols),
            grad_keys.reshape(group_rows, k_cols),
            grad_values.reshape(group_rows, k_cols),
        ),
        axis=1,
    ).astype(bf16)
    grad_parts = gather_rows(grad_parts).reshape(n, group_rows, -1)

    def whole_heads(parts):
        if share > 1:
            parts = parts.reshape(KV, share, group_rows, HEAD_SIZE).astype(f32).sum(axis=1).astype(bf16)
        return parts.transpose(1, 0, 2).reshape(group_rows, -1)

    grad_qkv = jnp.concatenate(
        (
            grad_parts[:, :, :q_cols].transpose(1, 0, 2).reshape(group_rows, -1),
            whole_heads(grad_parts[:, :, q_cols : q_cols + k_cols]),
            whole_heads(grad_parts[:, :, q_cols + k_cols :]),
        ),
        axis=1,
    )
    qkv_local = jnp.concatenate((w_query, w_key, w_value), axis=1)
    grad_normed = jnp.einsum("tj,dj->td", grad_qkv, qkv_local, preferred_element_type=f32)
    grad_normed = exchange(grad_normed.astype(bf16).reshape(n, tok_rows, part_rows))
    grad_normed = grad_normed.transpose(1, 0, 2).reshape(tok_rows, width).astype(f32)
    normed_cols = lax.dynamic_slice_in_dim(normed_all, me * part_rows, part_rows, axis=1)
    qkv_part = jnp.einsum("td,tj->dj", normed_cols, grad_qkv, preferred_element_type=f32)
    grad_resid_part, grad_gain_one = norm_back(residual, rms_one, gain_one, grad_normed)
    grad_tokens = (grad_middle + grad_resid_part).astype(bf16)
    gain_parts = jnp.stack((grad_gain_one, grad_gain_two, grad_gain_three, grad_gain_four))
    gain_sums = lax.all_gather(gain_parts, ("rep", "shard"), axis=0).sum(axis=0)
    down_sum, gate_sum, up_sum, out_sum, qkv_sum = rep_sum(
        (down_part, gate_part, up_part, out_part, qkv_part), width
    )
    q_width = w_query.shape[1]
    k_width = w_key.shape[1]
    return (
        output,
        grad_tokens,
        gain_sums[0],
        qkv_sum[:, :q_width],
        qkv_sum[:, q_width : q_width + k_width],
        qkv_sum[:, q_width + k_width :],
        out_sum,
        gain_sums[1],
        gain_sums[2],
        gate_sum,
        up_sum,
        down_sum,
        gain_sums[3],
    )


def solution(mesh):
    return jax.shard_map(
        body,
        mesh=mesh,
        in_specs=(
            P(("rep", "shard"), None),
            P(("rep", "shard")),
            P("rep", None),
            P(),
            P("shard", None),
            P("shard", None),
            P("shard", None),
            P("shard", None),
            P(),
            P(),
            P(None, "shard"),
            P(None, "shard"),
            P("shard", None),
            P(),
            P(("rep", "shard"), None),
        ),
        out_specs=(
            P(("rep", "shard"), None),
            P(("rep", "shard"), None),
            P(),
            P("shard", None),
            P("shard", None),
            P("shard", None),
            P("shard", None),
            P(),
            P(),
            P(None, "shard"),
            P(None, "shard"),
            P("shard", None),
            P(),
        ),
        check_vma=False,
    )
```

```python
import functools
import math
import types

import jax
import jax.numpy as jnp
from jax import lax
from jax.experimental import pallas as pl
from jax.experimental.pallas import tpu as pltpu
from jax.sharding import PartitionSpec as P

SLOTS = 8
CHUNK = 64


def remote(src, dst, send_sem, recv_sem, where):
    return pltpu.make_async_remote_copy(
        src_ref=src,
        dst_ref=dst,
        send_sem=send_sem,
        recv_sem=recv_sem,
        device_id=where,
        device_id_type=pl.DeviceIdType.MESH,
    )


def add_low(left, right):
    return (left.astype(jnp.float32) + right.astype(jnp.float32)).astype(jnp.bfloat16)


def chain_kernel(counts, chunk, *refs):
    jobs = len(counts)
    ins, outs = refs[:jobs], refs[jobs : 2 * jobs]
    (
        mine, sib, acc, outer_in, inner_in, total,
        load_sem, sib_send, sib_recv, up_send, outer_recv, inner_recv,
        down_send, pair_send, pair_recv, store_sem,
        sib_credit, up_credit, down_credit,
    ) = refs[2 * jobs :]
    slots = mine.shape[0]
    steps = sum(counts)
    place = lax.axis_index("rep")
    chips = lax.axis_size("rep") // 2
    chip, core = place // 2, place % 2
    left = chip < chips // 2
    is_end = (chip == 0) | (chip == chips - 1)
    is_mid = (chip == chips // 2 - 1) | (chip == chips // 2)
    twin = {"rep": place + 1 - 2 * core}
    inner = {"rep": jnp.where(left, place + 2, place - 2)}
    outer = {"rep": jnp.where(is_end, place, jnp.where(left, place - 2, place + 2))}

    def tell(sem, where):
        pl.semaphore_signal(sem, inc=1, device_id=where, device_id_type=pl.DeviceIdType.MESH)

    barrier = pltpu.get_barrier_semaphore()
    tell(barrier, twin)
    tell(barrier, inner)

    @pl.when(is_end)
    def _():
        pl.semaphore_wait(barrier, 2)

    @pl.when(jnp.logical_not(is_end))
    def _():
        tell(barrier, outer)
        pl.semaphore_wait(barrier, 3)

    def with_rows(step, which, use):
        low = 0
        for job, count in enumerate(counts):
            first = low

            @pl.when((step >= low) & (step < low + count))
            def _():
                row = pl.multiple_of(((step - first) * 2 + which) * chunk, chunk)
                use(job, pl.ds(row, chunk))

            low += count

    def pair_copy(job, rows, slot, step):
        return remote(total.at[slot], outs[job].at[rows], pair_send.at[slot], pair_recv.at[step], twin)

    def up_copy(slot, dst, sem):
        return remote(acc.at[slot], dst.at[slot], up_send.at[slot], sem.at[slot], inner)

    def down_copy(slot):
        return remote(total.at[slot], inner_in.at[slot], down_send.at[slot], inner_recv.at[slot], outer)

    def sib_copy(job, rows, slot):
        return remote(ins[job].at[rows], sib.at[slot], sib_send.at[slot], sib_recv.at[slot], twin)

    def load_copy(job, rows, slot):
        return pltpu.make_async_copy(ins[job].at[rows], mine.at[slot], load_sem.at[slot])

    def store_copy(job, rows, slot):
        return pltpu.make_async_copy(total.at[slot], outs[job].at[rows], store_sem.at[slot])

    some = pl.ds(0, chunk)

    def take(step):
        slot = step % slots

        @pl.when(step >= slots)
        def _():
            pl.semaphore_wait(sib_credit, 1)

        with_rows(step, 1 - core, lambda job, rows: sib_copy(job, rows, slot).start())
        with_rows(step, core, lambda job, rows: load_copy(job, rows, slot).start())

    def send_up(step):
        slot = step % slots

        @pl.when(step >= slots)
        def _():
            pl.semaphore_wait(up_credit, 1)

        @pl.when(is_mid)
        def _():
            up_copy(slot, inner_in, inner_recv).start()

        @pl.when(jnp.logical_not(is_mid))
        def _():
            up_copy(slot, outer_in, outer_recv).start()

    def pair_up(step):
        slot = step % slots
        load_copy(0, some, slot).wait()
        sib_copy(0, some, slot).wait()

        @pl.when(step >= slots)
        def _():
            up_copy(slot, outer_in, outer_recv).wait_send()

        acc[slot] = add_low(mine[slot], sib[slot])

        @pl.when(step + slots < steps)
        def _():
            tell(sib_credit, twin)

        @pl.when(is_end)
        def _():
            send_up(step)

    def from_outer(step):
        slot = step % slots
        up_copy(slot, outer_in, outer_recv).wait_recv()
        acc[slot] = add_low(acc[slot], outer_in[slot])

        @pl.when(step + slots < steps)
        def _():
            tell(up_credit, outer)

        send_up(step)

    def sends_done(slot):
        pair_copy(0, some, slot, 0).wait_send()
        store_copy(0, some, slot).wait()

        @pl.when(jnp.logical_not(is_end))
        def _():
            down_copy(slot).wait_send()

    def from_inner(step):
        slot = step % slots
        down_copy(slot).wait_recv()

        @pl.when(step >= slots)
        def _():
            sends_done(slot)

        @pl.when(is_mid)
        def _():
            total[slot] = add_low(acc[slot], inner_in[slot])

            @pl.when(step + slots < steps)
            def _():
                tell(up_credit, inner)

        @pl.when(jnp.logical_not(is_mid))
        def _():
            total[slot] = inner_in[slot]

            @pl.when(step + slots < steps)
            def _():
                tell(down_credit, inner)

        @pl.when(jnp.logical_not(is_end))
        def _():
            @pl.when(step >= slots)
            def _():
                pl.semaphore_wait(down_credit, 1)

            down_copy(slot).start()

        with_rows(step, core, lambda job, rows: pair_copy(job, rows, slot, step).start())
        with_rows(step, core, lambda job, rows: store_copy(job, rows, slot).start())

    lag_outer = 3
    lag_inner = jnp.where(is_end, 8, 6)

    def tick(step, carry):
        @pl.when(step < steps)
        def _():
            take(step)

        @pl.when((step >= 1) & (step - 1 < steps))
        def _():
            pair_up(step - 1)

        @pl.when(jnp.logical_not(is_end) & (step >= lag_outer) & (step - lag_outer < steps))
        def _():
            from_outer(step - lag_outer)

        @pl.when((step >= lag_inner) & (step - lag_inner < steps))
        def _():
            from_inner(step - lag_inner)

        return carry

    lax.fori_loop(0, steps + 8, tick, 0)

    def finish(step, carry):
        slot = step % slots
        sends_done(slot)
        up_copy(slot, outer_in, outer_recv).wait_send()
        return carry

    lax.fori_loop(steps - slots, steps, finish, 0)

    def arrived(step, carry):
        pair_copy(0, some, 0, step).wait_recv()
        return carry

    lax.fori_loop(0, steps, arrived, 0)


def chain_sum(parts, chunk=CHUNK, collective_id=1):
    width = parts[0].shape[1]
    counts = tuple(part.shape[0] // (2 * chunk) for part in parts)
    steps = sum(counts)
    slots = min(SLOTS, steps)
    any_space = pl.BlockSpec(memory_space=pl.ANY)
    block = pltpu.VMEM((slots, chunk, width), jnp.bfloat16)
    sems = pltpu.SemaphoreType.DMA((slots,))
    credit = pltpu.SemaphoreType.REGULAR
    return pl.pallas_call(
        functools.partial(chain_kernel, counts, chunk),
        out_shape=[jax.ShapeDtypeStruct(part.shape, part.dtype) for part in parts],
        in_specs=[any_space] * len(parts),
        out_specs=[any_space] * len(parts),
        scratch_shapes=[block] * 6
        + [sems] * 8
        + [pltpu.SemaphoreType.DMA((steps,)), sems, credit, credit, credit],
        compiler_params=pltpu.CompilerParams(
            collective_id=collective_id, has_side_effects=True, vmem_limit_bytes=48 * 1024 * 1024
        ),
        cost_estimate=pl.CostEstimate(
            flops=0, bytes_accessed=8 * sum(part.size for part in parts), transcendentals=0
        ),
    )(*parts)


def plane_places():
    me = lax.axis_index("shard")
    x_other = me + 1 - 2 * (me % 2)
    y_other = (me + 2) % 4
    far = x_other + y_other - me
    return me, x_other, y_other, far


def greet(places):
    barrier = pltpu.get_barrier_semaphore()
    for place in places:
        pl.semaphore_signal(
            barrier, inc=1, device_id={"shard": place}, device_id_type=pl.DeviceIdType.MESH
        )
    pl.semaphore_wait(barrier, len(places))


TILE = 256
PAIR = 2 * CHUNK
LINE = 32
DEEP = 12
LAST = 6
ROOT_TWO_PI = math.sqrt(2.0 / math.pi)


def dot_rows(left, right):
    return lax.dot_general(left, right, (((1,), (1,)), ((), ())), preferred_element_type=jnp.float32)


def dot_plain(left, right):
    return lax.dot_general(left, right, (((1,), (0,)), ((), ())), preferred_element_type=jnp.float32)


def dot_columns(left, right):
    return lax.dot_general(left, right, (((0,), (0,)), ((), ())), preferred_element_type=jnp.float32)


def column_pieces(width):
    return 3 if width % 384 == 0 else 2


def backward_kernel(dims, names, *refs):
    r = types.SimpleNamespace(**dict(zip(names, refs)))
    tokens, local, width, inner_width, head_cols = dims
    f32, bf16 = jnp.float32, jnp.bfloat16
    half = local // 2
    q_cols = head_cols // 2
    k_cols = head_cols // 4
    heads = q_cols // HEAD_SIZE
    part = width // 4
    part_wide = r.normed_cols.shape[1]
    side = 2 * head_cols
    n_a = inner_width // TILE
    n_b = width // TILE
    block = min(TILE, tokens)
    n_blocks = tokens // block
    pieces = column_pieces(width)
    piece = width // pieces
    group = PAIR * pieces

    counts = (
        inner_width // PAIR, width // PAIR, width // PAIR, r.w_out.shape[0] // PAIR,
        part // (2 * LINE),
    )
    first = [sum(counts[:job]) for job in range(6)]
    units = first[5]
    steps = 2 * units
    a_at = pieces + 1
    b_at = a_at + (n_a + 1) // 2
    c_at = b_at + n_b
    d_at = c_at + 5
    f_at = d_at + 5
    g_at = f_at + 1
    h_at = g_at + heads * n_blocks
    i_at = h_at + 9
    k_at = i_at + 3
    assert b_at <= first[1] and f_at < first[3] and i_at < first[4] and first[1] <= i_at
    assert first[2] <= i_at and k_at + 5 <= units + 5 and counts[0] // pieces >= 2

    place = lax.axis_index("rep")
    chips = lax.axis_size("rep") // 2
    chip, core = place // 2, place % 2
    left = chip < chips // 2
    is_end = (chip == 0) | (chip == chips - 1)
    is_mid = (chip == chips // 2 - 1) | (chip == chips // 2)
    twin = {"rep": place + 1 - 2 * core}
    inner = {"rep": jnp.where(left, place + 2, place - 2)}
    outer = {"rep": jnp.where(is_end, place, jnp.where(left, place - 2, place + 2))}
    next_chip = {"rep": place + 2 - 4 * (chip % 2)}
    far_chip = {"rep": (place + 4) % 8}
    me, x_place, y_place, far_place = plane_places()
    x_other, y_other = {"shard": x_place}, {"shard": y_place}
    plane = [{"shard": (me + step) % 4} for step in (1, 2, 3)]

    def tell(sem, where):
        pl.semaphore_signal(sem, inc=1, device_id=where, device_id_type=pl.DeviceIdType.MESH)

    def load(src, dst, index):
        return pltpu.make_async_copy(src, dst, r.load_sem.at[index])

    load_ffn = load(
        r.grad_ffn,
        r.ffn_buf.at[pl.ds(pl.multiple_of(me * local, 16), local), pl.ds(0, width)], 0,
    )
    load_hidden = load(r.hidden, r.hidden_buf.at[:, pl.ds(0, inner_width)], 1)
    load_two = load(r.normed_two, r.two_buf, 2)
    load_small = (
        load(r.middle, r.middle_buf, 3),
        load(r.attn_out, r.attn_buf, 4),
        load(r.cotangent, r.cot_buf, 5),
        load(r.qkv, r.qkv_buf, 6),
        load(r.mixed, r.mixed_buf, 7),
        load(r.normed_cols, r.cols_buf, 8),
        load(r.tokens, r.token_buf, 9),
    )

    def weight_tile(index):
        return r.weights.at[pl.ds(pl.multiple_of(index * TILE, TILE), TILE)]

    def a_loads(tile, buf):
        rows = pl.ds(pl.multiple_of(tile * TILE, TILE), TILE)
        return (
            load(r.w_down.at[rows], weight_tile(buf).at[:, pl.ds(0, width)], 10 + buf),
            load(r.gate.at[:, rows], r.gate_buf.at[buf], 12 + buf),
            load(r.up.at[:, rows], r.up_buf.at[buf], 14 + buf),
        )

    def b_loads(tile):
        rows = pl.ds(pl.multiple_of(tile * TILE, TILE), TILE)
        buf = 2 - 2 * (tile % 2)
        sem = 16 + 2 * (tile % 2)
        return (
            load(r.w_gate.at[rows], weight_tile(buf).at[:, pl.ds(0, inner_width)], sem),
            load(r.w_up.at[rows], weight_tile(buf + 1).at[:, pl.ds(0, inner_width)], sem + 1),
        )

    def b_store(tile):
        columns = pl.ds(pl.multiple_of(tile * TILE, TILE), TILE)
        return pltpu.make_async_copy(
            r.stage.at[tile % 2], r.partial.at[:, columns], r.stage_sem.at[tile % 2]
        )

    for index, gain in enumerate((r.post_attn_gain, r.ffn_gain, r.post_ffn_gain, r.attn_gain)):
        r.gains[index : index + 1] = gain[...].astype(jnp.float32).reshape(1, gain.shape[0])
    load_ffn.start()
    load_hidden.start()
    for buf in range(2):
        for copy in a_loads(buf, buf):
            copy.start()
    load_two.start()
    for copy in load_small:
        copy.start()
    for copy in b_loads(0):
        copy.start()

    barrier = pltpu.get_barrier_semaphore()
    for where in [twin, inner, far_chip] + plane:
        tell(barrier, where)

    @pl.when(is_end)
    def _():
        pl.semaphore_wait(barrier, 6)

    @pl.when(jnp.logical_not(is_end))
    def _():
        tell(barrier, outer)
        pl.semaphore_wait(barrier, 7)

    def ffn_copies(index):
        across = pl.ds(index * piece, piece)

        def send(owner, which, at, where, own):
            here = pl.ds(pl.multiple_of(owner * local + which * half, 16), half)
            src = r.grad_ffn.at[pl.ds(which * half, half), across]
            return remote(
                src if own else r.ffn_buf.at[here, across], r.ffn_buf.at[here, across],
                r.ffn_send.at[index, at], r.ffn_recv.at[index, at], where,
            )

        starts = (
            send(me, 0, 0, x_other, True), send(me, 1, 1, y_other, True),
            send(me, 1, 2, x_other, True), send(me, 0, 3, y_other, True),
        )
        return starts, (send(x_place, 0, 4, y_other, False), send(y_place, 1, 5, x_other, False))

    ffn_pieces = [ffn_copies(index) for index in range(pieces)]

    def ffn_pass(index):
        starts, passes = ffn_pieces[index]
        for i in range(2):
            starts[i].wait_recv()
            passes[i].start()

    def ffn_arrived(index):
        starts, passes = ffn_pieces[index]
        for copy in starts[2:] + passes:
            copy.wait_recv()

    def ffn_sent():
        for starts, passes in ffn_pieces:
            for copy in starts + passes:
                copy.wait_send()

    for copy in ffn_pieces[0][0]:
        copy.start()
    ffn_pass(0)
    for starts, _ in ffn_pieces[1:]:
        for copy in starts:
            copy.start()
    load_ffn.wait()
    load_hidden.wait()
    ffn_arrived(0)

    def a_tile(tile, buf):
        for copy in a_loads(tile, buf):
            copy.wait()
        r.wide[...] = dot_rows(r.ffn_buf[:, pl.ds(0, width)], weight_tile(buf)[:, pl.ds(0, width)])
        columns = pl.ds(pl.multiple_of(tile * TILE, TILE), TILE)

        def rows_of(index, carry):
            rows = pl.ds(pl.multiple_of(index * 128, 128), 128)
            grad = r.wide[rows]
            gate = r.gate_buf[buf, rows].astype(f32)
            up = r.up_buf[buf, rows].astype(f32)
            curve = jnp.tanh(ROOT_TWO_PI * (gate + 0.044715 * gate * gate * gate))
            slope = (1.0 - curve * curve) * (ROOT_TWO_PI * (1.0 + 3.0 * 0.044715 * gate * gate))
            gelu_slope = 0.5 * (1.0 + curve) + 0.5 * gate * slope
            r.gate_grad[rows, columns] = (grad * up * gelu_slope).astype(bf16)
            r.up_grad[rows, columns] = (grad * (0.5 * gate * (1.0 + curve))).astype(bf16)
            return carry

        lax.fori_loop(0, tokens // 128, rows_of, 0)

        @pl.when(tile + 2 < n_a)
        def _():
            for copy in a_loads(tile + 2, buf):
                copy.start()

    def b_tile(tile):
        for copy in b_loads(tile):
            copy.wait()

        @pl.when(tile >= 2)
        def _():
            b_store(tile - 2).wait()

        buf = 2 - 2 * (tile % 2)
        some = dot_rows(r.gate_grad[:, pl.ds(0, inner_width)], weight_tile(buf)[:, pl.ds(0, inner_width)])
        some += dot_rows(r.up_grad[...], weight_tile(buf + 1)[:, pl.ds(0, inner_width)])
        r.stage[tile % 2] = some.astype(bf16)
        b_store(tile).start()

        @pl.when(tile + 2 < n_b)
        def _():
            for copy in b_loads(tile + 2):
                copy.start()

    def partial_rows(owner, which):
        return r.partial.at[pl.ds(pl.multiple_of(owner * local + which * half, 16), half)]

    c_own = (
        load(partial_rows(y_place, 0), r.c_mine.at[0], 20),
        load(partial_rows(x_place, 1), r.c_mine.at[1], 21),
        load(partial_rows(me, 0), r.c_mine.at[2], 22),
        load(partial_rows(me, 1), r.c_mine.at[3], 23),
    )

    def c_send(src, index, where):
        return remote(src, r.c_landed.at[index], r.c_send.at[index], r.c_recv.at[index], where)

    c_first = (
        c_send(partial_rows(far_place, 0), 0, x_other),
        c_send(partial_rows(far_place, 1), 1, y_other),
        c_send(partial_rows(x_place, 0), 2, x_other),
        c_send(partial_rows(y_place, 1), 3, y_other),
    )
    c_on = (c_send(r.c_mine.at[0], 4, y_other), c_send(r.c_mine.at[1], 5, x_other))

    def c_start():
        b_store(n_b - 2).wait()
        b_store(n_b - 1).wait()
        for copy in c_first + c_own:
            copy.start()

    def c_pass():
        for copy in c_own:
            copy.wait()
        for index in range(2):
            c_first[index].wait_recv()
            r.c_mine[index] = add_low(r.c_mine[index], r.c_landed[index])
            c_on[index].start()

    def d_norms():
        for copy in load_small:
            copy.wait()
        for copy in c_first:
            copy.wait_send()
        for copy in c_first[2:] + c_on:
            copy.wait_recv()
        r.gain_own[...] = r.gain_parts[...]

        def rows_of(which, index, carry):
            here = pl.ds(pl.multiple_of(index * 16, 16), 16)
            rows = pl.ds(pl.multiple_of(which * half + index * 16, 16), 16)
            grad = (
                r.c_mine[2 + which, here].astype(f32)
                + r.c_landed[2 + which, here].astype(f32)
                + r.c_landed[4 + which, here].astype(f32)
            )
            middle = r.middle_buf[rows]
            inv = lax.rsqrt(jnp.mean(middle * middle, axis=-1, keepdims=True) + norm_eps)
            weighted = grad * r.gains[1:2]
            mean = jnp.mean(weighted * middle, axis=-1, keepdims=True)
            r.gain_own[2:3, 0:width] += jnp.sum(grad * middle * inv, axis=0, keepdims=True)
            grad_mid = (
                r.cot_buf[rows].astype(f32) + inv * weighted - middle * (inv * inv * inv) * mean
            )
            r.middle_buf[rows] = grad_mid
            attn = r.attn_buf[rows]
            inv = lax.rsqrt(jnp.mean(attn * attn, axis=-1, keepdims=True) + norm_eps)
            weighted = grad_mid * r.gains[0:1]
            mean = jnp.mean(weighted * attn, axis=-1, keepdims=True)
            r.gain_own[1:2, 0:width] += jnp.sum(grad_mid * attn * inv, axis=0, keepdims=True)
            grad_attn = inv * weighted - attn * (inv * inv * inv) * mean
            r.all_grad[pl.ds(pl.multiple_of(me * local + which * half + index * 16, 16), 16)] = (
                grad_attn.astype(bf16)
            )
            return carry

        for which in range(2):
            lax.fori_loop(0, half // 16, functools.partial(rows_of, which), 0)
        for copy in c_on:
            copy.wait_send()

    def gather_copies(rows, source, target, send_sem, recv_sem):
        def send(owner, which, index, where, src):
            here = pl.ds(pl.multiple_of(owner * 2 * rows + which * rows, 16), rows)
            return remote(
                src.at[here] if src is target else src.at[pl.ds(which * rows, rows)],
                target.at[here], send_sem.at[index], recv_sem.at[index], where,
            )

        starts = (
            send(me, 0, 0, x_other, source),
            send(me, 1, 1, y_other, source),
            send(me, 1, 2, x_other, source),
            send(me, 0, 3, y_other, source),
        )
        passes = (
            send(x_place, 0, 4, y_other, target), send(y_place, 1, 5, x_other, target)
        )
        return starts, passes

    e_first, e_on = gather_copies(half, r.all_grad, r.all_grad, r.e_send, r.e_recv)
    h_first, h_on = gather_copies(tokens // 2, r.head_grad, r.grad_qkv, r.h_send, r.h_recv)
    h_own = pltpu.make_async_copy(
        r.head_grad, r.grad_qkv.at[pl.ds(pl.multiple_of(me * tokens, 16), tokens)], r.keep_sem.at[1]
    )

    def pass_on(starts, passes):
        for index in range(2):
            starts[index].wait_recv()
            passes[index].start()

    def gathered(starts, passes):
        for copy in starts[2:] + passes:
            copy.wait_recv()
        for copy in starts + passes:
            copy.wait_send()

    load_out = load(r.w_out, r.weights.at[pl.ds(0, r.w_out.shape[0]), pl.ds(0, width)], 24)

    def g_loads(item):
        head, rows = item // n_blocks, pl.ds(pl.multiple_of((item % n_blocks) * block, block), block)
        return (
            load(r.probs.at[head, rows], r.probs_buf, 25),
            load(r.tanh.at[head, rows], r.tanh_buf, 26),
        )

    def f_mixed():
        gathered(e_first, e_on)
        load_out.wait()
        r.mixed_grad[...] = dot_rows(
            r.all_grad[...], r.weights[pl.ds(0, r.w_out.shape[0]), pl.ds(0, width)]
        ).astype(bf16)
        r.kv_grad[...] = jnp.zeros_like(r.kv_grad)
        for copy in g_loads(0):
            copy.start()

    def g_attention(item):
        head = item // n_blocks
        rows = pl.ds(pl.multiple_of((item % n_blocks) * block, block), block)
        columns = pl.ds(pl.multiple_of(head * HEAD_SIZE, HEAD_SIZE), HEAD_SIZE)
        for copy in g_loads(item):
            copy.wait()
        grad_out = r.mixed_grad[rows, columns]
        values = r.qkv_buf[:, pl.ds(q_cols + k_cols, k_cols)]
        r.score_grad[...] = dot_rows(grad_out, values)

        def rows_of(index, carry):
            here = pl.ds(pl.multiple_of(index * 64, 64), 64)
            probs = r.probs_buf[here]
            grad = r.score_grad[here]
            curve = r.tanh_buf[here]
            total = jnp.sum(probs * grad, axis=-1, keepdims=True)
            grad = probs * (grad - total) * (1.0 - curve * curve) * (HEAD_SIZE ** (-0.5))
            r.dots_grad[here] = grad.astype(bf16)
            r.probs_low[here] = probs.astype(bf16)
            return carry

        lax.fori_loop(0, block // 64, rows_of, 0)

        @pl.when(item + 1 < heads * n_blocks)
        def _():
            for copy in g_loads(item + 1):
                copy.start()

        keys = r.qkv_buf[:, pl.ds(q_cols, k_cols)]
        r.head_grad[rows, columns] = dot_plain(r.dots_grad[...], keys).astype(bf16)
        r.kv_grad[0] += dot_columns(r.dots_grad[...], r.qkv_buf[rows, columns])
        r.kv_grad[1] += dot_columns(r.probs_low[...], grad_out)

    def h_start():
        r.head_grad[:, pl.ds(q_cols, k_cols)] = r.kv_grad[0].astype(bf16)
        r.head_grad[:, pl.ds(q_cols + k_cols, k_cols)] = r.kv_grad[1].astype(bf16)
        for copy in h_first:
            copy.start()
        h_own.start()

    def side_of(owner, kind):
        buf = r.hidden_buf if owner < 2 else r.ffn_buf
        size = (q_cols, k_cols, k_cols)[kind]
        start = (0, 2 * q_cols, 2 * q_cols + 2 * k_cols)[kind] + (owner % 2) * size
        return buf.at[:, pl.ds(start, size)]

    i_loads = [
        load(
            r.grad_qkv.at[
                pl.ds(owner * tokens, tokens),
                pl.ds((0, q_cols, q_cols + k_cols)[kind], (q_cols, k_cols, k_cols)[kind]),
            ],
            side_of(owner, kind),
            27 + 3 * owner + kind,
        )
        for owner in range(4)
        for kind in range(3)
    ] + [
        load(r.w_query, r.gate_grad.at[pl.ds(0, part), pl.ds(0, 4 * q_cols)], 39),
        load(r.w_key, r.weights.at[pl.ds(0, part), pl.ds(0, 4 * k_cols)], 40),
        load(r.w_value, r.weights.at[pl.ds(0, part), pl.ds(4 * k_cols, 4 * k_cols)], 41),
    ]
    i_copies = [
        remote(
            r.head_grad.at[pl.ds(pl.multiple_of(((me + step) % 4) * local, 16), local), pl.ds(0, part_wide)],
            r.norm_grad.at[me], r.i_send.at[step - 1], r.i_recv.at[step - 1], plane[step - 1],
        )
        for step in (1, 2, 3)
    ]

    def i_start():
        gathered(h_first, h_on)
        h_own.wait()
        for copy in i_loads:
            copy.start()
        for copy in i_loads:
            copy.wait()

    def i_norm():
        def rows_of(index, carry):
            rows = pl.ds(pl.multiple_of(index * block, block), block)
            some = jnp.zeros((block, part_wide), f32)
            for owner in range(4):
                for kind, size in enumerate((q_cols, k_cols, k_cols)):
                    held = r.gate_grad if kind == 0 else r.weights
                    start = (0, 0, 4 * k_cols)[kind] + owner * size
                    some += dot_rows(
                        side_of(owner, kind)[rows], held[pl.ds(0, part_wide), pl.ds(start, size)]
                    )
            r.head_grad[rows, pl.ds(0, part_wide)] = some.astype(bf16)
            return carry

        lax.fori_loop(0, n_blocks, rows_of, 0)
        for copy in i_copies:
            copy.start()
        r.norm_grad[me] = r.head_grad[
            pl.ds(pl.multiple_of(me * local, 16), local), pl.ds(0, part_wide)
        ]

    def k_norm():
        for copy in i_copies:
            copy.wait()

        def rows_of(index, carry):
            rows = pl.ds(pl.multiple_of(index * 16, 16), 16)
            grad = jnp.concatenate(
                [r.norm_grad[owner, rows].astype(f32)[:, :part] for owner in range(4)], axis=1
            )
            values = r.token_buf[rows].astype(f32)
            inv = lax.rsqrt(jnp.mean(values * values, axis=-1, keepdims=True) + norm_eps)
            weighted = grad * r.gains[3:4]
            mean = jnp.mean(weighted * values, axis=-1, keepdims=True)
            r.gain_own[3:4] += jnp.sum(grad * values * inv, axis=0, keepdims=True)
            r.cot_buf[rows] = (
                r.middle_buf[rows] + inv * weighted - values * (inv * inv * inv) * mean
            ).astype(bf16)
            return carry

        lax.fori_loop(0, local // 16, rows_of, 0)
        keep_part.start()
        for copy in gain_plane:
            copy.start()

    keep_part = pltpu.make_async_copy(r.cot_buf, r.grad_tokens, r.keep_sem.at[0])
    gain_plane = [
        remote(r.gain_own, r.gain_plane.at[me], r.gain_send.at[i], r.gain_recv.at[i], where)
        for i, where in enumerate(plane)
    ]
    gain_rep = [
        remote(r.gain_mine.at[i], r.gain_theirs.at[i], r.gain_send.at[3 + i], r.gain_recv.at[3 + i], where)
        for i, where in enumerate((twin, next_chip, far_chip))
    ]

    def k_plane():
        for copy in gain_plane:
            copy.wait()
        r.gain_plane[me] = r.gain_own[...]
        r.gain_mine[0] = (r.gain_plane[0] + r.gain_plane[1]) + (r.gain_plane[2] + r.gain_plane[3])
        gain_rep[0].start()

    def k_rep(index):
        gain_rep[index].wait()
        total = r.gain_mine[index] + r.gain_theirs[index]
        if index < 2:
            r.gain_mine[index + 1] = total
            gain_rep[index + 1].start()
        else:
            r.gain_total[...] = total
            keep_gains.start()

    keep_gains = pltpu.make_async_copy(r.gain_total, r.gain_sums, r.keep_sem.at[3])

    sums = (r.down_sum, r.gate_sum, r.up_sum, r.out_sum)

    def by_job(step, use, scale=2):
        for job in range(5):

            @pl.when((step >= scale * first[job]) & (step < scale * first[job + 1]))
            def _():
                use(job, step - scale * first[job])

    def by_width(step, use):
        if side == r.acc.shape[2]:
            use(pl.ds(0, side))
            return

        @pl.when(step < 2 * first[4])
        def _():
            use(pl.ds(0, r.acc.shape[2]))

        @pl.when(step >= 2 * first[4])
        def _():
            use(pl.ds(0, side))

    def results(job, index, slot):
        if job == 0:
            unit, which = index // 2, index % 2
            low = (unit % (inner_width // group)) * group + (2 * which + core) * pieces * LINE
            across = pl.ds(pl.multiple_of(unit // (inner_width // group) * piece, 128), piece)
            return [
                (
                    r.total.at[slot, :, pl.ds(i * piece, piece)],
                    r.down_sum.at[pl.ds(pl.multiple_of(low + i * LINE, LINE), LINE), across],
                )
                for i in range(pieces)
            ]
        if job < 4:
            rows = pl.ds(pl.multiple_of((2 * index + core) * LINE, LINE), LINE)
            return [(r.total.at[slot, :, pl.ds(0, sums[job].shape[1])], sums[job].at[rows])]
        rows = pl.ds(pl.multiple_of(index * LINE, LINE), LINE)
        pairs, start = [], 0
        for ref in (r.query_sum, r.key_sum, r.value_sum):
            size = ref.shape[1] // 2
            columns = pl.ds(pl.multiple_of(core * size, 128), size)
            pairs.append((r.total.at[slot, :, pl.ds(start, size)], ref.at[rows, columns]))
            start += size
        return pairs

    def pair_copies(job, index, step):
        slot = step % LAST
        return [
            remote(src, dst, r.pair_send.at[slot, i], r.pair_recv.at[step, i], twin)
            for i, (src, dst) in enumerate(results(job, index, slot))
        ]

    def store_copies(job, index, step):
        slot = step % LAST
        return [
            pltpu.make_async_copy(src, dst, r.store_sem.at[slot, i])
            for i, (src, dst) in enumerate(results(job, index, slot))
        ]

    def made_rows(step, owner):
        return pl.ds(pl.multiple_of((step % 2) * 2 * LINE + owner * LINE, LINE), LINE)

    def sib_copy(step, across):
        return remote(
            r.made.at[step // 2 % 2, made_rows(step, 1 - core), across],
            r.sib.at[step % 4, :, across], r.sib_send.at[step % 4], r.sib_recv.at[step % 4], twin,
        )

    def up_copy(step, across, dst, sem):
        slot = step % DEEP
        return remote(
            r.acc.at[slot, :, across], dst.at[slot, :, across], r.up_send.at[slot], sem.at[slot], inner
        )

    def down_copy(step, across):
        return remote(
            r.total.at[step % LAST, :, across], r.inner_in.at[step % DEEP, :, across],
            r.down_send.at[step % LAST], r.inner_recv.at[step % DEEP], outer,
        )

    def up_sent(step):
        by_width(step, lambda across: up_copy(step, across, r.outer_in, r.outer_recv).wait_send())

    def make(unit):
        slot = unit % 2

        def product(job, index):
            if job == 0:
                n_groups = inner_width // group
                rows = pl.ds(pl.multiple_of(index % n_groups * group, PAIR), group)
                across = pl.ds(pl.multiple_of(index // n_groups * piece, 128), piece)
                some = dot_columns(r.hidden_buf[:, rows], r.ffn_buf[:, across]).astype(bf16)
                for row in range(4):
                    for i in range(pieces):
                        low = (row * pieces + i) * LINE
                        r.made[slot, pl.ds(row * LINE, LINE), pl.ds(i * piece, piece)] = some[
                            low : low + LINE
                        ]
                return
            if job < 4:
                left_buf = (None, r.two_buf, r.two_buf, r.mixed_buf)[job]
                right_buf = (None, r.gate_grad, r.up_grad, r.all_grad)[job]
                columns = pl.ds(pl.multiple_of(index * PAIR, PAIR), PAIR)
                across = pl.ds(0, sums[job].shape[1])
                r.made[slot, :, across] = dot_columns(
                    left_buf[:, columns], right_buf[:, across]
                ).astype(bf16)
                return
            columns = pl.ds(pl.multiple_of((index // 2) * PAIR, PAIR), PAIR)
            for which, buf in enumerate((r.hidden_buf, r.ffn_buf)):
                r.both[...] = dot_columns(r.cols_buf[:, columns], buf[:, pl.ds(0, side)]).astype(bf16)
                for row in range(2):
                    low = pl.multiple_of((index % 2) * 2 * LINE + row * LINE, LINE)
                    r.made[slot, pl.ds((2 * row + which) * LINE, LINE), pl.ds(0, side)] = r.both[
                        pl.ds(low, LINE)
                    ]

        by_job(unit, product, 1)

    def give(step):
        @pl.when(step >= 4)
        def _():
            pl.semaphore_wait(r.sib_credit, 1)

        by_width(step, lambda across: sib_copy(step, across).start())

    def send_up(step):
        @pl.when(step >= DEEP)
        def _():
            pl.semaphore_wait(r.up_credit, 1)

        @pl.when(is_mid)
        def _():
            by_width(step, lambda across: up_copy(step, across, r.inner_in, r.inner_recv).start())

        @pl.when(jnp.logical_not(is_mid))
        def _():
            by_width(step, lambda across: up_copy(step, across, r.outer_in, r.outer_recv).start())

    def pair_up(step):
        slot = step % DEEP
        by_width(step, lambda across: sib_copy(step, across).wait())

        @pl.when(step >= DEEP)
        def _():
            up_sent(step - DEEP)

        r.acc[slot] = add_low(r.made[step // 2 % 2, made_rows(step, core)], r.sib[step % 4])

        @pl.when(step + 4 < steps)
        def _():
            tell(r.sib_credit, twin)

        @pl.when(is_end)
        def _():
            send_up(step)

    def from_outer(step):
        slot = step % DEEP
        by_width(step, lambda across: up_copy(step, across, r.outer_in, r.outer_recv).wait_recv())
        r.acc[slot] = add_low(r.acc[slot], r.outer_in[slot])

        @pl.when(step + DEEP < steps)
        def _():
            tell(r.up_credit, outer)

        send_up(step)

    def sends_done(step):
        def use(job, index):
            for copy in pair_copies(job, index, step):
                copy.wait_send()
            for copy in store_copies(job, index, step):
                copy.wait()

        by_job(step, use)

        @pl.when(jnp.logical_not(is_end))
        def _():
            by_width(step, lambda across: down_copy(step, across).wait_send())

    def from_inner(step):
        slot = step % DEEP
        by_width(step, lambda across: down_copy(step, across).wait_recv())

        @pl.when(step >= LAST)
        def _():
            sends_done(step - LAST)

        @pl.when(is_mid)
        def _():
            r.total[step % LAST] = add_low(r.acc[slot], r.inner_in[slot])

            @pl.when(step + DEEP < steps)
            def _():
                tell(r.up_credit, inner)

        @pl.when(jnp.logical_not(is_mid))
        def _():
            r.total[step % LAST] = r.inner_in[slot]

            @pl.when(step + DEEP < steps)
            def _():
                tell(r.down_credit, inner)

        @pl.when(jnp.logical_not(is_end))
        def _():
            @pl.when(step >= DEEP)
            def _():
                pl.semaphore_wait(r.down_credit, 1)

            by_width(step, lambda across: down_copy(step, across).start())

        def use(job, index):
            for copy in pair_copies(job, index, step) + store_copies(job, index, step):
                copy.start()

        by_job(step, use)

    lag_outer = 3
    lag_inner = jnp.where(is_end, 10, 6)

    def at(now, step, use):
        @pl.when(now == step)
        def _():
            use()

    def work(now):
        @pl.when(now == 0)
        def _():
            load_two.wait()

        for index in range(1, pieces):
            at(now, index, functools.partial(ffn_pass, index))

            at(now, index + 1, functools.partial(ffn_arrived, index))

        at(now, b_at, ffn_sent)

        for buf in range(2):

            @pl.when((now >= a_at) & (2 * (now - a_at) + buf < n_a))
            def _():
                a_tile(2 * (now - a_at) + buf, buf)

        @pl.when(now == b_at - 1)
        def _():
            for copy in b_loads(1):
                copy.start()

        @pl.when((now >= b_at) & (now < c_at))
        def _():
            b_tile(now - b_at)

        at(now, c_at, c_start)
        at(now, c_at + 1, load_out.start)
        at(now, c_at + 2, c_pass)

        @pl.when(now == d_at)
        def _():
            d_norms()
            for copy in e_first:
                copy.start()

        at(now, d_at + 2, lambda: pass_on(e_first, e_on))
        at(now, f_at, f_mixed)

        @pl.when((now >= g_at) & (now < h_at))
        def _():
            g_attention(now - g_at)

        at(now, h_at, h_start)
        at(now, h_at + 4, lambda: pass_on(h_first, h_on))
        at(now, i_at, i_start)
        at(now, i_at + 1, i_norm)
        at(now, k_at, k_norm)
        at(now, k_at + 1, k_plane)
        for index in range(3):
            at(now, k_at + 2 + index, functools.partial(k_rep, index))

    def tick(now, carry):
        @pl.when((now % 2 == 0) & (now < steps))
        def _():
            make(now // 2)

        @pl.when(now < steps)
        def _():
            give(now)

        @pl.when((now >= 1) & (now - 1 < steps))
        def _():
            pair_up(now - 1)

        @pl.when(jnp.logical_not(is_end) & (now >= lag_outer) & (now - lag_outer < steps))
        def _():
            from_outer(now - lag_outer)

        @pl.when((now >= lag_inner) & (now - lag_inner < steps))
        def _():
            from_inner(now - lag_inner)

        @pl.when(now % 2 == 1)
        def _():
            work(now // 2)

        return carry

    lax.fori_loop(0, steps + 10, tick, 0)

    def finish(step, carry):
        sends_done(step)
        return carry

    lax.fori_loop(steps - LAST, steps, finish, 0)

    def finish_up(step, carry):
        up_sent(step)
        return carry

    lax.fori_loop(steps - DEEP, steps, finish_up, 0)

    def arrived(step, carry):
        def use(job, index):
            for copy in pair_copies(job, index, step):
                copy.wait_recv()

        by_job(step, use)
        return carry

    lax.fori_loop(0, steps, arrived, 0)
    for copy in (keep_part, keep_gains):
        copy.wait()


def backward(collective_id, **args):
    f32, bf16 = jnp.float32, jnp.bfloat16
    given = types.SimpleNamespace(**args)
    tokens, width = given.normed_two.shape
    inner_width = given.hidden.shape[1]
    local = tokens // 4
    half = local // 2
    head_cols = given.qkv.shape[1]
    part = width // 4
    part_wide = given.normed_cols.shape[1]
    out_rows = given.w_out.shape[0]
    side = 2 * head_cols
    slot_width = max(width, inner_width, side)
    pieces = column_pieces(width)
    block = min(TILE, tokens)
    steps = 2 * ((inner_width + 2 * width + out_rows) // PAIR + part // (2 * LINE))
    vmem, dma, credit = pltpu.VMEM, pltpu.SemaphoreType.DMA, pltpu.SemaphoreType.REGULAR
    shape = jax.ShapeDtypeStruct
    outs = dict(
        down_sum=shape((inner_width, width), bf16),
        gate_sum=shape((width, inner_width), bf16),
        up_sum=shape((width, inner_width), bf16),
        out_sum=shape((out_rows, width), bf16),
        query_sum=shape((part, side), bf16),
        key_sum=shape((part, side // 2), bf16),
        value_sum=shape((part, side // 2), bf16),
        grad_tokens=shape((local, width), bf16),
        gain_sums=shape((8, width), f32),
        partial=shape((tokens, width), bf16),
        grad_qkv=shape((4 * tokens, head_cols), bf16),
    )
    scratch = dict(
        ffn_buf=vmem((tokens, slot_width), bf16),
        hidden_buf=vmem((tokens, slot_width), bf16),
        two_buf=vmem((tokens, width), bf16),
        gate_grad=vmem((tokens, slot_width), bf16),
        up_grad=vmem((tokens, inner_width), bf16),
        weights=vmem((4 * TILE, slot_width), bf16),
        gate_buf=vmem((2, tokens, TILE), bf16),
        up_buf=vmem((2, tokens, TILE), bf16),
        wide=vmem((tokens, TILE), f32),
        stage=vmem((2, tokens, TILE), bf16),
        c_mine=vmem((4, half, width), bf16),
        c_landed=vmem((6, half, width), bf16),
        middle_buf=vmem((local, width), f32),
        attn_buf=vmem((local, width), f32),
        cot_buf=vmem((local, width), bf16),
        qkv_buf=vmem((tokens, head_cols), bf16),
        mixed_buf=vmem((tokens, out_rows), bf16),
        cols_buf=vmem((tokens, -(-part // PAIR) * PAIR), bf16),
        token_buf=vmem((local, width), bf16),
        all_grad=vmem((tokens, width), bf16),
        mixed_grad=vmem((tokens, out_rows), bf16),
        probs_buf=vmem((block, tokens), f32),
        tanh_buf=vmem((block, tokens), f32),
        score_grad=vmem((block, tokens), f32),
        dots_grad=vmem((block, tokens), bf16),
        probs_low=vmem((block, tokens), bf16),
        kv_grad=vmem((2, tokens, head_cols // 4), f32),
        head_grad=vmem((tokens, head_cols), bf16),
        norm_grad=vmem((4, local, part_wide), bf16),
        gains=vmem((8, width), f32),
        gain_own=vmem((8, width), f32),
        gain_plane=vmem((4, 8, width), f32),
        gain_mine=vmem((3, 8, width), f32),
        gain_theirs=vmem((3, 8, width), f32),
        gain_total=vmem((8, width), f32),
        made=vmem((2, PAIR, slot_width), bf16),
        both=vmem((PAIR, side), bf16),
        sib=vmem((4, LINE, slot_width), bf16),
        acc=vmem((DEEP, LINE, slot_width), bf16),
        outer_in=vmem((DEEP, LINE, slot_width), bf16),
        inner_in=vmem((DEEP, LINE, slot_width), bf16),
        total=vmem((LAST, LINE, slot_width), bf16),
        load_sem=dma((42,)),
        stage_sem=dma((2,)),
        keep_sem=dma((4,)),
        ffn_send=dma((pieces, 6)),
        ffn_recv=dma((pieces, 6)),
        c_send=dma((6,)),
        c_recv=dma((6,)),
        e_send=dma((6,)),
        e_recv=dma((6,)),
        h_send=dma((6,)),
        h_recv=dma((6,)),
        i_send=dma((3,)),
        i_recv=dma((3,)),
        gain_send=dma((6,)),
        gain_recv=dma((6,)),
        sib_send=dma((4,)),
        sib_recv=dma((4,)),
        up_send=dma((DEEP,)),
        outer_recv=dma((DEEP,)),
        inner_recv=dma((DEEP,)),
        down_send=dma((LAST,)),
        pair_send=dma((LAST, pieces)),
        pair_recv=dma((steps, pieces)),
        store_sem=dma((LAST, pieces)),
        sib_credit=credit,
        up_credit=credit,
        down_credit=credit,
    )
    any_space = pl.BlockSpec(memory_space=pl.ANY)
    small = pl.BlockSpec(memory_space=pltpu.VMEM)
    in_specs = [
        small if value.ndim == 1 or value.shape[0] == 8 else any_space for value in args.values()
    ]
    results = pl.pallas_call(
        functools.partial(
            backward_kernel,
            (tokens, local, width, inner_width, head_cols),
            tuple(args) + tuple(outs) + tuple(scratch),
        ),
        out_shape=list(outs.values()),
        in_specs=in_specs,
        out_specs=[any_space] * len(outs),
        scratch_shapes=list(scratch.values()),
        compiler_params=pltpu.CompilerParams(
            collective_id=collective_id,
            has_side_effects=True,
            vmem_limit_bytes=VMEM_LIMIT,
        ),
        cost_estimate=pl.CostEstimate(
            flops=80 * tokens * width * width, bytes_accessed=400 * 2**20, transcendentals=0
        ),
    )(*args.values())
    return types.SimpleNamespace(**dict(zip(outs, results)))


VMEM_LIMIT = 63 * 2**20


def forward_kernel(names, *refs):
    r = types.SimpleNamespace(**dict(zip(names, refs)))
    f32, bf16 = jnp.float32, jnp.bfloat16
    tokens, inner_width = r.hidden.shape
    local, width = r.tokens.shape
    half = local // 2
    me, x_place, y_place, far_place = plane_places()
    x_other, y_other = {"shard": x_place}, {"shard": y_place}

    def load(src, dst, index):
        return pltpu.make_async_copy(src, dst, r.load_sem.at[index])

    def block_rows(owner):
        return pl.ds(pl.multiple_of(owner * local, 16), local)

    def half_rows(owner, which):
        return pl.ds(pl.multiple_of(owner * local + which * half, 16), half)

    early = (load(r.mixed, r.mixed_buf, 0), load(r.w_out, r.out_buf, 1))
    small = (load(r.tokens, r.token_buf, 2), load(r.cotangent, r.cot_buf, 3))
    big = (
        load(r.w_gate, r.gate_weight, 4),
        load(r.w_up, r.up_weight, 5),
        load(r.w_down, r.down_weight, 6),
    )
    for copy in early + small + big:
        copy.start()
    for index, gain in enumerate((r.post_attn_gain, r.ffn_gain, r.post_ffn_gain, r.attn_gain)):
        r.gains[index : index + 1] = gain[...].astype(jnp.float32).reshape(1, gain.shape[0])
    greet((x_place, y_place))

    def summing(landed, send_sem, recv_sem):
        def send(src, index, where):
            return remote(src, landed.at[index], send_sem.at[index], recv_sem.at[index], where)

        far = (
            send(r.partial.at[half_rows(far_place, 0)], 0, x_other),
            send(r.partial.at[half_rows(far_place, 1)], 1, y_other),
        )
        near = (
            send(r.partial.at[half_rows(x_place, 0)], 2, x_other),
            send(r.partial.at[half_rows(y_place, 1)], 3, y_other),
        )
        on = (send(r.passed.at[0], 4, y_other), send(r.passed.at[1], 5, x_other))
        return far, near, on

    def pass_sums(landed, far, on):
        for index, owner in enumerate((y_place, x_place)):
            far[index].wait_recv()
            r.passed[index] = add_low(r.partial[half_rows(owner, index)], landed[index])
            on[index].start()

    def gathering(source, target, send_sem, recv_sem):
        def send(owner, which, index, where, src):
            return remote(
                src, target.at[half_rows(owner, which)],
                send_sem.at[index], recv_sem.at[index], where,
            )

        starts = [
            [send(me, which, 2 * which + i, where, source(which)) for i, where in enumerate((x_other, y_other))]
            for which in range(2)
        ]
        on = (
            send(x_place, 0, 4, y_other, target.at[half_rows(x_place, 0)]),
            send(y_place, 1, 5, x_other, target.at[half_rows(y_place, 1)]),
        )
        return starts, on

    a_far, a_near, a_on = summing(r.a_landed, r.a_send, r.a_recv)
    c_far, c_near, c_on = summing(r.c_landed, r.c_send, r.c_recv)
    b_starts, b_on = gathering(
        lambda which: r.two_buf.at[half_rows(me, which)], r.two_buf, r.b_send, r.b_recv
    )

    for copy in early:
        copy.wait()

    def project(owner):
        rows = block_rows(owner)
        r.partial[rows] = dot_plain(r.mixed_buf[rows], r.out_buf[...]).astype(bf16)

    project(far_place)
    for copy in a_far:
        copy.start()
    project(x_place)
    a_near[0].start()
    project(y_place)
    a_near[1].start()
    project(me)
    pass_sums(r.a_landed, a_far, a_on)
    for copy in small:
        copy.wait()

    def sum_rows(landed, which, index):
        rows = pl.ds(pl.multiple_of(me * local + which * half + index * 32, 16), 32)
        here = pl.ds(pl.multiple_of(index * 32, 16), 32)
        return (
            r.partial[rows].astype(f32)
            + landed[2 + which, here].astype(f32)
            + landed[4 + which, here].astype(f32)
        )

    def middle_rows(which, index, carry):
        rows = pl.ds(pl.multiple_of(which * half + index * 32, 16), 32)
        attn = sum_rows(r.a_landed, which, index)
        r.attn_buf[rows] = attn
        inv = lax.rsqrt(jnp.mean(attn * attn, axis=-1, keepdims=True) + norm_eps)
        middle = r.token_buf[rows].astype(f32) + attn * inv * r.gains[0:1]
        r.middle_buf[rows] = middle
        inv = lax.rsqrt(jnp.mean(middle * middle, axis=-1, keepdims=True) + norm_eps)
        r.two_buf[pl.ds(pl.multiple_of(me * local + which * half + index * 32, 16), 32)] = (
            middle * inv * r.gains[1:2]
        ).astype(bf16)
        return carry

    for which in range(2):
        a_near[which].wait_recv()
        a_on[which].wait_recv()
        lax.fori_loop(0, half // 32, functools.partial(middle_rows, which), 0)
        for copy in b_starts[which]:
            copy.start()
    keep = [
        pltpu.make_async_copy(r.attn_buf, r.attn_out, r.keep_sem.at[0]),
        pltpu.make_async_copy(r.middle_buf, r.middle, r.keep_sem.at[1]),
    ]
    for copy in keep:
        copy.start()
    for copy in a_far + a_near + a_on:
        copy.wait_send()

    def keep_block(owner):
        rows = block_rows(owner)
        return [
            pltpu.make_async_copy(buf, dst.at[rows], r.keep_sem.at[2 + i])
            for i, (buf, dst) in enumerate(
                ((r.gate_stage, r.gate), (r.up_stage, r.up), (r.hidden_buf.at[rows], r.hidden))
            )
        ]

    def feed(owner, before):
        rows = block_rows(owner)
        if before is not None:
            for copy in keep_block(before):
                copy.wait()

        def tile(index, carry):
            columns = pl.ds(pl.multiple_of(index * TILE, TILE), TILE)
            block = r.two_buf[rows]
            r.gate_wide[...] = dot_plain(block, r.gate_weight[:, columns])
            r.up_wide[...] = dot_plain(block, r.up_weight[:, columns])

            def rows_of(index, carry):
                here = pl.ds(pl.multiple_of(index * half, 16), half)
                gate, up = r.gate_wide[here], r.up_wide[here]
                r.gate_stage[here, columns] = gate.astype(bf16)
                r.up_stage[here, columns] = up.astype(bf16)
                curve = jnp.tanh(ROOT_TWO_PI * (gate + 0.044715 * (gate * gate * gate)))
                r.hidden_buf[
                    pl.ds(pl.multiple_of(owner * local + index * half, 16), half), columns
                ] = (0.5 * gate * (1.0 + curve) * up).astype(bf16)
                return carry

            lax.fori_loop(0, 2, rows_of, 0)
            return carry

        lax.fori_loop(0, inner_width // TILE, tile, 0)
        for copy in keep_block(owner):
            copy.start()

    def shrink(owner):
        rows = block_rows(owner)

        def tile(index, carry):
            columns = pl.ds(pl.multiple_of(index * TILE, TILE), TILE)
            r.partial[rows, columns] = dot_plain(
                r.hidden_buf[rows], r.down_weight[:, columns]
            ).astype(bf16)
            return carry

        lax.fori_loop(0, width // TILE, tile, 0)

    big[0].wait()
    big[1].wait()
    feed(me, None)
    big[2].wait()
    b_starts[0][0].wait_recv()
    b_on[0].start()
    b_starts[1][1].wait_recv()
    b_on[1].start()
    shrink(me)
    b_starts[1][0].wait_recv()
    feed(x_place, me)
    shrink(x_place)
    c_near[0].start()
    b_starts[0][1].wait_recv()
    feed(y_place, x_place)
    shrink(y_place)
    c_near[1].start()
    for copy in b_on:
        copy.wait_recv()
    feed(far_place, y_place)
    shrink(far_place)
    for copy in c_far:
        copy.start()
    keep_two = pltpu.make_async_copy(r.two_buf, r.normed_two, r.keep_sem.at[5])
    keep_two.start()
    r.gain_part[...] = jnp.zeros_like(r.gain_part)
    pass_sums(r.c_landed, c_far, c_on)

    def last_rows(which, index, carry):
        rows = pl.ds(pl.multiple_of(which * half + index * 32, 16), 32)
        ffn = sum_rows(r.c_landed, which, index)
        inv = lax.rsqrt(jnp.mean(ffn * ffn, axis=-1, keepdims=True) + norm_eps)
        r.token_buf[rows] = (r.middle_buf[rows] + ffn * inv * r.gains[2:3]).astype(bf16)
        grad = r.cot_buf[rows].astype(f32)
        weighted = grad * r.gains[2:3]
        mean = jnp.mean(weighted * ffn, axis=-1, keepdims=True)
        r.gain_part[0:1] += jnp.sum(grad * ffn * inv, axis=0, keepdims=True)
        r.cot_buf[rows] = (inv * weighted - ffn * (inv * inv * inv) * mean).astype(bf16)
        return carry

    for which in range(2):
        c_near[which].wait_recv()
        c_on[which].wait_recv()
        lax.fori_loop(0, half // 32, functools.partial(last_rows, which), 0)
    keep_own = pltpu.make_async_copy(r.cot_buf, r.grad_ffn, r.keep_sem.at[6])
    keep_out = pltpu.make_async_copy(r.token_buf, r.output, r.keep_sem.at[7])
    keep_own.start()
    keep_out.start()
    for copy in b_starts[0] + b_starts[1] + list(b_on + c_far + c_near + c_on):
        copy.wait_send()
    for copy in keep + keep_block(far_place) + [keep_two, keep_own, keep_out]:
        copy.wait()


def forward(collective_id, **args):
    f32, bf16 = jnp.float32, jnp.bfloat16
    given = types.SimpleNamespace(**args)
    local, width = given.tokens.shape
    tokens = 4 * local
    half = local // 2
    inner_width = given.w_down.shape[0]
    vmem, dma, shape = pltpu.VMEM, pltpu.SemaphoreType.DMA, jax.ShapeDtypeStruct
    outs = dict(
        grad_ffn=shape((local, width), bf16),
        hidden=shape((tokens, inner_width), bf16),
        gate=shape((tokens, inner_width), bf16),
        up=shape((tokens, inner_width), bf16),
        normed_two=shape((tokens, width), bf16),
        middle=shape((local, width), f32),
        attn_out=shape((local, width), f32),
        output=shape((local, width), bf16),
        gain_part=shape((8, width), f32),
    )
    scratch = dict(
        mixed_buf=vmem(given.mixed.shape, bf16),
        out_buf=vmem(given.w_out.shape, bf16),
        token_buf=vmem((local, width), bf16),
        cot_buf=vmem((local, width), bf16),
        gate_weight=vmem((width, inner_width), bf16),
        up_weight=vmem((width, inner_width), bf16),
        down_weight=vmem((inner_width, width), bf16),
        partial=vmem((tokens, width), bf16),
        passed=vmem((2, half, width), bf16),
        a_landed=vmem((6, half, width), bf16),
        c_landed=vmem((6, half, width), bf16),
        gains=vmem((8, width), f32),
        attn_buf=vmem((local, width), f32),
        middle_buf=vmem((local, width), f32),
        two_buf=vmem((tokens, width), bf16),
        hidden_buf=vmem((tokens, inner_width), bf16),
        gate_stage=vmem((local, inner_width), bf16),
        up_stage=vmem((local, inner_width), bf16),
        gate_wide=vmem((local, TILE), f32),
        up_wide=vmem((local, TILE), f32),
        load_sem=dma((7,)),
        keep_sem=dma((8,)),
        a_send=dma((6,)),
        a_recv=dma((6,)),
        b_send=dma((6,)),
        b_recv=dma((6,)),
        c_send=dma((6,)),
        c_recv=dma((6,)),
    )
    any_space = pl.BlockSpec(memory_space=pl.ANY)
    small = pl.BlockSpec(memory_space=pltpu.VMEM)
    results = pl.pallas_call(
        functools.partial(forward_kernel, tuple(args) + tuple(outs) + tuple(scratch)),
        out_shape=list(outs.values()),
        in_specs=[
            small if value.ndim == 1 else any_space
            for value in args.values()
        ],
        out_specs=[small if value.shape[0] <= 8 else any_space for value in outs.values()],
        scratch_shapes=list(scratch.values()),
        compiler_params=pltpu.CompilerParams(
            collective_id=collective_id, has_side_effects=True, vmem_limit_bytes=VMEM_LIMIT
        ),
        cost_estimate=pl.CostEstimate(
            flops=8 * tokens * width * inner_width, bytes_accessed=100 * 2**20, transcendentals=0
        ),
    )(*args.values())
    return types.SimpleNamespace(**dict(zip(outs, results)))


def attend_kernel(names, *refs):
    r = types.SimpleNamespace(**dict(zip(names, refs)))
    f32, bf16 = jnp.float32, jnp.bfloat16
    local, width = r.tokens.shape
    tokens, head_cols = r.qkv.shape
    part = r.w_query.shape[0]
    piece = part // 4
    half = local // 2
    weights = (r.w_query, r.w_key, r.w_value)
    sizes = [weight.shape[1] // 4 for weight in weights]
    starts = (0, sizes[0], sizes[0] + sizes[1])
    q_cols, k_cols = sizes[0], sizes[1]
    heads = q_cols // HEAD_SIZE
    block = min(TILE, tokens)
    n_blocks = tokens // block
    head_scale = HEAD_SIZE ** (-0.5)

    me, x_place, y_place, far_place = plane_places()
    others = (x_place, y_place, far_place)
    x_other, y_other = {"shard": x_place}, {"shard": y_place}
    place = lax.axis_index("rep")
    chip, core = place // 2, place % 2
    twin = {"rep": place + 1 - 2 * core}
    next_chip = {"rep": place + 2 - 4 * (chip % 2)}
    quarter = (chip % 2) * 2 + core
    next_quarter = (1 - chip % 2) * 2 + core

    load_tokens = pltpu.make_async_copy(r.tokens, r.token_buf, r.load_sem.at[0])
    load_heads = [
        pltpu.make_async_copy(
            weights[kind].at[:, pl.ds(pl.multiple_of(me * sizes[kind], 128), sizes[kind])],
            r.heads_buf.at[
                pl.ds(pl.multiple_of(me * part, 16), part), pl.ds(starts[kind], sizes[kind])
            ],
            r.load_sem.at[2 + kind],
        )
        for kind in range(3)
    ]
    load_tokens.start()
    for copy in load_heads:
        copy.start()

    def lookup(ident):
        found = jnp.full_like(ident, -1)
        for label in range(SEGS):
            found = jnp.where(ident == label, r.parents[0, label], found)
        return found

    ident = r.seg_ids[...]
    parent_one = lookup(ident)
    lanes = lax.broadcasted_iota(jnp.int32, ident.shape, 1)
    codes = jnp.where(ident < SEGS, ident, jnp.where(lanes == 3, -2, -1))
    codes = jnp.where(lanes == 1, parent_one, jnp.where(lanes == 2, lookup(parent_one), codes))
    info_rows = pl.ds(pl.multiple_of(me * local, 16), local)
    r.info_buf[info_rows] = codes.astype(f32).astype(bf16)
    r.gain[...] = r.attn_gain[...].astype(f32).reshape(1, width)

    barrier = pltpu.get_barrier_semaphore()
    for where in [{"shard": other} for other in others] + [twin, next_chip]:
        pl.semaphore_signal(barrier, inc=1, device_id=where, device_id_type=pl.DeviceIdType.MESH)
    pl.semaphore_wait(barrier, 5)

    def piece_rows(owner, which):
        return pl.ds(pl.multiple_of(owner * part + which * piece, 16), piece)

    fetch = [
        [
            remote(
                weights[kind].at[
                    pl.ds(pl.multiple_of(quarter * piece, 16), piece),
                    pl.ds(pl.multiple_of(other * sizes[kind], 128), sizes[kind]),
                ],
                r.heads_buf.at[piece_rows(me, quarter), pl.ds(starts[kind], sizes[kind])],
                r.fetch_send.at[i, kind], r.fetch_recv.at[i, kind], {"shard": other},
            )
            for kind in range(3)
        ]
        for i, other in enumerate(others)
    ]
    for i in (2, 0, 1):
        for copy in fetch[i]:
            copy.start()
    tell_info = [
        remote(
            r.info_buf.at[info_rows], r.info_buf.at[info_rows],
            r.info_send.at[i], r.info_recv.at[i], {"shard": other},
        )
        for i, other in enumerate(others)
    ]
    for copy in tell_info:
        copy.start()

    def pass_piece(i, which, where, index):
        ref = r.heads_buf.at[piece_rows(others[i], which)]
        return remote(ref, ref, r.pass_send.at[index, i], r.pass_recv.at[index, i], where)

    to_chip = [pass_piece(i, quarter, next_chip, 0) for i in range(3)]
    to_twin = [pass_piece(i, quarter, twin, 1) for i in range(3)]
    on_twin = [pass_piece(i, next_quarter, twin, 2) for i in range(3)]

    def half_rows(owner, which):
        return r.all_buf.at[pl.ds(pl.multiple_of(owner * local + which * half, 16), half)]

    def send(owner, which, index, where):
        ref = half_rows(owner, which)
        return remote(ref, ref, r.all_send.at[index], r.all_recv.at[index], where)

    own = [
        [send(me, which, 2 * which + i, where) for i, where in enumerate((x_other, y_other))]
        for which in range(2)
    ]
    on = (send(x_place, 0, 4, y_other), send(y_place, 1, 5, x_other))

    load_tokens.wait()

    def norm_rows(which, index, carry):
        rows = pl.ds(pl.multiple_of(which * half + index * 32, 16), 32)
        values = r.token_buf[rows].astype(f32)
        inv = lax.rsqrt(jnp.mean(values * values, axis=-1, keepdims=True) + norm_eps)
        r.all_buf[pl.ds(pl.multiple_of(me * local + which * half + index * 32, 16), 32)] = (
            values * inv * r.gain[...]
        ).astype(bf16)
        return carry

    for which in range(2):
        lax.fori_loop(0, half // 32, functools.partial(norm_rows, which), 0)
        for copy in own[which]:
            copy.start()

    for i in (2, 0, 1):
        for copy in fetch[i]:
            copy.wait_recv()
        to_chip[i].start()
        to_twin[i].start()
    own[0][0].wait_recv()
    on[0].start()
    own[1][1].wait_recv()
    on[1].start()
    for i in (2, 0, 1):
        to_chip[i].wait_recv()
        on_twin[i].start()

    for copy in tell_info:
        copy.wait_recv()
    r.key_info[...] = jnp.transpose(r.info_buf[...].astype(f32))[0:8]
    for copy in load_heads:
        copy.wait()
    for copy in to_twin + on_twin:
        copy.wait_recv()

    def project(owner):
        rows = pl.ds(pl.multiple_of(owner * local, 16), local)
        r.qkv_buf[rows] = dot_plain(r.all_buf[rows], r.heads_buf[...]).astype(bf16)

    project(me)
    own[1][0].wait_recv()
    project(x_place)
    own[0][1].wait_recv()
    project(y_place)
    for copy in on:
        copy.wait_recv()
    project(far_place)
    keep = [pltpu.make_async_copy(r.qkv_buf, r.qkv, r.keep_sem.at[0])]
    keep[0].start()

    def keep_item(item):
        head, rows = item // n_blocks, pl.ds((item % n_blocks) * block, block)
        slot = item % 2
        return [
            pltpu.make_async_copy(r.probs_stage.at[slot], r.probs.at[head, rows], r.stage_sem.at[slot, 0]),
            pltpu.make_async_copy(r.tanh_stage.at[slot], r.tanh.at[head, rows], r.stage_sem.at[slot, 1]),
        ]

    for item in range(heads * n_blocks):
        head, first, slot = item // n_blocks, (item % n_blocks) * block, item % 2
        limit = first + block
        columns = pl.ds(head * HEAD_SIZE, HEAD_SIZE)
        r.score[:, pl.ds(0, limit)] = dot_rows(
            r.qkv_buf[pl.ds(first, block), columns], r.qkv_buf[pl.ds(0, limit), pl.ds(q_cols, k_cols)]
        )
        if item >= 2:
            for copy in keep_item(item - 2):
                copy.wait()
        if limit < tokens:
            nothing = jnp.zeros((block, tokens - limit), f32)
            r.probs_stage[slot, :, pl.ds(limit, tokens - limit)] = nothing
            r.tanh_stage[slot, :, pl.ds(limit, tokens - limit)] = nothing

        def rows_of(index, carry, first=first, limit=limit, slot=slot):
            here = pl.ds(pl.multiple_of(index * 64, 64), 64)
            info = r.info_buf[pl.ds(pl.multiple_of(first + index * 64, 64), 64)].astype(f32)
            keys = r.key_info[3:4, pl.ds(0, limit)]
            query_at = lax.broadcasted_iota(jnp.int32, (64, limit), 0) + (first + index * 64)
            key_at = lax.broadcasted_iota(jnp.int32, (64, limit), 1)
            related = (keys == info[:, 0:1]) | (keys == info[:, 1:2]) | (keys == info[:, 2:3])
            visible = ((key_at <= query_at) & related) | (key_at == query_at)
            curve = jnp.tanh(r.score[here, pl.ds(0, limit)] * (head_scale / softcap))
            masked = jnp.where(visible, softcap * curve, -1e30)
            terms = jnp.exp(masked - jnp.max(masked, axis=-1, keepdims=True))
            probs = terms / jnp.sum(terms, axis=-1, keepdims=True)
            r.tanh_stage[slot, here, pl.ds(0, limit)] = curve
            r.probs_stage[slot, here, pl.ds(0, limit)] = probs
            r.probs_low[here, pl.ds(0, limit)] = probs.astype(bf16)
            return carry

        lax.fori_loop(0, block // 64, rows_of, 0)
        for copy in keep_item(item):
            copy.start()
        r.mixed_buf[pl.ds(first, block), columns] = dot_plain(
            r.probs_low[:, pl.ds(0, limit)],
            r.qkv_buf[pl.ds(0, limit), pl.ds(q_cols + k_cols, k_cols)],
        ).astype(bf16)

    keep.append(pltpu.make_async_copy(r.mixed_buf, r.mixed, r.keep_sem.at[1]))
    keep[1].start()

    wide = r.cols_buf.shape[1]
    for owner in range(4):

        @pl.when(me == owner)
        def _():
            def rows_of(index, carry):
                rows = pl.ds(pl.multiple_of(index * 64, 64), 64)
                some = r.all_buf[rows, owner * part : (owner + 1) * part]
                if wide > part:
                    some = jnp.concatenate((some, jnp.zeros((64, wide - part), bf16)), axis=1)
                r.cols_buf[rows] = some
                return carry

            lax.fori_loop(0, tokens // 64, rows_of, 0)

    keep.append(pltpu.make_async_copy(r.cols_buf, r.normed_cols, r.keep_sem.at[2]))
    keep[2].start()
    for group in fetch + own:
        for copy in group:
            copy.wait_send()
    for copy in list(on) + tell_info + to_chip + to_twin + on_twin:
        copy.wait_send()
    last = heads * n_blocks
    for item in range(max(0, last - 2), last):
        for copy in keep_item(item):
            copy.wait()
    for copy in keep:
        copy.wait()


def attend(collective_id, **args):
    f32, bf16 = jnp.float32, jnp.bfloat16
    given = types.SimpleNamespace(**args)
    local, width = given.tokens.shape
    tokens = 4 * local
    part = given.w_query.shape[0]
    part_wide = -(-part // PAIR) * PAIR
    q_cols, k_cols = given.w_query.shape[1] // 4, given.w_key.shape[1] // 4
    head_cols = q_cols + 2 * k_cols
    heads = q_cols // HEAD_SIZE
    block = min(TILE, tokens)
    vmem, dma, shape = pltpu.VMEM, pltpu.SemaphoreType.DMA, jax.ShapeDtypeStruct
    outs = dict(
        qkv=shape((tokens, head_cols), bf16),
        mixed=shape((tokens, q_cols), bf16),
        probs=shape((heads, tokens, tokens), f32),
        tanh=shape((heads, tokens, tokens), f32),
        normed_cols=shape((tokens, part_wide), bf16),
    )
    scratch = dict(
        token_buf=vmem((local, width), bf16),
        all_buf=vmem((tokens, width), bf16),
        heads_buf=vmem((width, head_cols), bf16),
        info_buf=vmem((tokens, 128), bf16),
        key_info=vmem((8, tokens), f32),
        gain=vmem((1, width), f32),
        qkv_buf=vmem((tokens, head_cols), bf16),
        mixed_buf=vmem((tokens, q_cols), bf16),
        cols_buf=vmem((tokens, part_wide), bf16),
        score=vmem((block, tokens), f32),
        probs_stage=vmem((2, block, tokens), f32),
        tanh_stage=vmem((2, block, tokens), f32),
        probs_low=vmem((block, tokens), bf16),
        load_sem=dma((5,)),
        keep_sem=dma((3,)),
        stage_sem=dma((2, 2)),
        fetch_send=dma((3, 3)),
        fetch_recv=dma((3, 3)),
        info_send=dma((3,)),
        info_recv=dma((3,)),
        pass_send=dma((3, 3)),
        pass_recv=dma((3, 3)),
        all_send=dma((6,)),
        all_recv=dma((6,)),
    )
    any_space = pl.BlockSpec(memory_space=pl.ANY)
    small = pl.BlockSpec(memory_space=pltpu.VMEM)
    results = pl.pallas_call(
        functools.partial(attend_kernel, tuple(args) + tuple(outs) + tuple(scratch)),
        out_shape=list(outs.values()),
        in_specs=[
            pl.BlockSpec(memory_space=pltpu.SMEM) if value.shape[0] == 1
            else small if value.ndim == 1 or value.shape[1] == 128 else any_space
            for value in args.values()
        ],
        out_specs=[any_space] * len(outs),
        scratch_shapes=list(scratch.values()),
        compiler_params=pltpu.CompilerParams(
            collective_id=collective_id, has_side_effects=True, vmem_limit_bytes=VMEM_LIMIT
        ),
        cost_estimate=pl.CostEstimate(
            flops=4 * tokens * width * head_cols, bytes_accessed=100 * 2**20, transcendentals=0
        ),
    )(*args.values())
    return types.SimpleNamespace(**dict(zip(outs, results)))


QUERY_HEADS = 8
KV = 4
HEAD_SIZE = 256
SEGS = 13


softcap = 50.0
norm_eps = 1e-06


def normalize(values, gain_vec):
    inv_rms = lax.rsqrt(jnp.mean(values * values, axis=-1, keepdims=True) + norm_eps)
    return (values * inv_rms * gain_vec, inv_rms)


def norm_back(values, inv_rms, gain_vec, grad_in):
    weighted = grad_in * gain_vec
    row_mean = jnp.mean(weighted * values, axis=-1, keepdims=True)
    grad_back = inv_rms * weighted - values * (inv_rms * inv_rms * inv_rms) * row_mean
    return (grad_back, jnp.sum(grad_in * values * inv_rms, axis=0))


def geglu(gate_pre, up_pre):
    return jax.nn.gelu(gate_pre, approximate=True) * up_pre


def gather_rows(block):
    return lax.all_gather(block, "shard", axis=0, tiled=True)


def scatter_rows(partial):
    summed = lax.psum_scatter(partial, "shard", scatter_dimension=0, tiled=True)
    return summed.astype(jnp.float32)


def exchange(blocks):
    return lax.all_to_all(blocks, "shard", 0, 0, tiled=True)


def first_gather(normed, seg_ids, w_query, w_key, w_value):
    n = lax.axis_size("shard")
    width = normed.shape[1]
    part_rows = w_query.shape[0]
    share = max(1, n // KV)

    def by_device(weight):
        heads = weight.reshape(part_rows, KV, -1)
        if share > 1:
            heads = jnp.repeat(heads, share, axis=1)
        return heads.reshape(part_rows, n, -1)

    parts = jnp.concatenate(
        (w_query.reshape(part_rows, n, -1), by_device(w_key), by_device(w_value)), axis=2
    ).transpose(1, 0, 2)
    heads = exchange(parts).reshape(width, -1)
    codes = gather_rows(seg_ids.astype(jnp.bfloat16))
    return gather_rows(normed), codes.astype(jnp.int32), heads


def rep_sum(grads, width):
    summed = chain_sum([grad.astype(jnp.bfloat16).reshape(-1, width) for grad in grads])
    return [
        total.reshape(grad.shape).astype(jnp.float32) for total, grad in zip(summed, grads)
    ]


def plane_layer(
    tokens, seg_ids, parents, attn_gain, w_query, w_key, w_value, w_out, post_attn_gain,
    ffn_gain, w_gate, w_up, w_down, post_ffn_gain, cotangent,
):
    f32 = jnp.float32
    heads = attend(
        2,
        tokens=tokens,
        attn_gain=attn_gain,
        seg_ids=jnp.broadcast_to(seg_ids[:, None], (tokens.shape[0], 128)),
        parents=parents,
        w_query=w_query,
        w_key=w_key,
        w_value=w_value,
    )
    gains = dict(
        attn_gain=attn_gain,
        post_attn_gain=post_attn_gain,
        ffn_gain=ffn_gain,
        post_ffn_gain=post_ffn_gain,
    )
    ahead = forward(
        3,
        mixed=heads.mixed,
        w_out=w_out,
        tokens=tokens,
        cotangent=cotangent,
        **gains,
        w_gate=w_gate,
        w_up=w_up,
        w_down=w_down,
    )
    found = backward(
        4,
        grad_ffn=ahead.grad_ffn,
        hidden=ahead.hidden,
        gate=ahead.gate,
        up=ahead.up,
        normed_two=ahead.normed_two,
        w_down=w_down,
        w_gate=w_gate,
        w_up=w_up,
        w_out=w_out,
        middle=ahead.middle,
        attn_out=ahead.attn_out,
        cotangent=cotangent,
        **gains,
        gain_parts=ahead.gain_part,
        qkv=heads.qkv,
        mixed=heads.mixed,
        probs=heads.probs,
        tanh=heads.tanh,
        normed_cols=heads.normed_cols,
        w_query=w_query,
        w_key=w_key,
        w_value=w_value,
        tokens=tokens,
    )
    gain_sums = found.gain_sums
    return (
        ahead.output,
        found.grad_tokens,
        gain_sums[3],
        found.query_sum.astype(f32),
        found.key_sum.astype(f32),
        found.value_sum.astype(f32),
        found.out_sum.astype(f32),
        gain_sums[1],
        gain_sums[2],
        found.gate_sum.astype(f32),
        found.up_sum.astype(f32),
        found.down_sum.astype(f32),
        gain_sums[0],
    )


def body(
    tokens,
    seg_ids,
    parents,
    attn_gain,
    w_query,
    w_key,
    w_value,
    w_out,
    post_attn_gain,
    ffn_gain,
    w_gate,
    w_up,
    w_down,
    post_ffn_gain,
    cotangent,
):
    if lax.axis_size("shard") == 4 and lax.axis_size("rep") == 8:
        return plane_layer(
            tokens, seg_ids, parents, attn_gain, w_query, w_key, w_value, w_out, post_attn_gain,
            ffn_gain, w_gate, w_up, w_down, post_ffn_gain, cotangent,
        )
    f32, bf16 = jnp.float32, jnp.bfloat16
    tok_rows, width = tokens.shape
    n = lax.axis_size("shard")
    me = lax.axis_index("shard")
    group_rows = tok_rows * n
    part_rows = w_query.shape[0]
    head_scale = HEAD_SIZE ** (-0.5)
    q_heads = QUERY_HEADS // n
    kv_heads = max(1, KV // n)
    share = n * kv_heads // KV
    repeat = q_heads // kv_heads
    q_cols = q_heads * HEAD_SIZE
    k_cols = kv_heads * HEAD_SIZE
    gain_one = attn_gain.astype(f32)
    gain_two = post_attn_gain.astype(f32)
    gain_three = ffn_gain.astype(f32)
    gain_four = post_ffn_gain.astype(f32)

    residual = tokens.astype(f32)
    normed, rms_one = normalize(residual, gain_one)
    normed_all, codes, qkv_heads = first_gather(
        normed.astype(bf16), seg_ids, w_query, w_key, w_value
    )
    qkv = jnp.dot(normed_all, qkv_heads, preferred_element_type=f32).astype(bf16)
    queries = qkv[:, :q_cols].reshape(group_rows, kv_heads, repeat, HEAD_SIZE)
    keys = qkv[:, q_cols : q_cols + k_cols].reshape(group_rows, kv_heads, HEAD_SIZE)
    values = qkv[:, q_cols + k_cols :].reshape(group_rows, kv_heads, HEAD_SIZE)

    parent_row = parents[0]
    labels = jnp.arange(SEGS)

    def lookup(ident):
        return jnp.sum(jnp.where(ident[:, None] == labels[None, :], parent_row[None, :], 0), axis=1)

    parent_one = lookup(codes)
    parent_two = lookup(parent_one)
    positions = jnp.arange(group_rows)
    real = codes < SEGS
    related = (
        (codes[None, :] == codes[:, None])
        | (codes[None, :] == parent_one[:, None])
        | (codes[None, :] == parent_two[:, None])
    )
    visible = (positions[None, :] <= positions[:, None]) & real[:, None] & real[
        None, :
    ] & related | (positions[None, :] == positions[:, None])

    score_matrix = jnp.einsum("tkrh,skh->krts", queries, keys, preferred_element_type=f32)
    tanh_part = jnp.tanh(score_matrix * (head_scale / softcap))
    masked = jnp.where(visible[None, None], softcap * tanh_part, -1e30)
    row_max = jnp.max(masked, axis=-1, keepdims=True)
    expo_terms = jnp.exp(masked - row_max)
    row_total = jnp.sum(expo_terms, axis=-1, keepdims=True)
    probs = expo_terms / row_total
    probs_b = probs.astype(bf16)
    mixed = jnp.einsum("krts,skh->tkrh", probs_b, values, preferred_element_type=f32)
    mixed = mixed.reshape(group_rows, q_cols).astype(bf16)
    attn_out = scatter_rows(jnp.dot(mixed, w_out, preferred_element_type=f32).astype(bf16))
    post_one, rms_two = normalize(attn_out, gain_two)
    middle = residual + post_one
    normed_two, rms_three = normalize(middle, gain_three)
    normed_two_all = gather_rows(normed_two.astype(bf16))
    gate_pre = jnp.dot(normed_two_all, w_gate, preferred_element_type=f32)
    up_pre = jnp.dot(normed_two_all, w_up, preferred_element_type=f32)
    hidden, geglu_back = jax.vjp(geglu, gate_pre, up_pre)
    hidden_b = hidden.astype(bf16)
    ffn_out = scatter_rows(jnp.dot(hidden_b, w_down, preferred_element_type=f32).astype(bf16))
    post_two, rms_four = normalize(ffn_out, gain_four)
    output = (middle + post_two).astype(bf16)

    grad_out = cotangent.astype(f32)
    grad_ffn, grad_gain_four = norm_back(ffn_out, rms_four, gain_four, grad_out)
    grad_ffn_all = gather_rows(grad_ffn.astype(bf16))
    down_part = jnp.einsum("tf,td->fd", hidden_b, grad_ffn_all, preferred_element_type=f32)
    grad_hidden = jnp.einsum("td,fd->tf", grad_ffn_all, w_down, preferred_element_type=f32)
    grad_gate, grad_up = geglu_back(grad_hidden)
    grad_gate_b = grad_gate.astype(bf16)
    grad_up_b = grad_up.astype(bf16)
    grad_normed_two = jnp.einsum("tf,df->td", grad_gate_b, w_gate, preferred_element_type=f32)
    grad_normed_two += jnp.einsum("tf,df->td", grad_up_b, w_up, preferred_element_type=f32)
    grad_normed_two = scatter_rows(grad_normed_two.astype(bf16))
    gate_part = jnp.einsum("td,tf->df", normed_two_all, grad_gate_b, preferred_element_type=f32)
    up_part = jnp.einsum("td,tf->df", normed_two_all, grad_up_b, preferred_element_type=f32)
    grad_middle_part, grad_gain_three = norm_back(middle, rms_three, gain_three, grad_normed_two)
    grad_middle = grad_out + grad_middle_part
    grad_attn, grad_gain_two = norm_back(attn_out, rms_two, gain_two, grad_middle)
    grad_attn_all = gather_rows(grad_attn.astype(bf16))
    out_part = jnp.einsum("tj,td->jd", mixed, grad_attn_all, preferred_element_type=f32)
    grad_mixed = jnp.einsum("td,jd->tj", grad_attn_all, w_out, preferred_element_type=f32)
    grad_mixed = grad_mixed.astype(bf16).reshape(group_rows, kv_heads, repeat, HEAD_SIZE)
    grad_probs = jnp.einsum("tkrh,skh->krts", grad_mixed, values, preferred_element_type=f32)
    row_inner = jnp.sum(probs * grad_probs, axis=-1, keepdims=True)
    grad_dots = (
        probs * (grad_probs - row_inner) * (1.0 - tanh_part * tanh_part) * head_scale
    ).astype(bf16)
    grad_queries = jnp.einsum("krts,skh->tkrh", grad_dots, keys, preferred_element_type=f32)
    grad_keys = jnp.einsum("krts,tkrh->skh", grad_dots, queries, preferred_element_type=f32)
    grad_values = jnp.einsum("krts,tkrh->skh", probs_b, grad_mixed, preferred_element_type=f32)
    grad_parts = jnp.concatenate(
        (
            grad_queries.reshape(group_rows, q_cols),
            grad_keys.reshape(group_rows, k_cols),
            grad_values.reshape(group_rows, k_cols),
        ),
        axis=1,
    ).astype(bf16)
    grad_parts = gather_rows(grad_parts).reshape(n, group_rows, -1)

    def whole_heads(parts):
        if share > 1:
            parts = parts.reshape(KV, share, group_rows, HEAD_SIZE).astype(f32).sum(axis=1).astype(bf16)
        return parts.transpose(1, 0, 2).reshape(group_rows, -1)

    grad_qkv = jnp.concatenate(
        (
            grad_parts[:, :, :q_cols].transpose(1, 0, 2).reshape(group_rows, -1),
            whole_heads(grad_parts[:, :, q_cols : q_cols + k_cols]),
            whole_heads(grad_parts[:, :, q_cols + k_cols :]),
        ),
        axis=1,
    )
    qkv_local = jnp.concatenate((w_query, w_key, w_value), axis=1)
    grad_normed = jnp.einsum("tj,dj->td", grad_qkv, qkv_local, preferred_element_type=f32)
    grad_normed = exchange(grad_normed.astype(bf16).reshape(n, tok_rows, part_rows))
    grad_normed = grad_normed.transpose(1, 0, 2).reshape(tok_rows, width).astype(f32)
    normed_cols = lax.dynamic_slice_in_dim(normed_all, me * part_rows, part_rows, axis=1)
    qkv_part = jnp.einsum("td,tj->dj", normed_cols, grad_qkv, preferred_element_type=f32)
    grad_resid_part, grad_gain_one = norm_back(residual, rms_one, gain_one, grad_normed)
    grad_tokens = (grad_middle + grad_resid_part).astype(bf16)
    gain_parts = jnp.stack((grad_gain_one, grad_gain_two, grad_gain_three, grad_gain_four))
    gain_sums = lax.all_gather(gain_parts, ("rep", "shard"), axis=0).sum(axis=0)
    down_sum, gate_sum, up_sum, out_sum, qkv_sum = rep_sum(
        (down_part, gate_part, up_part, out_part, qkv_part), width
    )
    q_width = w_query.shape[1]
    k_width = w_key.shape[1]
    return (
        output,
        grad_tokens,
        gain_sums[0],
        qkv_sum[:, :q_width],
        qkv_sum[:, q_width : q_width + k_width],
        qkv_sum[:, q_width + k_width :],
        out_sum,
        gain_sums[1],
        gain_sums[2],
        gate_sum,
        up_sum,
        down_sum,
        gain_sums[3],
    )


def solution(mesh):
    return jax.shard_map(
        body,
        mesh=mesh,
        in_specs=(
            P(("rep", "shard"), None),
            P(("rep", "shard")),
            P("rep", None),
            P(),
            P("shard", None),
            P("shard", None),
            P("shard", None),
            P("shard", None),
            P(),
            P(),
            P(None, "shard"),
            P(None, "shard"),
            P("shard", None),
            P(),
            P(("rep", "shard"), None),
        ),
        out_specs=(
            P(("rep", "shard"), None),
            P(("rep", "shard"), None),
            P(),
            P("shard", None),
            P("shard", None),
            P("shard", None),
            P("shard", None),
            P(),
            P(),
            P(None, "shard"),
            P(None, "shard"),
            P("shard", None),
            P(),
        ),
        check_vma=False,
    )
```

```python
import functools
import math
import types

import jax
import jax.numpy as jnp
from jax import lax
from jax.experimental import pallas as pl
from jax.experimental.pallas import tpu as pltpu
from jax.sharding import PartitionSpec as P

SLOTS = 8
CHUNK = 64


def remote(src, dst, send_sem, recv_sem, where):
    return pltpu.make_async_remote_copy(
        src_ref=src,
        dst_ref=dst,
        send_sem=send_sem,
        recv_sem=recv_sem,
        device_id=where,
        device_id_type=pl.DeviceIdType.MESH,
    )


def add_low(left, right):
    return (left.astype(jnp.float32) + right.astype(jnp.float32)).astype(jnp.bfloat16)


def chain_kernel(counts, chunk, *refs):
    jobs = len(counts)
    ins, outs = refs[:jobs], refs[jobs : 2 * jobs]
    (
        mine, sib, acc, outer_in, inner_in, total,
        load_sem, sib_send, sib_recv, up_send, outer_recv, inner_recv,
        down_send, pair_send, pair_recv, store_sem,
        sib_credit, up_credit, down_credit,
    ) = refs[2 * jobs :]
    slots = mine.shape[0]
    steps = sum(counts)
    place = lax.axis_index("rep")
    chips = lax.axis_size("rep") // 2
    chip, core = place // 2, place % 2
    left = chip < chips // 2
    is_end = (chip == 0) | (chip == chips - 1)
    is_mid = (chip == chips // 2 - 1) | (chip == chips // 2)
    twin = {"rep": place + 1 - 2 * core}
    inner = {"rep": jnp.where(left, place + 2, place - 2)}
    outer = {"rep": jnp.where(is_end, place, jnp.where(left, place - 2, place + 2))}

    def tell(sem, where):
        pl.semaphore_signal(sem, inc=1, device_id=where, device_id_type=pl.DeviceIdType.MESH)

    barrier = pltpu.get_barrier_semaphore()
    tell(barrier, twin)
    tell(barrier, inner)

    @pl.when(is_end)
    def _():
        pl.semaphore_wait(barrier, 2)

    @pl.when(jnp.logical_not(is_end))
    def _():
        tell(barrier, outer)
        pl.semaphore_wait(barrier, 3)

    def with_rows(step, which, use):
        low = 0
        for job, count in enumerate(counts):
            first = low

            @pl.when((step >= low) & (step < low + count))
            def _():
                row = pl.multiple_of(((step - first) * 2 + which) * chunk, chunk)
                use(job, pl.ds(row, chunk))

            low += count

    def pair_copy(job, rows, slot, step):
        return remote(total.at[slot], outs[job].at[rows], pair_send.at[slot], pair_recv.at[step], twin)

    def up_copy(slot, dst, sem):
        return remote(acc.at[slot], dst.at[slot], up_send.at[slot], sem.at[slot], inner)

    def down_copy(slot):
        return remote(total.at[slot], inner_in.at[slot], down_send.at[slot], inner_recv.at[slot], outer)

    def sib_copy(job, rows, slot):
        return remote(ins[job].at[rows], sib.at[slot], sib_send.at[slot], sib_recv.at[slot], twin)

    def load_copy(job, rows, slot):
        return pltpu.make_async_copy(ins[job].at[rows], mine.at[slot], load_sem.at[slot])

    def store_copy(job, rows, slot):
        return pltpu.make_async_copy(total.at[slot], outs[job].at[rows], store_sem.at[slot])

    some = pl.ds(0, chunk)

    def take(step):
        slot = step % slots

        @pl.when(step >= slots)
        def _():
            pl.semaphore_wait(sib_credit, 1)

        with_rows(step, 1 - core, lambda job, rows: sib_copy(job, rows, slot).start())
        with_rows(step, core, lambda job, rows: load_copy(job, rows, slot).start())

    def send_up(step):
        slot = step % slots

        @pl.when(step >= slots)
        def _():
            pl.semaphore_wait(up_credit, 1)

        @pl.when(is_mid)
        def _():
            up_copy(slot, inner_in, inner_recv).start()

        @pl.when(jnp.logical_not(is_mid))
        def _():
            up_copy(slot, outer_in, outer_recv).start()

    def pair_up(step):
        slot = step % slots
        load_copy(0, some, slot).wait()
        sib_copy(0, some, slot).wait()

        @pl.when(step >= slots)
        def _():
            up_copy(slot, outer_in, outer_recv).wait_send()

        acc[slot] = add_low(mine[slot], sib[slot])

        @pl.when(step + slots < steps)
        def _():
            tell(sib_credit, twin)

        @pl.when(is_end)
        def _():
            send_up(step)

    def from_outer(step):
        slot = step % slots
        up_copy(slot, outer_in, outer_recv).wait_recv()
        acc[slot] = add_low(acc[slot], outer_in[slot])

        @pl.when(step + slots < steps)
        def _():
            tell(up_credit, outer)

        send_up(step)

    def sends_done(slot):
        pair_copy(0, some, slot, 0).wait_send()
        store_copy(0, some, slot).wait()

        @pl.when(jnp.logical_not(is_end))
        def _():
            down_copy(slot).wait_send()

    def from_inner(step):
        slot = step % slots
        down_copy(slot).wait_recv()

        @pl.when(step >= slots)
        def _():
            sends_done(slot)

        @pl.when(is_mid)
        def _():
            total[slot] = add_low(acc[slot], inner_in[slot])

            @pl.when(step + slots < steps)
            def _():
                tell(up_credit, inner)

        @pl.when(jnp.logical_not(is_mid))
        def _():
            total[slot] = inner_in[slot]

            @pl.when(step + slots < steps)
            def _():
                tell(down_credit, inner)

        @pl.when(jnp.logical_not(is_end))
        def _():
            @pl.when(step >= slots)
            def _():
                pl.semaphore_wait(down_credit, 1)

            down_copy(slot).start()

        with_rows(step, core, lambda job, rows: pair_copy(job, rows, slot, step).start())
        with_rows(step, core, lambda job, rows: store_copy(job, rows, slot).start())

    lag_outer = 3
    lag_inner = jnp.where(is_end, 8, 6)

    def tick(step, carry):
        @pl.when(step < steps)
        def _():
            take(step)

        @pl.when((step >= 1) & (step - 1 < steps))
        def _():
            pair_up(step - 1)

        @pl.when(jnp.logical_not(is_end) & (step >= lag_outer) & (step - lag_outer < steps))
        def _():
            from_outer(step - lag_outer)

        @pl.when((step >= lag_inner) & (step - lag_inner < steps))
        def _():
            from_inner(step - lag_inner)

        return carry

    lax.fori_loop(0, steps + 8, tick, 0)

    def finish(step, carry):
        slot = step % slots
        sends_done(slot)
        up_copy(slot, outer_in, outer_recv).wait_send()
        return carry

    lax.fori_loop(steps - slots, steps, finish, 0)

    def arrived(step, carry):
        pair_copy(0, some, 0, step).wait_recv()
        return carry

    lax.fori_loop(0, steps, arrived, 0)


def chain_sum(parts, chunk=CHUNK, collective_id=1):
    width = parts[0].shape[1]
    counts = tuple(part.shape[0] // (2 * chunk) for part in parts)
    steps = sum(counts)
    slots = min(SLOTS, steps)
    any_space = pl.BlockSpec(memory_space=pl.ANY)
    block = pltpu.VMEM((slots, chunk, width), jnp.bfloat16)
    sems = pltpu.SemaphoreType.DMA((slots,))
    credit = pltpu.SemaphoreType.REGULAR
    return pl.pallas_call(
        functools.partial(chain_kernel, counts, chunk),
        out_shape=[jax.ShapeDtypeStruct(part.shape, part.dtype) for part in parts],
        in_specs=[any_space] * len(parts),
        out_specs=[any_space] * len(parts),
        scratch_shapes=[block] * 6
        + [sems] * 8
        + [pltpu.SemaphoreType.DMA((steps,)), sems, credit, credit, credit],
        compiler_params=pltpu.CompilerParams(
            collective_id=collective_id, has_side_effects=True, vmem_limit_bytes=48 * 1024 * 1024
        ),
        cost_estimate=pl.CostEstimate(
            flops=0, bytes_accessed=8 * sum(part.size for part in parts), transcendentals=0
        ),
    )(*parts)


def plane_places():
    me = lax.axis_index("shard")
    x_other = me + 1 - 2 * (me % 2)
    y_other = (me + 2) % 4
    far = x_other + y_other - me
    return me, x_other, y_other, far


def greet(places):
    barrier = pltpu.get_barrier_semaphore()
    for place in places:
        pl.semaphore_signal(
            barrier, inc=1, device_id={"shard": place}, device_id_type=pl.DeviceIdType.MESH
        )
    pl.semaphore_wait(barrier, len(places))


TILE = 256
PAIR = 2 * CHUNK
LINE = 32
DEEP = 12
LAST = 6
ROOT_TWO_PI = math.sqrt(2.0 / math.pi)


def dot_rows(left, right):
    return lax.dot_general(left, right, (((1,), (1,)), ((), ())), preferred_element_type=jnp.float32)


def dot_plain(left, right):
    return lax.dot_general(left, right, (((1,), (0,)), ((), ())), preferred_element_type=jnp.float32)


def dot_columns(left, right):
    return lax.dot_general(left, right, (((0,), (0,)), ((), ())), preferred_element_type=jnp.float32)


def column_pieces(width):
    return 3 if width % 384 == 0 else 2


def backward_kernel(dims, names, *refs):
    r = types.SimpleNamespace(**dict(zip(names, refs)))
    tokens, local, width, inner_width, head_cols = dims
    f32, bf16 = jnp.float32, jnp.bfloat16
    half = local // 2
    q_cols = head_cols // 2
    k_cols = head_cols // 4
    heads = q_cols // HEAD_SIZE
    part = width // 4
    part_wide = r.normed_cols.shape[1]
    side = 2 * head_cols
    n_a = inner_width // TILE
    n_b = width // TILE
    block = min(TILE, tokens)
    n_blocks = tokens // block
    pieces = column_pieces(width)
    piece = width // pieces
    group = PAIR * pieces

    counts = (
        inner_width // PAIR, width // PAIR, width // PAIR, r.w_out.shape[0] // PAIR,
        part // (2 * LINE),
    )
    first = [sum(counts[:job]) for job in range(6)]
    units = first[5]
    steps = 2 * units
    a_at = pieces + 1
    b_at = a_at + (n_a + 1) // 2
    c_at = b_at + n_b
    d_at = c_at + 6
    f_at = d_at + 7
    g_at = f_at + 1
    h_at = g_at + heads * n_blocks
    i_at = h_at + 10
    k_at = i_at + n_blocks + 2
    assert b_at <= first[1] and f_at < first[3] and i_at < first[4] and first[1] <= i_at
    assert first[2] <= i_at and k_at + 5 <= units + 5 and counts[0] // pieces >= 2

    place = lax.axis_index("rep")
    chips = lax.axis_size("rep") // 2
    chip, core = place // 2, place % 2
    left = chip < chips // 2
    is_end = (chip == 0) | (chip == chips - 1)
    is_mid = (chip == chips // 2 - 1) | (chip == chips // 2)
    twin = {"rep": place + 1 - 2 * core}
    inner = {"rep": jnp.where(left, place + 2, place - 2)}
    outer = {"rep": jnp.where(is_end, place, jnp.where(left, place - 2, place + 2))}
    next_chip = {"rep": place + 2 - 4 * (chip % 2)}
    far_chip = {"rep": (place + 4) % 8}
    me, x_place, y_place, far_place = plane_places()
    x_other, y_other = {"shard": x_place}, {"shard": y_place}
    plane = [{"shard": (me + step) % 4} for step in (1, 2, 3)]

    def tell(sem, where):
        pl.semaphore_signal(sem, inc=1, device_id=where, device_id_type=pl.DeviceIdType.MESH)

    def load(src, dst, index):
        return pltpu.make_async_copy(src, dst, r.load_sem.at[index])

    load_ffn = load(
        r.grad_ffn,
        r.ffn_buf.at[pl.ds(pl.multiple_of(me * local, 16), local), pl.ds(0, width)], 0,
    )
    load_hidden = load(r.hidden, r.hidden_buf.at[:, pl.ds(0, inner_width)], 1)
    load_two = load(r.normed_two, r.two_buf, 2)
    load_small = (
        load(r.middle, r.middle_buf, 3),
        load(r.attn_out, r.attn_buf, 4),
        load(r.cotangent, r.cot_buf, 5),
        load(r.qkv, r.qkv_buf, 6),
        load(r.mixed, r.mixed_buf, 7),
        load(r.normed_cols, r.cols_buf, 8),
        load(r.tokens, r.token_buf, 9),
    )

    def weight_tile(index):
        return r.weights.at[pl.ds(pl.multiple_of(index * TILE, TILE), TILE)]

    def a_loads(tile, buf):
        rows = pl.ds(pl.multiple_of(tile * TILE, TILE), TILE)
        return (
            load(r.w_down.at[rows], weight_tile(buf).at[:, pl.ds(0, width)], 10 + buf),
            load(r.gate.at[:, rows], r.gate_buf.at[buf], 12 + buf),
            load(r.up.at[:, rows], r.up_buf.at[buf], 14 + buf),
        )

    def b_loads(tile):
        rows = pl.ds(pl.multiple_of(tile * TILE, TILE), TILE)
        buf = 2 - 2 * (tile % 2)
        sem = 16 + 2 * (tile % 2)
        return (
            load(r.w_gate.at[rows], weight_tile(buf).at[:, pl.ds(0, inner_width)], sem),
            load(r.w_up.at[rows], weight_tile(buf + 1).at[:, pl.ds(0, inner_width)], sem + 1),
        )

    def b_store(tile):
        columns = pl.ds(pl.multiple_of(tile * TILE, TILE), TILE)
        return pltpu.make_async_copy(
            r.stage.at[tile % 2], r.partial.at[:, columns], r.stage_sem.at[tile % 2]
        )

    for index, gain in enumerate((r.post_attn_gain, r.ffn_gain, r.post_ffn_gain, r.attn_gain)):
        r.gains[index : index + 1] = gain[...].astype(jnp.float32).reshape(1, gain.shape[0])
    load_ffn.start()
    load_hidden.start()
    for buf in range(2):
        for copy in a_loads(buf, buf):
            copy.start()
    load_two.start()
    for copy in load_small:
        copy.start()
    for copy in b_loads(0):
        copy.start()

    barrier = pltpu.get_barrier_semaphore()
    for where in [twin, inner, far_chip] + plane:
        tell(barrier, where)

    @pl.when(is_end)
    def _():
        pl.semaphore_wait(barrier, 6)

    @pl.when(jnp.logical_not(is_end))
    def _():
        tell(barrier, outer)
        pl.semaphore_wait(barrier, 7)

    def ffn_copies(index):
        across = pl.ds(index * piece, piece)

        def send(owner, which, at, where, own):
            here = pl.ds(pl.multiple_of(owner * local + which * half, 16), half)
            src = r.grad_ffn.at[pl.ds(which * half, half), across]
            return remote(
                src if own else r.ffn_buf.at[here, across], r.ffn_buf.at[here, across],
                r.ffn_send.at[index, at], r.ffn_recv.at[index, at], where,
            )

        starts = (
            send(me, 0, 0, x_other, True), send(me, 1, 1, y_other, True),
            send(me, 1, 2, x_other, True), send(me, 0, 3, y_other, True),
        )
        return starts, (send(x_place, 0, 4, y_other, False), send(y_place, 1, 5, x_other, False))

    ffn_pieces = [ffn_copies(index) for index in range(pieces)]

    def ffn_pass(index):
        starts, passes = ffn_pieces[index]
        for i in range(2):
            starts[i].wait_recv()
            passes[i].start()

    def ffn_arrived(index):
        starts, passes = ffn_pieces[index]
        for copy in starts[2:] + passes:
            copy.wait_recv()

    def ffn_sent():
        for starts, passes in ffn_pieces:
            for copy in starts + passes:
                copy.wait_send()

    for copy in ffn_pieces[0][0]:
        copy.start()
    ffn_pass(0)
    for starts, _ in ffn_pieces[1:]:
        for copy in starts:
            copy.start()
    load_ffn.wait()
    load_hidden.wait()
    ffn_arrived(0)

    def a_tile(tile, buf):
        for copy in a_loads(tile, buf):
            copy.wait()
        r.wide[...] = dot_rows(r.ffn_buf[:, pl.ds(0, width)], weight_tile(buf)[:, pl.ds(0, width)])
        columns = pl.ds(pl.multiple_of(tile * TILE, TILE), TILE)

        def rows_of(index, carry):
            rows = pl.ds(pl.multiple_of(index * 128, 128), 128)
            grad = r.wide[rows]
            gate = r.gate_buf[buf, rows].astype(f32)
            up = r.up_buf[buf, rows].astype(f32)
            curve = jnp.tanh(ROOT_TWO_PI * (gate + 0.044715 * gate * gate * gate))
            slope = (1.0 - curve * curve) * (ROOT_TWO_PI * (1.0 + 3.0 * 0.044715 * gate * gate))
            gelu_slope = 0.5 * (1.0 + curve) + 0.5 * gate * slope
            r.gate_grad[rows, columns] = (grad * up * gelu_slope).astype(bf16)
            r.up_grad[rows, columns] = (grad * (0.5 * gate * (1.0 + curve))).astype(bf16)
            return carry

        lax.fori_loop(0, tokens // 128, rows_of, 0)

        @pl.when(tile + 2 < n_a)
        def _():
            for copy in a_loads(tile + 2, buf):
                copy.start()

    def b_tile(tile):
        for copy in b_loads(tile):
            copy.wait()

        @pl.when(tile >= 2)
        def _():
            b_store(tile - 2).wait()

        buf = 2 - 2 * (tile % 2)
        some = dot_rows(r.gate_grad[:, pl.ds(0, inner_width)], weight_tile(buf)[:, pl.ds(0, inner_width)])
        some += dot_rows(r.up_grad[...], weight_tile(buf + 1)[:, pl.ds(0, inner_width)])
        r.stage[tile % 2] = some.astype(bf16)
        b_store(tile).start()

        @pl.when(tile + 2 < n_b)
        def _():
            for copy in b_loads(tile + 2):
                copy.start()

    def partial_rows(owner, which):
        return r.partial.at[pl.ds(pl.multiple_of(owner * local + which * half, 16), half)]

    c_own = (
        load(partial_rows(y_place, 0), r.c_mine.at[0], 20),
        load(partial_rows(x_place, 1), r.c_mine.at[1], 21),
        load(partial_rows(me, 0), r.c_mine.at[2], 22),
        load(partial_rows(me, 1), r.c_mine.at[3], 23),
    )

    def c_send(src, index, where):
        return remote(src, r.c_landed.at[index], r.c_send.at[index], r.c_recv.at[index], where)

    c_first = (
        c_send(partial_rows(far_place, 0), 0, x_other),
        c_send(partial_rows(far_place, 1), 1, y_other),
        c_send(partial_rows(x_place, 0), 2, x_other),
        c_send(partial_rows(y_place, 1), 3, y_other),
    )
    c_on = (c_send(r.c_mine.at[0], 4, y_other), c_send(r.c_mine.at[1], 5, x_other))

    def c_start():
        b_store(n_b - 2).wait()
        b_store(n_b - 1).wait()
        for copy in c_first + c_own:
            copy.start()

    def c_pass():
        for copy in c_own:
            copy.wait()
        for index in range(2):
            c_first[index].wait_recv()
            r.c_mine[index] = add_low(r.c_mine[index], r.c_landed[index])
            c_on[index].start()

    def d_norms(which):
        if which == 0:
            for copy in load_small:
                copy.wait()
            for copy in c_first:
                copy.wait_send()
            r.gain_own[...] = r.gain_parts[...]
        c_first[2 + which].wait_recv()
        c_on[which].wait_recv()

        def rows_of(which, index, carry):
            here = pl.ds(pl.multiple_of(index * 16, 16), 16)
            rows = pl.ds(pl.multiple_of(which * half + index * 16, 16), 16)
            grad = (
                r.c_mine[2 + which, here].astype(f32)
                + r.c_landed[2 + which, here].astype(f32)
                + r.c_landed[4 + which, here].astype(f32)
            )
            middle = r.middle_buf[rows]
            inv = lax.rsqrt(jnp.mean(middle * middle, axis=-1, keepdims=True) + norm_eps)
            weighted = grad * r.gains[1:2]
            mean = jnp.mean(weighted * middle, axis=-1, keepdims=True)
            r.gain_own[2:3, 0:width] += jnp.sum(grad * middle * inv, axis=0, keepdims=True)
            grad_mid = (
                r.cot_buf[rows].astype(f32) + inv * weighted - middle * (inv * inv * inv) * mean
            )
            r.middle_buf[rows] = grad_mid
            attn = r.attn_buf[rows]
            inv = lax.rsqrt(jnp.mean(attn * attn, axis=-1, keepdims=True) + norm_eps)
            weighted = grad_mid * r.gains[0:1]
            mean = jnp.mean(weighted * attn, axis=-1, keepdims=True)
            r.gain_own[1:2, 0:width] += jnp.sum(grad_mid * attn * inv, axis=0, keepdims=True)
            grad_attn = inv * weighted - attn * (inv * inv * inv) * mean
            r.all_grad[pl.ds(pl.multiple_of(me * local + which * half + index * 16, 16), 16)] = (
                grad_attn.astype(bf16)
            )
            return carry

        lax.fori_loop(0, half // 16, functools.partial(rows_of, which), 0)
        for index in ((0, 3), (1, 2))[which]:
            e_first[index].start()
        if which == 1:
            for copy in c_on:
                copy.wait_send()

    def gather_copies(rows, source, target, send_sem, recv_sem):
        def send(owner, which, index, where, src):
            here = pl.ds(pl.multiple_of(owner * 2 * rows + which * rows, 16), rows)
            return remote(
                src.at[here] if src is target else src.at[pl.ds(which * rows, rows)],
                target.at[here], send_sem.at[index], recv_sem.at[index], where,
            )

        starts = (
            send(me, 0, 0, x_other, source),
            send(me, 1, 1, y_other, source),
            send(me, 1, 2, x_other, source),
            send(me, 0, 3, y_other, source),
        )
        passes = (
            send(x_place, 0, 4, y_other, target), send(y_place, 1, 5, x_other, target)
        )
        return starts, passes

    e_first, e_on = gather_copies(half, r.all_grad, r.all_grad, r.e_send, r.e_recv)
    h_first, h_on = gather_copies(tokens // 2, r.head_grad, r.grad_qkv, r.h_send, r.h_recv)
    h_own = pltpu.make_async_copy(
        r.head_grad, r.grad_qkv.at[pl.ds(pl.multiple_of(me * tokens, 16), tokens)], r.keep_sem.at[1]
    )

    def pass_on(starts, passes):
        for index in range(2):
            starts[index].wait_recv()
            passes[index].start()

    def gathered(starts, passes):
        for copy in starts[2:] + passes:
            copy.wait_recv()
        for copy in starts + passes:
            copy.wait_send()

    load_out = load(r.w_out, r.weights.at[pl.ds(0, r.w_out.shape[0]), pl.ds(0, width)], 24)

    def g_loads(item):
        head, rows = item // n_blocks, pl.ds(pl.multiple_of((item % n_blocks) * block, block), block)
        return (
            load(r.probs.at[head, rows], r.probs_buf, 25),
            load(r.tanh.at[head, rows], r.tanh_buf, 26),
        )

    def f_mixed():
        gathered(e_first, e_on)
        load_out.wait()
        r.mixed_grad[...] = dot_rows(
            r.all_grad[...], r.weights[pl.ds(0, r.w_out.shape[0]), pl.ds(0, width)]
        ).astype(bf16)
        r.kv_grad[...] = jnp.zeros_like(r.kv_grad)
        for copy in g_loads(0):
            copy.start()

    def g_attention(item):
        head = item // n_blocks
        rows = pl.ds(pl.multiple_of((item % n_blocks) * block, block), block)
        columns = pl.ds(pl.multiple_of(head * HEAD_SIZE, HEAD_SIZE), HEAD_SIZE)
        for copy in g_loads(item):
            copy.wait()
        grad_out = r.mixed_grad[rows, columns]
        values = r.qkv_buf[:, pl.ds(q_cols + k_cols, k_cols)]
        r.score_grad[...] = dot_rows(grad_out, values)

        def rows_of(index, carry):
            here = pl.ds(pl.multiple_of(index * 64, 64), 64)
            probs = r.probs_buf[here]
            grad = r.score_grad[here]
            curve = r.tanh_buf[here]
            total = jnp.sum(probs * grad, axis=-1, keepdims=True)
            grad = probs * (grad - total) * (1.0 - curve * curve) * (HEAD_SIZE ** (-0.5))
            r.dots_grad[here] = grad.astype(bf16)
            r.probs_low[here] = probs.astype(bf16)
            return carry

        lax.fori_loop(0, block // 64, rows_of, 0)

        @pl.when(item + 1 < heads * n_blocks)
        def _():
            for copy in g_loads(item + 1):
                copy.start()

        keys = r.qkv_buf[:, pl.ds(q_cols, k_cols)]
        r.head_grad[rows, columns] = dot_plain(r.dots_grad[...], keys).astype(bf16)
        r.kv_grad[0] += dot_columns(r.dots_grad[...], r.qkv_buf[rows, columns])
        r.kv_grad[1] += dot_columns(r.probs_low[...], grad_out)

    def h_start():
        r.head_grad[:, pl.ds(q_cols, k_cols)] = r.kv_grad[0].astype(bf16)
        r.head_grad[:, pl.ds(q_cols + k_cols, k_cols)] = r.kv_grad[1].astype(bf16)
        for copy in h_first:
            copy.start()
        h_own.start()

    def side_of(owner, kind):
        buf = r.hidden_buf if owner < 2 else r.ffn_buf
        size = (q_cols, k_cols, k_cols)[kind]
        start = (0, 2 * q_cols, 2 * q_cols + 2 * k_cols)[kind] + (owner % 2) * size
        return buf.at[:, pl.ds(start, size)]

    i_loads = [
        load(
            r.grad_qkv.at[
                pl.ds(owner * tokens, tokens),
                pl.ds((0, q_cols, q_cols + k_cols)[kind], (q_cols, k_cols, k_cols)[kind]),
            ],
            side_of(owner, kind),
            27 + 3 * owner + kind,
        )
        for owner in range(4)
        for kind in range(3)
    ] + [
        load(r.w_query, r.gate_grad.at[pl.ds(0, part), pl.ds(0, 4 * q_cols)], 39),
        load(r.w_key, r.weights.at[pl.ds(0, part), pl.ds(0, 4 * k_cols)], 40),
        load(r.w_value, r.weights.at[pl.ds(0, part), pl.ds(4 * k_cols, 4 * k_cols)], 41),
    ]
    i_copies = [
        remote(
            r.head_grad.at[pl.ds(pl.multiple_of(((me + step) % 4) * local, 16), local), pl.ds(0, part_wide)],
            r.norm_grad.at[me], r.i_send.at[step - 1], r.i_recv.at[step - 1], plane[step - 1],
        )
        for step in (1, 2, 3)
    ]

    def i_start():
        gathered(h_first, h_on)
        h_own.wait()
        for copy in i_loads:
            copy.start()
        for copy in i_loads:
            copy.wait()

    def i_norm(index):
        rows = pl.ds(index * block, block)
        some = jnp.zeros((block, part_wide), f32)
        for owner in range(4):
            for kind, size in enumerate((q_cols, k_cols, k_cols)):
                held = r.gate_grad if kind == 0 else r.weights
                start = (0, 0, 4 * k_cols)[kind] + owner * size
                some += dot_rows(
                    side_of(owner, kind)[rows], held[pl.ds(0, part_wide), pl.ds(start, size)]
                )
        r.head_grad[rows, pl.ds(0, part_wide)] = some.astype(bf16)
        if index < n_blocks - 1:
            return
        for copy in i_copies:
            copy.start()
        r.norm_grad[me] = r.head_grad[
            pl.ds(pl.multiple_of(me * local, 16), local), pl.ds(0, part_wide)
        ]

    def k_norm():
        for copy in i_copies:
            copy.wait()

        def rows_of(index, carry):
            rows = pl.ds(pl.multiple_of(index * 16, 16), 16)
            grad = jnp.concatenate(
                [r.norm_grad[owner, rows].astype(f32)[:, :part] for owner in range(4)], axis=1
            )
            values = r.token_buf[rows].astype(f32)
            inv = lax.rsqrt(jnp.mean(values * values, axis=-1, keepdims=True) + norm_eps)
            weighted = grad * r.gains[3:4]
            mean = jnp.mean(weighted * values, axis=-1, keepdims=True)
            r.gain_own[3:4] += jnp.sum(grad * values * inv, axis=0, keepdims=True)
            r.cot_buf[rows] = (
                r.middle_buf[rows] + inv * weighted - values * (inv * inv * inv) * mean
            ).astype(bf16)
            return carry

        lax.fori_loop(0, local // 16, rows_of, 0)
        keep_part.start()
        for copy in gain_plane:
            copy.start()

    keep_part = pltpu.make_async_copy(r.cot_buf, r.grad_tokens, r.keep_sem.at[0])
    gain_plane = [
        remote(r.gain_own, r.gain_plane.at[me], r.gain_send.at[i], r.gain_recv.at[i], where)
        for i, where in enumerate(plane)
    ]
    gain_rep = [
        remote(r.gain_mine.at[i], r.gain_theirs.at[i], r.gain_send.at[3 + i], r.gain_recv.at[3 + i], where)
        for i, where in enumerate((twin, next_chip, far_chip))
    ]

    def k_plane():
        for copy in gain_plane:
            copy.wait()
        r.gain_plane[me] = r.gain_own[...]
        r.gain_mine[0] = (r.gain_plane[0] + r.gain_plane[1]) + (r.gain_plane[2] + r.gain_plane[3])
        gain_rep[0].start()

    def k_rep(index):
        gain_rep[index].wait()
        total = r.gain_mine[index] + r.gain_theirs[index]
        if index < 2:
            r.gain_mine[index + 1] = total
            gain_rep[index + 1].start()
        else:
            r.gain_total[...] = total
            keep_gains.start()

    keep_gains = pltpu.make_async_copy(r.gain_total, r.gain_sums, r.keep_sem.at[3])

    sums = (r.down_sum, r.gate_sum, r.up_sum, r.out_sum)

    def by_job(step, use, scale=2):
        for job in range(5):

            @pl.when((step >= scale * first[job]) & (step < scale * first[job + 1]))
            def _():
                use(job, step - scale * first[job])

    def by_width(step, use):
        if side == r.acc.shape[2]:
            use(pl.ds(0, side))
            return

        @pl.when(step < 2 * first[4])
        def _():
            use(pl.ds(0, r.acc.shape[2]))

        @pl.when(step >= 2 * first[4])
        def _():
            use(pl.ds(0, side))

    def results(job, index, slot):
        if job == 0:
            unit, which = index // 2, index % 2
            low = (unit % (inner_width // group)) * group + (2 * which + core) * pieces * LINE
            across = pl.ds(pl.multiple_of(unit // (inner_width // group) * piece, 128), piece)
            return [
                (
                    r.total.at[slot, :, pl.ds(i * piece, piece)],
                    r.down_sum.at[pl.ds(pl.multiple_of(low + i * LINE, LINE), LINE), across],
                )
                for i in range(pieces)
            ]
        if job < 4:
            rows = pl.ds(pl.multiple_of((2 * index + core) * LINE, LINE), LINE)
            return [(r.total.at[slot, :, pl.ds(0, sums[job].shape[1])], sums[job].at[rows])]
        rows = pl.ds(pl.multiple_of(index * LINE, LINE), LINE)
        pairs, start = [], 0
        for ref in (r.query_sum, r.key_sum, r.value_sum):
            size = ref.shape[1] // 2
            columns = pl.ds(pl.multiple_of(core * size, 128), size)
            pairs.append((r.total.at[slot, :, pl.ds(start, size)], ref.at[rows, columns]))
            start += size
        return pairs

    def pair_copies(job, index, step):
        slot = step % LAST
        return [
            remote(src, dst, r.pair_send.at[slot, i], r.pair_recv.at[step, i], twin)
            for i, (src, dst) in enumerate(results(job, index, slot))
        ]

    def store_copies(job, index, step):
        slot = step % LAST
        return [
            pltpu.make_async_copy(src, dst, r.store_sem.at[slot, i])
            for i, (src, dst) in enumerate(results(job, index, slot))
        ]

    def made_rows(step, owner):
        return pl.ds(pl.multiple_of((step % 2) * 2 * LINE + owner * LINE, LINE), LINE)

    def sib_copy(step, across):
        return remote(
            r.made.at[step // 2 % 2, made_rows(step, 1 - core), across],
            r.sib.at[step % 4, :, across], r.sib_send.at[step % 4], r.sib_recv.at[step % 4], twin,
        )

    def up_copy(step, across, dst, sem):
        slot = step % DEEP
        return remote(
            r.acc.at[slot, :, across], dst.at[slot, :, across], r.up_send.at[slot], sem.at[slot], inner
        )

    def down_copy(step, across):
        return remote(
            r.total.at[step % LAST, :, across], r.inner_in.at[step % DEEP, :, across],
            r.down_send.at[step % LAST], r.inner_recv.at[step % DEEP], outer,
        )

    def up_sent(step):
        by_width(step, lambda across: up_copy(step, across, r.outer_in, r.outer_recv).wait_send())

    def make(unit):
        slot = unit % 2

        def product(job, index):
            if job == 0:
                n_groups = inner_width // group
                rows = pl.ds(pl.multiple_of(index % n_groups * group, PAIR), group)
                across = pl.ds(pl.multiple_of(index // n_groups * piece, 128), piece)
                some = dot_columns(r.hidden_buf[:, rows], r.ffn_buf[:, across]).astype(bf16)
                for row in range(4):
                    for i in range(pieces):
                        low = (row * pieces + i) * LINE
                        r.made[slot, pl.ds(row * LINE, LINE), pl.ds(i * piece, piece)] = some[
                            low : low + LINE
                        ]
                return
            if job < 4:
                left_buf = (None, r.two_buf, r.two_buf, r.mixed_buf)[job]
                right_buf = (None, r.gate_grad, r.up_grad, r.all_grad)[job]
                columns = pl.ds(pl.multiple_of(index * PAIR, PAIR), PAIR)
                across = pl.ds(0, sums[job].shape[1])
                r.made[slot, :, across] = dot_columns(
                    left_buf[:, columns], right_buf[:, across]
                ).astype(bf16)
                return
            columns = pl.ds(pl.multiple_of((index // 2) * PAIR, PAIR), PAIR)
            for which, buf in enumerate((r.hidden_buf, r.ffn_buf)):
                r.both[...] = dot_columns(r.cols_buf[:, columns], buf[:, pl.ds(0, side)]).astype(bf16)
                for row in range(2):
                    low = pl.multiple_of((index % 2) * 2 * LINE + row * LINE, LINE)
                    r.made[slot, pl.ds((2 * row + which) * LINE, LINE), pl.ds(0, side)] = r.both[
                        pl.ds(low, LINE)
                    ]

        by_job(unit, product, 1)

    def give(step):
        @pl.when(step >= 4)
        def _():
            pl.semaphore_wait(r.sib_credit, 1)

        by_width(step, lambda across: sib_copy(step, across).start())

    def send_up(step):
        @pl.when(step >= DEEP)
        def _():
            pl.semaphore_wait(r.up_credit, 1)

        @pl.when(is_mid)
        def _():
            by_width(step, lambda across: up_copy(step, across, r.inner_in, r.inner_recv).start())

        @pl.when(jnp.logical_not(is_mid))
        def _():
            by_width(step, lambda across: up_copy(step, across, r.outer_in, r.outer_recv).start())

    def pair_up(step):
        slot = step % DEEP
        by_width(step, lambda across: sib_copy(step, across).wait())

        @pl.when(step >= DEEP)
        def _():
            up_sent(step - DEEP)

        r.acc[slot] = add_low(r.made[step // 2 % 2, made_rows(step, core)], r.sib[step % 4])

        @pl.when(step + 4 < steps)
        def _():
            tell(r.sib_credit, twin)

        @pl.when(is_end)
        def _():
            send_up(step)

    def from_outer(step):
        slot = step % DEEP
        by_width(step, lambda across: up_copy(step, across, r.outer_in, r.outer_recv).wait_recv())
        r.acc[slot] = add_low(r.acc[slot], r.outer_in[slot])

        @pl.when(step + DEEP < steps)
        def _():
            tell(r.up_credit, outer)

        send_up(step)

    def sends_done(step):
        def use(job, index):
            for copy in pair_copies(job, index, step):
                copy.wait_send()
            for copy in store_copies(job, index, step):
                copy.wait()

        by_job(step, use)

        @pl.when(jnp.logical_not(is_end))
        def _():
            by_width(step, lambda across: down_copy(step, across).wait_send())

    def from_inner(step):
        slot = step % DEEP
        by_width(step, lambda across: down_copy(step, across).wait_recv())

        @pl.when(step >= LAST)
        def _():
            sends_done(step - LAST)

        @pl.when(is_mid)
        def _():
            r.total[step % LAST] = add_low(r.acc[slot], r.inner_in[slot])

            @pl.when(step + DEEP < steps)
            def _():
                tell(r.up_credit, inner)

        @pl.when(jnp.logical_not(is_mid))
        def _():
            r.total[step % LAST] = r.inner_in[slot]

            @pl.when(step + DEEP < steps)
            def _():
                tell(r.down_credit, inner)

        @pl.when(jnp.logical_not(is_end))
        def _():
            @pl.when(step >= DEEP)
            def _():
                pl.semaphore_wait(r.down_credit, 1)

            by_width(step, lambda across: down_copy(step, across).start())

        def use(job, index):
            for copy in pair_copies(job, index, step) + store_copies(job, index, step):
                copy.start()

        by_job(step, use)

    lag_outer = 3
    lag_inner = jnp.where(is_end, 10, 6)

    def at(now, step, use):
        @pl.when(now == step)
        def _():
            use()

    def work(now):
        @pl.when(now == 0)
        def _():
            load_two.wait()

        for index in range(1, pieces):
            at(now, index, functools.partial(ffn_pass, index))

            at(now, index + 1, functools.partial(ffn_arrived, index))

        at(now, b_at, ffn_sent)

        for buf in range(2):

            @pl.when((now >= a_at) & (2 * (now - a_at) + buf < n_a))
            def _():
                a_tile(2 * (now - a_at) + buf, buf)

        @pl.when(now == b_at - 1)
        def _():
            for copy in b_loads(1):
                copy.start()

        @pl.when((now >= b_at) & (now < c_at))
        def _():
            b_tile(now - b_at)

        at(now, c_at, c_start)
        at(now, c_at + 1, load_out.start)
        at(now, c_at + 2, c_pass)

        at(now, d_at, lambda: d_norms(0))
        at(now, d_at + 1, lambda: d_norms(1))
        at(now, d_at + 3, lambda: pass_on(e_first, e_on))
        at(now, f_at, f_mixed)

        @pl.when((now >= g_at) & (now < h_at))
        def _():
            g_attention(now - g_at)

        at(now, h_at, h_start)
        at(now, h_at + 4, lambda: pass_on(h_first, h_on))
        at(now, i_at, i_start)
        for index in range(n_blocks):
            at(now, i_at + 1 + index, functools.partial(i_norm, index))
        at(now, k_at, k_norm)
        at(now, k_at + 1, k_plane)
        for index in range(3):
            at(now, k_at + 2 + index, functools.partial(k_rep, index))

    def tick(now, carry):
        @pl.when((now % 2 == 0) & (now < steps))
        def _():
            make(now // 2)

        @pl.when(now < steps)
        def _():
            give(now)

        @pl.when((now >= 1) & (now - 1 < steps))
        def _():
            pair_up(now - 1)

        @pl.when(jnp.logical_not(is_end) & (now >= lag_outer) & (now - lag_outer < steps))
        def _():
            from_outer(now - lag_outer)

        @pl.when((now >= lag_inner) & (now - lag_inner < steps))
        def _():
            from_inner(now - lag_inner)

        @pl.when(now % 2 == 1)
        def _():
            work(now // 2)

        return carry

    lax.fori_loop(0, steps + 10, tick, 0)

    def finish(step, carry):
        sends_done(step)
        return carry

    lax.fori_loop(steps - LAST, steps, finish, 0)

    def finish_up(step, carry):
        up_sent(step)
        return carry

    lax.fori_loop(steps - DEEP, steps, finish_up, 0)

    def arrived(step, carry):
        def use(job, index):
            for copy in pair_copies(job, index, step):
                copy.wait_recv()

        by_job(step, use)
        return carry

    lax.fori_loop(0, steps, arrived, 0)
    for copy in (keep_part, keep_gains):
        copy.wait()


def backward(collective_id, **args):
    f32, bf16 = jnp.float32, jnp.bfloat16
    given = types.SimpleNamespace(**args)
    tokens, width = given.normed_two.shape
    inner_width = given.hidden.shape[1]
    local = tokens // 4
    half = local // 2
    head_cols = given.qkv.shape[1]
    part = width // 4
    part_wide = given.normed_cols.shape[1]
    out_rows = given.w_out.shape[0]
    side = 2 * head_cols
    slot_width = max(width, inner_width, side)
    pieces = column_pieces(width)
    block = min(TILE, tokens)
    steps = 2 * ((inner_width + 2 * width + out_rows) // PAIR + part // (2 * LINE))
    vmem, dma, credit = pltpu.VMEM, pltpu.SemaphoreType.DMA, pltpu.SemaphoreType.REGULAR
    shape = jax.ShapeDtypeStruct
    outs = dict(
        down_sum=shape((inner_width, width), bf16),
        gate_sum=shape((width, inner_width), bf16),
        up_sum=shape((width, inner_width), bf16),
        out_sum=shape((out_rows, width), bf16),
        query_sum=shape((part, side), bf16),
        key_sum=shape((part, side // 2), bf16),
        value_sum=shape((part, side // 2), bf16),
        grad_tokens=shape((local, width), bf16),
        gain_sums=shape((8, width), f32),
        partial=shape((tokens, width), bf16),
        grad_qkv=shape((4 * tokens, head_cols), bf16),
    )
    scratch = dict(
        ffn_buf=vmem((tokens, slot_width), bf16),
        hidden_buf=vmem((tokens, slot_width), bf16),
        two_buf=vmem((tokens, width), bf16),
        gate_grad=vmem((tokens, slot_width), bf16),
        up_grad=vmem((tokens, inner_width), bf16),
        weights=vmem((4 * TILE, slot_width), bf16),
        gate_buf=vmem((2, tokens, TILE), bf16),
        up_buf=vmem((2, tokens, TILE), bf16),
        wide=vmem((tokens, TILE), f32),
        stage=vmem((2, tokens, TILE), bf16),
        c_mine=vmem((4, half, width), bf16),
        c_landed=vmem((6, half, width), bf16),
        middle_buf=vmem((local, width), f32),
        attn_buf=vmem((local, width), f32),
        cot_buf=vmem((local, width), bf16),
        qkv_buf=vmem((tokens, head_cols), bf16),
        mixed_buf=vmem((tokens, out_rows), bf16),
        cols_buf=vmem((tokens, -(-part // PAIR) * PAIR), bf16),
        token_buf=vmem((local, width), bf16),
        all_grad=vmem((tokens, width), bf16),
        mixed_grad=vmem((tokens, out_rows), bf16),
        probs_buf=vmem((block, tokens), f32),
        tanh_buf=vmem((block, tokens), f32),
        score_grad=vmem((block, tokens), f32),
        dots_grad=vmem((block, tokens), bf16),
        probs_low=vmem((block, tokens), bf16),
        kv_grad=vmem((2, tokens, head_cols // 4), f32),
        head_grad=vmem((tokens, head_cols), bf16),
        norm_grad=vmem((4, local, part_wide), bf16),
        gains=vmem((8, width), f32),
        gain_own=vmem((8, width), f32),
        gain_plane=vmem((4, 8, width), f32),
        gain_mine=vmem((3, 8, width), f32),
        gain_theirs=vmem((3, 8, width), f32),
        gain_total=vmem((8, width), f32),
        made=vmem((2, PAIR, slot_width), bf16),
        both=vmem((PAIR, side), bf16),
        sib=vmem((4, LINE, slot_width), bf16),
        acc=vmem((DEEP, LINE, slot_width), bf16),
        outer_in=vmem((DEEP, LINE, slot_width), bf16),
        inner_in=vmem((DEEP, LINE, slot_width), bf16),
        total=vmem((LAST, LINE, slot_width), bf16),
        load_sem=dma((42,)),
        stage_sem=dma((2,)),
        keep_sem=dma((4,)),
        ffn_send=dma((pieces, 6)),
        ffn_recv=dma((pieces, 6)),
        c_send=dma((6,)),
        c_recv=dma((6,)),
        e_send=dma((6,)),
        e_recv=dma((6,)),
        h_send=dma((6,)),
        h_recv=dma((6,)),
        i_send=dma((3,)),
        i_recv=dma((3,)),
        gain_send=dma((6,)),
        gain_recv=dma((6,)),
        sib_send=dma((4,)),
        sib_recv=dma((4,)),
        up_send=dma((DEEP,)),
        outer_recv=dma((DEEP,)),
        inner_recv=dma((DEEP,)),
        down_send=dma((LAST,)),
        pair_send=dma((LAST, pieces)),
        pair_recv=dma((steps, pieces)),
        store_sem=dma((LAST, pieces)),
        sib_credit=credit,
        up_credit=credit,
        down_credit=credit,
    )
    any_space = pl.BlockSpec(memory_space=pl.ANY)
    small = pl.BlockSpec(memory_space=pltpu.VMEM)
    in_specs = [
        small if value.ndim == 1 or value.shape[0] == 8 else any_space for value in args.values()
    ]
    results = pl.pallas_call(
        functools.partial(
            backward_kernel,
            (tokens, local, width, inner_width, head_cols),
            tuple(args) + tuple(outs) + tuple(scratch),
        ),
        out_shape=list(outs.values()),
        in_specs=in_specs,
        out_specs=[any_space] * len(outs),
        scratch_shapes=list(scratch.values()),
        compiler_params=pltpu.CompilerParams(
            collective_id=collective_id,
            has_side_effects=True,
            vmem_limit_bytes=VMEM_LIMIT,
        ),
        cost_estimate=pl.CostEstimate(
            flops=80 * tokens * width * width, bytes_accessed=400 * 2**20, transcendentals=0
        ),
    )(*args.values())
    return types.SimpleNamespace(**dict(zip(outs, results)))


VMEM_LIMIT = 63 * 2**20


def forward_kernel(names, *refs):
    r = types.SimpleNamespace(**dict(zip(names, refs)))
    f32, bf16 = jnp.float32, jnp.bfloat16
    tokens, inner_width = r.hidden.shape
    local, width = r.tokens.shape
    half = local // 2
    me, x_place, y_place, far_place = plane_places()
    x_other, y_other = {"shard": x_place}, {"shard": y_place}

    def load(src, dst, index):
        return pltpu.make_async_copy(src, dst, r.load_sem.at[index])

    def block_rows(owner):
        return pl.ds(pl.multiple_of(owner * local, 16), local)

    def half_rows(owner, which):
        return pl.ds(pl.multiple_of(owner * local + which * half, 16), half)

    early = (load(r.mixed, r.mixed_buf, 0), load(r.w_out, r.out_buf, 1))
    small = (load(r.tokens, r.token_buf, 2), load(r.cotangent, r.cot_buf, 3))
    big = (
        load(r.w_gate, r.gate_weight, 4),
        load(r.w_up, r.up_weight, 5),
        load(r.w_down, r.down_weight, 6),
    )
    for copy in early + small + big:
        copy.start()
    for index, gain in enumerate((r.post_attn_gain, r.ffn_gain, r.post_ffn_gain, r.attn_gain)):
        r.gains[index : index + 1] = gain[...].astype(jnp.float32).reshape(1, gain.shape[0])
    greet((x_place, y_place))

    def summing(landed, send_sem, recv_sem):
        def send(src, index, where):
            return remote(src, landed.at[index], send_sem.at[index], recv_sem.at[index], where)

        far = (
            send(r.partial.at[half_rows(far_place, 0)], 0, x_other),
            send(r.partial.at[half_rows(far_place, 1)], 1, y_other),
        )
        near = (
            send(r.partial.at[half_rows(x_place, 0)], 2, x_other),
            send(r.partial.at[half_rows(y_place, 1)], 3, y_other),
        )
        on = (send(r.passed.at[0], 4, y_other), send(r.passed.at[1], 5, x_other))
        return far, near, on

    def pass_sums(landed, far, on):
        for index, owner in enumerate((y_place, x_place)):
            far[index].wait_recv()
            r.passed[index] = add_low(r.partial[half_rows(owner, index)], landed[index])
            on[index].start()

    def gathering(source, target, send_sem, recv_sem):
        def send(owner, which, index, where, src):
            return remote(
                src, target.at[half_rows(owner, which)],
                send_sem.at[index], recv_sem.at[index], where,
            )

        starts = [
            [send(me, which, 2 * which + i, where, source(which)) for i, where in enumerate((x_other, y_other))]
            for which in range(2)
        ]
        on = (
            send(x_place, 0, 4, y_other, target.at[half_rows(x_place, 0)]),
            send(y_place, 1, 5, x_other, target.at[half_rows(y_place, 1)]),
        )
        return starts, on

    a_far, a_near, a_on = summing(r.a_landed, r.a_send, r.a_recv)
    c_far, c_near, c_on = summing(r.c_landed, r.c_send, r.c_recv)
    b_starts, b_on = gathering(
        lambda which: r.two_buf.at[half_rows(me, which)], r.two_buf, r.b_send, r.b_recv
    )

    for copy in early:
        copy.wait()

    def project(owner):
        rows = block_rows(owner)
        r.partial[rows] = dot_plain(r.mixed_buf[rows], r.out_buf[...]).astype(bf16)

    project(far_place)
    for copy in a_far:
        copy.start()
    project(x_place)
    a_near[0].start()
    project(y_place)
    a_near[1].start()
    project(me)
    pass_sums(r.a_landed, a_far, a_on)
    for copy in small:
        copy.wait()

    def sum_rows(landed, which, index):
        rows = pl.ds(pl.multiple_of(me * local + which * half + index * 32, 16), 32)
        here = pl.ds(pl.multiple_of(index * 32, 16), 32)
        return (
            r.partial[rows].astype(f32)
            + landed[2 + which, here].astype(f32)
            + landed[4 + which, here].astype(f32)
        )

    def middle_rows(which, index, carry):
        rows = pl.ds(pl.multiple_of(which * half + index * 32, 16), 32)
        attn = sum_rows(r.a_landed, which, index)
        r.attn_buf[rows] = attn
        inv = lax.rsqrt(jnp.mean(attn * attn, axis=-1, keepdims=True) + norm_eps)
        middle = r.token_buf[rows].astype(f32) + attn * inv * r.gains[0:1]
        r.middle_buf[rows] = middle
        inv = lax.rsqrt(jnp.mean(middle * middle, axis=-1, keepdims=True) + norm_eps)
        r.two_buf[pl.ds(pl.multiple_of(me * local + which * half + index * 32, 16), 32)] = (
            middle * inv * r.gains[1:2]
        ).astype(bf16)
        return carry

    for which in range(2):
        a_near[which].wait_recv()
        a_on[which].wait_recv()
        lax.fori_loop(0, half // 32, functools.partial(middle_rows, which), 0)
        b_starts[which][which].start()
    for which in range(2):
        b_starts[which][1 - which].start()
    keep = [
        pltpu.make_async_copy(r.attn_buf, r.attn_out, r.keep_sem.at[0]),
        pltpu.make_async_copy(r.middle_buf, r.middle, r.keep_sem.at[1]),
    ]
    for copy in keep:
        copy.start()
    for copy in a_far + a_near + a_on:
        copy.wait_send()

    def keep_block(halves):
        return [
            pltpu.make_async_copy(src, dst.at[half_rows(*halves[i])], r.keep_sem.at[2 + 2 * kind + i])
            for i in range(2)
            for kind, (src, dst) in enumerate(
                (
                    (r.gate_stage.at[pl.ds(i * half, half)], r.gate),
                    (r.up_stage.at[pl.ds(i * half, half)], r.up),
                    (r.hidden_buf.at[half_rows(*halves[i])], r.hidden),
                )
            )
        ]

    def feed(halves, before):
        for i in range(2):
            r.block[pl.ds(i * half, half), pl.ds(0, width)] = r.two_buf[half_rows(*halves[i])]
        if before is not None:
            for copy in keep_block(before):
                copy.wait()

        def tile(index, carry):
            columns = pl.ds(pl.multiple_of(index * TILE, TILE), TILE)
            r.gate_wide[...] = dot_plain(r.block[:, pl.ds(0, width)], r.gate_weight[:, columns])
            r.up_wide[...] = dot_plain(r.block[:, pl.ds(0, width)], r.up_weight[:, columns])
            for i in range(2):
                here = pl.ds(i * half, half)
                gate, up = r.gate_wide[here], r.up_wide[here]
                r.gate_stage[here, columns] = gate.astype(bf16)
                r.up_stage[here, columns] = up.astype(bf16)
                curve = jnp.tanh(ROOT_TWO_PI * (gate + 0.044715 * (gate * gate * gate)))
                r.hidden_buf[half_rows(*halves[i]), columns] = (
                    0.5 * gate * (1.0 + curve) * up
                ).astype(bf16)
            return carry

        lax.fori_loop(0, inner_width // TILE, tile, 0)
        for copy in keep_block(halves):
            copy.start()

    def shrink(halves):
        for i in range(2):
            r.block[pl.ds(i * half, half), pl.ds(0, inner_width)] = r.hidden_buf[half_rows(*halves[i])]

        def tile(index, carry):
            columns = pl.ds(pl.multiple_of(index * TILE, TILE), TILE)
            some = dot_plain(r.block[:, pl.ds(0, inner_width)], r.down_weight[:, columns]).astype(bf16)
            for i in range(2):
                r.partial[half_rows(*halves[i]), columns] = some[i * half : (i + 1) * half]
            return carry

        lax.fori_loop(0, width // TILE, tile, 0)

    mine = ((me, 0), (me, 1))
    early_halves = ((x_place, 0), (y_place, 1))
    late_halves = ((x_place, 1), (y_place, 0))
    far_halves = ((far_place, 0), (far_place, 1))
    big[0].wait()
    big[1].wait()
    feed(mine, None)
    big[2].wait()
    b_starts[0][0].wait_recv()
    b_on[0].start()
    b_starts[1][1].wait_recv()
    b_on[1].start()
    feed(early_halves, mine)
    shrink(early_halves)
    for copy in c_near:
        copy.start()
    b_starts[1][0].wait_recv()
    b_starts[0][1].wait_recv()
    feed(late_halves, early_halves)
    for copy in b_on:
        copy.wait_recv()
    feed(far_halves, late_halves)
    shrink(far_halves)
    for copy in c_far:
        copy.start()
    shrink(late_halves)
    shrink(mine)
    keep_two = pltpu.make_async_copy(r.two_buf, r.normed_two, r.keep_sem.at[8])
    keep_two.start()
    r.gain_part[...] = jnp.zeros_like(r.gain_part)
    pass_sums(r.c_landed, c_far, c_on)

    def last_rows(which, index, carry):
        rows = pl.ds(pl.multiple_of(which * half + index * 32, 16), 32)
        ffn = sum_rows(r.c_landed, which, index)
        inv = lax.rsqrt(jnp.mean(ffn * ffn, axis=-1, keepdims=True) + norm_eps)
        r.token_buf[rows] = (r.middle_buf[rows] + ffn * inv * r.gains[2:3]).astype(bf16)
        grad = r.cot_buf[rows].astype(f32)
        weighted = grad * r.gains[2:3]
        mean = jnp.mean(weighted * ffn, axis=-1, keepdims=True)
        r.gain_part[0:1] += jnp.sum(grad * ffn * inv, axis=0, keepdims=True)
        r.cot_buf[rows] = (inv * weighted - ffn * (inv * inv * inv) * mean).astype(bf16)
        return carry

    for which in range(2):
        c_near[which].wait_recv()
        c_on[which].wait_recv()
        lax.fori_loop(0, half // 32, functools.partial(last_rows, which), 0)
    keep_own = pltpu.make_async_copy(r.cot_buf, r.grad_ffn, r.keep_sem.at[9])
    keep_out = pltpu.make_async_copy(r.token_buf, r.output, r.keep_sem.at[10])
    keep_own.start()
    keep_out.start()
    for copy in b_starts[0] + b_starts[1] + list(b_on + c_far + c_near + c_on):
        copy.wait_send()
    for copy in keep + keep_block(far_halves) + [keep_two, keep_own, keep_out]:
        copy.wait()


def forward(collective_id, **args):
    f32, bf16 = jnp.float32, jnp.bfloat16
    given = types.SimpleNamespace(**args)
    local, width = given.tokens.shape
    tokens = 4 * local
    half = local // 2
    inner_width = given.w_down.shape[0]
    vmem, dma, shape = pltpu.VMEM, pltpu.SemaphoreType.DMA, jax.ShapeDtypeStruct
    outs = dict(
        grad_ffn=shape((local, width), bf16),
        hidden=shape((tokens, inner_width), bf16),
        gate=shape((tokens, inner_width), bf16),
        up=shape((tokens, inner_width), bf16),
        normed_two=shape((tokens, width), bf16),
        middle=shape((local, width), f32),
        attn_out=shape((local, width), f32),
        output=shape((local, width), bf16),
        gain_part=shape((8, width), f32),
    )
    scratch = dict(
        mixed_buf=vmem(given.mixed.shape, bf16),
        out_buf=vmem(given.w_out.shape, bf16),
        token_buf=vmem((local, width), bf16),
        cot_buf=vmem((local, width), bf16),
        gate_weight=vmem((width, inner_width), bf16),
        up_weight=vmem((width, inner_width), bf16),
        down_weight=vmem((inner_width, width), bf16),
        partial=vmem((tokens, width), bf16),
        passed=vmem((2, half, width), bf16),
        a_landed=vmem((6, half, width), bf16),
        c_landed=vmem((6, half, width), bf16),
        gains=vmem((8, width), f32),
        attn_buf=vmem((local, width), f32),
        middle_buf=vmem((local, width), f32),
        two_buf=vmem((tokens, width), bf16),
        hidden_buf=vmem((tokens, inner_width), bf16),
        gate_stage=vmem((local, inner_width), bf16),
        up_stage=vmem((local, inner_width), bf16),
        block=vmem((local, max(width, inner_width)), bf16),
        gate_wide=vmem((local, TILE), f32),
        up_wide=vmem((local, TILE), f32),
        load_sem=dma((7,)),
        keep_sem=dma((11,)),
        a_send=dma((6,)),
        a_recv=dma((6,)),
        b_send=dma((6,)),
        b_recv=dma((6,)),
        c_send=dma((6,)),
        c_recv=dma((6,)),
    )
    any_space = pl.BlockSpec(memory_space=pl.ANY)
    small = pl.BlockSpec(memory_space=pltpu.VMEM)
    results = pl.pallas_call(
        functools.partial(forward_kernel, tuple(args) + tuple(outs) + tuple(scratch)),
        out_shape=list(outs.values()),
        in_specs=[
            small if value.ndim == 1 else any_space
            for value in args.values()
        ],
        out_specs=[small if value.shape[0] <= 8 else any_space for value in outs.values()],
        scratch_shapes=list(scratch.values()),
        compiler_params=pltpu.CompilerParams(
            collective_id=collective_id, has_side_effects=True, vmem_limit_bytes=VMEM_LIMIT
        ),
        cost_estimate=pl.CostEstimate(
            flops=8 * tokens * width * inner_width, bytes_accessed=100 * 2**20, transcendentals=0
        ),
    )(*args.values())
    return types.SimpleNamespace(**dict(zip(outs, results)))


def attend_kernel(names, *refs):
    r = types.SimpleNamespace(**dict(zip(names, refs)))
    f32, bf16 = jnp.float32, jnp.bfloat16
    local, width = r.tokens.shape
    tokens, head_cols = r.qkv.shape
    part = r.w_query.shape[0]
    piece = part // 4
    half = local // 2
    weights = (r.w_query, r.w_key, r.w_value)
    sizes = [weight.shape[1] // 4 for weight in weights]
    starts = (0, sizes[0], sizes[0] + sizes[1])
    q_cols, k_cols = sizes[0], sizes[1]
    heads = q_cols // HEAD_SIZE
    block = min(TILE, tokens)
    n_blocks = tokens // block
    head_scale = HEAD_SIZE ** (-0.5)

    me, x_place, y_place, far_place = plane_places()
    others = (x_place, y_place, far_place)
    x_other, y_other = {"shard": x_place}, {"shard": y_place}
    place = lax.axis_index("rep")
    chip, core = place // 2, place % 2
    twin = {"rep": place + 1 - 2 * core}
    next_chip = {"rep": place + 2 - 4 * (chip % 2)}
    quarter = (chip % 2) * 2 + core
    next_quarter = (1 - chip % 2) * 2 + core

    load_tokens = pltpu.make_async_copy(r.tokens, r.token_buf, r.load_sem.at[0])
    load_heads = [
        pltpu.make_async_copy(
            weights[kind].at[:, pl.ds(pl.multiple_of(me * sizes[kind], 128), sizes[kind])],
            r.heads_buf.at[
                pl.ds(pl.multiple_of(me * part, 16), part), pl.ds(starts[kind], sizes[kind])
            ],
            r.load_sem.at[2 + kind],
        )
        for kind in range(3)
    ]
    load_tokens.start()
    for copy in load_heads:
        copy.start()

    def lookup(ident):
        found = jnp.full_like(ident, -1)
        for label in range(SEGS):
            found = jnp.where(ident == label, r.parents[0, label], found)
        return found

    ident = r.seg_ids[...]
    parent_one = lookup(ident)
    lanes = lax.broadcasted_iota(jnp.int32, ident.shape, 1)
    codes = jnp.where(ident < SEGS, ident, jnp.where(lanes == 3, -2, -1))
    codes = jnp.where(lanes == 1, parent_one, jnp.where(lanes == 2, lookup(parent_one), codes))
    info_rows = pl.ds(pl.multiple_of(me * local, 16), local)
    r.info_buf[info_rows] = codes.astype(f32).astype(bf16)
    r.gain[...] = r.attn_gain[...].astype(f32).reshape(1, width)

    barrier = pltpu.get_barrier_semaphore()
    for where in [{"shard": other} for other in others] + [twin, next_chip]:
        pl.semaphore_signal(barrier, inc=1, device_id=where, device_id_type=pl.DeviceIdType.MESH)
    pl.semaphore_wait(barrier, 5)

    def piece_rows(owner, which):
        return pl.ds(pl.multiple_of(owner * part + which * piece, 16), piece)

    fetch = [
        [
            remote(
                weights[kind].at[
                    pl.ds(pl.multiple_of(quarter * piece, 16), piece),
                    pl.ds(pl.multiple_of(other * sizes[kind], 128), sizes[kind]),
                ],
                r.heads_buf.at[piece_rows(me, quarter), pl.ds(starts[kind], sizes[kind])],
                r.fetch_send.at[i, kind], r.fetch_recv.at[i, kind], {"shard": other},
            )
            for kind in range(3)
        ]
        for i, other in enumerate(others)
    ]
    for i in (2, 0, 1):
        for copy in fetch[i]:
            copy.start()
    tell_info = [
        remote(
            r.info_buf.at[info_rows], r.info_buf.at[info_rows],
            r.info_send.at[i], r.info_recv.at[i], {"shard": other},
        )
        for i, other in enumerate(others)
    ]
    for copy in tell_info:
        copy.start()

    def pass_piece(i, which, where, index):
        ref = r.heads_buf.at[piece_rows(others[i], which)]
        return remote(ref, ref, r.pass_send.at[index, i], r.pass_recv.at[index, i], where)

    to_chip = [pass_piece(i, quarter, next_chip, 0) for i in range(3)]
    to_twin = [pass_piece(i, quarter, twin, 1) for i in range(3)]
    on_twin = [pass_piece(i, next_quarter, twin, 2) for i in range(3)]

    def half_rows(owner, which):
        return r.all_buf.at[pl.ds(pl.multiple_of(owner * local + which * half, 16), half)]

    def send(owner, which, index, where):
        ref = half_rows(owner, which)
        return remote(ref, ref, r.all_send.at[index], r.all_recv.at[index], where)

    own = [
        [send(me, which, 2 * which + i, where) for i, where in enumerate((x_other, y_other))]
        for which in range(2)
    ]
    on = (send(x_place, 0, 4, y_other), send(y_place, 1, 5, x_other))

    load_tokens.wait()

    def norm_rows(which, index, carry):
        rows = pl.ds(pl.multiple_of(which * half + index * 32, 16), 32)
        values = r.token_buf[rows].astype(f32)
        inv = lax.rsqrt(jnp.mean(values * values, axis=-1, keepdims=True) + norm_eps)
        r.all_buf[pl.ds(pl.multiple_of(me * local + which * half + index * 32, 16), 32)] = (
            values * inv * r.gain[...]
        ).astype(bf16)
        return carry

    for which in range(2):
        lax.fori_loop(0, half // 32, functools.partial(norm_rows, which), 0)
        for copy in own[which]:
            copy.start()

    for i in (2, 0, 1):
        for copy in fetch[i]:
            copy.wait_recv()
        to_chip[i].start()
        to_twin[i].start()
    own[0][0].wait_recv()
    on[0].start()
    own[1][1].wait_recv()
    on[1].start()
    for i in (2, 0, 1):
        to_chip[i].wait_recv()
        on_twin[i].start()

    for copy in tell_info:
        copy.wait_recv()
    r.key_info[...] = jnp.transpose(r.info_buf[...].astype(f32))[0:8]
    for copy in load_heads:
        copy.wait()
    for copy in to_twin + on_twin:
        copy.wait_recv()

    def project(owner):
        rows = pl.ds(pl.multiple_of(owner * local, 16), local)
        r.qkv_buf[rows] = dot_plain(r.all_buf[rows], r.heads_buf[...]).astype(bf16)

    project(me)
    own[1][0].wait_recv()
    project(x_place)
    own[0][1].wait_recv()
    project(y_place)
    for copy in on:
        copy.wait_recv()
    project(far_place)
    keep = [pltpu.make_async_copy(r.qkv_buf, r.qkv, r.keep_sem.at[0])]
    keep[0].start()

    def keep_item(item):
        head, rows = item // n_blocks, pl.ds((item % n_blocks) * block, block)
        slot = item % 2
        return [
            pltpu.make_async_copy(r.probs_stage.at[slot], r.probs.at[head, rows], r.stage_sem.at[slot, 0]),
            pltpu.make_async_copy(r.tanh_stage.at[slot], r.tanh.at[head, rows], r.stage_sem.at[slot, 1]),
        ]

    for item in range(heads * n_blocks):
        head, first, slot = item // n_blocks, (item % n_blocks) * block, item % 2
        limit = first + block
        columns = pl.ds(head * HEAD_SIZE, HEAD_SIZE)
        r.score[:, pl.ds(0, limit)] = dot_rows(
            r.qkv_buf[pl.ds(first, block), columns], r.qkv_buf[pl.ds(0, limit), pl.ds(q_cols, k_cols)]
        )
        if item >= 2:
            for copy in keep_item(item - 2):
                copy.wait()
        if limit < tokens:
            nothing = jnp.zeros((block, tokens - limit), f32)
            r.probs_stage[slot, :, pl.ds(limit, tokens - limit)] = nothing
            r.tanh_stage[slot, :, pl.ds(limit, tokens - limit)] = nothing

        def rows_of(index, carry, first=first, limit=limit, slot=slot):
            here = pl.ds(pl.multiple_of(index * 64, 64), 64)
            info = r.info_buf[pl.ds(pl.multiple_of(first + index * 64, 64), 64)].astype(f32)
            keys = r.key_info[3:4, pl.ds(0, limit)]
            query_at = lax.broadcasted_iota(jnp.int32, (64, limit), 0) + (first + index * 64)
            key_at = lax.broadcasted_iota(jnp.int32, (64, limit), 1)
            related = (keys == info[:, 0:1]) | (keys == info[:, 1:2]) | (keys == info[:, 2:3])
            visible = ((key_at <= query_at) & related) | (key_at == query_at)
            curve = jnp.tanh(r.score[here, pl.ds(0, limit)] * (head_scale / softcap))
            masked = jnp.where(visible, softcap * curve, -1e30)
            terms = jnp.exp(masked - jnp.max(masked, axis=-1, keepdims=True))
            probs = terms / jnp.sum(terms, axis=-1, keepdims=True)
            r.tanh_stage[slot, here, pl.ds(0, limit)] = curve
            r.probs_stage[slot, here, pl.ds(0, limit)] = probs
            r.probs_low[here, pl.ds(0, limit)] = probs.astype(bf16)
            return carry

        lax.fori_loop(0, block // 64, rows_of, 0)
        for copy in keep_item(item):
            copy.start()
        r.mixed_buf[pl.ds(first, block), columns] = dot_plain(
            r.probs_low[:, pl.ds(0, limit)],
            r.qkv_buf[pl.ds(0, limit), pl.ds(q_cols + k_cols, k_cols)],
        ).astype(bf16)

    keep.append(pltpu.make_async_copy(r.mixed_buf, r.mixed, r.keep_sem.at[1]))
    keep[1].start()

    wide = r.cols_buf.shape[1]
    for owner in range(4):

        @pl.when(me == owner)
        def _():
            def rows_of(index, carry):
                rows = pl.ds(pl.multiple_of(index * 64, 64), 64)
                some = r.all_buf[rows, owner * part : (owner + 1) * part]
                if wide > part:
                    some = jnp.concatenate((some, jnp.zeros((64, wide - part), bf16)), axis=1)
                r.cols_buf[rows] = some
                return carry

            lax.fori_loop(0, tokens // 64, rows_of, 0)

    keep.append(pltpu.make_async_copy(r.cols_buf, r.normed_cols, r.keep_sem.at[2]))
    keep[2].start()
    for group in fetch + own:
        for copy in group:
            copy.wait_send()
    for copy in list(on) + tell_info + to_chip + to_twin + on_twin:
        copy.wait_send()
    last = heads * n_blocks
    for item in range(max(0, last - 2), last):
        for copy in keep_item(item):
            copy.wait()
    for copy in keep:
        copy.wait()


def attend(collective_id, **args):
    f32, bf16 = jnp.float32, jnp.bfloat16
    given = types.SimpleNamespace(**args)
    local, width = given.tokens.shape
    tokens = 4 * local
    part = given.w_query.shape[0]
    part_wide = -(-part // PAIR) * PAIR
    q_cols, k_cols = given.w_query.shape[1] // 4, given.w_key.shape[1] // 4
    head_cols = q_cols + 2 * k_cols
    heads = q_cols // HEAD_SIZE
    block = min(TILE, tokens)
    vmem, dma, shape = pltpu.VMEM, pltpu.SemaphoreType.DMA, jax.ShapeDtypeStruct
    outs = dict(
        qkv=shape((tokens, head_cols), bf16),
        mixed=shape((tokens, q_cols), bf16),
        probs=shape((heads, tokens, tokens), f32),
        tanh=shape((heads, tokens, tokens), f32),
        normed_cols=shape((tokens, part_wide), bf16),
    )
    scratch = dict(
        token_buf=vmem((local, width), bf16),
        all_buf=vmem((tokens, width), bf16),
        heads_buf=vmem((width, head_cols), bf16),
        info_buf=vmem((tokens, 128), bf16),
        key_info=vmem((8, tokens), f32),
        gain=vmem((1, width), f32),
        qkv_buf=vmem((tokens, head_cols), bf16),
        mixed_buf=vmem((tokens, q_cols), bf16),
        cols_buf=vmem((tokens, part_wide), bf16),
        score=vmem((block, tokens), f32),
        probs_stage=vmem((2, block, tokens), f32),
        tanh_stage=vmem((2, block, tokens), f32),
        probs_low=vmem((block, tokens), bf16),
        load_sem=dma((5,)),
        keep_sem=dma((3,)),
        stage_sem=dma((2, 2)),
        fetch_send=dma((3, 3)),
        fetch_recv=dma((3, 3)),
        info_send=dma((3,)),
        info_recv=dma((3,)),
        pass_send=dma((3, 3)),
        pass_recv=dma((3, 3)),
        all_send=dma((6,)),
        all_recv=dma((6,)),
    )
    any_space = pl.BlockSpec(memory_space=pl.ANY)
    small = pl.BlockSpec(memory_space=pltpu.VMEM)
    results = pl.pallas_call(
        functools.partial(attend_kernel, tuple(args) + tuple(outs) + tuple(scratch)),
        out_shape=list(outs.values()),
        in_specs=[
            pl.BlockSpec(memory_space=pltpu.SMEM) if value.shape[0] == 1
            else small if value.ndim == 1 or value.shape[1] == 128 else any_space
            for value in args.values()
        ],
        out_specs=[any_space] * len(outs),
        scratch_shapes=list(scratch.values()),
        compiler_params=pltpu.CompilerParams(
            collective_id=collective_id, has_side_effects=True, vmem_limit_bytes=VMEM_LIMIT
        ),
        cost_estimate=pl.CostEstimate(
            flops=4 * tokens * width * head_cols, bytes_accessed=100 * 2**20, transcendentals=0
        ),
    )(*args.values())
    return types.SimpleNamespace(**dict(zip(outs, results)))


QUERY_HEADS = 8
KV = 4
HEAD_SIZE = 256
SEGS = 13


softcap = 50.0
norm_eps = 1e-06


def normalize(values, gain_vec):
    inv_rms = lax.rsqrt(jnp.mean(values * values, axis=-1, keepdims=True) + norm_eps)
    return (values * inv_rms * gain_vec, inv_rms)


def norm_back(values, inv_rms, gain_vec, grad_in):
    weighted = grad_in * gain_vec
    row_mean = jnp.mean(weighted * values, axis=-1, keepdims=True)
    grad_back = inv_rms * weighted - values * (inv_rms * inv_rms * inv_rms) * row_mean
    return (grad_back, jnp.sum(grad_in * values * inv_rms, axis=0))


def geglu(gate_pre, up_pre):
    return jax.nn.gelu(gate_pre, approximate=True) * up_pre


def gather_rows(block):
    return lax.all_gather(block, "shard", axis=0, tiled=True)


def scatter_rows(partial):
    summed = lax.psum_scatter(partial, "shard", scatter_dimension=0, tiled=True)
    return summed.astype(jnp.float32)


def exchange(blocks):
    return lax.all_to_all(blocks, "shard", 0, 0, tiled=True)


def first_gather(normed, seg_ids, w_query, w_key, w_value):
    n = lax.axis_size("shard")
    width = normed.shape[1]
    part_rows = w_query.shape[0]
    share = max(1, n // KV)

    def by_device(weight):
        heads = weight.reshape(part_rows, KV, -1)
        if share > 1:
            heads = jnp.repeat(heads, share, axis=1)
        return heads.reshape(part_rows, n, -1)

    parts = jnp.concatenate(
        (w_query.reshape(part_rows, n, -1), by_device(w_key), by_device(w_value)), axis=2
    ).transpose(1, 0, 2)
    heads = exchange(parts).reshape(width, -1)
    codes = gather_rows(seg_ids.astype(jnp.bfloat16))
    return gather_rows(normed), codes.astype(jnp.int32), heads


def rep_sum(grads, width):
    summed = chain_sum([grad.astype(jnp.bfloat16).reshape(-1, width) for grad in grads])
    return [
        total.reshape(grad.shape).astype(jnp.float32) for total, grad in zip(summed, grads)
    ]


def plane_layer(
    tokens, seg_ids, parents, attn_gain, w_query, w_key, w_value, w_out, post_attn_gain,
    ffn_gain, w_gate, w_up, w_down, post_ffn_gain, cotangent,
):
    f32 = jnp.float32
    heads = attend(
        2,
        tokens=tokens,
        attn_gain=attn_gain,
        seg_ids=jnp.broadcast_to(seg_ids[:, None], (tokens.shape[0], 128)),
        parents=parents,
        w_query=w_query,
        w_key=w_key,
        w_value=w_value,
    )
    gains = dict(
        attn_gain=attn_gain,
        post_attn_gain=post_attn_gain,
        ffn_gain=ffn_gain,
        post_ffn_gain=post_ffn_gain,
    )
    ahead = forward(
        3,
        mixed=heads.mixed,
        w_out=w_out,
        tokens=tokens,
        cotangent=cotangent,
        **gains,
        w_gate=w_gate,
        w_up=w_up,
        w_down=w_down,
    )
    found = backward(
        4,
        grad_ffn=ahead.grad_ffn,
        hidden=ahead.hidden,
        gate=ahead.gate,
        up=ahead.up,
        normed_two=ahead.normed_two,
        w_down=w_down,
        w_gate=w_gate,
        w_up=w_up,
        w_out=w_out,
        middle=ahead.middle,
        attn_out=ahead.attn_out,
        cotangent=cotangent,
        **gains,
        gain_parts=ahead.gain_part,
        qkv=heads.qkv,
        mixed=heads.mixed,
        probs=heads.probs,
        tanh=heads.tanh,
        normed_cols=heads.normed_cols,
        w_query=w_query,
        w_key=w_key,
        w_value=w_value,
        tokens=tokens,
    )
    gain_sums = found.gain_sums
    return (
        ahead.output,
        found.grad_tokens,
        gain_sums[3],
        found.query_sum.astype(f32),
        found.key_sum.astype(f32),
        found.value_sum.astype(f32),
        found.out_sum.astype(f32),
        gain_sums[1],
        gain_sums[2],
        found.gate_sum.astype(f32),
        found.up_sum.astype(f32),
        found.down_sum.astype(f32),
        gain_sums[0],
    )


def body(
    tokens,
    seg_ids,
    parents,
    attn_gain,
    w_query,
    w_key,
    w_value,
    w_out,
    post_attn_gain,
    ffn_gain,
    w_gate,
    w_up,
    w_down,
    post_ffn_gain,
    cotangent,
):
    if lax.axis_size("shard") == 4 and lax.axis_size("rep") == 8:
        return plane_layer(
            tokens, seg_ids, parents, attn_gain, w_query, w_key, w_value, w_out, post_attn_gain,
            ffn_gain, w_gate, w_up, w_down, post_ffn_gain, cotangent,
        )
    f32, bf16 = jnp.float32, jnp.bfloat16
    tok_rows, width = tokens.shape
    n = lax.axis_size("shard")
    me = lax.axis_index("shard")
    group_rows = tok_rows * n
    part_rows = w_query.shape[0]
    head_scale = HEAD_SIZE ** (-0.5)
    q_heads = QUERY_HEADS // n
    kv_heads = max(1, KV // n)
    share = n * kv_heads // KV
    repeat = q_heads // kv_heads
    q_cols = q_heads * HEAD_SIZE
    k_cols = kv_heads * HEAD_SIZE
    gain_one = attn_gain.astype(f32)
    gain_two = post_attn_gain.astype(f32)
    gain_three = ffn_gain.astype(f32)
    gain_four = post_ffn_gain.astype(f32)

    residual = tokens.astype(f32)
    normed, rms_one = normalize(residual, gain_one)
    normed_all, codes, qkv_heads = first_gather(
        normed.astype(bf16), seg_ids, w_query, w_key, w_value
    )
    qkv = jnp.dot(normed_all, qkv_heads, preferred_element_type=f32).astype(bf16)
    queries = qkv[:, :q_cols].reshape(group_rows, kv_heads, repeat, HEAD_SIZE)
    keys = qkv[:, q_cols : q_cols + k_cols].reshape(group_rows, kv_heads, HEAD_SIZE)
    values = qkv[:, q_cols + k_cols :].reshape(group_rows, kv_heads, HEAD_SIZE)

    parent_row = parents[0]
    labels = jnp.arange(SEGS)

    def lookup(ident):
        return jnp.sum(jnp.where(ident[:, None] == labels[None, :], parent_row[None, :], 0), axis=1)

    parent_one = lookup(codes)
    parent_two = lookup(parent_one)
    positions = jnp.arange(group_rows)
    real = codes < SEGS
    related = (
        (codes[None, :] == codes[:, None])
        | (codes[None, :] == parent_one[:, None])
        | (codes[None, :] == parent_two[:, None])
    )
    visible = (positions[None, :] <= positions[:, None]) & real[:, None] & real[
        None, :
    ] & related | (positions[None, :] == positions[:, None])

    score_matrix = jnp.einsum("tkrh,skh->krts", queries, keys, preferred_element_type=f32)
    tanh_part = jnp.tanh(score_matrix * (head_scale / softcap))
    masked = jnp.where(visible[None, None], softcap * tanh_part, -1e30)
    row_max = jnp.max(masked, axis=-1, keepdims=True)
    expo_terms = jnp.exp(masked - row_max)
    row_total = jnp.sum(expo_terms, axis=-1, keepdims=True)
    probs = expo_terms / row_total
    probs_b = probs.astype(bf16)
    mixed = jnp.einsum("krts,skh->tkrh", probs_b, values, preferred_element_type=f32)
    mixed = mixed.reshape(group_rows, q_cols).astype(bf16)
    attn_out = scatter_rows(jnp.dot(mixed, w_out, preferred_element_type=f32).astype(bf16))
    post_one, rms_two = normalize(attn_out, gain_two)
    middle = residual + post_one
    normed_two, rms_three = normalize(middle, gain_three)
    normed_two_all = gather_rows(normed_two.astype(bf16))
    gate_pre = jnp.dot(normed_two_all, w_gate, preferred_element_type=f32)
    up_pre = jnp.dot(normed_two_all, w_up, preferred_element_type=f32)
    hidden, geglu_back = jax.vjp(geglu, gate_pre, up_pre)
    hidden_b = hidden.astype(bf16)
    ffn_out = scatter_rows(jnp.dot(hidden_b, w_down, preferred_element_type=f32).astype(bf16))
    post_two, rms_four = normalize(ffn_out, gain_four)
    output = (middle + post_two).astype(bf16)

    grad_out = cotangent.astype(f32)
    grad_ffn, grad_gain_four = norm_back(ffn_out, rms_four, gain_four, grad_out)
    grad_ffn_all = gather_rows(grad_ffn.astype(bf16))
    down_part = jnp.einsum("tf,td->fd", hidden_b, grad_ffn_all, preferred_element_type=f32)
    grad_hidden = jnp.einsum("td,fd->tf", grad_ffn_all, w_down, preferred_element_type=f32)
    grad_gate, grad_up = geglu_back(grad_hidden)
    grad_gate_b = grad_gate.astype(bf16)
    grad_up_b = grad_up.astype(bf16)
    grad_normed_two = jnp.einsum("tf,df->td", grad_gate_b, w_gate, preferred_element_type=f32)
    grad_normed_two += jnp.einsum("tf,df->td", grad_up_b, w_up, preferred_element_type=f32)
    grad_normed_two = scatter_rows(grad_normed_two.astype(bf16))
    gate_part = jnp.einsum("td,tf->df", normed_two_all, grad_gate_b, preferred_element_type=f32)
    up_part = jnp.einsum("td,tf->df", normed_two_all, grad_up_b, preferred_element_type=f32)
    grad_middle_part, grad_gain_three = norm_back(middle, rms_three, gain_three, grad_normed_two)
    grad_middle = grad_out + grad_middle_part
    grad_attn, grad_gain_two = norm_back(attn_out, rms_two, gain_two, grad_middle)
    grad_attn_all = gather_rows(grad_attn.astype(bf16))
    out_part = jnp.einsum("tj,td->jd", mixed, grad_attn_all, preferred_element_type=f32)
    grad_mixed = jnp.einsum("td,jd->tj", grad_attn_all, w_out, preferred_element_type=f32)
    grad_mixed = grad_mixed.astype(bf16).reshape(group_rows, kv_heads, repeat, HEAD_SIZE)
    grad_probs = jnp.einsum("tkrh,skh->krts", grad_mixed, values, preferred_element_type=f32)
    row_inner = jnp.sum(probs * grad_probs, axis=-1, keepdims=True)
    grad_dots = (
        probs * (grad_probs - row_inner) * (1.0 - tanh_part * tanh_part) * head_scale
    ).astype(bf16)
    grad_queries = jnp.einsum("krts,skh->tkrh", grad_dots, keys, preferred_element_type=f32)
    grad_keys = jnp.einsum("krts,tkrh->skh", grad_dots, queries, preferred_element_type=f32)
    grad_values = jnp.einsum("krts,tkrh->skh", probs_b, grad_mixed, preferred_element_type=f32)
    grad_parts = jnp.concatenate(
        (
            grad_queries.reshape(group_rows, q_cols),
            grad_keys.reshape(group_rows, k_cols),
            grad_values.reshape(group_rows, k_cols),
        ),
        axis=1,
    ).astype(bf16)
    grad_parts = gather_rows(grad_parts).reshape(n, group_rows, -1)

    def whole_heads(parts):
        if share > 1:
            parts = parts.reshape(KV, share, group_rows, HEAD_SIZE).astype(f32).sum(axis=1).astype(bf16)
        return parts.transpose(1, 0, 2).reshape(group_rows, -1)

    grad_qkv = jnp.concatenate(
        (
            grad_parts[:, :, :q_cols].transpose(1, 0, 2).reshape(group_rows, -1),
            whole_heads(grad_parts[:, :, q_cols : q_cols + k_cols]),
            whole_heads(grad_parts[:, :, q_cols + k_cols :]),
        ),
        axis=1,
    )
    qkv_local = jnp.concatenate((w_query, w_key, w_value), axis=1)
    grad_normed = jnp.einsum("tj,dj->td", grad_qkv, qkv_local, preferred_element_type=f32)
    grad_normed = exchange(grad_normed.astype(bf16).reshape(n, tok_rows, part_rows))
    grad_normed = grad_normed.transpose(1, 0, 2).reshape(tok_rows, width).astype(f32)
    normed_cols = lax.dynamic_slice_in_dim(normed_all, me * part_rows, part_rows, axis=1)
    qkv_part = jnp.einsum("td,tj->dj", normed_cols, grad_qkv, preferred_element_type=f32)
    grad_resid_part, grad_gain_one = norm_back(residual, rms_one, gain_one, grad_normed)
    grad_tokens = (grad_middle + grad_resid_part).astype(bf16)
    gain_parts = jnp.stack((grad_gain_one, grad_gain_two, grad_gain_three, grad_gain_four))
    gain_sums = lax.all_gather(gain_parts, ("rep", "shard"), axis=0).sum(axis=0)
    down_sum, gate_sum, up_sum, out_sum, qkv_sum = rep_sum(
        (down_part, gate_part, up_part, out_part, qkv_part), width
    )
    q_width = w_query.shape[1]
    k_width = w_key.shape[1]
    return (
        output,
        grad_tokens,
        gain_sums[0],
        qkv_sum[:, :q_width],
        qkv_sum[:, q_width : q_width + k_width],
        qkv_sum[:, q_width + k_width :],
        out_sum,
        gain_sums[1],
        gain_sums[2],
        gate_sum,
        up_sum,
        down_sum,
        gain_sums[3],
    )


def solution(mesh):
    return jax.shard_map(
        body,
        mesh=mesh,
        in_specs=(
            P(("rep", "shard"), None),
            P(("rep", "shard")),
            P("rep", None),
            P(),
            P("shard", None),
            P("shard", None),
            P("shard", None),
            P("shard", None),
            P(),
            P(),
            P(None, "shard"),
            P(None, "shard"),
            P("shard", None),
            P(),
            P(("rep", "shard"), None),
        ),
        out_specs=(
            P(("rep", "shard"), None),
            P(("rep", "shard"), None),
            P(),
            P("shard", None),
            P("shard", None),
            P("shard", None),
            P("shard", None),
            P(),
            P(),
            P(None, "shard"),
            P(None, "shard"),
            P("shard", None),
            P(),
        ),
        check_vma=False,
    )
```

```python
import functools
import math
import types

import jax
import jax.numpy as jnp
from jax import lax
from jax.experimental import pallas as pl
from jax.experimental.pallas import tpu as pltpu
from jax.sharding import PartitionSpec as P

SLOTS = 8
CHUNK = 64


def remote(src, dst, send_sem, recv_sem, where):
    return pltpu.make_async_remote_copy(
        src_ref=src,
        dst_ref=dst,
        send_sem=send_sem,
        recv_sem=recv_sem,
        device_id=where,
        device_id_type=pl.DeviceIdType.MESH,
    )


def add_low(left, right):
    return (left.astype(jnp.float32) + right.astype(jnp.float32)).astype(jnp.bfloat16)


def chain_kernel(counts, chunk, *refs):
    jobs = len(counts)
    ins, outs = refs[:jobs], refs[jobs : 2 * jobs]
    (
        mine, sib, acc, outer_in, inner_in, total,
        load_sem, sib_send, sib_recv, up_send, outer_recv, inner_recv,
        down_send, pair_send, pair_recv, store_sem,
        sib_credit, up_credit, down_credit,
    ) = refs[2 * jobs :]
    slots = mine.shape[0]
    steps = sum(counts)
    place = lax.axis_index("rep")
    chips = lax.axis_size("rep") // 2
    chip, core = place // 2, place % 2
    left = chip < chips // 2
    is_end = (chip == 0) | (chip == chips - 1)
    is_mid = (chip == chips // 2 - 1) | (chip == chips // 2)
    twin = {"rep": place + 1 - 2 * core}
    inner = {"rep": jnp.where(left, place + 2, place - 2)}
    outer = {"rep": jnp.where(is_end, place, jnp.where(left, place - 2, place + 2))}

    def tell(sem, where):
        pl.semaphore_signal(sem, inc=1, device_id=where, device_id_type=pl.DeviceIdType.MESH)

    barrier = pltpu.get_barrier_semaphore()
    tell(barrier, twin)
    tell(barrier, inner)

    @pl.when(is_end)
    def _():
        pl.semaphore_wait(barrier, 2)

    @pl.when(jnp.logical_not(is_end))
    def _():
        tell(barrier, outer)
        pl.semaphore_wait(barrier, 3)

    def with_rows(step, which, use):
        low = 0
        for job, count in enumerate(counts):
            first = low

            @pl.when((step >= low) & (step < low + count))
            def _():
                row = pl.multiple_of(((step - first) * 2 + which) * chunk, chunk)
                use(job, pl.ds(row, chunk))

            low += count

    def pair_copy(job, rows, slot, step):
        return remote(total.at[slot], outs[job].at[rows], pair_send.at[slot], pair_recv.at[step], twin)

    def up_copy(slot, dst, sem):
        return remote(acc.at[slot], dst.at[slot], up_send.at[slot], sem.at[slot], inner)

    def down_copy(slot):
        return remote(total.at[slot], inner_in.at[slot], down_send.at[slot], inner_recv.at[slot], outer)

    def sib_copy(job, rows, slot):
        return remote(ins[job].at[rows], sib.at[slot], sib_send.at[slot], sib_recv.at[slot], twin)

    def load_copy(job, rows, slot):
        return pltpu.make_async_copy(ins[job].at[rows], mine.at[slot], load_sem.at[slot])

    def store_copy(job, rows, slot):
        return pltpu.make_async_copy(total.at[slot], outs[job].at[rows], store_sem.at[slot])

    some = pl.ds(0, chunk)

    def take(step):
        slot = step % slots

        @pl.when(step >= slots)
        def _():
            pl.semaphore_wait(sib_credit, 1)

        with_rows(step, 1 - core, lambda job, rows: sib_copy(job, rows, slot).start())
        with_rows(step, core, lambda job, rows: load_copy(job, rows, slot).start())

    def send_up(step):
        slot = step % slots

        @pl.when(step >= slots)
        def _():
            pl.semaphore_wait(up_credit, 1)

        @pl.when(is_mid)
        def _():
            up_copy(slot, inner_in, inner_recv).start()

        @pl.when(jnp.logical_not(is_mid))
        def _():
            up_copy(slot, outer_in, outer_recv).start()

    def pair_up(step):
        slot = step % slots
        load_copy(0, some, slot).wait()
        sib_copy(0, some, slot).wait()

        @pl.when(step >= slots)
        def _():
            up_copy(slot, outer_in, outer_recv).wait_send()

        acc[slot] = add_low(mine[slot], sib[slot])

        @pl.when(step + slots < steps)
        def _():
            tell(sib_credit, twin)

        @pl.when(is_end)
        def _():
            send_up(step)

    def from_outer(step):
        slot = step % slots
        up_copy(slot, outer_in, outer_recv).wait_recv()
        acc[slot] = add_low(acc[slot], outer_in[slot])

        @pl.when(step + slots < steps)
        def _():
            tell(up_credit, outer)

        send_up(step)

    def sends_done(slot):
        pair_copy(0, some, slot, 0).wait_send()
        store_copy(0, some, slot).wait()

        @pl.when(jnp.logical_not(is_end))
        def _():
            down_copy(slot).wait_send()

    def from_inner(step):
        slot = step % slots
        down_copy(slot).wait_recv()

        @pl.when(step >= slots)
        def _():
            sends_done(slot)

        @pl.when(is_mid)
        def _():
            total[slot] = add_low(acc[slot], inner_in[slot])

            @pl.when(step + slots < steps)
            def _():
                tell(up_credit, inner)

        @pl.when(jnp.logical_not(is_mid))
        def _():
            total[slot] = inner_in[slot]

            @pl.when(step + slots < steps)
            def _():
                tell(down_credit, inner)

        @pl.when(jnp.logical_not(is_end))
        def _():
            @pl.when(step >= slots)
            def _():
                pl.semaphore_wait(down_credit, 1)

            down_copy(slot).start()

        with_rows(step, core, lambda job, rows: pair_copy(job, rows, slot, step).start())
        with_rows(step, core, lambda job, rows: store_copy(job, rows, slot).start())

    lag_outer = 3
    lag_inner = jnp.where(is_end, 8, 6)

    def tick(step, carry):
        @pl.when(step < steps)
        def _():
            take(step)

        @pl.when((step >= 1) & (step - 1 < steps))
        def _():
            pair_up(step - 1)

        @pl.when(jnp.logical_not(is_end) & (step >= lag_outer) & (step - lag_outer < steps))
        def _():
            from_outer(step - lag_outer)

        @pl.when((step >= lag_inner) & (step - lag_inner < steps))
        def _():
            from_inner(step - lag_inner)

        return carry

    lax.fori_loop(0, steps + 8, tick, 0)

    def finish(step, carry):
        slot = step % slots
        sends_done(slot)
        up_copy(slot, outer_in, outer_recv).wait_send()
        return carry

    lax.fori_loop(steps - slots, steps, finish, 0)

    def arrived(step, carry):
        pair_copy(0, some, 0, step).wait_recv()
        return carry

    lax.fori_loop(0, steps, arrived, 0)


def chain_sum(parts, chunk=CHUNK, collective_id=1):
    width = parts[0].shape[1]
    counts = tuple(part.shape[0] // (2 * chunk) for part in parts)
    steps = sum(counts)
    slots = min(SLOTS, steps)
    any_space = pl.BlockSpec(memory_space=pl.ANY)
    block = pltpu.VMEM((slots, chunk, width), jnp.bfloat16)
    sems = pltpu.SemaphoreType.DMA((slots,))
    credit = pltpu.SemaphoreType.REGULAR
    return pl.pallas_call(
        functools.partial(chain_kernel, counts, chunk),
        out_shape=[jax.ShapeDtypeStruct(part.shape, part.dtype) for part in parts],
        in_specs=[any_space] * len(parts),
        out_specs=[any_space] * len(parts),
        scratch_shapes=[block] * 6
        + [sems] * 8
        + [pltpu.SemaphoreType.DMA((steps,)), sems, credit, credit, credit],
        compiler_params=pltpu.CompilerParams(
            collective_id=collective_id, has_side_effects=True, vmem_limit_bytes=48 * 1024 * 1024
        ),
        cost_estimate=pl.CostEstimate(
            flops=0, bytes_accessed=8 * sum(part.size for part in parts), transcendentals=0
        ),
    )(*parts)


def plane_places():
    me = lax.axis_index("shard")
    x_other = me + 1 - 2 * (me % 2)
    y_other = (me + 2) % 4
    far = x_other + y_other - me
    return me, x_other, y_other, far


def greet(places):
    barrier = pltpu.get_barrier_semaphore()
    for place in places:
        pl.semaphore_signal(
            barrier, inc=1, device_id={"shard": place}, device_id_type=pl.DeviceIdType.MESH
        )
    pl.semaphore_wait(barrier, len(places))


TILE = 256
PAIR = 2 * CHUNK
LINE = 32
DEEP = 10
LAST = 6
ROOT_TWO_PI = math.sqrt(2.0 / math.pi)


def dot_rows(left, right):
    return lax.dot_general(left, right, (((1,), (1,)), ((), ())), preferred_element_type=jnp.float32)


def dot_plain(left, right):
    return lax.dot_general(left, right, (((1,), (0,)), ((), ())), preferred_element_type=jnp.float32)


def dot_columns(left, right):
    return lax.dot_general(left, right, (((0,), (0,)), ((), ())), preferred_element_type=jnp.float32)


def column_pieces(width):
    return 3 if width % 384 == 0 else 2


def backward_kernel(dims, names, *refs):
    r = types.SimpleNamespace(**dict(zip(names, refs)))
    tokens, local, width, inner_width, head_cols = dims
    f32, bf16 = jnp.float32, jnp.bfloat16
    half = local // 2
    q_cols = head_cols // 2
    k_cols = head_cols // 4
    heads = q_cols // HEAD_SIZE
    part = width // 4
    part_wide = r.normed_cols.shape[1]
    side = 2 * head_cols
    n_a = inner_width // TILE
    n_b = width // TILE
    block = min(TILE, tokens)
    n_blocks = tokens // block
    pieces = column_pieces(width)
    piece = width // pieces
    group = PAIR * pieces

    counts = (
        inner_width // PAIR, width // PAIR, width // PAIR, r.w_out.shape[0] // PAIR,
        part // (2 * LINE),
    )
    first = [sum(counts[:job]) for job in range(6)]
    units = first[5]
    steps = 2 * units
    a_at = pieces + 1
    b_at = a_at + (n_a + 1) // 2
    c_at = b_at + n_b
    d_at = c_at + 6
    f_at = d_at + 7
    g_at = f_at + 1
    h_at = g_at + heads * n_blocks
    i_at = h_at + 10
    k_at = i_at + n_blocks + 2
    assert b_at <= first[1] and f_at < first[3] and i_at < first[4] and first[1] <= i_at
    assert first[2] <= i_at and k_at + 5 <= units + 5 and counts[0] // pieces >= 2

    place = lax.axis_index("rep")
    chips = lax.axis_size("rep") // 2
    chip, core = place // 2, place % 2
    left = chip < chips // 2
    is_end = (chip == 0) | (chip == chips - 1)
    is_mid = (chip == chips // 2 - 1) | (chip == chips // 2)
    twin = {"rep": place + 1 - 2 * core}
    inner = {"rep": jnp.where(left, place + 2, place - 2)}
    outer = {"rep": jnp.where(is_end, place, jnp.where(left, place - 2, place + 2))}
    next_chip = {"rep": place + 2 - 4 * (chip % 2)}
    far_chip = {"rep": (place + 4) % 8}
    me, x_place, y_place, far_place = plane_places()
    x_other, y_other = {"shard": x_place}, {"shard": y_place}
    plane = [{"shard": (me + step) % 4} for step in (1, 2, 3)]

    def tell(sem, where):
        pl.semaphore_signal(sem, inc=1, device_id=where, device_id_type=pl.DeviceIdType.MESH)

    def load(src, dst, index):
        return pltpu.make_async_copy(src, dst, r.load_sem.at[index])

    load_ffn = load(
        r.grad_ffn,
        r.ffn_buf.at[pl.ds(pl.multiple_of(me * local, 16), local), pl.ds(0, width)], 0,
    )
    load_hidden = load(r.hidden, r.hidden_buf.at[:, pl.ds(0, inner_width)], 1)
    load_two = load(r.normed_two, r.two_buf, 2)
    load_small = (
        load(r.middle, r.middle_buf, 3),
        load(r.attn_out, r.attn_buf, 4),
        load(r.cotangent, r.cot_buf, 5),
        load(r.qkv, r.qkv_buf, 6),
        load(r.mixed, r.mixed_buf, 7),
        load(r.normed_cols, r.cols_buf, 8),
        load(r.tokens, r.token_buf, 9),
    )

    def weight_tile(index):
        return r.weights.at[pl.ds(pl.multiple_of(index * TILE, TILE), TILE)]

    def a_loads(tile, buf):
        rows = pl.ds(pl.multiple_of(tile * TILE, TILE), TILE)
        return (
            load(r.w_down.at[rows], weight_tile(buf).at[:, pl.ds(0, width)], 10 + buf),
            load(r.gate.at[:, rows], r.gate_buf.at[buf], 12 + buf),
            load(r.up.at[:, rows], r.up_buf.at[buf], 14 + buf),
        )

    def b_loads(tile):
        rows = pl.ds(pl.multiple_of(tile * TILE, TILE), TILE)
        buf = 2 - 2 * (tile % 2)
        sem = 16 + 2 * (tile % 2)
        return (
            load(r.w_gate.at[rows], weight_tile(buf).at[:, pl.ds(0, inner_width)], sem),
            load(r.w_up.at[rows], weight_tile(buf + 1).at[:, pl.ds(0, inner_width)], sem + 1),
        )

    def b_store(tile):
        columns = pl.ds(pl.multiple_of(tile * TILE, TILE), TILE)
        return pltpu.make_async_copy(
            r.stage.at[tile % 2], r.partial.at[:, columns], r.stage_sem.at[tile % 2]
        )

    for index, gain in enumerate((r.post_attn_gain, r.ffn_gain, r.post_ffn_gain, r.attn_gain)):
        r.gains[index : index + 1] = gain[...].astype(jnp.float32).reshape(1, gain.shape[0])
    load_ffn.start()
    load_hidden.start()
    for buf in range(2):
        for copy in a_loads(buf, buf):
            copy.start()
    load_two.start()
    for copy in load_small:
        copy.start()
    for copy in b_loads(0):
        copy.start()

    barrier = pltpu.get_barrier_semaphore()
    for where in [twin, inner, far_chip] + plane:
        tell(barrier, where)

    @pl.when(is_end)
    def _():
        pl.semaphore_wait(barrier, 6)

    @pl.when(jnp.logical_not(is_end))
    def _():
        tell(barrier, outer)
        pl.semaphore_wait(barrier, 7)

    def ffn_copies(index):
        across = pl.ds(index * piece, piece)

        def send(owner, which, at, where, own):
            here = pl.ds(pl.multiple_of(owner * local + which * half, 16), half)
            src = r.grad_ffn.at[pl.ds(which * half, half), across]
            return remote(
                src if own else r.ffn_buf.at[here, across], r.ffn_buf.at[here, across],
                r.ffn_send.at[index, at], r.ffn_recv.at[index, at], where,
            )

        starts = (
            send(me, 0, 0, x_other, True), send(me, 1, 1, y_other, True),
            send(me, 1, 2, x_other, True), send(me, 0, 3, y_other, True),
        )
        return starts, (send(x_place, 0, 4, y_other, False), send(y_place, 1, 5, x_other, False))

    ffn_pieces = [ffn_copies(index) for index in range(pieces)]

    def ffn_pass(index):
        starts, passes = ffn_pieces[index]
        for i in range(2):
            starts[i].wait_recv()
            passes[i].start()

    def ffn_arrived(index):
        starts, passes = ffn_pieces[index]
        for copy in starts[2:] + passes:
            copy.wait_recv()

    def ffn_sent():
        for starts, passes in ffn_pieces:
            for copy in starts + passes:
                copy.wait_send()

    for copy in ffn_pieces[0][0]:
        copy.start()
    ffn_pass(0)
    for starts, _ in ffn_pieces[1:]:
        for copy in starts:
            copy.start()
    load_ffn.wait()
    load_hidden.wait()
    ffn_arrived(0)

    def a_tile(tile, buf):
        for copy in a_loads(tile, buf):
            copy.wait()
        r.wide[...] = dot_rows(r.ffn_buf[:, pl.ds(0, width)], weight_tile(buf)[:, pl.ds(0, width)])
        columns = pl.ds(pl.multiple_of(tile * TILE, TILE), TILE)

        def rows_of(index, carry):
            rows = pl.ds(pl.multiple_of(index * 128, 128), 128)
            grad = r.wide[rows]
            gate = r.gate_buf[buf, rows].astype(f32)
            up = r.up_buf[buf, rows].astype(f32)
            curve = jnp.tanh(ROOT_TWO_PI * (gate + 0.044715 * gate * gate * gate))
            slope = (1.0 - curve * curve) * (ROOT_TWO_PI * (1.0 + 3.0 * 0.044715 * gate * gate))
            gelu_slope = 0.5 * (1.0 + curve) + 0.5 * gate * slope
            r.gate_grad[rows, columns] = (grad * up * gelu_slope).astype(bf16)
            r.up_grad[rows, columns] = (grad * (0.5 * gate * (1.0 + curve))).astype(bf16)
            return carry

        lax.fori_loop(0, tokens // 128, rows_of, 0)

        @pl.when(tile + 2 < n_a)
        def _():
            for copy in a_loads(tile + 2, buf):
                copy.start()

    def b_tile(tile):
        for copy in b_loads(tile):
            copy.wait()

        @pl.when(tile >= 2)
        def _():
            b_store(tile - 2).wait()

        buf = 2 - 2 * (tile % 2)
        some = dot_rows(r.gate_grad[:, pl.ds(0, inner_width)], weight_tile(buf)[:, pl.ds(0, inner_width)])
        some += dot_rows(r.up_grad[...], weight_tile(buf + 1)[:, pl.ds(0, inner_width)])
        r.stage[tile % 2] = some.astype(bf16)
        b_store(tile).start()

        @pl.when(tile + 2 < n_b)
        def _():
            for copy in b_loads(tile + 2):
                copy.start()

    def partial_rows(owner, which):
        return r.partial.at[pl.ds(pl.multiple_of(owner * local + which * half, 16), half)]

    c_own = (
        load(partial_rows(y_place, 0), r.c_mine.at[0], 20),
        load(partial_rows(x_place, 1), r.c_mine.at[1], 21),
        load(partial_rows(me, 0), r.c_mine.at[2], 22),
        load(partial_rows(me, 1), r.c_mine.at[3], 23),
    )

    def c_send(src, index, where):
        return remote(src, r.c_landed.at[index], r.c_send.at[index], r.c_recv.at[index], where)

    c_first = (
        c_send(partial_rows(far_place, 0), 0, x_other),
        c_send(partial_rows(far_place, 1), 1, y_other),
        c_send(partial_rows(x_place, 0), 2, x_other),
        c_send(partial_rows(y_place, 1), 3, y_other),
    )
    c_on = (c_send(r.c_mine.at[0], 4, y_other), c_send(r.c_mine.at[1], 5, x_other))

    def c_start():
        b_store(n_b - 2).wait()
        b_store(n_b - 1).wait()
        for copy in c_first + c_own:
            copy.start()

    def c_pass():
        for copy in c_own:
            copy.wait()
        for index in range(2):
            c_first[index].wait_recv()
            r.c_mine[index] = add_low(r.c_mine[index], r.c_landed[index])
            c_on[index].start()

    def d_norms(which):
        if which == 0:
            for copy in load_small:
                copy.wait()
            for copy in c_first:
                copy.wait_send()
            r.gain_own[...] = r.gain_parts[...]
        c_first[2 + which].wait_recv()
        c_on[which].wait_recv()

        def rows_of(which, index, carry):
            here = pl.ds(pl.multiple_of(index * 16, 16), 16)
            rows = pl.ds(pl.multiple_of(which * half + index * 16, 16), 16)
            grad = (
                r.c_mine[2 + which, here].astype(f32)
                + r.c_landed[2 + which, here].astype(f32)
                + r.c_landed[4 + which, here].astype(f32)
            )
            middle = r.middle_buf[rows]
            inv = lax.rsqrt(jnp.mean(middle * middle, axis=-1, keepdims=True) + norm_eps)
            weighted = grad * r.gains[1:2]
            mean = jnp.mean(weighted * middle, axis=-1, keepdims=True)
            r.gain_own[2:3, 0:width] += jnp.sum(grad * middle * inv, axis=0, keepdims=True)
            grad_mid = (
                r.cot_buf[rows].astype(f32) + inv * weighted - middle * (inv * inv * inv) * mean
            )
            r.middle_buf[rows] = grad_mid
            attn = r.attn_buf[rows]
            inv = lax.rsqrt(jnp.mean(attn * attn, axis=-1, keepdims=True) + norm_eps)
            weighted = grad_mid * r.gains[0:1]
            mean = jnp.mean(weighted * attn, axis=-1, keepdims=True)
            r.gain_own[1:2, 0:width] += jnp.sum(grad_mid * attn * inv, axis=0, keepdims=True)
            grad_attn = inv * weighted - attn * (inv * inv * inv) * mean
            r.all_grad[pl.ds(pl.multiple_of(me * local + which * half + index * 16, 16), 16)] = (
                grad_attn.astype(bf16)
            )
            return carry

        lax.fori_loop(0, half // 16, functools.partial(rows_of, which), 0)
        for index in ((0, 3), (1, 2))[which]:
            e_first[index].start()
        if which == 1:
            for copy in c_on:
                copy.wait_send()

    def gather_copies(rows, source, target, send_sem, recv_sem):
        def send(owner, which, index, where, src):
            here = pl.ds(pl.multiple_of(owner * 2 * rows + which * rows, 16), rows)
            return remote(
                src.at[here] if src is target else src.at[pl.ds(which * rows, rows)],
                target.at[here], send_sem.at[index], recv_sem.at[index], where,
            )

        starts = (
            send(me, 0, 0, x_other, source),
            send(me, 1, 1, y_other, source),
            send(me, 1, 2, x_other, source),
            send(me, 0, 3, y_other, source),
        )
        passes = (
            send(x_place, 0, 4, y_other, target), send(y_place, 1, 5, x_other, target)
        )
        return starts, passes

    e_first, e_on = gather_copies(half, r.all_grad, r.all_grad, r.e_send, r.e_recv)
    h_first, h_on = gather_copies(tokens // 2, r.head_grad, r.grad_qkv, r.h_send, r.h_recv)
    h_own = pltpu.make_async_copy(
        r.head_grad, r.grad_qkv.at[pl.ds(pl.multiple_of(me * tokens, 16), tokens)], r.keep_sem.at[1]
    )

    def pass_on(starts, passes):
        for index in range(2):
            starts[index].wait_recv()
            passes[index].start()

    def gathered(starts, passes):
        for copy in starts[2:] + passes:
            copy.wait_recv()
        for copy in starts + passes:
            copy.wait_send()

    load_out = load(r.w_out, r.weights.at[pl.ds(0, r.w_out.shape[0]), pl.ds(0, width)], 24)

    def g_loads(item):
        head, rows = item // n_blocks, pl.ds(pl.multiple_of((item % n_blocks) * block, block), block)
        return (
            load(r.probs.at[head, rows], r.probs_buf, 25),
            load(r.tanh.at[head, rows], r.tanh_buf, 26),
        )

    def f_mixed():
        gathered(e_first, e_on)
        load_out.wait()
        r.mixed_grad[...] = dot_rows(
            r.all_grad[...], r.weights[pl.ds(0, r.w_out.shape[0]), pl.ds(0, width)]
        ).astype(bf16)
        r.kv_grad[...] = jnp.zeros_like(r.kv_grad)
        for copy in g_loads(0):
            copy.start()

    def g_attention(item):
        head = item // n_blocks
        rows = pl.ds(pl.multiple_of((item % n_blocks) * block, block), block)
        columns = pl.ds(pl.multiple_of(head * HEAD_SIZE, HEAD_SIZE), HEAD_SIZE)
        for copy in g_loads(item):
            copy.wait()
        grad_out = r.mixed_grad[rows, columns]
        values = r.qkv_buf[:, pl.ds(q_cols + k_cols, k_cols)]
        r.score_grad[...] = dot_rows(grad_out, values)

        def rows_of(index, carry):
            here = pl.ds(pl.multiple_of(index * 64, 64), 64)
            probs = r.probs_buf[here]
            grad = r.score_grad[here]
            curve = r.tanh_buf[here]
            total = jnp.sum(probs * grad, axis=-1, keepdims=True)
            grad = probs * (grad - total) * (1.0 - curve * curve) * (HEAD_SIZE ** (-0.5))
            r.dots_grad[here] = grad.astype(bf16)
            r.probs_low[here] = probs.astype(bf16)
            return carry

        lax.fori_loop(0, block // 64, rows_of, 0)

        @pl.when(item + 1 < heads * n_blocks)
        def _():
            for copy in g_loads(item + 1):
                copy.start()

        keys = r.qkv_buf[:, pl.ds(q_cols, k_cols)]
        r.head_grad[rows, columns] = dot_plain(r.dots_grad[...], keys).astype(bf16)
        r.kv_grad[0] += dot_columns(r.dots_grad[...], r.qkv_buf[rows, columns])
        r.kv_grad[1] += dot_columns(r.probs_low[...], grad_out)

    def h_start():
        r.head_grad[:, pl.ds(q_cols, k_cols)] = r.kv_grad[0].astype(bf16)
        r.head_grad[:, pl.ds(q_cols + k_cols, k_cols)] = r.kv_grad[1].astype(bf16)
        for copy in h_first:
            copy.start()
        h_own.start()

    def side_of(owner, kind):
        buf = r.hidden_buf if owner < 2 else r.ffn_buf
        size = (q_cols, k_cols, k_cols)[kind]
        start = (0, 2 * q_cols, 2 * q_cols + 2 * k_cols)[kind] + (owner % 2) * size
        return buf.at[:, pl.ds(start, size)]

    i_loads = [
        load(
            r.grad_qkv.at[
                pl.ds(owner * tokens, tokens),
                pl.ds((0, q_cols, q_cols + k_cols)[kind], (q_cols, k_cols, k_cols)[kind]),
            ],
            side_of(owner, kind),
            27 + 3 * owner + kind,
        )
        for owner in range(4)
        for kind in range(3)
    ] + [
        load(r.w_query, r.gate_grad.at[pl.ds(0, part), pl.ds(0, 4 * q_cols)], 39),
        load(r.w_key, r.weights.at[pl.ds(0, part), pl.ds(0, 4 * k_cols)], 40),
        load(r.w_value, r.weights.at[pl.ds(0, part), pl.ds(4 * k_cols, 4 * k_cols)], 41),
    ]
    i_copies = [
        remote(
            r.head_grad.at[pl.ds(pl.multiple_of(((me + step) % 4) * local, 16), local), pl.ds(0, part_wide)],
            r.norm_grad.at[me], r.i_send.at[step - 1], r.i_recv.at[step - 1], plane[step - 1],
        )
        for step in (1, 2, 3)
    ]

    def i_start():
        gathered(h_first, h_on)
        h_own.wait()
        for copy in i_loads:
            copy.start()
        for copy in i_loads:
            copy.wait()

    def i_norm(index):
        rows = pl.ds(index * block, block)
        some = jnp.zeros((block, part_wide), f32)
        for owner in range(4):
            for kind, size in enumerate((q_cols, k_cols, k_cols)):
                held = r.gate_grad if kind == 0 else r.weights
                start = (0, 0, 4 * k_cols)[kind] + owner * size
                some += dot_rows(
                    side_of(owner, kind)[rows], held[pl.ds(0, part_wide), pl.ds(start, size)]
                )
        r.head_grad[rows, pl.ds(0, part_wide)] = some.astype(bf16)
        if index < n_blocks - 1:
            return
        for copy in i_copies:
            copy.start()
        r.norm_grad[me] = r.head_grad[
            pl.ds(pl.multiple_of(me * local, 16), local), pl.ds(0, part_wide)
        ]

    def k_norm():
        for copy in i_copies:
            copy.wait()

        def rows_of(index, carry):
            rows = pl.ds(pl.multiple_of(index * 16, 16), 16)
            grad = jnp.concatenate(
                [r.norm_grad[owner, rows].astype(f32)[:, :part] for owner in range(4)], axis=1
            )
            values = r.token_buf[rows].astype(f32)
            inv = lax.rsqrt(jnp.mean(values * values, axis=-1, keepdims=True) + norm_eps)
            weighted = grad * r.gains[3:4]
            mean = jnp.mean(weighted * values, axis=-1, keepdims=True)
            r.gain_own[3:4] += jnp.sum(grad * values * inv, axis=0, keepdims=True)
            r.cot_buf[rows] = (
                r.middle_buf[rows] + inv * weighted - values * (inv * inv * inv) * mean
            ).astype(bf16)
            return carry

        lax.fori_loop(0, local // 16, rows_of, 0)
        keep_part.start()
        for copy in gain_plane:
            copy.start()

    keep_part = pltpu.make_async_copy(r.cot_buf, r.grad_tokens, r.keep_sem.at[0])
    gain_plane = [
        remote(r.gain_own, r.gain_plane.at[me], r.gain_send.at[i], r.gain_recv.at[i], where)
        for i, where in enumerate(plane)
    ]
    gain_rep = [
        remote(r.gain_mine.at[i], r.gain_theirs.at[i], r.gain_send.at[3 + i], r.gain_recv.at[3 + i], where)
        for i, where in enumerate((twin, next_chip, far_chip))
    ]

    def k_plane():
        for copy in gain_plane:
            copy.wait()
        r.gain_plane[me] = r.gain_own[...]
        r.gain_mine[0] = (r.gain_plane[0] + r.gain_plane[1]) + (r.gain_plane[2] + r.gain_plane[3])
        gain_rep[0].start()

    def k_rep(index):
        gain_rep[index].wait()
        total = r.gain_mine[index] + r.gain_theirs[index]
        if index < 2:
            r.gain_mine[index + 1] = total
            gain_rep[index + 1].start()
        else:
            r.gain_total[...] = total
            keep_gains.start()

    keep_gains = pltpu.make_async_copy(r.gain_total, r.gain_sums, r.keep_sem.at[3])

    sums = (r.down_sum, r.gate_sum, r.up_sum, r.out_sum)

    def by_job(step, use, scale=2):
        for job in range(5):

            @pl.when((step >= scale * first[job]) & (step < scale * first[job + 1]))
            def _():
                use(job, step - scale * first[job])

    def by_width(step, use):
        if side == r.acc.shape[2]:
            use(pl.ds(0, side))
            return

        @pl.when(step < 2 * first[4])
        def _():
            use(pl.ds(0, r.acc.shape[2]))

        @pl.when(step >= 2 * first[4])
        def _():
            use(pl.ds(0, side))

    def results(job, index, slot):
        if job == 0:
            unit, which = index // 2, index % 2
            low = (unit % (inner_width // group)) * group + (2 * which + core) * pieces * LINE
            across = pl.ds(pl.multiple_of(unit // (inner_width // group) * piece, 128), piece)
            return [
                (
                    r.total.at[slot, :, pl.ds(i * piece, piece)],
                    r.down_sum.at[pl.ds(pl.multiple_of(low + i * LINE, LINE), LINE), across],
                )
                for i in range(pieces)
            ]
        if job < 4:
            rows = pl.ds(pl.multiple_of((2 * index + core) * LINE, LINE), LINE)
            return [(r.total.at[slot, :, pl.ds(0, sums[job].shape[1])], sums[job].at[rows])]
        rows = pl.ds(pl.multiple_of(index * LINE, LINE), LINE)
        pairs, start = [], 0
        for ref in (r.query_sum, r.key_sum, r.value_sum):
            size = ref.shape[1] // 2
            columns = pl.ds(pl.multiple_of(core * size, 128), size)
            pairs.append((r.total.at[slot, :, pl.ds(start, size)], ref.at[rows, columns]))
            start += size
        return pairs

    def pair_copies(job, index, step):
        slot = step % LAST
        return [
            remote(src, dst, r.pair_send.at[slot, i], r.pair_recv.at[step, i], twin)
            for i, (src, dst) in enumerate(results(job, index, slot))
        ]

    def store_copies(job, index, step):
        slot = step % LAST
        return [
            pltpu.make_async_copy(src, dst, r.store_sem.at[slot, i])
            for i, (src, dst) in enumerate(results(job, index, slot))
        ]

    def made_rows(step, owner):
        return pl.ds(pl.multiple_of((step % 2) * 2 * LINE + owner * LINE, LINE), LINE)

    def sib_copy(step, across):
        return remote(
            r.made.at[step // 2 % 2, made_rows(step, 1 - core), across],
            r.sib.at[step % 4, :, across], r.sib_send.at[step % 4], r.sib_recv.at[step % 4], twin,
        )

    def up_copy(step, across, dst, sem):
        slot = step % DEEP
        return remote(
            r.acc.at[slot, :, across], dst.at[slot, :, across], r.up_send.at[slot], sem.at[slot], inner
        )

    def down_copy(step, across):
        return remote(
            r.total.at[step % LAST, :, across], r.inner_in.at[step % DEEP, :, across],
            r.down_send.at[step % LAST], r.inner_recv.at[step % DEEP], outer,
        )

    def up_sent(step):
        by_width(step, lambda across: up_copy(step, across, r.outer_in, r.outer_recv).wait_send())

    def make(unit):
        slot = unit % 2

        def product(job, index):
            if job == 0:
                n_groups = inner_width // group
                rows = pl.ds(pl.multiple_of(index % n_groups * group, PAIR), group)
                across = pl.ds(pl.multiple_of(index // n_groups * piece, 128), piece)
                some = dot_columns(r.hidden_buf[:, rows], r.ffn_buf[:, across]).astype(bf16)
                for row in range(4):
                    for i in range(pieces):
                        low = (row * pieces + i) * LINE
                        r.made[slot, pl.ds(row * LINE, LINE), pl.ds(i * piece, piece)] = some[
                            low : low + LINE
                        ]
                return
            if job < 4:
                left_buf = (None, r.two_buf, r.two_buf, r.mixed_buf)[job]
                right_buf = (None, r.gate_grad, r.up_grad, r.all_grad)[job]
                columns = pl.ds(pl.multiple_of(index * PAIR, PAIR), PAIR)
                across = pl.ds(0, sums[job].shape[1])
                r.made[slot, :, across] = dot_columns(
                    left_buf[:, columns], right_buf[:, across]
                ).astype(bf16)
                return
            columns = pl.ds(pl.multiple_of((index // 2) * PAIR, PAIR), PAIR)
            for which, buf in enumerate((r.hidden_buf, r.ffn_buf)):
                r.both[...] = dot_columns(r.cols_buf[:, columns], buf[:, pl.ds(0, side)]).astype(bf16)
                for row in range(2):
                    low = pl.multiple_of((index % 2) * 2 * LINE + row * LINE, LINE)
                    r.made[slot, pl.ds((2 * row + which) * LINE, LINE), pl.ds(0, side)] = r.both[
                        pl.ds(low, LINE)
                    ]

        by_job(unit, product, 1)

    def give(step):
        @pl.when(step >= 4)
        def _():
            pl.semaphore_wait(r.sib_credit, 1)

        by_width(step, lambda across: sib_copy(step, across).start())

    def send_up(step):
        @pl.when(step >= DEEP)
        def _():
            pl.semaphore_wait(r.up_credit, 1)

        @pl.when(is_mid)
        def _():
            by_width(step, lambda across: up_copy(step, across, r.inner_in, r.inner_recv).start())

        @pl.when(jnp.logical_not(is_mid))
        def _():
            by_width(step, lambda across: up_copy(step, across, r.outer_in, r.outer_recv).start())

    def pair_up(step):
        slot = step % DEEP
        by_width(step, lambda across: sib_copy(step, across).wait())

        @pl.when(step >= DEEP)
        def _():
            up_sent(step - DEEP)

        r.acc[slot] = add_low(r.made[step // 2 % 2, made_rows(step, core)], r.sib[step % 4])

        @pl.when(step + 4 < steps)
        def _():
            tell(r.sib_credit, twin)

        @pl.when(is_end)
        def _():
            send_up(step)

    def from_outer(step):
        slot = step % DEEP
        by_width(step, lambda across: up_copy(step, across, r.outer_in, r.outer_recv).wait_recv())
        r.acc[slot] = add_low(r.acc[slot], r.outer_in[slot])

        @pl.when(step + DEEP < steps)
        def _():
            tell(r.up_credit, outer)

        send_up(step)

    def sends_done(step):
        def use(job, index):
            for copy in pair_copies(job, index, step):
                copy.wait_send()
            for copy in store_copies(job, index, step):
                copy.wait()

        by_job(step, use)

        @pl.when(jnp.logical_not(is_end))
        def _():
            by_width(step, lambda across: down_copy(step, across).wait_send())

    def from_inner(step):
        slot = step % DEEP
        by_width(step, lambda across: down_copy(step, across).wait_recv())

        @pl.when(step >= LAST)
        def _():
            sends_done(step - LAST)

        @pl.when(is_mid)
        def _():
            r.total[step % LAST] = add_low(r.acc[slot], r.inner_in[slot])

            @pl.when(step + DEEP < steps)
            def _():
                tell(r.up_credit, inner)

        @pl.when(jnp.logical_not(is_mid))
        def _():
            r.total[step % LAST] = r.inner_in[slot]

            @pl.when(step + DEEP < steps)
            def _():
                tell(r.down_credit, inner)

        @pl.when(jnp.logical_not(is_end))
        def _():
            @pl.when(step >= DEEP)
            def _():
                pl.semaphore_wait(r.down_credit, 1)

            by_width(step, lambda across: down_copy(step, across).start())

        def use(job, index):
            for copy in pair_copies(job, index, step) + store_copies(job, index, step):
                copy.start()

        by_job(step, use)

    lag_outer = 3
    lag_inner = jnp.where(is_end, 8, 5)

    def at(now, step, use):
        @pl.when(now == step)
        def _():
            use()

    def work(now):
        @pl.when(now == 0)
        def _():
            load_two.wait()

        for index in range(1, pieces):
            at(now, index, functools.partial(ffn_pass, index))

            at(now, index + 1, functools.partial(ffn_arrived, index))

        at(now, b_at, ffn_sent)

        for buf in range(2):

            @pl.when((now >= a_at) & (2 * (now - a_at) + buf < n_a))
            def _():
                a_tile(2 * (now - a_at) + buf, buf)

        @pl.when(now == b_at - 1)
        def _():
            for copy in b_loads(1):
                copy.start()

        @pl.when((now >= b_at) & (now < c_at))
        def _():
            b_tile(now - b_at)

        at(now, c_at, c_start)
        at(now, c_at + 1, load_out.start)
        at(now, c_at + 2, c_pass)

        at(now, d_at, lambda: d_norms(0))
        at(now, d_at + 1, lambda: d_norms(1))
        at(now, d_at + 3, lambda: pass_on(e_first, e_on))
        at(now, f_at, f_mixed)

        @pl.when((now >= g_at) & (now < h_at))
        def _():
            g_attention(now - g_at)

        at(now, h_at, h_start)
        at(now, h_at + 4, lambda: pass_on(h_first, h_on))
        at(now, i_at, i_start)
        for index in range(n_blocks):
            at(now, i_at + 1 + index, functools.partial(i_norm, index))
        at(now, k_at, k_norm)
        at(now, k_at + 1, k_plane)
        for index in range(3):
            at(now, k_at + 2 + index, functools.partial(k_rep, index))

    def tick(now, carry):
        @pl.when((now % 2 == 0) & (now < steps))
        def _():
            make(now // 2)

        @pl.when(now < steps)
        def _():
            give(now)

        @pl.when((now >= 1) & (now - 1 < steps))
        def _():
            pair_up(now - 1)

        @pl.when(jnp.logical_not(is_end) & (now >= lag_outer) & (now - lag_outer < steps))
        def _():
            from_outer(now - lag_outer)

        @pl.when((now >= lag_inner) & (now - lag_inner < steps))
        def _():
            from_inner(now - lag_inner)

        @pl.when(now % 2 == 1)
        def _():
            work(now // 2)

        return carry

    lax.fori_loop(0, steps + 10, tick, 0)

    def finish(step, carry):
        sends_done(step)
        return carry

    lax.fori_loop(steps - LAST, steps, finish, 0)

    def finish_up(step, carry):
        up_sent(step)
        return carry

    lax.fori_loop(steps - DEEP, steps, finish_up, 0)

    def arrived(step, carry):
        def use(job, index):
            for copy in pair_copies(job, index, step):
                copy.wait_recv()

        by_job(step, use)
        return carry

    lax.fori_loop(0, steps, arrived, 0)
    for copy in (keep_part, keep_gains):
        copy.wait()


def backward(collective_id, **args):
    f32, bf16 = jnp.float32, jnp.bfloat16
    given = types.SimpleNamespace(**args)
    tokens, width = given.normed_two.shape
    inner_width = given.hidden.shape[1]
    local = tokens // 4
    half = local // 2
    head_cols = given.qkv.shape[1]
    part = width // 4
    part_wide = given.normed_cols.shape[1]
    out_rows = given.w_out.shape[0]
    side = 2 * head_cols
    slot_width = max(width, inner_width, side)
    pieces = column_pieces(width)
    block = min(TILE, tokens)
    steps = 2 * ((inner_width + 2 * width + out_rows) // PAIR + part // (2 * LINE))
    vmem, dma, credit = pltpu.VMEM, pltpu.SemaphoreType.DMA, pltpu.SemaphoreType.REGULAR
    shape = jax.ShapeDtypeStruct
    outs = dict(
        down_sum=shape((inner_width, width), bf16),
        gate_sum=shape((width, inner_width), bf16),
        up_sum=shape((width, inner_width), bf16),
        out_sum=shape((out_rows, width), bf16),
        query_sum=shape((part, side), bf16),
        key_sum=shape((part, side // 2), bf16),
        value_sum=shape((part, side // 2), bf16),
        grad_tokens=shape((local, width), bf16),
        gain_sums=shape((8, width), f32),
        partial=shape((tokens, width), bf16),
        grad_qkv=shape((4 * tokens, head_cols), bf16),
    )
    scratch = dict(
        ffn_buf=vmem((tokens, slot_width), bf16),
        hidden_buf=vmem((tokens, slot_width), bf16),
        two_buf=vmem((tokens, width), bf16),
        gate_grad=vmem((tokens, slot_width), bf16),
        up_grad=vmem((tokens, inner_width), bf16),
        weights=vmem((4 * TILE, slot_width), bf16),
        gate_buf=vmem((2, tokens, TILE), bf16),
        up_buf=vmem((2, tokens, TILE), bf16),
        wide=vmem((tokens, TILE), f32),
        stage=vmem((2, tokens, TILE), bf16),
        c_mine=vmem((4, half, width), bf16),
        c_landed=vmem((6, half, width), bf16),
        middle_buf=vmem((local, width), f32),
        attn_buf=vmem((local, width), f32),
        cot_buf=vmem((local, width), bf16),
        qkv_buf=vmem((tokens, head_cols), bf16),
        mixed_buf=vmem((tokens, out_rows), bf16),
        cols_buf=vmem((tokens, -(-part // PAIR) * PAIR), bf16),
        token_buf=vmem((local, width), bf16),
        all_grad=vmem((tokens, width), bf16),
        mixed_grad=vmem((tokens, out_rows), bf16),
        probs_buf=vmem((block, tokens), f32),
        tanh_buf=vmem((block, tokens), f32),
        score_grad=vmem((block, tokens), f32),
        dots_grad=vmem((block, tokens), bf16),
        probs_low=vmem((block, tokens), bf16),
        kv_grad=vmem((2, tokens, head_cols // 4), f32),
        head_grad=vmem((tokens, head_cols), bf16),
        norm_grad=vmem((4, local, part_wide), bf16),
        gains=vmem((8, width), f32),
        gain_own=vmem((8, width), f32),
        gain_plane=vmem((4, 8, width), f32),
        gain_mine=vmem((3, 8, width), f32),
        gain_theirs=vmem((3, 8, width), f32),
        gain_total=vmem((8, width), f32),
        made=vmem((2, PAIR, slot_width), bf16),
        both=vmem((PAIR, side), bf16),
        sib=vmem((4, LINE, slot_width), bf16),
        acc=vmem((DEEP, LINE, slot_width), bf16),
        outer_in=vmem((DEEP, LINE, slot_width), bf16),
        inner_in=vmem((DEEP, LINE, slot_width), bf16),
        total=vmem((LAST, LINE, slot_width), bf16),
        load_sem=dma((42,)),
        stage_sem=dma((2,)),
        keep_sem=dma((4,)),
        ffn_send=dma((pieces, 6)),
        ffn_recv=dma((pieces, 6)),
        c_send=dma((6,)),
        c_recv=dma((6,)),
        e_send=dma((6,)),
        e_recv=dma((6,)),
        h_send=dma((6,)),
        h_recv=dma((6,)),
        i_send=dma((3,)),
        i_recv=dma((3,)),
        gain_send=dma((6,)),
        gain_recv=dma((6,)),
        sib_send=dma((4,)),
        sib_recv=dma((4,)),
        up_send=dma((DEEP,)),
        outer_recv=dma((DEEP,)),
        inner_recv=dma((DEEP,)),
        down_send=dma((LAST,)),
        pair_send=dma((LAST, pieces)),
        pair_recv=dma((steps, pieces)),
        store_sem=dma((LAST, pieces)),
        sib_credit=credit,
        up_credit=credit,
        down_credit=credit,
    )
    any_space = pl.BlockSpec(memory_space=pl.ANY)
    small = pl.BlockSpec(memory_space=pltpu.VMEM)
    in_specs = [
        small if value.ndim == 1 or value.shape[0] == 8 else any_space for value in args.values()
    ]
    results = pl.pallas_call(
        functools.partial(
            backward_kernel,
            (tokens, local, width, inner_width, head_cols),
            tuple(args) + tuple(outs) + tuple(scratch),
        ),
        out_shape=list(outs.values()),
        in_specs=in_specs,
        out_specs=[any_space] * len(outs),
        scratch_shapes=list(scratch.values()),
        compiler_params=pltpu.CompilerParams(
            collective_id=collective_id,
            has_side_effects=True,
            vmem_limit_bytes=VMEM_LIMIT,
        ),
        cost_estimate=pl.CostEstimate(
            flops=80 * tokens * width * width, bytes_accessed=400 * 2**20, transcendentals=0
        ),
    )(*args.values())
    return types.SimpleNamespace(**dict(zip(outs, results)))


VMEM_LIMIT = 63 * 2**20


def forward_kernel(names, *refs):
    r = types.SimpleNamespace(**dict(zip(names, refs)))
    f32, bf16 = jnp.float32, jnp.bfloat16
    tokens, inner_width = r.hidden.shape
    local, width = r.tokens.shape
    half = local // 2
    me, x_place, y_place, far_place = plane_places()
    x_other, y_other = {"shard": x_place}, {"shard": y_place}

    def load(src, dst, index):
        return pltpu.make_async_copy(src, dst, r.load_sem.at[index])

    def block_rows(owner):
        return pl.ds(pl.multiple_of(owner * local, 16), local)

    def half_rows(owner, which):
        return pl.ds(pl.multiple_of(owner * local + which * half, 16), half)

    early = (load(r.mixed, r.mixed_buf, 0), load(r.w_out, r.out_buf, 1))
    small = (load(r.tokens, r.token_buf, 2), load(r.cotangent, r.cot_buf, 3))
    big = (
        load(r.w_gate, r.gate_weight, 4),
        load(r.w_up, r.up_weight, 5),
        load(r.w_down, r.down_weight, 6),
    )
    for copy in early + small + big:
        copy.start()
    for index, gain in enumerate((r.post_attn_gain, r.ffn_gain, r.post_ffn_gain, r.attn_gain)):
        r.gains[index : index + 1] = gain[...].astype(jnp.float32).reshape(1, gain.shape[0])
    greet((x_place, y_place))

    def summing(landed, send_sem, recv_sem):
        def send(src, index, where):
            return remote(src, landed.at[index], send_sem.at[index], recv_sem.at[index], where)

        far = (
            send(r.partial.at[half_rows(far_place, 0)], 0, x_other),
            send(r.partial.at[half_rows(far_place, 1)], 1, y_other),
        )
        near = (
            send(r.partial.at[half_rows(x_place, 0)], 2, x_other),
            send(r.partial.at[half_rows(y_place, 1)], 3, y_other),
        )
        on = (send(r.passed.at[0], 4, y_other), send(r.passed.at[1], 5, x_other))
        return far, near, on

    def pass_sums(landed, far, on):
        for index, owner in enumerate((y_place, x_place)):
            far[index].wait_recv()
            r.passed[index] = add_low(r.partial[half_rows(owner, index)], landed[index])
            on[index].start()

    def gathering(source, target, send_sem, recv_sem):
        def send(owner, which, index, where, src):
            return remote(
                src, target.at[half_rows(owner, which)],
                send_sem.at[index], recv_sem.at[index], where,
            )

        starts = [
            [send(me, which, 2 * which + i, where, source(which)) for i, where in enumerate((x_other, y_other))]
            for which in range(2)
        ]
        on = (
            send(x_place, 0, 4, y_other, target.at[half_rows(x_place, 0)]),
            send(y_place, 1, 5, x_other, target.at[half_rows(y_place, 1)]),
        )
        return starts, on

    a_far, a_near, a_on = summing(r.a_landed, r.a_send, r.a_recv)
    c_far, c_near, c_on = summing(r.c_landed, r.c_send, r.c_recv)
    b_starts, b_on = gathering(
        lambda which: r.two_buf.at[half_rows(me, which)], r.two_buf, r.b_send, r.b_recv
    )

    for copy in early:
        copy.wait()

    def project(owner):
        rows = block_rows(owner)
        r.partial[rows] = dot_plain(r.mixed_buf[rows], r.out_buf[...]).astype(bf16)

    project(far_place)
    for copy in a_far:
        copy.start()
    project(x_place)
    a_near[0].start()
    project(y_place)
    a_near[1].start()
    project(me)
    pass_sums(r.a_landed, a_far, a_on)
    for copy in small:
        copy.wait()

    def sum_rows(landed, which, index):
        rows = pl.ds(pl.multiple_of(me * local + which * half + index * 32, 16), 32)
        here = pl.ds(pl.multiple_of(index * 32, 16), 32)
        return (
            r.partial[rows].astype(f32)
            + landed[2 + which, here].astype(f32)
            + landed[4 + which, here].astype(f32)
        )

    def middle_rows(which, index, carry):
        rows = pl.ds(pl.multiple_of(which * half + index * 32, 16), 32)
        attn = sum_rows(r.a_landed, which, index)
        r.attn_buf[rows] = attn
        inv = lax.rsqrt(jnp.mean(attn * attn, axis=-1, keepdims=True) + norm_eps)
        middle = r.token_buf[rows].astype(f32) + attn * inv * r.gains[0:1]
        r.middle_buf[rows] = middle
        inv = lax.rsqrt(jnp.mean(middle * middle, axis=-1, keepdims=True) + norm_eps)
        r.two_buf[pl.ds(pl.multiple_of(me * local + which * half + index * 32, 16), 32)] = (
            middle * inv * r.gains[1:2]
        ).astype(bf16)
        return carry

    for which in range(2):
        a_near[which].wait_recv()
        a_on[which].wait_recv()
        lax.fori_loop(0, half // 32, functools.partial(middle_rows, which), 0)
        b_starts[which][which].start()
    for which in range(2):
        b_starts[which][1 - which].start()
    keep = [
        pltpu.make_async_copy(r.attn_buf, r.attn_out, r.keep_sem.at[0]),
        pltpu.make_async_copy(r.middle_buf, r.middle, r.keep_sem.at[1]),
    ]
    for copy in keep:
        copy.start()
    for copy in a_far + a_near + a_on:
        copy.wait_send()

    def keep_block(halves):
        return [
            pltpu.make_async_copy(src, dst.at[half_rows(*halves[i])], r.keep_sem.at[2 + 2 * kind + i])
            for i in range(2)
            for kind, (src, dst) in enumerate(
                (
                    (r.gate_stage.at[pl.ds(i * half, half)], r.gate),
                    (r.up_stage.at[pl.ds(i * half, half)], r.up),
                    (r.hidden_buf.at[half_rows(*halves[i])], r.hidden),
                )
            )
        ]

    def feed(halves, before):
        for i in range(2):
            r.block[pl.ds(i * half, half), pl.ds(0, width)] = r.two_buf[half_rows(*halves[i])]
        if before is not None:
            for copy in keep_block(before):
                copy.wait()

        def tile(index, carry):
            columns = pl.ds(pl.multiple_of(index * TILE, TILE), TILE)
            r.gate_wide[...] = dot_plain(r.block[:, pl.ds(0, width)], r.gate_weight[:, columns])
            r.up_wide[...] = dot_plain(r.block[:, pl.ds(0, width)], r.up_weight[:, columns])
            for i in range(2):
                here = pl.ds(i * half, half)
                gate, up = r.gate_wide[here], r.up_wide[here]
                r.gate_stage[here, columns] = gate.astype(bf16)
                r.up_stage[here, columns] = up.astype(bf16)
                curve = jnp.tanh(ROOT_TWO_PI * (gate + 0.044715 * (gate * gate * gate)))
                r.hidden_buf[half_rows(*halves[i]), columns] = (
                    0.5 * gate * (1.0 + curve) * up
                ).astype(bf16)
            return carry

        lax.fori_loop(0, inner_width // TILE, tile, 0)
        for copy in keep_block(halves):
            copy.start()

    def shrink(halves):
        for i in range(2):
            r.block[pl.ds(i * half, half), pl.ds(0, inner_width)] = r.hidden_buf[half_rows(*halves[i])]

        def tile(index, carry):
            columns = pl.ds(pl.multiple_of(index * TILE, TILE), TILE)
            some = dot_plain(r.block[:, pl.ds(0, inner_width)], r.down_weight[:, columns]).astype(bf16)
            for i in range(2):
                r.partial[half_rows(*halves[i]), columns] = some[i * half : (i + 1) * half]
            return carry

        lax.fori_loop(0, width // TILE, tile, 0)

    mine = ((me, 0), (me, 1))
    early_halves = ((x_place, 0), (y_place, 1))
    late_halves = ((x_place, 1), (y_place, 0))
    far_halves = ((far_place, 0), (far_place, 1))
    big[0].wait()
    big[1].wait()
    feed(mine, None)
    big[2].wait()
    b_starts[0][0].wait_recv()
    b_on[0].start()
    b_starts[1][1].wait_recv()
    b_on[1].start()
    feed(early_halves, mine)
    shrink(early_halves)
    for copy in c_near:
        copy.start()
    b_starts[1][0].wait_recv()
    b_starts[0][1].wait_recv()
    feed(late_halves, early_halves)
    for copy in b_on:
        copy.wait_recv()
    feed(far_halves, late_halves)
    shrink(far_halves)
    for copy in c_far:
        copy.start()
    shrink(late_halves)
    shrink(mine)
    keep_two = pltpu.make_async_copy(r.two_buf, r.normed_two, r.keep_sem.at[8])
    keep_two.start()
    r.gain_part[...] = jnp.zeros_like(r.gain_part)
    pass_sums(r.c_landed, c_far, c_on)

    def last_rows(which, index, carry):
        rows = pl.ds(pl.multiple_of(which * half + index * 32, 16), 32)
        ffn = sum_rows(r.c_landed, which, index)
        inv = lax.rsqrt(jnp.mean(ffn * ffn, axis=-1, keepdims=True) + norm_eps)
        r.token_buf[rows] = (r.middle_buf[rows] + ffn * inv * r.gains[2:3]).astype(bf16)
        grad = r.cot_buf[rows].astype(f32)
        weighted = grad * r.gains[2:3]
        mean = jnp.mean(weighted * ffn, axis=-1, keepdims=True)
        r.gain_part[0:1] += jnp.sum(grad * ffn * inv, axis=0, keepdims=True)
        r.cot_buf[rows] = (inv * weighted - ffn * (inv * inv * inv) * mean).astype(bf16)
        return carry

    for which in range(2):
        c_near[which].wait_recv()
        c_on[which].wait_recv()
        lax.fori_loop(0, half // 32, functools.partial(last_rows, which), 0)
    keep_own = pltpu.make_async_copy(r.cot_buf, r.grad_ffn, r.keep_sem.at[9])
    keep_out = pltpu.make_async_copy(r.token_buf, r.output, r.keep_sem.at[10])
    keep_own.start()
    keep_out.start()
    for copy in b_starts[0] + b_starts[1] + list(b_on + c_far + c_near + c_on):
        copy.wait_send()
    for copy in keep + keep_block(far_halves) + [keep_two, keep_own, keep_out]:
        copy.wait()


def forward(collective_id, **args):
    f32, bf16 = jnp.float32, jnp.bfloat16
    given = types.SimpleNamespace(**args)
    local, width = given.tokens.shape
    tokens = 4 * local
    half = local // 2
    inner_width = given.w_down.shape[0]
    vmem, dma, shape = pltpu.VMEM, pltpu.SemaphoreType.DMA, jax.ShapeDtypeStruct
    outs = dict(
        grad_ffn=shape((local, width), bf16),
        hidden=shape((tokens, inner_width), bf16),
        gate=shape((tokens, inner_width), bf16),
        up=shape((tokens, inner_width), bf16),
        normed_two=shape((tokens, width), bf16),
        middle=shape((local, width), f32),
        attn_out=shape((local, width), f32),
        output=shape((local, width), bf16),
        gain_part=shape((8, width), f32),
    )
    scratch = dict(
        mixed_buf=vmem(given.mixed.shape, bf16),
        out_buf=vmem(given.w_out.shape, bf16),
        token_buf=vmem((local, width), bf16),
        cot_buf=vmem((local, width), bf16),
        gate_weight=vmem((width, inner_width), bf16),
        up_weight=vmem((width, inner_width), bf16),
        down_weight=vmem((inner_width, width), bf16),
        partial=vmem((tokens, width), bf16),
        passed=vmem((2, half, width), bf16),
        a_landed=vmem((6, half, width), bf16),
        c_landed=vmem((6, half, width), bf16),
        gains=vmem((8, width), f32),
        attn_buf=vmem((local, width), f32),
        middle_buf=vmem((local, width), f32),
        two_buf=vmem((tokens, width), bf16),
        hidden_buf=vmem((tokens, inner_width), bf16),
        gate_stage=vmem((local, inner_width), bf16),
        up_stage=vmem((local, inner_width), bf16),
        block=vmem((local, max(width, inner_width)), bf16),
        gate_wide=vmem((local, TILE), f32),
        up_wide=vmem((local, TILE), f32),
        load_sem=dma((7,)),
        keep_sem=dma((11,)),
        a_send=dma((6,)),
        a_recv=dma((6,)),
        b_send=dma((6,)),
        b_recv=dma((6,)),
        c_send=dma((6,)),
        c_recv=dma((6,)),
    )
    any_space = pl.BlockSpec(memory_space=pl.ANY)
    small = pl.BlockSpec(memory_space=pltpu.VMEM)
    results = pl.pallas_call(
        functools.partial(forward_kernel, tuple(args) + tuple(outs) + tuple(scratch)),
        out_shape=list(outs.values()),
        in_specs=[
            small if value.ndim == 1 else any_space
            for value in args.values()
        ],
        out_specs=[small if value.shape[0] <= 8 else any_space for value in outs.values()],
        scratch_shapes=list(scratch.values()),
        compiler_params=pltpu.CompilerParams(
            collective_id=collective_id, has_side_effects=True, vmem_limit_bytes=VMEM_LIMIT
        ),
        cost_estimate=pl.CostEstimate(
            flops=8 * tokens * width * inner_width, bytes_accessed=100 * 2**20, transcendentals=0
        ),
    )(*args.values())
    return types.SimpleNamespace(**dict(zip(outs, results)))


def attend_kernel(names, *refs):
    r = types.SimpleNamespace(**dict(zip(names, refs)))
    f32, bf16 = jnp.float32, jnp.bfloat16
    local, width = r.tokens.shape
    tokens, head_cols = r.qkv.shape
    part = r.w_query.shape[0]
    piece = part // 4
    half = local // 2
    weights = (r.w_query, r.w_key, r.w_value)
    sizes = [weight.shape[1] // 4 for weight in weights]
    starts = (0, sizes[0], sizes[0] + sizes[1])
    q_cols, k_cols = sizes[0], sizes[1]
    heads = q_cols // HEAD_SIZE
    block = min(TILE, tokens)
    n_blocks = tokens // block
    head_scale = HEAD_SIZE ** (-0.5)

    me, x_place, y_place, far_place = plane_places()
    others = (x_place, y_place, far_place)
    x_other, y_other = {"shard": x_place}, {"shard": y_place}
    place = lax.axis_index("rep")
    chip, core = place // 2, place % 2
    twin = {"rep": place + 1 - 2 * core}
    next_chip = {"rep": place + 2 - 4 * (chip % 2)}
    quarter = (chip % 2) * 2 + core
    next_quarter = (1 - chip % 2) * 2 + core

    load_tokens = pltpu.make_async_copy(r.tokens, r.token_buf, r.load_sem.at[0])
    load_heads = [
        pltpu.make_async_copy(
            weights[kind].at[:, pl.ds(pl.multiple_of(me * sizes[kind], 128), sizes[kind])],
            r.heads_buf.at[
                pl.ds(pl.multiple_of(me * part, 16), part), pl.ds(starts[kind], sizes[kind])
            ],
            r.load_sem.at[2 + kind],
        )
        for kind in range(3)
    ]
    load_tokens.start()
    for copy in load_heads:
        copy.start()

    def lookup(ident):
        found = jnp.full_like(ident, -1)
        for label in range(SEGS):
            found = jnp.where(ident == label, r.parents[0, label], found)
        return found

    ident = r.seg_ids[...]
    parent_one = lookup(ident)
    lanes = lax.broadcasted_iota(jnp.int32, ident.shape, 1)
    codes = jnp.where(ident < SEGS, ident, jnp.where(lanes == 3, -2, -1))
    codes = jnp.where(lanes == 1, parent_one, jnp.where(lanes == 2, lookup(parent_one), codes))
    info_rows = pl.ds(pl.multiple_of(me * local, 16), local)
    r.info_buf[info_rows] = codes.astype(f32).astype(bf16)
    r.gain[...] = r.attn_gain[...].astype(f32).reshape(1, width)

    barrier = pltpu.get_barrier_semaphore()
    for where in [{"shard": other} for other in others] + [twin, next_chip]:
        pl.semaphore_signal(barrier, inc=1, device_id=where, device_id_type=pl.DeviceIdType.MESH)
    pl.semaphore_wait(barrier, 5)

    def piece_rows(owner, which):
        return pl.ds(pl.multiple_of(owner * part + which * piece, 16), piece)

    fetch = [
        [
            remote(
                weights[kind].at[
                    pl.ds(pl.multiple_of(quarter * piece, 16), piece),
                    pl.ds(pl.multiple_of(other * sizes[kind], 128), sizes[kind]),
                ],
                r.heads_buf.at[piece_rows(me, quarter), pl.ds(starts[kind], sizes[kind])],
                r.fetch_send.at[i, kind], r.fetch_recv.at[i, kind], {"shard": other},
            )
            for kind in range(3)
        ]
        for i, other in enumerate(others)
    ]
    for i in (2, 0, 1):
        for copy in fetch[i]:
            copy.start()
    tell_info = [
        remote(
            r.info_buf.at[info_rows], r.info_buf.at[info_rows],
            r.info_send.at[i], r.info_recv.at[i], {"shard": other},
        )
        for i, other in enumerate(others)
    ]
    for copy in tell_info:
        copy.start()

    def pass_piece(i, which, where, index):
        ref = r.heads_buf.at[piece_rows(others[i], which)]
        return remote(ref, ref, r.pass_send.at[index, i], r.pass_recv.at[index, i], where)

    to_chip = [pass_piece(i, quarter, next_chip, 0) for i in range(3)]
    to_twin = [pass_piece(i, quarter, twin, 1) for i in range(3)]
    on_twin = [pass_piece(i, next_quarter, twin, 2) for i in range(3)]

    def half_rows(owner, which):
        return r.all_buf.at[pl.ds(pl.multiple_of(owner * local + which * half, 16), half)]

    def send(owner, which, index, where):
        ref = half_rows(owner, which)
        return remote(ref, ref, r.all_send.at[index], r.all_recv.at[index], where)

    own = [
        [send(me, which, 2 * which + i, where) for i, where in enumerate((x_other, y_other))]
        for which in range(2)
    ]
    on = (send(x_place, 0, 4, y_other), send(y_place, 1, 5, x_other))

    load_tokens.wait()

    def norm_rows(which, index, carry):
        rows = pl.ds(pl.multiple_of(which * half + index * 32, 16), 32)
        values = r.token_buf[rows].astype(f32)
        inv = lax.rsqrt(jnp.mean(values * values, axis=-1, keepdims=True) + norm_eps)
        r.all_buf[pl.ds(pl.multiple_of(me * local + which * half + index * 32, 16), 32)] = (
            values * inv * r.gain[...]
        ).astype(bf16)
        return carry

    for which in range(2):
        lax.fori_loop(0, half // 32, functools.partial(norm_rows, which), 0)
        own[which][which].start()
    for which in range(2):
        own[which][1 - which].start()

    for i in (2, 0, 1):
        for copy in fetch[i]:
            copy.wait_recv()
        to_chip[i].start()
        to_twin[i].start()
    own[0][0].wait_recv()
    on[0].start()
    own[1][1].wait_recv()
    on[1].start()
    for i in (2, 0, 1):
        to_chip[i].wait_recv()
        on_twin[i].start()

    for copy in tell_info:
        copy.wait_recv()
    r.key_info[...] = jnp.transpose(r.info_buf[...].astype(f32))[0:8]
    for copy in load_heads:
        copy.wait()
    for copy in to_twin + on_twin:
        copy.wait_recv()

    wide = r.cols_buf.shape[1]

    def keep_columns(block_of):
        for owner in range(4):

            @pl.when(me == owner)
            def _():
                def rows_of(index, carry):
                    rows = pl.ds(pl.multiple_of(block_of * local + index * half, 16), half)
                    some = r.all_buf[rows, owner * part : (owner + 1) * part]
                    if wide > part:
                        some = jnp.concatenate((some, jnp.zeros((half, wide - part), bf16)), axis=1)
                    r.cols_buf[rows] = some
                    return carry

                lax.fori_loop(0, 2, rows_of, 0)

    def project(owner):
        rows = pl.ds(pl.multiple_of(owner * local, 16), local)
        r.qkv_buf[rows] = dot_plain(r.all_buf[rows], r.heads_buf[...]).astype(bf16)

    project(me)
    own[1][0].wait_recv()
    project(x_place)
    own[0][1].wait_recv()
    project(y_place)
    for owner in (me, x_place, y_place):
        keep_columns(owner)
    for copy in on:
        copy.wait_recv()
    project(far_place)
    keep_columns(far_place)
    keep = [
        pltpu.make_async_copy(r.qkv_buf, r.qkv, r.keep_sem.at[0]),
        pltpu.make_async_copy(r.cols_buf, r.normed_cols, r.keep_sem.at[2]),
    ]
    for copy in keep:
        copy.start()

    def keep_item(item):
        head, rows = item // n_blocks, pl.ds((item % n_blocks) * block, block)
        slot = item % 2
        return [
            pltpu.make_async_copy(r.probs_stage.at[slot], r.probs.at[head, rows], r.stage_sem.at[slot, 0]),
            pltpu.make_async_copy(r.tanh_stage.at[slot], r.tanh.at[head, rows], r.stage_sem.at[slot, 1]),
        ]

    for item in range(heads * n_blocks):
        head, first, slot = item // n_blocks, (item % n_blocks) * block, item % 2
        limit = first + block
        columns = pl.ds(head * HEAD_SIZE, HEAD_SIZE)
        r.score[:, pl.ds(0, limit)] = dot_rows(
            r.qkv_buf[pl.ds(first, block), columns], r.qkv_buf[pl.ds(0, limit), pl.ds(q_cols, k_cols)]
        )
        if item >= 2:
            for copy in keep_item(item - 2):
                copy.wait()
        if limit < tokens:
            nothing = jnp.zeros((block, tokens - limit), f32)
            r.probs_stage[slot, :, pl.ds(limit, tokens - limit)] = nothing
            r.tanh_stage[slot, :, pl.ds(limit, tokens - limit)] = nothing

        def rows_of(index, carry, first=first, limit=limit, slot=slot):
            here = pl.ds(pl.multiple_of(index * 64, 64), 64)
            info = r.info_buf[pl.ds(pl.multiple_of(first + index * 64, 64), 64)].astype(f32)
            keys = r.key_info[3:4, pl.ds(0, limit)]
            query_at = lax.broadcasted_iota(jnp.int32, (64, limit), 0) + (first + index * 64)
            key_at = lax.broadcasted_iota(jnp.int32, (64, limit), 1)
            related = (keys == info[:, 0:1]) | (keys == info[:, 1:2]) | (keys == info[:, 2:3])
            visible = ((key_at <= query_at) & related) | (key_at == query_at)
            curve = jnp.tanh(r.score[here, pl.ds(0, limit)] * (head_scale / softcap))
            masked = jnp.where(visible, softcap * curve, -1e30)
            terms = jnp.exp(masked - jnp.max(masked, axis=-1, keepdims=True))
            probs = terms * (1.0 / jnp.sum(terms, axis=-1, keepdims=True))
            r.tanh_stage[slot, here, pl.ds(0, limit)] = curve
            r.probs_stage[slot, here, pl.ds(0, limit)] = probs
            r.probs_low[here, pl.ds(0, limit)] = probs.astype(bf16)
            return carry

        lax.fori_loop(0, block // 64, rows_of, 0)
        for copy in keep_item(item):
            copy.start()
        r.mixed_buf[pl.ds(first, block), columns] = dot_plain(
            r.probs_low[:, pl.ds(0, limit)],
            r.qkv_buf[pl.ds(0, limit), pl.ds(q_cols + k_cols, k_cols)],
        ).astype(bf16)

    keep.append(pltpu.make_async_copy(r.mixed_buf, r.mixed, r.keep_sem.at[1]))
    keep[2].start()

    for group in fetch + own:
        for copy in group:
            copy.wait_send()
    for copy in list(on) + tell_info + to_chip + to_twin + on_twin:
        copy.wait_send()
    last = heads * n_blocks
    for item in range(max(0, last - 2), last):
        for copy in keep_item(item):
            copy.wait()
    for copy in keep:
        copy.wait()


def attend(collective_id, **args):
    f32, bf16 = jnp.float32, jnp.bfloat16
    given = types.SimpleNamespace(**args)
    local, width = given.tokens.shape
    tokens = 4 * local
    part = given.w_query.shape[0]
    part_wide = -(-part // PAIR) * PAIR
    q_cols, k_cols = given.w_query.shape[1] // 4, given.w_key.shape[1] // 4
    head_cols = q_cols + 2 * k_cols
    heads = q_cols // HEAD_SIZE
    block = min(TILE, tokens)
    vmem, dma, shape = pltpu.VMEM, pltpu.SemaphoreType.DMA, jax.ShapeDtypeStruct
    outs = dict(
        qkv=shape((tokens, head_cols), bf16),
        mixed=shape((tokens, q_cols), bf16),
        probs=shape((heads, tokens, tokens), f32),
        tanh=shape((heads, tokens, tokens), f32),
        normed_cols=shape((tokens, part_wide), bf16),
    )
    scratch = dict(
        token_buf=vmem((local, width), bf16),
        all_buf=vmem((tokens, width), bf16),
        heads_buf=vmem((width, head_cols), bf16),
        info_buf=vmem((tokens, 128), bf16),
        key_info=vmem((8, tokens), f32),
        gain=vmem((1, width), f32),
        qkv_buf=vmem((tokens, head_cols), bf16),
        mixed_buf=vmem((tokens, q_cols), bf16),
        cols_buf=vmem((tokens, part_wide), bf16),
        score=vmem((block, tokens), f32),
        probs_stage=vmem((2, block, tokens), f32),
        tanh_stage=vmem((2, block, tokens), f32),
        probs_low=vmem((block, tokens), bf16),
        load_sem=dma((5,)),
        keep_sem=dma((3,)),
        stage_sem=dma((2, 2)),
        fetch_send=dma((3, 3)),
        fetch_recv=dma((3, 3)),
        info_send=dma((3,)),
        info_recv=dma((3,)),
        pass_send=dma((3, 3)),
        pass_recv=dma((3, 3)),
        all_send=dma((6,)),
        all_recv=dma((6,)),
    )
    any_space = pl.BlockSpec(memory_space=pl.ANY)
    small = pl.BlockSpec(memory_space=pltpu.VMEM)
    results = pl.pallas_call(
        functools.partial(attend_kernel, tuple(args) + tuple(outs) + tuple(scratch)),
        out_shape=list(outs.values()),
        in_specs=[
            pl.BlockSpec(memory_space=pltpu.SMEM) if value.shape[0] == 1
            else small if value.ndim == 1 or value.shape[1] == 128 else any_space
            for value in args.values()
        ],
        out_specs=[any_space] * len(outs),
        scratch_shapes=list(scratch.values()),
        compiler_params=pltpu.CompilerParams(
            collective_id=collective_id, has_side_effects=True, vmem_limit_bytes=VMEM_LIMIT
        ),
        cost_estimate=pl.CostEstimate(
            flops=4 * tokens * width * head_cols, bytes_accessed=100 * 2**20, transcendentals=0
        ),
    )(*args.values())
    return types.SimpleNamespace(**dict(zip(outs, results)))


QUERY_HEADS = 8
KV = 4
HEAD_SIZE = 256
SEGS = 13


softcap = 50.0
norm_eps = 1e-06


def normalize(values, gain_vec):
    inv_rms = lax.rsqrt(jnp.mean(values * values, axis=-1, keepdims=True) + norm_eps)
    return (values * inv_rms * gain_vec, inv_rms)


def norm_back(values, inv_rms, gain_vec, grad_in):
    weighted = grad_in * gain_vec
    row_mean = jnp.mean(weighted * values, axis=-1, keepdims=True)
    grad_back = inv_rms * weighted - values * (inv_rms * inv_rms * inv_rms) * row_mean
    return (grad_back, jnp.sum(grad_in * values * inv_rms, axis=0))


def geglu(gate_pre, up_pre):
    return jax.nn.gelu(gate_pre, approximate=True) * up_pre


def gather_rows(block):
    return lax.all_gather(block, "shard", axis=0, tiled=True)


def scatter_rows(partial):
    summed = lax.psum_scatter(partial, "shard", scatter_dimension=0, tiled=True)
    return summed.astype(jnp.float32)


def exchange(blocks):
    return lax.all_to_all(blocks, "shard", 0, 0, tiled=True)


def first_gather(normed, seg_ids, w_query, w_key, w_value):
    n = lax.axis_size("shard")
    width = normed.shape[1]
    part_rows = w_query.shape[0]
    share = max(1, n // KV)

    def by_device(weight):
        heads = weight.reshape(part_rows, KV, -1)
        if share > 1:
            heads = jnp.repeat(heads, share, axis=1)
        return heads.reshape(part_rows, n, -1)

    parts = jnp.concatenate(
        (w_query.reshape(part_rows, n, -1), by_device(w_key), by_device(w_value)), axis=2
    ).transpose(1, 0, 2)
    heads = exchange(parts).reshape(width, -1)
    codes = gather_rows(seg_ids.astype(jnp.bfloat16))
    return gather_rows(normed), codes.astype(jnp.int32), heads


def rep_sum(grads, width):
    summed = chain_sum([grad.astype(jnp.bfloat16).reshape(-1, width) for grad in grads])
    return [
        total.reshape(grad.shape).astype(jnp.float32) for total, grad in zip(summed, grads)
    ]


def plane_layer(
    tokens, seg_ids, parents, attn_gain, w_query, w_key, w_value, w_out, post_attn_gain,
    ffn_gain, w_gate, w_up, w_down, post_ffn_gain, cotangent,
):
    f32 = jnp.float32
    heads = attend(
        2,
        tokens=tokens,
        attn_gain=attn_gain,
        seg_ids=jnp.broadcast_to(seg_ids[:, None], (tokens.shape[0], 128)),
        parents=parents,
        w_query=w_query,
        w_key=w_key,
        w_value=w_value,
    )
    gains = dict(
        attn_gain=attn_gain,
        post_attn_gain=post_attn_gain,
        ffn_gain=ffn_gain,
        post_ffn_gain=post_ffn_gain,
    )
    ahead = forward(
        3,
        mixed=heads.mixed,
        w_out=w_out,
        tokens=tokens,
        cotangent=cotangent,
        **gains,
        w_gate=w_gate,
        w_up=w_up,
        w_down=w_down,
    )
    found = backward(
        4,
        grad_ffn=ahead.grad_ffn,
        hidden=ahead.hidden,
        gate=ahead.gate,
        up=ahead.up,
        normed_two=ahead.normed_two,
        w_down=w_down,
        w_gate=w_gate,
        w_up=w_up,
        w_out=w_out,
        middle=ahead.middle,
        attn_out=ahead.attn_out,
        cotangent=cotangent,
        **gains,
        gain_parts=ahead.gain_part,
        qkv=heads.qkv,
        mixed=heads.mixed,
        probs=heads.probs,
        tanh=heads.tanh,
        normed_cols=heads.normed_cols,
        w_query=w_query,
        w_key=w_key,
        w_value=w_value,
        tokens=tokens,
    )
    gain_sums = found.gain_sums
    return (
        ahead.output,
        found.grad_tokens,
        gain_sums[3],
        found.query_sum.astype(f32),
        found.key_sum.astype(f32),
        found.value_sum.astype(f32),
        found.out_sum.astype(f32),
        gain_sums[1],
        gain_sums[2],
        found.gate_sum.astype(f32),
        found.up_sum.astype(f32),
        found.down_sum.astype(f32),
        gain_sums[0],
    )


def body(
    tokens,
    seg_ids,
    parents,
    attn_gain,
    w_query,
    w_key,
    w_value,
    w_out,
    post_attn_gain,
    ffn_gain,
    w_gate,
    w_up,
    w_down,
    post_ffn_gain,
    cotangent,
):
    if lax.axis_size("shard") == 4 and lax.axis_size("rep") == 8:
        return plane_layer(
            tokens, seg_ids, parents, attn_gain, w_query, w_key, w_value, w_out, post_attn_gain,
            ffn_gain, w_gate, w_up, w_down, post_ffn_gain, cotangent,
        )
    f32, bf16 = jnp.float32, jnp.bfloat16
    tok_rows, width = tokens.shape
    n = lax.axis_size("shard")
    me = lax.axis_index("shard")
    group_rows = tok_rows * n
    part_rows = w_query.shape[0]
    head_scale = HEAD_SIZE ** (-0.5)
    q_heads = QUERY_HEADS // n
    kv_heads = max(1, KV // n)
    share = n * kv_heads // KV
    repeat = q_heads // kv_heads
    q_cols = q_heads * HEAD_SIZE
    k_cols = kv_heads * HEAD_SIZE
    gain_one = attn_gain.astype(f32)
    gain_two = post_attn_gain.astype(f32)
    gain_three = ffn_gain.astype(f32)
    gain_four = post_ffn_gain.astype(f32)

    residual = tokens.astype(f32)
    normed, rms_one = normalize(residual, gain_one)
    normed_all, codes, qkv_heads = first_gather(
        normed.astype(bf16), seg_ids, w_query, w_key, w_value
    )
    qkv = jnp.dot(normed_all, qkv_heads, preferred_element_type=f32).astype(bf16)
    queries = qkv[:, :q_cols].reshape(group_rows, kv_heads, repeat, HEAD_SIZE)
    keys = qkv[:, q_cols : q_cols + k_cols].reshape(group_rows, kv_heads, HEAD_SIZE)
    values = qkv[:, q_cols + k_cols :].reshape(group_rows, kv_heads, HEAD_SIZE)

    parent_row = parents[0]
    labels = jnp.arange(SEGS)

    def lookup(ident):
        return jnp.sum(jnp.where(ident[:, None] == labels[None, :], parent_row[None, :], 0), axis=1)

    parent_one = lookup(codes)
    parent_two = lookup(parent_one)
    positions = jnp.arange(group_rows)
    real = codes < SEGS
    related = (
        (codes[None, :] == codes[:, None])
        | (codes[None, :] == parent_one[:, None])
        | (codes[None, :] == parent_two[:, None])
    )
    visible = (positions[None, :] <= positions[:, None]) & real[:, None] & real[
        None, :
    ] & related | (positions[None, :] == positions[:, None])

    score_matrix = jnp.einsum("tkrh,skh->krts", queries, keys, preferred_element_type=f32)
    tanh_part = jnp.tanh(score_matrix * (head_scale / softcap))
    masked = jnp.where(visible[None, None], softcap * tanh_part, -1e30)
    row_max = jnp.max(masked, axis=-1, keepdims=True)
    expo_terms = jnp.exp(masked - row_max)
    row_total = jnp.sum(expo_terms, axis=-1, keepdims=True)
    probs = expo_terms / row_total
    probs_b = probs.astype(bf16)
    mixed = jnp.einsum("krts,skh->tkrh", probs_b, values, preferred_element_type=f32)
    mixed = mixed.reshape(group_rows, q_cols).astype(bf16)
    attn_out = scatter_rows(jnp.dot(mixed, w_out, preferred_element_type=f32).astype(bf16))
    post_one, rms_two = normalize(attn_out, gain_two)
    middle = residual + post_one
    normed_two, rms_three = normalize(middle, gain_three)
    normed_two_all = gather_rows(normed_two.astype(bf16))
    gate_pre = jnp.dot(normed_two_all, w_gate, preferred_element_type=f32)
    up_pre = jnp.dot(normed_two_all, w_up, preferred_element_type=f32)
    hidden, geglu_back = jax.vjp(geglu, gate_pre, up_pre)
    hidden_b = hidden.astype(bf16)
    ffn_out = scatter_rows(jnp.dot(hidden_b, w_down, preferred_element_type=f32).astype(bf16))
    post_two, rms_four = normalize(ffn_out, gain_four)
    output = (middle + post_two).astype(bf16)

    grad_out = cotangent.astype(f32)
    grad_ffn, grad_gain_four = norm_back(ffn_out, rms_four, gain_four, grad_out)
    grad_ffn_all = gather_rows(grad_ffn.astype(bf16))
    down_part = jnp.einsum("tf,td->fd", hidden_b, grad_ffn_all, preferred_element_type=f32)
    grad_hidden = jnp.einsum("td,fd->tf", grad_ffn_all, w_down, preferred_element_type=f32)
    grad_gate, grad_up = geglu_back(grad_hidden)
    grad_gate_b = grad_gate.astype(bf16)
    grad_up_b = grad_up.astype(bf16)
    grad_normed_two = jnp.einsum("tf,df->td", grad_gate_b, w_gate, preferred_element_type=f32)
    grad_normed_two += jnp.einsum("tf,df->td", grad_up_b, w_up, preferred_element_type=f32)
    grad_normed_two = scatter_rows(grad_normed_two.astype(bf16))
    gate_part = jnp.einsum("td,tf->df", normed_two_all, grad_gate_b, preferred_element_type=f32)
    up_part = jnp.einsum("td,tf->df", normed_two_all, grad_up_b, preferred_element_type=f32)
    grad_middle_part, grad_gain_three = norm_back(middle, rms_three, gain_three, grad_normed_two)
    grad_middle = grad_out + grad_middle_part
    grad_attn, grad_gain_two = norm_back(attn_out, rms_two, gain_two, grad_middle)
    grad_attn_all = gather_rows(grad_attn.astype(bf16))
    out_part = jnp.einsum("tj,td->jd", mixed, grad_attn_all, preferred_element_type=f32)
    grad_mixed = jnp.einsum("td,jd->tj", grad_attn_all, w_out, preferred_element_type=f32)
    grad_mixed = grad_mixed.astype(bf16).reshape(group_rows, kv_heads, repeat, HEAD_SIZE)
    grad_probs = jnp.einsum("tkrh,skh->krts", grad_mixed, values, preferred_element_type=f32)
    row_inner = jnp.sum(probs * grad_probs, axis=-1, keepdims=True)
    grad_dots = (
        probs * (grad_probs - row_inner) * (1.0 - tanh_part * tanh_part) * head_scale
    ).astype(bf16)
    grad_queries = jnp.einsum("krts,skh->tkrh", grad_dots, keys, preferred_element_type=f32)
    grad_keys = jnp.einsum("krts,tkrh->skh", grad_dots, queries, preferred_element_type=f32)
    grad_values = jnp.einsum("krts,tkrh->skh", probs_b, grad_mixed, preferred_element_type=f32)
    grad_parts = jnp.concatenate(
        (
            grad_queries.reshape(group_rows, q_cols),
            grad_keys.reshape(group_rows, k_cols),
            grad_values.reshape(group_rows, k_cols),
        ),
        axis=1,
    ).astype(bf16)
    grad_parts = gather_rows(grad_parts).reshape(n, group_rows, -1)

    def whole_heads(parts):
        if share > 1:
            parts = parts.reshape(KV, share, group_rows, HEAD_SIZE).astype(f32).sum(axis=1).astype(bf16)
        return parts.transpose(1, 0, 2).reshape(group_rows, -1)

    grad_qkv = jnp.concatenate(
        (
            grad_parts[:, :, :q_cols].transpose(1, 0, 2).reshape(group_rows, -1),
            whole_heads(grad_parts[:, :, q_cols : q_cols + k_cols]),
            whole_heads(grad_parts[:, :, q_cols + k_cols :]),
        ),
        axis=1,
    )
    qkv_local = jnp.concatenate((w_query, w_key, w_value), axis=1)
    grad_normed = jnp.einsum("tj,dj->td", grad_qkv, qkv_local, preferred_element_type=f32)
    grad_normed = exchange(grad_normed.astype(bf16).reshape(n, tok_rows, part_rows))
    grad_normed = grad_normed.transpose(1, 0, 2).reshape(tok_rows, width).astype(f32)
    normed_cols = lax.dynamic_slice_in_dim(normed_all, me * part_rows, part_rows, axis=1)
    qkv_part = jnp.einsum("td,tj->dj", normed_cols, grad_qkv, preferred_element_type=f32)
    grad_resid_part, grad_gain_one = norm_back(residual, rms_one, gain_one, grad_normed)
    grad_tokens = (grad_middle + grad_resid_part).astype(bf16)
    gain_parts = jnp.stack((grad_gain_one, grad_gain_two, grad_gain_three, grad_gain_four))
    gain_sums = lax.all_gather(gain_parts, ("rep", "shard"), axis=0).sum(axis=0)
    down_sum, gate_sum, up_sum, out_sum, qkv_sum = rep_sum(
        (down_part, gate_part, up_part, out_part, qkv_part), width
    )
    q_width = w_query.shape[1]
    k_width = w_key.shape[1]
    return (
        output,
        grad_tokens,
        gain_sums[0],
        qkv_sum[:, :q_width],
        qkv_sum[:, q_width : q_width + k_width],
        qkv_sum[:, q_width + k_width :],
        out_sum,
        gain_sums[1],
        gain_sums[2],
        gate_sum,
        up_sum,
        down_sum,
        gain_sums[3],
    )


def solution(mesh):
    return jax.shard_map(
        body,
        mesh=mesh,
        in_specs=(
            P(("rep", "shard"), None),
            P(("rep", "shard")),
            P("rep", None),
            P(),
            P("shard", None),
            P("shard", None),
            P("shard", None),
            P("shard", None),
            P(),
            P(),
            P(None, "shard"),
            P(None, "shard"),
            P("shard", None),
            P(),
            P(("rep", "shard"), None),
        ),
        out_specs=(
            P(("rep", "shard"), None),
            P(("rep", "shard"), None),
            P(),
            P("shard", None),
            P("shard", None),
            P("shard", None),
            P("shard", None),
            P(),
            P(),
            P(None, "shard"),
            P(None, "shard"),
            P("shard", None),
            P(),
        ),
        check_vma=False,
    )
```
